32 devices in a mesh: groups: 2 (over y), adapter: 4 (over z), mp: 4 (over x, core).
Axes of the slice: x: 2, y: 2, z: 4, core: 2. Of those that a mesh axis runs over, the one named last changes fastest.
Arguments:
- tokens: bfloat16 [3072, 8192], P(('groups', 'adapter'), 'mp'), parts along dimension 0, may hold values from -6 to 6
- base_key_weight: bfloat16 [8192, 512], P('mp'), may hold values from -0.0625 to 0.0625
- stacked_down_weight: bfloat16 [8192, 1024], P('mp', 'adapter'), may hold values from -0.0625 to 0.0625
- stacked_up_weight: bfloat16 [1024, 512], P('adapter', 'mp'), may hold values from -1.5 to 1.5
- request_adapter_owner: int32 [3072, 1], P(('groups', 'adapter')), parts along dimension 0, may hold values from 0 to 3; in each aligned block of 384 rows (0 to 383, 384 to 767, ...) at most 144 rows name the same one
- request_adapter_slot: int32 [3072], P(('groups', 'adapter')), parts along dimension 0, may hold values from 0 to 15
Outputs:
- keys_out: bfloat16 [3072, 512], P(('groups', 'adapter'), 'mp'), parts along dimension 0
The draws below stay inside these ranges and needn't reach their ends.
There are 2 independent parts, one for each index of `groups`. The reference program is written for one: setup_inputs(seed, part) draws one part's arguments, and reference() takes and returns one part's arrays. A program takes and returns all parts, laid end to end along the dimension named above; an argument that names none is the same for every part. Nothing has to cross between parts.
Inputs may be any that keep to these rules, and one draw needn't show every extreme that they name: `request_adapter_owner`: in each aligned block of 384 rows (the rows of one device) at most 144 rows name the same owner, a bound that some block reaches.
All inputs are finite; a program needn't handle non-finite values.
Results may differ from the reference program's by a relative error of at most 0.0054.
Values may be sent and summed in bfloat16 or wider, within the bound.
No kernel may reach another device: no remote copies, remote signals or barrier semaphores. Data moves between devices by JAX's collectives and lax.ppermute only.
A program may use at most 64 MiB of HBM per device.

```python
import math
import jax
import jax.numpy as jnp
import numpy as np
from jax import lax

MODEL_WIDTH = 8192
KEY_FEATURES = 512
ADAPTER_RANK = 16
AD_DEV = 16
TOK_DEV = 384
ADAPTER_TOTAL = 64
TOKENS = 1536
CAP = 144
N_ADAPTER = 4


def with_ends(array, stream_key, low, top_value):
    longest = array.shape.index(max(array.shape))
    spots = []
    for shift in (0, 1):
        where = [jax.random.randint(jax.random.fold_in(stream_key, axis), (), 0, length) for axis, length in enumerate(array.shape)]
        where[longest] = (where[longest] + shift) % array.shape[longest]
        spots.append(tuple(where))
    return array.at[spots[0]].set(low).at[spots[1]].set(top_value)


def levels(own_key, extent, cuts, low, largest):
    def one(position, blocks):
        draws = jax.random.uniform(jax.random.fold_in(jax.random.fold_in(own_key, 6), position), (blocks,), jnp.float32, low / len(cuts), largest / len(cuts))
        return jnp.repeat(jnp.exp(draws), extent[position] // blocks).reshape((-1,) + (1,) * (len(extent) - position - 1))

    factor_of = one(*cuts[0])
    for cut in cuts[1:]:
        factor_of = factor_of * one(*cut)
    return factor_of


def assign_block(own_key, own, number, rows, amount, top, reach, lean):
    order = jax.random.permutation(own_key, amount)
    heavy_load, ordinary = shares(amount, rows * top, reach, lean, True), shares(amount, rows * top, reach, lean, False)
    places = jnp.arange(amount)

    def named(sizes, turn):
        used = int((sizes > 0).sum())
        fixed = max(1, used // 4)
        passed = fixed + (places - fixed + turn * (used - fixed)) % max(1, amount - fixed)
        return jnp.zeros((amount,), jnp.int32).at[order[jnp.where(places < fixed, places, passed)]].set(jnp.asarray(sizes, jnp.int32))

    sizes = jnp.where(number % 4 == 0, named(heavy_load, number // 4), named(ordinary, number - number // 4 - 1))
    mixed = jax.random.permutation(jax.random.fold_in(own, 3), amount)
    giver, taker = mixed[0:amount // 2 * 2:2], mixed[1:amount // 2 * 2:2]
    margin = jnp.minimum(sizes[giver] - 1, reach - sizes[taker]) // 2
    margin = jnp.where((giver == order[0]) | (taker == order[0]) | (sizes[taker] == 0), 0, jnp.maximum(margin, 0))
    passed = jax.random.randint(jax.random.fold_in(own, 4), (amount // 2,), 0, 1 << 20) % (margin + 1)
    sizes = sizes.at[giver].add(-passed).at[taker].add(passed)
    members = jnp.searchsorted(jnp.cumsum(sizes), jnp.arange(rows * top), side="right").astype(jnp.int32)
    listing = members.reshape(top, rows).T
    listing = listing[jax.random.permutation(jax.random.fold_in(own, 1), rows)]
    turn = jax.random.randint(jax.random.fold_in(own, 2), (rows, 1), 0, top)
    return jnp.take_along_axis(listing, (jnp.arange(top)[None, :] + turn) % top, axis=1)


def shares(count, total, bound, slope, full):
    portions = [(1 << 20) // math.isqrt(rank ** slope) + 1 for rank in range(1, count + 1)]
    largest = bound if full else min(bound, max(-(-total // count), total * portions[0] // sum(portions)))
    least = 1 if total - largest >= count - 1 else 0
    counts, surplus = [largest] + [least] * (count - 1), total - largest - least * (count - 1)
    while surplus > 0:
        candidates = [i for i in range(1, count) if counts[i] < largest] or [i for i in range(1, count) if counts[i] < bound]
        mass, budget = sum([portions[i] for i in candidates]), surplus
        for i in candidates:
            extra = min(bound - counts[i], max(1, budget * portions[i] // mass), surplus)
            counts[i] = counts[i] + extra
            surplus = surplus - extra
    return np.array(counts)


def centred(own_key, dims, spread, bound, cuts=(), held_as=jnp.bfloat16):
    gain = levels(own_key, dims, cuts, -0.22, 0.18) if cuts else 1.0
    drawn = jax.random.normal(own_key, dims, jnp.float32) * spread * gain
    return jnp.minimum(jnp.maximum(drawn, -bound), bound).astype(held_as)


def setup_inputs(seed: int = 0, part: int = 0) -> dict:
    splits = jax.random.split(jax.random.key(seed), 7)
    part_keys = jax.random.split(jax.random.fold_in(splits[6], part), 7)
    tokens = centred(part_keys[0], (TOKENS, MODEL_WIDTH), 1.0, 6.0, ((0, 4), (1, 4)))
    base_key_weight = centred(splits[1], (MODEL_WIDTH, KEY_FEATURES), MODEL_WIDTH ** -0.5, 0.0625, ((0, 4),))
    stacked_down_weight = centred(splits[2], (MODEL_WIDTH, ADAPTER_TOTAL * ADAPTER_RANK), MODEL_WIDTH ** -0.5, 0.0625, ((0, 4), (1, 4)))
    stacked_up_weight = centred(splits[3], (ADAPTER_TOTAL * ADAPTER_RANK, KEY_FEATURES), ADAPTER_RANK ** -0.5, 1.5, ((0, 4), (1, 4)))
    request_adapter_owner_keys = jax.random.split(jax.random.fold_in(part_keys[4], 1), TOKENS // TOK_DEV)
    request_adapter_owner_turns = jax.random.permutation(jax.random.fold_in(part_keys[4], 3), TOKENS // TOK_DEV)
    request_adapter_owner = jax.vmap(lambda own, number: assign_block(jax.random.fold_in(part_keys[4], 2), own, number, TOK_DEV, N_ADAPTER, 1, CAP, 2))(request_adapter_owner_keys, request_adapter_owner_turns).reshape((TOKENS, 1))
    request_adapter_slot = with_ends(jax.random.randint(part_keys[5], (TOKENS,), 0, AD_DEV), jax.random.fold_in(part_keys[5], 1), 0, AD_DEV - 1).astype(jnp.int32)
    return dict(tokens=tokens, base_key_weight=base_key_weight, stacked_down_weight=stacked_down_weight, stacked_up_weight=stacked_up_weight, request_adapter_owner=request_adapter_owner, request_adapter_slot=request_adapter_slot)


ADAPTER_SCALE = 2.0


def reference(tokens, base_key_weight, stacked_down_weight, stacked_up_weight, request_adapter_owner, request_adapter_slot):
    adapter_ids = (request_adapter_owner.reshape(-1) * AD_DEV + request_adapter_slot).astype(jnp.int32)
    base_output = jnp.dot(tokens, base_key_weight, preferred_element_type=jnp.float32)
    down_projection_rows = stacked_down_weight.T.reshape(ADAPTER_TOTAL, ADAPTER_RANK, MODEL_WIDTH)
    up_projection_rows = stacked_up_weight.reshape(ADAPTER_TOTAL, ADAPTER_RANK, KEY_FEATURES)

    def one_block(inputs):
        block_rows, block_ids = inputs
        down_taken = down_projection_rows[block_ids].astype(jnp.float32)
        shrunk = jnp.einsum("td,trd->tr", block_rows.astype(jnp.float32), down_taken)
        shrunk_bf = lax.optimization_barrier(shrunk.astype(jnp.bfloat16))
        up_taken = up_projection_rows[block_ids].astype(jnp.float32)
        adapter_updates = jnp.einsum("tr,trk->tk", shrunk_bf.astype(jnp.float32), up_taken)
        return adapter_updates.astype(jnp.bfloat16)

    blocks = TOKENS // TOK_DEV
    adapter_updates = lax.map(one_block, (tokens.reshape(blocks, TOK_DEV, MODEL_WIDTH), adapter_ids.reshape(blocks, TOK_DEV)))
    adapter_updates = adapter_updates.reshape(TOKENS, KEY_FEATURES)
    return (base_output + ADAPTER_SCALE * adapter_updates.astype(jnp.float32)).astype(jnp.bfloat16)
```

```python
import jax
import jax.numpy as jnp
from jax import lax
from jax.sharding import PartitionSpec as P

ADAPTER_RANK = 16


ADAPTER_SCALE = 2.0


def dispatch(
    tokens,
    base_key_weight,
    stacked_down_weight,
    stacked_up_weight,
    request_adapter_owner,
    request_adapter_slot,
):
    rows_here = tokens.shape[0]
    feature_share = tokens.shape[1]
    owner_count = lax.axis_size("adapter")
    capacity = max(2, 3 * rows_here // (2 * owner_count))
    local_adapters = stacked_down_weight.shape[1] // ADAPTER_RANK
    key_output_share = stacked_up_weight.shape[1]
    owners = request_adapter_owner.reshape(-1)
    onehot = (owners[:, None] == jnp.arange(owner_count, dtype=jnp.int32)[None, :]).astype(
        jnp.int32
    )
    before = jnp.sum((jnp.cumsum(onehot, axis=0) - onehot) * onehot, axis=1)
    places = owners * capacity + before
    send_rows = (
        jnp.zeros((owner_count * capacity, feature_share), jnp.bfloat16).at[places].set(tokens)
    )
    send_rows = send_rows.reshape(owner_count, capacity, feature_share)
    send_slots = (
        jnp.full((owner_count * capacity,), -1, jnp.int32).at[places].set(request_adapter_slot)
    )
    send_slots = send_slots.reshape(owner_count, capacity)
    input_rows = lax.all_to_all(send_rows, "adapter", split_axis=0, concat_axis=0, tiled=True)
    slots_in = lax.all_to_all(send_slots, "adapter", split_axis=0, concat_axis=0, tiled=True)
    key_projection_output = jnp.einsum(
        "rzq,qt->rzt", input_rows, stacked_down_weight, preferred_element_type=jnp.float32
    )
    key_projection_output = key_projection_output.reshape(
        input_rows.shape[0], input_rows.shape[1], local_adapters, ADAPTER_RANK
    )
    chosen = slots_in[:, :, None] == jnp.arange(local_adapters, dtype=jnp.int32)[None, None, :]
    partial_low = jnp.sum(jnp.where(chosen[:, :, :, None], key_projection_output, 0.0), axis=2)
    shrunk = lax.psum(partial_low, "mp")
    shrunk_bf = shrunk.astype(jnp.bfloat16)
    returned = lax.all_to_all(shrunk_bf, "adapter", split_axis=0, concat_axis=0, tiled=True)
    low_rows = returned.reshape(owner_count * capacity, ADAPTER_RANK)[places]
    gathered_up_weight = lax.all_gather(stacked_up_weight, "adapter", axis=0, tiled=True)
    adapter_ids = owners * local_adapters + request_adapter_slot
    up_taken = gathered_up_weight.reshape(-1, ADAPTER_RANK, key_output_share)[adapter_ids]
    adapter_updates = jnp.einsum(
        "tr,trk->tk", low_rows, up_taken, preferred_element_type=jnp.float32
    ).astype(jnp.bfloat16)
    base_output_share = lax.psum_scatter(
        lax.dot_general(
            base_key_weight, tokens, (((0,), (1,)), ((), ())), preferred_element_type=jnp.float32
        ),
        "mp",
        scatter_dimension=0,
        tiled=True,
    )
    return (base_output_share.T + ADAPTER_SCALE * adapter_updates.astype(jnp.float32)).astype(
        jnp.bfloat16
    )


AXES = ("groups", "adapter", "mp")


def mesh_shift(x, group_step, mp_step):
    groups, owners, shares = (lax.axis_size(name) for name in AXES)

    def number(g, a, m):
        return (g * owners + a) * shares + m

    pairs = [
        (number(g, a, m), number((g + group_step) % groups, a, (m + mp_step) % shares))
        for g in range(groups)
        for a in range(owners)
        for m in range(shares)
    ]
    return lax.ppermute(x, AXES, pairs)


def gather(
    tokens,
    base_key_weight,
    stacked_down_weight,
    stacked_up_weight,
    request_adapter_owner,
    request_adapter_slot,
):
    rows, features = tokens.shape
    groups, owner_count, shares = (lax.axis_size(name) for name in AXES)
    g, a, m = (lax.axis_index(name) for name in AXES)
    columns = stacked_down_weight.shape[1]
    keys = stacked_up_weight.shape[1]
    part = features // groups
    owner = request_adapter_owner.reshape(1, rows)
    slot = request_adapter_slot.reshape(1, rows)

    half = columns // keys
    up_rows = columns // half
    up_wide = jnp.concatenate(
        [stacked_up_weight[i * up_rows : (i + 1) * up_rows] for i in range(half)], axis=1
    )
    down_own = lax.dynamic_slice(stacked_down_weight, (g * part, 0), (part, columns))
    cut = part // 2
    pieces = [jnp.concatenate([up_wide, down_own[:cut]], axis=0), down_own[cut:]]

    blocks = [(a, pieces)]
    forward, backward = pieces, pieces
    for d in range(1, owner_count):
        ahead = [(i, i + 1) for i in range(d - 1, owner_count - 1)]
        back = [(i + 1, i) for i in range(0, owner_count - d)]
        forward = [lax.ppermute(piece, "adapter", ahead) for piece in forward]
        backward = [lax.ppermute(piece, "adapter", back) for piece in backward]
        blocks.append((a - d, forward))
        blocks.append((a + d, backward))

    token_parts, owner_parts, slot_parts = [], [], []
    for step in range(groups):
        wanted = (g + step) % groups
        mine = lax.dynamic_slice(tokens, (0, wanted * part), (rows, part))
        if step:
            token_parts.append(mesh_shift(mine, step, 0))
            ids = mesh_shift(jnp.concatenate([owner, slot], axis=0), step, 0)
            owner_parts.append(ids[:1])
            slot_parts.append(ids[1:])
        else:
            token_parts.append(mine)
            owner_parts.append(owner)
            slot_parts.append(slot)
    all_tokens = jnp.concatenate(token_parts, axis=0)
    all_owner = jnp.concatenate(owner_parts, axis=1)
    all_slot = jnp.concatenate(slot_parts, axis=1)

    base_part = jnp.dot(tokens, base_key_weight, preferred_element_type=jnp.float32)
    base = lax.dynamic_slice(base_part, (0, m * keys), (rows, keys))
    for step in range(1, shares):
        block = lax.dynamic_slice(base_part, (0, (m + step) % shares * keys), (rows, keys))
        base = base + mesh_shift(block, 0, step)

    contract = (((0,), (1,)), ((), ()))
    picked = jnp.zeros((columns, groups * rows), jnp.float32)
    for number, (first, second) in blocks:
        wide = lax.dot_general(
            first[up_rows:], all_tokens[:, :cut], contract, preferred_element_type=jnp.float32
        ) + lax.dot_general(
            second, all_tokens[:, cut:], contract, preferred_element_type=jnp.float32
        )
        picked = jnp.where(all_owner == number, wide, picked)
    adapter = lax.broadcasted_iota(jnp.int32, (columns, 1), 0) // ADAPTER_RANK
    picked = jnp.where(adapter == all_slot, picked, 0.0)
    low = jnp.sum(picked.reshape(-1, ADAPTER_RANK, groups * rows), axis=0)

    shrunk = low[:, :rows]
    for group_step in range(groups):
        mine = low[:, group_step * rows : (group_step + 1) * rows]
        for mp_step in range(shares):
            if group_step or mp_step:
                shrunk = shrunk + mesh_shift(mine, -group_step, mp_step)

    shrunk_bf = shrunk.astype(jnp.bfloat16)
    spread = jnp.concatenate([shrunk_bf] * (columns // ADAPTER_RANK), axis=0)
    spread = jnp.where(adapter == slot, spread, jnp.bfloat16(0))
    updates = jnp.zeros((rows, keys), jnp.float32)
    for number, (first, _) in blocks:
        up = jnp.concatenate(
            [first[:up_rows, i * keys : (i + 1) * keys] for i in range(half)], axis=0
        )
        chosen = jnp.where(owner == number, spread, jnp.bfloat16(0))
        updates = updates + lax.dot_general(
            chosen, up, (((0,), (0,)), ((), ())), preferred_element_type=jnp.float32
        )
    updates = updates.astype(jnp.bfloat16).astype(jnp.float32)
    return (base + ADAPTER_SCALE * updates).astype(jnp.bfloat16)


def local(*args):
    rows, columns = args[0].shape[0], args[2].shape[1]
    capacity = max(2, 3 * rows // (2 * lax.axis_size("adapter")))
    travels = columns <= lax.axis_size("groups") * capacity
    return (gather if travels else dispatch)(*args)


def solution(mesh):
    placed = (
        P(("groups", "adapter"), "mp"),
        P("mp", None),
        P("mp", "adapter"),
        P("adapter", "mp"),
        P(("groups", "adapter"), None),
        P(("groups", "adapter")),
    )
    return jax.shard_map(
        local, mesh=mesh, in_specs=placed, out_specs=P(("groups", "adapter"), "mp"), check_vma=False
    )
```

```python
import functools

import jax
import jax.numpy as jnp
from jax import lax
from jax.experimental import pallas as pl
from jax.experimental.pallas import tpu as pltpu
from jax.sharding import PartitionSpec as P

ADAPTER_RANK = 16


ADAPTER_SCALE = 2.0


def dispatch(
    tokens,
    base_key_weight,
    stacked_down_weight,
    stacked_up_weight,
    request_adapter_owner,
    request_adapter_slot,
):
    rows_here = tokens.shape[0]
    feature_share = tokens.shape[1]
    owner_count = lax.axis_size("adapter")
    capacity = max(2, 3 * rows_here // (2 * owner_count))
    local_adapters = stacked_down_weight.shape[1] // ADAPTER_RANK
    key_output_share = stacked_up_weight.shape[1]
    owners = request_adapter_owner.reshape(-1)
    onehot = (owners[:, None] == jnp.arange(owner_count, dtype=jnp.int32)[None, :]).astype(
        jnp.int32
    )
    before = jnp.sum((jnp.cumsum(onehot, axis=0) - onehot) * onehot, axis=1)
    places = owners * capacity + before
    send_rows = (
        jnp.zeros((owner_count * capacity, feature_share), jnp.bfloat16).at[places].set(tokens)
    )
    send_rows = send_rows.reshape(owner_count, capacity, feature_share)
    send_slots = (
        jnp.full((owner_count * capacity,), -1, jnp.int32).at[places].set(request_adapter_slot)
    )
    send_slots = send_slots.reshape(owner_count, capacity)
    input_rows = lax.all_to_all(send_rows, "adapter", split_axis=0, concat_axis=0, tiled=True)
    slots_in = lax.all_to_all(send_slots, "adapter", split_axis=0, concat_axis=0, tiled=True)
    key_projection_output = jnp.einsum(
        "rzq,qt->rzt", input_rows, stacked_down_weight, preferred_element_type=jnp.float32
    )
    key_projection_output = key_projection_output.reshape(
        input_rows.shape[0], input_rows.shape[1], local_adapters, ADAPTER_RANK
    )
    chosen = slots_in[:, :, None] == jnp.arange(local_adapters, dtype=jnp.int32)[None, None, :]
    partial_low = jnp.sum(jnp.where(chosen[:, :, :, None], key_projection_output, 0.0), axis=2)
    shrunk = lax.psum(partial_low, "mp")
    shrunk_bf = shrunk.astype(jnp.bfloat16)
    returned = lax.all_to_all(shrunk_bf, "adapter", split_axis=0, concat_axis=0, tiled=True)
    low_rows = returned.reshape(owner_count * capacity, ADAPTER_RANK)[places]
    gathered_up_weight = lax.all_gather(stacked_up_weight, "adapter", axis=0, tiled=True)
    adapter_ids = owners * local_adapters + request_adapter_slot
    up_taken = gathered_up_weight.reshape(-1, ADAPTER_RANK, key_output_share)[adapter_ids]
    adapter_updates = jnp.einsum(
        "tr,trk->tk", low_rows, up_taken, preferred_element_type=jnp.float32
    ).astype(jnp.bfloat16)
    base_output_share = lax.psum_scatter(
        lax.dot_general(
            base_key_weight, tokens, (((0,), (1,)), ((), ())), preferred_element_type=jnp.float32
        ),
        "mp",
        scatter_dimension=0,
        tiled=True,
    )
    return (base_output_share.T + ADAPTER_SCALE * adapter_updates.astype(jnp.float32)).astype(
        jnp.bfloat16
    )


AXES = ("groups", "adapter", "mp")
ID_ROWS = 16


def mesh_shift(x, group_step, mp_step):
    groups, owners, shares = (lax.axis_size(name) for name in AXES)

    def number(g, a, m):
        return (g * owners + a) * shares + m

    pairs = [
        (number(g, a, m), number((g + group_step) % groups, a, (m + mp_step) % shares))
        for g in range(groups)
        for a in range(owners)
        for m in range(shares)
    ]
    return lax.ppermute(x, AXES, pairs)


def whole(body, outs, *operands, **params):
    spec = pl.BlockSpec(memory_space=pltpu.VMEM)
    return pl.pallas_call(
        body,
        out_shape=outs,
        in_specs=[spec] * len(operands),
        out_specs=jax.tree.map(lambda _: spec, outs),
        compiler_params=pltpu.CompilerParams(vmem_limit_bytes=40 * 1024 * 1024),
        **params,
    )(*operands)


def base_body(keys, tokens, weights, out):
    wide = jnp.dot(tokens[...], weights[...], preferred_element_type=jnp.float32)
    for k in range(out.shape[0]):
        out[k] = wide[:, k * keys : (k + 1) * keys]


def shrink_body(distances, cuts, rows, first, last, *refs):
    groups, shares = lax.axis_size("groups"), lax.axis_size("mp")
    a, g = lax.axis_index("adapter"), lax.axis_index("groups")
    token_refs, rest = refs[:groups], refs[groups:]
    picked_in = None
    if not first:
        picked_in, rest = rest[0], rest[1:]
    blocks, out = rest[:-1], rest[-1]
    columns = blocks[0].shape[1]
    eye = (
        lax.broadcasted_iota(jnp.int32, (ID_ROWS, ID_ROWS), 0)
        == lax.broadcasted_iota(jnp.int32, (ID_ROWS, ID_ROWS), 1)
    ).astype(jnp.bfloat16)
    for part, tokens in enumerate(token_refs):
        ids = lax.dot_general(
            tokens[rows : rows + ID_ROWS, :rows],
            eye,
            (((0,), (0,)), ((), ())),
            preferred_element_type=jnp.float32,
        )
        owner, slot = ids[:, 0:1], ids[:, 1:2]
        picked = jnp.zeros((rows, columns), jnp.float32) if first else picked_in[part]
        for i, distance in enumerate(distances):
            wide = None
            for p, (start, stop) in enumerate(cuts):
                term = jnp.dot(
                    tokens[:rows, start:stop],
                    blocks[i * len(cuts) + p][: stop - start],
                    preferred_element_type=jnp.float32,
                )
                wide = term if wide is None else wide + term
            picked = jnp.where(owner == (a + distance).astype(jnp.float32), wide, picked)
        if not last:
            out[part] = picked
            continue
        column = lax.broadcasted_iota(jnp.int32, (rows, columns), 1)
        adapter = (column // ADAPTER_RANK).astype(jnp.float32)
        picked = jnp.where(adapter == slot, picked, 0.0)
        lanes = 128
        folded = picked[:, :lanes]
        for k in range(1, columns // lanes):
            folded = folded + picked[:, k * lanes : (k + 1) * lanes]
        turned = folded.T
        low = turned[:ADAPTER_RANK]
        for k in range(1, lanes // ADAPTER_RANK):
            low = low + turned[k * ADAPTER_RANK : (k + 1) * ADAPTER_RANK]
        target = lax.rem(g + part, groups) * shares
        for m in range(shares):
            out[target + m] = low


def ups_body(distances, up_start, own, *refs):
    a, owners = lax.axis_index("adapter"), lax.axis_size("adapter")
    blocks, out = refs[:-1], refs[-1]
    rows, keys = own.shape
    out[pl.ds(pl.multiple_of(a * rows, rows), rows), :] = own[...]
    for distance, block in zip(distances, blocks):
        number = a + distance

        @pl.when((number >= 0) & (number < owners))
        def _():
            taken = block[up_start:, :]
            count = taken.shape[1] // keys
            size = rows // count
            for k in range(count):
                start = pl.multiple_of(number * rows + k * size, size)
                out[pl.ds(start, size), :] = taken[:, k * keys : (k + 1) * keys]


def finish_body(parts, bases, ids, ups, out):
    shrunk = parts[0]
    for k in range(1, parts.shape[0]):
        shrunk = shrunk + parts[k]
    base = bases[0]
    for k in range(1, bases.shape[0]):
        base = base + bases[k]
    rank_total = ups.shape[0]
    column = lax.broadcasted_iota(jnp.int32, (ADAPTER_RANK, rank_total), 1)
    row = lax.broadcasted_iota(jnp.int32, (ADAPTER_RANK, rank_total), 0)
    repeat = (lax.rem(column, ADAPTER_RANK) == row).astype(jnp.bfloat16)
    spread = lax.dot_general(
        shrunk.astype(jnp.bfloat16),
        repeat,
        (((0,), (0,)), ((), ())),
        preferred_element_type=jnp.float32,
    )
    adapter = lax.broadcasted_iota(jnp.int32, spread.shape, 1) // ADAPTER_RANK
    spread = jnp.where(adapter == ids[...], spread, 0.0).astype(jnp.bfloat16)
    updates = jnp.dot(spread, ups[...], preferred_element_type=jnp.float32)
    updates = updates.astype(jnp.bfloat16).astype(jnp.float32)
    out[...] = (base + ADAPTER_SCALE * updates).astype(jnp.bfloat16)


def gather(
    tokens,
    base_key_weight,
    stacked_down_weight,
    stacked_up_weight,
    request_adapter_owner,
    request_adapter_slot,
):
    rows, features = tokens.shape
    groups, owner_count, shares = (lax.axis_size(name) for name in AXES)
    g = lax.axis_index("groups")
    columns = stacked_down_weight.shape[1]
    keys = stacked_up_weight.shape[1]
    local_adapters = columns // ADAPTER_RANK
    part = features // groups

    half = columns // keys
    up_rows = columns // half
    up_wide = jnp.concatenate(
        [stacked_up_weight[i * up_rows : (i + 1) * up_rows] for i in range(half)], axis=1
    )
    down_own = lax.dynamic_slice(stacked_down_weight, (g * part, 0), (part, columns))
    cut = part // 2
    cuts = ((0, cut), (cut, part))
    pieces = [down_own[:cut], jnp.concatenate([down_own[cut:], up_wide], axis=0)]

    steps = []
    forward, backward = pieces, pieces
    for d in range(1, owner_count):
        ahead = [(i, i + 1) for i in range(d - 1, owner_count - 1)]
        back = [(i + 1, i) for i in range(0, owner_count - d)]
        nexts = [
            (lax.ppermute(f, "adapter", ahead), lax.ppermute(b, "adapter", back))
            for f, b in zip(forward, backward)
        ]
        forward, backward = [x[0] for x in nexts], [x[1] for x in nexts]
        steps.append((forward, backward))

    id_rows = jnp.concatenate(
        [request_adapter_owner.reshape(1, rows), request_adapter_slot.reshape(1, rows)], axis=0
    ).astype(jnp.bfloat16)
    id_rows = jnp.pad(id_rows, ((0, ID_ROWS - 2), (0, part - rows)))
    token_parts = []
    for step in range(groups):
        wanted = (g + step) % groups
        taken = lax.dynamic_slice(tokens, (0, wanted * part), (rows, part))
        taken = jnp.concatenate([taken, id_rows], axis=0)
        token_parts.append(mesh_shift(taken, step, 0) if step else taken)

    bases = whole(
        functools.partial(base_body, keys),
        jax.ShapeDtypeStruct((shares, rows, keys), jnp.float32),
        tokens,
        base_key_weight,
    )
    bases = lax.all_to_all(bases, "mp", 0, 0, tiled=True)

    picked_shape = jax.ShapeDtypeStruct((groups, rows, columns), jnp.float32)
    low_shape = jax.ShapeDtypeStruct((groups * shares, ADAPTER_RANK, rows), jnp.float32)
    picked = whole(
        functools.partial(shrink_body, (0,), cuts, rows, True, False),
        picked_shape,
        *token_parts,
        *pieces,
    )
    for d, (forward, backward) in enumerate(steps, 1):
        last = d == owner_count - 1
        picked = whole(
            functools.partial(shrink_body, (-d, d), cuts, rows, False, last),
            low_shape if last else picked_shape,
            *token_parts,
            picked,
            *forward,
            *backward,
        )
    parts = lax.all_to_all(picked, ("groups", "mp"), 0, 0, tiled=True)

    distances = [d for step in range(1, owner_count) for d in (-step, step)]
    ups = whole(
        functools.partial(ups_body, distances, part - cut),
        jax.ShapeDtypeStruct((owner_count * columns, keys), jnp.bfloat16),
        stacked_up_weight,
        *[block[-1] for step in steps for block in step],
    )
    ids = request_adapter_owner * local_adapters + request_adapter_slot.reshape(rows, 1)
    return whole(
        finish_body, jax.ShapeDtypeStruct((rows, keys), jnp.bfloat16), parts, bases, ids, ups
    )


def local(*args):
    rows, columns = args[0].shape[0], args[2].shape[1]
    capacity = max(2, 3 * rows // (2 * lax.axis_size("adapter")))
    travels = columns <= lax.axis_size("groups") * capacity
    return (gather if travels else dispatch)(*args)


def solution(mesh):
    placed = (
        P(("groups", "adapter"), "mp"),
        P("mp", None),
        P("mp", "adapter"),
        P("adapter", "mp"),
        P(("groups", "adapter"), None),
        P(("groups", "adapter")),
    )
    return jax.shard_map(
        local, mesh=mesh, in_specs=placed, out_specs=P(("groups", "adapter"), "mp"), check_vma=False
    )
```

```python
import functools

import jax
import jax.numpy as jnp
from jax import lax
from jax.experimental import pallas as pl
from jax.experimental.pallas import tpu as pltpu
from jax.sharding import PartitionSpec as P

ADAPTER_RANK = 16


ADAPTER_SCALE = 2.0


def dispatch(
    tokens,
    base_key_weight,
    stacked_down_weight,
    stacked_up_weight,
    request_adapter_owner,
    request_adapter_slot,
):
    rows_here = tokens.shape[0]
    feature_share = tokens.shape[1]
    owner_count = lax.axis_size("adapter")
    capacity = max(2, 3 * rows_here // (2 * owner_count))
    local_adapters = stacked_down_weight.shape[1] // ADAPTER_RANK
    key_output_share = stacked_up_weight.shape[1]
    owners = request_adapter_owner.reshape(-1)
    onehot = (owners[:, None] == jnp.arange(owner_count, dtype=jnp.int32)[None, :]).astype(
        jnp.int32
    )
    before = jnp.sum((jnp.cumsum(onehot, axis=0) - onehot) * onehot, axis=1)
    places = owners * capacity + before
    send_rows = (
        jnp.zeros((owner_count * capacity, feature_share), jnp.bfloat16).at[places].set(tokens)
    )
    send_rows = send_rows.reshape(owner_count, capacity, feature_share)
    send_slots = (
        jnp.full((owner_count * capacity,), -1, jnp.int32).at[places].set(request_adapter_slot)
    )
    send_slots = send_slots.reshape(owner_count, capacity)
    input_rows = lax.all_to_all(send_rows, "adapter", split_axis=0, concat_axis=0, tiled=True)
    slots_in = lax.all_to_all(send_slots, "adapter", split_axis=0, concat_axis=0, tiled=True)
    key_projection_output = jnp.einsum(
        "rzq,qt->rzt", input_rows, stacked_down_weight, preferred_element_type=jnp.float32
    )
    key_projection_output = key_projection_output.reshape(
        input_rows.shape[0], input_rows.shape[1], local_adapters, ADAPTER_RANK
    )
    chosen = slots_in[:, :, None] == jnp.arange(local_adapters, dtype=jnp.int32)[None, None, :]
    partial_low = jnp.sum(jnp.where(chosen[:, :, :, None], key_projection_output, 0.0), axis=2)
    shrunk = lax.psum(partial_low, "mp")
    shrunk_bf = shrunk.astype(jnp.bfloat16)
    returned = lax.all_to_all(shrunk_bf, "adapter", split_axis=0, concat_axis=0, tiled=True)
    low_rows = returned.reshape(owner_count * capacity, ADAPTER_RANK)[places]
    gathered_up_weight = lax.all_gather(stacked_up_weight, "adapter", axis=0, tiled=True)
    adapter_ids = owners * local_adapters + request_adapter_slot
    up_taken = gathered_up_weight.reshape(-1, ADAPTER_RANK, key_output_share)[adapter_ids]
    adapter_updates = jnp.einsum(
        "tr,trk->tk", low_rows, up_taken, preferred_element_type=jnp.float32
    ).astype(jnp.bfloat16)
    base_output_share = lax.psum_scatter(
        lax.dot_general(
            base_key_weight, tokens, (((0,), (1,)), ((), ())), preferred_element_type=jnp.float32
        ),
        "mp",
        scatter_dimension=0,
        tiled=True,
    )
    return (base_output_share.T + ADAPTER_SCALE * adapter_updates.astype(jnp.float32)).astype(
        jnp.bfloat16
    )


AXES = ("groups", "adapter", "mp")
ID_ROWS = 16
OWNERS = 4


def swap(x, group_bits, owner_bits, share_bits):
    groups, owners, shares = (lax.axis_size(name) for name in AXES)

    def number(g, a, m):
        return (g * owners + a) * shares + m

    pairs = [
        (number(g, a, m), number(g ^ group_bits, a ^ owner_bits, m ^ share_bits))
        for g in range(groups)
        for a in range(owners)
        for m in range(shares)
    ]
    return lax.ppermute(x, AXES, pairs)


def kernel(body, outs, operands, spaces=None, scratch=()):
    inner = pl.BlockSpec(memory_space=pltpu.VMEM)
    specs = [inner if s is None else pl.BlockSpec(memory_space=s) for s in spaces or ()]
    return pl.pallas_call(
        body,
        out_shape=outs,
        in_specs=specs or [inner] * len(operands),
        out_specs=jax.tree.map(lambda _: inner, outs),
        scratch_shapes=scratch,
        compiler_params=pltpu.CompilerParams(vmem_limit_bytes=16 * 1024 * 1024),
    )(*operands)


def pack_body(down, up, out, sems):
    g = lax.axis_index("groups")
    columns, keys = down.shape[1], up.shape[1]
    count = columns // keys
    size = up.shape[0] // count
    part = out.shape[0] - size
    copies = [
        pltpu.make_async_copy(
            down.at[pl.ds(pl.multiple_of(g * part, part), part), :],
            out.at[pl.ds(0, part), :],
            sems.at[count],
        )
    ]
    for k in range(count):
        copies.append(
            pltpu.make_async_copy(
                up.at[pl.ds(k * size, size), :],
                out.at[pl.ds(part, size), pl.ds(k * keys, keys)],
                sems.at[k],
            )
        )
    for copy in copies:
        copy.start()
    for copy in copies:
        copy.wait()


def base_body(keys, tokens, weights, out):
    wide = jnp.dot(tokens[...], weights[...], preferred_element_type=jnp.float32)
    for k in range(out.shape[0]):
        out[k] = wide[:, k * keys : (k + 1) * keys]


def shrink_body(bits, part, rows, first, last, *refs):
    groups = lax.axis_size("groups")
    a = lax.axis_index("adapter")
    token_refs, rest = refs[:groups], refs[groups:]
    picked_in = None
    if not first:
        picked_in, rest = rest[0], rest[1:]
    blocks, outs = rest[: len(bits)], rest[len(bits) :]
    if not first and not last:
        bases, outs = outs[0], outs[1:]
        base = bases[0]
        for k in range(1, bases.shape[0]):
            base = base + bases[k]
        outs[1][...] = base
    columns = blocks[0].shape[1]
    eye = (
        lax.broadcasted_iota(jnp.int32, (ID_ROWS, ID_ROWS), 0)
        == lax.broadcasted_iota(jnp.int32, (ID_ROWS, ID_ROWS), 1)
    ).astype(jnp.bfloat16)
    for n, tokens in enumerate(token_refs):
        ids = lax.dot_general(
            tokens[rows : rows + ID_ROWS, :rows],
            eye,
            (((0,), (0,)), ((), ())),
            preferred_element_type=jnp.float32,
        )
        owner, slot = ids[:, 0:1], ids[:, 1:2]
        picked = jnp.zeros((rows, columns), jnp.float32) if first else picked_in[n]
        for bit, block in zip(bits, blocks):
            wide = jnp.dot(tokens[:rows, :], block[:part, :], preferred_element_type=jnp.float32)
            picked = jnp.where(owner == (a ^ bit).astype(jnp.float32), wide, picked)
        if not last:
            outs[0][n] = picked
            continue
        column = lax.broadcasted_iota(jnp.int32, (rows, columns), 1)
        adapter = (column // ADAPTER_RANK).astype(jnp.float32)
        picked = jnp.where(adapter == slot, picked, 0.0)
        lanes = 128
        folded = picked[:, :lanes]
        for k in range(1, columns // lanes):
            folded = folded + picked[:, k * lanes : (k + 1) * lanes]
        turned = folded.T
        low = turned[:ADAPTER_RANK]
        for k in range(1, lanes // ADAPTER_RANK):
            low = low + turned[k * ADAPTER_RANK : (k + 1) * ADAPTER_RANK]
        outs[n][...] = low


def finish_body(bits, part, near, far, base, ids, *refs):
    a = lax.axis_index("adapter")
    blocks, out = refs[:-1], refs[-1]
    rows, keys = out.shape
    columns = blocks[0].shape[1]
    column = lax.broadcasted_iota(jnp.int32, (ADAPTER_RANK, columns), 1)
    row = lax.broadcasted_iota(jnp.int32, (ADAPTER_RANK, columns), 0)
    repeat = (lax.rem(column, ADAPTER_RANK) == row).astype(jnp.bfloat16)
    shrunk = (near[...] + far[...]).astype(jnp.bfloat16)
    spread = lax.dot_general(
        shrunk, repeat, (((0,), (0,)), ((), ())), preferred_element_type=jnp.float32
    )
    adapter = lax.broadcasted_iota(jnp.int32, (rows, columns), 1) // ADAPTER_RANK
    updates = jnp.zeros((rows, keys), jnp.float32)
    for bit, block in zip(bits, blocks):
        wide = block[part:, :]
        up = jnp.concatenate([wide[:, k * keys : (k + 1) * keys] for k in range(columns // keys)])
        first = (a ^ bit) * (columns // ADAPTER_RANK)
        chosen = jnp.where(adapter + first == ids[...], spread, 0.0).astype(jnp.bfloat16)
        updates = updates + jnp.dot(chosen, up, preferred_element_type=jnp.float32)
    updates = updates.astype(jnp.bfloat16).astype(jnp.float32)
    out[...] = (base[...] + ADAPTER_SCALE * updates).astype(jnp.bfloat16)


def gather(
    tokens,
    base_key_weight,
    stacked_down_weight,
    stacked_up_weight,
    request_adapter_owner,
    request_adapter_slot,
):
    rows, features = tokens.shape
    groups, _, shares = (lax.axis_size(name) for name in AXES)
    g = lax.axis_index("groups")
    columns = stacked_down_weight.shape[1]
    keys = stacked_up_weight.shape[1]
    local_adapters = columns // ADAPTER_RANK
    part = features // groups
    half = columns // keys

    own = kernel(
        pack_body,
        jax.ShapeDtypeStruct((part + columns // half, columns), jnp.bfloat16),
        (stacked_down_weight, stacked_up_weight),
        (pl.ANY, pl.ANY),
        [pltpu.SemaphoreType.DMA((half + 1,))],
    )
    across = swap(own, 0, 3, 0)
    beside = swap(own, 0, 1, 0)
    behind = swap(across, 0, 1, 0)

    id_rows = jnp.concatenate(
        [request_adapter_owner.reshape(1, rows), request_adapter_slot.reshape(1, rows)], axis=0
    ).astype(jnp.bfloat16)
    id_rows = jnp.pad(id_rows, ((0, ID_ROWS - 2), (0, part - rows)))
    token_parts = []
    for step in range(groups):
        taken = lax.dynamic_slice(tokens, (0, (g ^ step) * part), (rows, part))
        taken = jnp.concatenate([taken, id_rows], axis=0)
        token_parts.append(swap(taken, step, 0, 0) if step else taken)

    bases = kernel(
        functools.partial(base_body, keys),
        jax.ShapeDtypeStruct((shares, rows, keys), jnp.float32),
        (tokens, base_key_weight),
    )
    bases = lax.all_to_all(bases, "mp", 0, 0, tiled=True)

    picked_shape = jax.ShapeDtypeStruct((groups, rows, columns), jnp.float32)
    low_shape = jax.ShapeDtypeStruct((ADAPTER_RANK, rows), jnp.float32)
    picked = kernel(
        functools.partial(shrink_body, (0,), part, rows, True, False),
        picked_shape,
        (*token_parts, own),
    )
    picked, base = kernel(
        functools.partial(shrink_body, (3, 1), part, rows, False, False),
        [picked_shape, jax.ShapeDtypeStruct((rows, keys), jnp.float32)],
        (*token_parts, picked, across, beside, bases),
    )
    low, low_away = kernel(
        functools.partial(shrink_body, (2,), part, rows, False, True),
        [low_shape] * groups,
        (*token_parts, picked, behind),
    )

    low = low + swap(low_away, 1, 0, 0)
    bit = shares // 2
    while bit > 1:
        low = low + swap(low, 0, 0, bit)
        bit //= 2
    low_far = swap(low, 0, 0, 1)

    ids = request_adapter_owner * local_adapters + request_adapter_slot.reshape(rows, 1)
    return kernel(
        functools.partial(finish_body, (0, 3, 1, 2), part),
        jax.ShapeDtypeStruct((rows, keys), jnp.bfloat16),
        (low, low_far, base, ids, own, across, beside, behind),
    )


def local(*args):
    rows, columns = args[0].shape[0], args[2].shape[1]
    groups, owners, shares = (lax.axis_size(name) for name in AXES)
    capacity = max(2, 3 * rows // (2 * owners))
    fits = owners == OWNERS and groups == 2 and shares > 1 and shares & (shares - 1) == 0
    travels = fits and columns <= groups * capacity
    return (gather if travels else dispatch)(*args)


def solution(mesh):
    placed = (
        P(("groups", "adapter"), "mp"),
        P("mp", None),
        P("mp", "adapter"),
        P("adapter", "mp"),
        P(("groups", "adapter"), None),
        P(("groups", "adapter")),
    )
    return jax.shard_map(
        local, mesh=mesh, in_specs=placed, out_specs=P(("groups", "adapter"), "mp"), check_vma=False
    )
```

```python
import functools

import jax
import jax.numpy as jnp
from jax import lax
from jax.experimental import pallas as pl
from jax.experimental.pallas import tpu as pltpu
from jax.sharding import PartitionSpec as P

ADAPTER_RANK = 16


ADAPTER_SCALE = 2.0


def dispatch(
    tokens,
    base_key_weight,
    stacked_down_weight,
    stacked_up_weight,
    request_adapter_owner,
    request_adapter_slot,
):
    rows_here = tokens.shape[0]
    feature_share = tokens.shape[1]
    owner_count = lax.axis_size("adapter")
    capacity = max(2, 3 * rows_here // (2 * owner_count))
    local_adapters = stacked_down_weight.shape[1] // ADAPTER_RANK
    key_output_share = stacked_up_weight.shape[1]
    owners = request_adapter_owner.reshape(-1)
    onehot = (owners[:, None] == jnp.arange(owner_count, dtype=jnp.int32)[None, :]).astype(
        jnp.int32
    )
    before = jnp.sum((jnp.cumsum(onehot, axis=0) - onehot) * onehot, axis=1)
    places = owners * capacity + before
    send_rows = (
        jnp.zeros((owner_count * capacity, feature_share), jnp.bfloat16).at[places].set(tokens)
    )
    send_rows = send_rows.reshape(owner_count, capacity, feature_share)
    send_slots = (
        jnp.full((owner_count * capacity,), -1, jnp.int32).at[places].set(request_adapter_slot)
    )
    send_slots = send_slots.reshape(owner_count, capacity)
    input_rows = lax.all_to_all(send_rows, "adapter", split_axis=0, concat_axis=0, tiled=True)
    slots_in = lax.all_to_all(send_slots, "adapter", split_axis=0, concat_axis=0, tiled=True)
    key_projection_output = jnp.einsum(
        "rzq,qt->rzt", input_rows, stacked_down_weight, preferred_element_type=jnp.float32
    )
    key_projection_output = key_projection_output.reshape(
        input_rows.shape[0], input_rows.shape[1], local_adapters, ADAPTER_RANK
    )
    chosen = slots_in[:, :, None] == jnp.arange(local_adapters, dtype=jnp.int32)[None, None, :]
    partial_low = jnp.sum(jnp.where(chosen[:, :, :, None], key_projection_output, 0.0), axis=2)
    shrunk = lax.psum(partial_low, "mp")
    shrunk_bf = shrunk.astype(jnp.bfloat16)
    returned = lax.all_to_all(shrunk_bf, "adapter", split_axis=0, concat_axis=0, tiled=True)
    low_rows = returned.reshape(owner_count * capacity, ADAPTER_RANK)[places]
    gathered_up_weight = lax.all_gather(stacked_up_weight, "adapter", axis=0, tiled=True)
    adapter_ids = owners * local_adapters + request_adapter_slot
    up_taken = gathered_up_weight.reshape(-1, ADAPTER_RANK, key_output_share)[adapter_ids]
    adapter_updates = jnp.einsum(
        "tr,trk->tk", low_rows, up_taken, preferred_element_type=jnp.float32
    ).astype(jnp.bfloat16)
    base_output_share = lax.psum_scatter(
        lax.dot_general(
            base_key_weight, tokens, (((0,), (1,)), ((), ())), preferred_element_type=jnp.float32
        ),
        "mp",
        scatter_dimension=0,
        tiled=True,
    )
    return (base_output_share.T + ADAPTER_SCALE * adapter_updates.astype(jnp.float32)).astype(
        jnp.bfloat16
    )


AXES = ("groups", "adapter", "mp")
ID_ROWS = 16
OWNERS = 4
LANES = 128


def exchange(x, group_bits, share_bits, owners):
    groups, count, shares = (lax.axis_size(name) for name in AXES)

    def number(g, a, m):
        return (g * count + a) * shares + m

    pairs = [
        (number(g, a, m), number(g ^ group_bits, b, m ^ share_bits))
        for g in range(groups)
        for a, b in owners
        for m in range(shares)
    ]
    return lax.ppermute(x, AXES, pairs)


SAME = tuple((a, a) for a in range(OWNERS))
BESIDE = ((0, 1), (1, 0), (2, 3), (3, 2))
ACROSS = ((0, 2), (1, 3), (2, 0), (3, 1))
MIRROR = ((0, 3), (1, 2), (2, 1), (3, 0))
MIDDLE = ((1, 2), (2, 1))
OUTWARD = ((1, 0), (2, 3))
INWARD = ((0, 1), (3, 2))


def after(x, *others):
    return lax.optimization_barrier((x, *others))[0]


def kernel(body, outs, operands, spaces=None, scratch=()):
    inner = pl.BlockSpec(memory_space=pltpu.VMEM)
    specs = [inner if s is None else pl.BlockSpec(memory_space=s) for s in spaces or ()]
    return pl.pallas_call(
        body,
        out_shape=outs,
        in_specs=specs or [inner] * len(operands),
        out_specs=jax.tree.map(lambda _: inner, outs),
        scratch_shapes=scratch,
        compiler_params=pltpu.CompilerParams(vmem_limit_bytes=16 * 1024 * 1024),
    )(*operands)


def pack_body(down, up, out, up_out, sems):
    g = lax.axis_index("groups")
    keys = up.shape[1]
    part, size = out.shape[0], up_out.shape[0]
    count = down.shape[1] // keys
    copies = [
        pltpu.make_async_copy(
            down.at[pl.ds(pl.multiple_of(g * part, part), part), :], out, sems.at[count]
        )
    ]
    for k in range(count):
        start = pl.multiple_of((g * count + k) * size, size)
        copies.append(
            pltpu.make_async_copy(
                up.at[pl.ds(start, size), :], up_out.at[:, pl.ds(k * keys, keys)], sems.at[k]
            )
        )
    for copy in copies:
        copy.start()
    for copy in copies:
        copy.wait()


def hop_body(capacity, tokens, id_rows, own, away, places):
    a, g = lax.axis_index("adapter"), lax.axis_index("groups")
    rows = tokens.shape[0]
    part = own.shape[1]
    ids = id_rows[:, :rows]
    match = (ids.astype(jnp.float32) == (OWNERS - 1 - a).astype(jnp.float32)).astype(jnp.bfloat16)
    earlier = lax.broadcasted_iota(jnp.int32, (rows, rows), 0) < lax.broadcasted_iota(
        jnp.int32, (rows, rows), 1
    )
    rank = jnp.dot(match, earlier.astype(jnp.bfloat16), preferred_element_type=jnp.float32)
    place = lax.broadcasted_iota(jnp.int32, (capacity, rows), 0).astype(jnp.float32)
    taken = (place == rank[0:1]) & (match[0:1].astype(jnp.float32) > 0)
    chosen = taken.astype(jnp.bfloat16)
    places[...] = chosen
    kept = lax.dot_general(ids, chosen, NT, preferred_element_type=jnp.float32)
    for out, half in ((own, g), (away, 1 - g)):
        block = tokens[:, pl.ds(pl.multiple_of(half * part, part), part)]
        packed = jnp.dot(chosen, block, preferred_element_type=jnp.float32)
        out[:capacity, :] = packed.astype(jnp.bfloat16)
        out[capacity:, :] = jnp.zeros((ID_ROWS, part), jnp.bfloat16)
        out[capacity:, :capacity] = kept.astype(jnp.bfloat16)


NT = (((1,), (1,)), ((), ()))
TN = (((0,), (0,)), ((), ()))


def base_body(keys, tokens, weights, out):
    wide = jnp.dot(tokens[...], weights[...], preferred_element_type=jnp.float32)
    for k in range(out.shape[0]):
        out[k] = wide[:, k * keys : (k + 1) * keys]


def id_columns(rows_ref, start, count):
    eye = (
        lax.broadcasted_iota(jnp.int32, (ID_ROWS, ID_ROWS), 0)
        == lax.broadcasted_iota(jnp.int32, (ID_ROWS, ID_ROWS), 1)
    ).astype(jnp.bfloat16)
    ids = lax.dot_general(
        rows_ref[start : start + ID_ROWS, :count], eye, TN, preferred_element_type=jnp.float32
    )
    return ids[:, 0:1], ids[:, 1:2]


def adapters(rows, columns):
    column = lax.broadcasted_iota(jnp.int32, (rows, columns), 1)
    return (column // ADAPTER_RANK).astype(jnp.float32)


def fold(wide):
    folded = wide[:, :LANES]
    for k in range(1, wide.shape[1] // LANES):
        folded = folded + wide[:, k * LANES : (k + 1) * LANES]
    return folded


def low_rank(folded):
    turned = folded.T
    low = turned[:ADAPTER_RANK]
    for k in range(1, LANES // ADAPTER_RANK):
        low = low + turned[k * ADAPTER_RANK : (k + 1) * ADAPTER_RANK]
    return low


def early_body(bits, part, rows, *refs):
    groups = lax.axis_size("groups")
    a = lax.axis_index("adapter")
    token_refs, rest = refs[:groups], refs[groups:]
    blocks, (bases, folded, mask, base) = rest[: len(bits)], rest[len(bits) :]
    columns = blocks[0].shape[1]
    total = bases[0]
    for k in range(1, bases.shape[0]):
        total = total + bases[k]
    base[...] = total
    adapter = adapters(rows, columns)
    for n, tokens in enumerate(token_refs):
        owner, slot = id_columns(tokens, rows, rows)
        right = adapter == slot
        picked = jnp.zeros((rows, columns), jnp.float32)
        for bit, block in zip(bits, blocks):
            wide = jnp.dot(tokens[:rows, :], block[...], preferred_element_type=jnp.float32)
            picked = jnp.where(owner == (a ^ bit).astype(jnp.float32), wide, picked)
        folded[n] = fold(jnp.where(right, picked, 0.0))
        mask[n] = jnp.where(owner == (a ^ 2).astype(jnp.float32), right.astype(jnp.float32), 0.0)


def last_body(part, rows, capacity, *refs):
    groups = lax.axis_size("groups")
    a = lax.axis_index("adapter")
    token_refs, rest = refs[:groups], refs[groups:]
    hops, rest = rest[:groups], rest[groups:]
    folded, mask, inside, outside = rest[:4]
    lows, hop_lows = rest[4 : 4 + groups], rest[4 + groups :]
    columns = inside.shape[1]

    def finish(block):
        for n, tokens in enumerate(token_refs):
            wide = jnp.dot(tokens[:rows, :], block[...], preferred_element_type=jnp.float32)
            kept = fold(jnp.where(mask[n] > 0, wide, 0.0))
            lows[n][...] = low_rank(folded[n] + kept)

    middle = (a == 1) | (a == 2)

    @pl.when(middle)
    def _():
        finish(inside)
        adapter = adapters(capacity, columns)
        for hop, out in zip(hops, hop_lows):
            _, slot = id_columns(hop, capacity, capacity)
            wide = jnp.dot(hop[:capacity, :], inside[...], preferred_element_type=jnp.float32)
            kept = fold(jnp.where(adapter == slot, wide, 0.0))
            rest_rows = -capacity % LANES
            kept = jnp.concatenate([kept, jnp.zeros((rest_rows, LANES), jnp.float32)], axis=0)
            out[...] = low_rank(kept)[:, :capacity]

    @pl.when(jnp.logical_not(middle))
    def _():
        finish(outside)
        for out in hop_lows:
            out[...] = jnp.zeros(out.shape, jnp.float32)


def merge_body(low, near, places, *refs):
    hops, out = refs[:-1], refs[-1]
    back = hops[0][...]
    for hop in hops[1:]:
        back = back + hop[...]
    spread = jnp.zeros(low.shape, jnp.float32)
    for _ in range(3):
        piece = back.astype(jnp.bfloat16)
        back = back - piece.astype(jnp.float32)
        spread = spread + jnp.dot(piece, places[...], preferred_element_type=jnp.float32)
    out[...] = low[...] + near[...] + spread


def ups_body(own, *refs):
    g = lax.axis_index("groups")
    blocks, out = refs[:-1], refs[-1]
    columns, keys = own.shape
    out[:columns, :] = own[...]
    size = columns // len(blocks)
    count = blocks[0].shape[1] // keys
    for n, block in enumerate(blocks):
        half = g if n == 0 else 1 - g
        height = block.shape[0] // (OWNERS - 1)
        for i in range(OWNERS - 1):
            for k in range(count):
                start = (i + 1) * columns + half * size + k * height
                start = pl.multiple_of(start, height)
                out[pl.ds(start, height), :] = block[
                    i * height : (i + 1) * height, k * keys : (k + 1) * keys
                ]


def finish_body(near, far, base, ids, ups, out):
    a = lax.axis_index("adapter")
    rows = out.shape[0]
    columns = ups.shape[0] // OWNERS
    column = lax.broadcasted_iota(jnp.int32, (ADAPTER_RANK, columns), 1)
    row = lax.broadcasted_iota(jnp.int32, (ADAPTER_RANK, columns), 0)
    repeat = (lax.rem(column, ADAPTER_RANK) == row).astype(jnp.bfloat16)
    shrunk = (near[...] + far[...]).astype(jnp.bfloat16)
    spread = lax.dot_general(shrunk, repeat, TN, preferred_element_type=jnp.float32)
    adapter = lax.broadcasted_iota(jnp.int32, (rows, columns), 1) // ADAPTER_RANK
    updates = jnp.zeros(out.shape, jnp.float32)
    for bit in range(OWNERS):
        wanted = ids[...] - (a ^ bit) * (columns // ADAPTER_RANK)
        chosen = jnp.where(adapter == wanted, spread, 0.0).astype(jnp.bfloat16)
        up = ups[bit * columns : (bit + 1) * columns, :]
        updates = updates + jnp.dot(chosen, up, preferred_element_type=jnp.float32)
    updates = updates.astype(jnp.bfloat16).astype(jnp.float32)
    out[...] = (base[...] + ADAPTER_SCALE * updates).astype(jnp.bfloat16)


def gather(
    tokens,
    base_key_weight,
    stacked_down_weight,
    stacked_up_weight,
    request_adapter_owner,
    request_adapter_slot,
):
    rows, features = tokens.shape
    groups, _, shares = (lax.axis_size(name) for name in AXES)
    g = lax.axis_index("groups")
    columns = stacked_down_weight.shape[1]
    keys = stacked_up_weight.shape[1]
    local_adapters = columns // ADAPTER_RANK
    part = features // groups
    half = columns // keys
    capacity = -(-row_limit(rows) // ID_ROWS) * ID_ROWS
    up_rows = columns // half // groups

    def shape(*dims, dtype=jnp.float32):
        return jax.ShapeDtypeStruct(dims, dtype)

    own, up_own = kernel(
        pack_body,
        [shape(part, columns, dtype=jnp.bfloat16), shape(up_rows, columns, dtype=jnp.bfloat16)],
        (stacked_down_weight, stacked_up_weight),
        (pl.ANY, pl.ANY),
        [pltpu.SemaphoreType.DMA((half + 1,))],
    )
    beside = exchange(own, 0, 0, BESIDE)
    mirror = exchange(own, 0, 0, MIDDLE)

    id_rows = jnp.concatenate(
        [request_adapter_owner.reshape(1, rows), request_adapter_slot.reshape(1, rows)], axis=0
    ).astype(jnp.bfloat16)
    id_rows = jnp.pad(id_rows, ((0, ID_ROWS - 2), (0, part - rows)))
    hop_shape = shape(capacity + ID_ROWS, part, dtype=jnp.bfloat16)
    hop_own, hop_away, places = kernel(
        functools.partial(hop_body, capacity),
        [hop_shape, hop_shape, shape(capacity, rows, dtype=jnp.bfloat16)],
        (tokens, id_rows),
    )
    hop_parts = [hop_own, exchange(hop_away, 1, 0, SAME)]
    token_parts = []
    for step in range(groups):
        taken = lax.dynamic_slice(tokens, (0, (g ^ step) * part), (rows, part))
        taken = after(jnp.concatenate([taken, id_rows], axis=0), hop_away)
        token_parts.append(exchange(taken, step, 0, SAME) if step else taken)

    up_parts = [exchange(up_own, 0, 0, to) for to in (BESIDE, ACROSS, MIRROR)]
    up_parts = jnp.concatenate(up_parts, axis=0)
    ups = kernel(
        ups_body,
        shape(OWNERS * columns, keys, dtype=jnp.bfloat16),
        (stacked_up_weight, up_parts, exchange(up_parts, 1, 0, SAME)),
    )

    bases = kernel(
        functools.partial(base_body, keys),
        shape(shares, rows, keys),
        (tokens, base_key_weight),
    )
    bases = lax.all_to_all(bases, "mp", 0, 0, tiled=True)

    inside = exchange(beside, 0, 0, MIDDLE)
    outside = exchange(mirror, 0, 0, OUTWARD)
    hops = [exchange(after(x, beside), 0, 0, INWARD) for x in hop_parts]

    folded, mask, base = kernel(
        functools.partial(early_body, (0, 1, 3), part, rows),
        [shape(groups, rows, LANES), shape(groups, rows, columns), shape(rows, keys)],
        (*token_parts, own, beside, mirror, bases),
    )
    low_shape, hop_low_shape = shape(ADAPTER_RANK, rows), shape(ADAPTER_RANK, capacity)
    low, low_away, back, back_away = kernel(
        functools.partial(last_body, part, rows, capacity),
        [low_shape] * groups + [hop_low_shape] * groups,
        (*token_parts, *hops, folded, mask, inside, outside),
    )

    near = exchange(low_away, 1, 0, SAME)
    back = exchange(back, 0, 0, OUTWARD)
    back_away = exchange(back_away, 1, 0, OUTWARD)
    low = kernel(merge_body, low_shape, (low, near, places, back, back_away))
    bit = shares // 2
    while bit > 1:
        low = low + exchange(low, 0, bit, SAME)
        bit //= 2
    low_far = exchange(low, 0, 1, SAME)

    ids = request_adapter_owner * local_adapters + request_adapter_slot.reshape(rows, 1)
    return kernel(finish_body, shape(rows, keys, dtype=jnp.bfloat16), (low, low_far, base, ids, ups))


def row_limit(rows):
    return max(2, 3 * rows // (2 * lax.axis_size("adapter")))


def local(*args):
    rows, columns = args[0].shape[0], args[2].shape[1]
    groups, owners, shares = (lax.axis_size(name) for name in AXES)
    fits = owners == OWNERS and groups == 2 and shares > 1 and shares & (shares - 1) == 0
    travels = fits and columns <= groups * row_limit(rows)
    return (gather if travels else dispatch)(*args)


def solution(mesh):
    placed = (
        P(("groups", "adapter"), "mp"),
        P("mp", None),
        P("mp", "adapter"),
        P("adapter", "mp"),
        P(("groups", "adapter"), None),
        P(("groups", "adapter")),
    )
    return jax.shard_map(
        local, mesh=mesh, in_specs=placed, out_specs=P(("groups", "adapter"), "mp"), check_vma=False
    )
```

```python
import functools

import jax
import jax.numpy as jnp
from jax import lax
from jax.experimental import pallas as pl
from jax.experimental.pallas import tpu as pltpu
from jax.sharding import PartitionSpec as P

ADAPTER_RANK = 16


ADAPTER_SCALE = 2.0


def dispatch(
    tokens,
    base_key_weight,
    stacked_down_weight,
    stacked_up_weight,
    request_adapter_owner,
    request_adapter_slot,
):
    rows_here = tokens.shape[0]
    feature_share = tokens.shape[1]
    owner_count = lax.axis_size("adapter")
    capacity = max(2, 3 * rows_here // (2 * owner_count))
    local_adapters = stacked_down_weight.shape[1] // ADAPTER_RANK
    key_output_share = stacked_up_weight.shape[1]
    owners = request_adapter_owner.reshape(-1)
    onehot = (owners[:, None] == jnp.arange(owner_count, dtype=jnp.int32)[None, :]).astype(
        jnp.int32
    )
    before = jnp.sum((jnp.cumsum(onehot, axis=0) - onehot) * onehot, axis=1)
    places = owners * capacity + before
    send_rows = (
        jnp.zeros((owner_count * capacity, feature_share), jnp.bfloat16).at[places].set(tokens)
    )
    send_rows = send_rows.reshape(owner_count, capacity, feature_share)
    send_slots = (
        jnp.full((owner_count * capacity,), -1, jnp.int32).at[places].set(request_adapter_slot)
    )
    send_slots = send_slots.reshape(owner_count, capacity)
    input_rows = lax.all_to_all(send_rows, "adapter", split_axis=0, concat_axis=0, tiled=True)
    slots_in = lax.all_to_all(send_slots, "adapter", split_axis=0, concat_axis=0, tiled=True)
    key_projection_output = jnp.einsum(
        "rzq,qt->rzt", input_rows, stacked_down_weight, preferred_element_type=jnp.float32
    )
    key_projection_output = key_projection_output.reshape(
        input_rows.shape[0], input_rows.shape[1], local_adapters, ADAPTER_RANK
    )
    chosen = slots_in[:, :, None] == jnp.arange(local_adapters, dtype=jnp.int32)[None, None, :]
    partial_low = jnp.sum(jnp.where(chosen[:, :, :, None], key_projection_output, 0.0), axis=2)
    shrunk = lax.psum(partial_low, "mp")
    shrunk_bf = shrunk.astype(jnp.bfloat16)
    returned = lax.all_to_all(shrunk_bf, "adapter", split_axis=0, concat_axis=0, tiled=True)
    low_rows = returned.reshape(owner_count * capacity, ADAPTER_RANK)[places]
    gathered_up_weight = lax.all_gather(stacked_up_weight, "adapter", axis=0, tiled=True)
    adapter_ids = owners * local_adapters + request_adapter_slot
    up_taken = gathered_up_weight.reshape(-1, ADAPTER_RANK, key_output_share)[adapter_ids]
    adapter_updates = jnp.einsum(
        "tr,trk->tk", low_rows, up_taken, preferred_element_type=jnp.float32
    ).astype(jnp.bfloat16)
    base_output_share = lax.psum_scatter(
        lax.dot_general(
            base_key_weight, tokens, (((0,), (1,)), ((), ())), preferred_element_type=jnp.float32
        ),
        "mp",
        scatter_dimension=0,
        tiled=True,
    )
    return (base_output_share.T + ADAPTER_SCALE * adapter_updates.astype(jnp.float32)).astype(
        jnp.bfloat16
    )


AXES = ("groups", "adapter", "mp")
ID_ROWS = 16
OWNERS = 4
LANES = 128


def exchange(x, group_bits, share_bits, owners):
    groups, count, shares = (lax.axis_size(name) for name in AXES)

    def number(g, a, m):
        return (g * count + a) * shares + m

    pairs = [
        (number(g, a, m), number(g ^ group_bits, b, m ^ share_bits))
        for g in range(groups)
        for a, b in owners
        for m in range(shares)
    ]
    return lax.ppermute(x, AXES, pairs)


SAME = tuple((a, a) for a in range(OWNERS))
BESIDE = ((0, 1), (1, 0), (2, 3), (3, 2))
ACROSS = ((0, 2), (1, 3), (2, 0), (3, 1))
MIRROR = ((0, 3), (1, 2), (2, 1), (3, 0))
MIDDLE = ((1, 2), (2, 1))
OUTWARD = ((1, 0), (2, 3))
INWARD = ((0, 1), (3, 2))


def after(x, *others):
    return lax.optimization_barrier((x, *others))[0]


def kernel(body, outs, operands, spaces=None, scratch=()):
    inner = pl.BlockSpec(memory_space=pltpu.VMEM)
    specs = [inner if s is None else pl.BlockSpec(memory_space=s) for s in spaces or ()]
    return pl.pallas_call(
        body,
        out_shape=outs,
        in_specs=specs or [inner] * len(operands),
        out_specs=jax.tree.map(lambda _: inner, outs),
        scratch_shapes=scratch,
        compiler_params=pltpu.CompilerParams(vmem_limit_bytes=16 * 1024 * 1024),
    )(*operands)


def copy_all(copies):
    for copy in copies:
        copy.start()
    for copy in copies:
        copy.wait()


def pack_body(down, up, out, ups_out, sems):
    g = lax.axis_index("groups")
    keys = up.shape[1]
    part, size = out.shape[0], ups_out.shape[1]
    count = down.shape[1] // keys
    mine = down.at[pl.ds(pl.multiple_of(g * part, part), part), :]
    copies = [pltpu.make_async_copy(mine, out, sems.at[0])]
    for i in range(ups_out.shape[0]):
        for k in range(count):
            start = pl.multiple_of((g * count + k) * size, size)
            copies.append(
                pltpu.make_async_copy(
                    up.at[pl.ds(start, size), :],
                    ups_out.at[i, :, pl.ds(k * keys, keys)],
                    sems.at[1 + i * count + k],
                )
            )
    copy_all(copies)


def split_body(tokens, owner, slot, own, away, sems):
    g = lax.axis_index("groups")
    rows, part = tokens.shape[0], own.shape[1]
    copies = []
    for n, (out, half) in enumerate(((own, g), (away, 1 - g))):
        taken = tokens.at[:, pl.ds(pl.multiple_of(half * part, part), part)]
        copies.append(pltpu.make_async_copy(taken, out.at[pl.ds(0, rows), :], sems.at[n]))
    for copy in copies:
        copy.start()
    row = lax.broadcasted_iota(jnp.int32, (ID_ROWS, rows), 0)
    ids = jnp.where(row == 0, owner[...], jnp.where(row == 1, slot[...], 0))
    ids = ids.astype(jnp.float32).astype(jnp.bfloat16)
    for out in (own, away):
        out[rows:, :rows] = ids
        out[rows:, rows:] = jnp.zeros((ID_ROWS, part - rows), jnp.bfloat16)
    for copy in copies:
        copy.wait()


def hop_body(rows, capacity, own, away, own_out, away_out, places):
    a = lax.axis_index("adapter")
    part = own.shape[1]
    ids = own[rows:, :rows]
    match = (ids.astype(jnp.float32) == (OWNERS - 1 - a).astype(jnp.float32)).astype(jnp.bfloat16)
    earlier = lax.broadcasted_iota(jnp.int32, (rows, rows), 0) < lax.broadcasted_iota(
        jnp.int32, (rows, rows), 1
    )
    rank = jnp.dot(match, earlier.astype(jnp.bfloat16), preferred_element_type=jnp.float32)
    place = lax.broadcasted_iota(jnp.int32, (capacity, rows), 0).astype(jnp.float32)
    taken = (place == rank[0:1]) & (match[0:1].astype(jnp.float32) > 0)
    chosen = taken.astype(jnp.bfloat16)
    places[...] = chosen
    kept = lax.dot_general(ids, chosen, NT, preferred_element_type=jnp.float32)
    for tokens, out in ((own, own_out), (away, away_out)):
        packed = jnp.dot(chosen, tokens[:rows, :], preferred_element_type=jnp.float32)
        out[:capacity, :] = packed.astype(jnp.bfloat16)
        out[capacity:, :] = jnp.zeros((ID_ROWS, part), jnp.bfloat16)
        out[capacity:, :capacity] = kept.astype(jnp.bfloat16)


NT = (((1,), (1,)), ((), ()))
TN = (((0,), (0,)), ((), ()))


def base_body(keys, tokens, weights, out):
    wide = jnp.dot(tokens[...], weights[...], preferred_element_type=jnp.float32)
    for k in range(out.shape[0]):
        out[k] = wide[:, k * keys : (k + 1) * keys]


def id_columns(rows_ref, start, count):
    eye = (
        lax.broadcasted_iota(jnp.int32, (ID_ROWS, ID_ROWS), 0)
        == lax.broadcasted_iota(jnp.int32, (ID_ROWS, ID_ROWS), 1)
    ).astype(jnp.bfloat16)
    ids = lax.dot_general(
        rows_ref[start : start + ID_ROWS, :count], eye, TN, preferred_element_type=jnp.float32
    )
    return ids[:, 0:1], ids[:, 1:2]


def adapters(rows, columns):
    column = lax.broadcasted_iota(jnp.int32, (rows, columns), 1)
    return (column // ADAPTER_RANK).astype(jnp.float32)


def fold(wide):
    folded = wide[:, :LANES]
    for k in range(1, wide.shape[1] // LANES):
        folded = folded + wide[:, k * LANES : (k + 1) * LANES]
    return folded


def low_rank(folded):
    turned = folded.T
    low = turned[:ADAPTER_RANK]
    for k in range(1, LANES // ADAPTER_RANK):
        low = low + turned[k * ADAPTER_RANK : (k + 1) * ADAPTER_RANK]
    return low


def early_body(bits, part, rows, *refs):
    groups = lax.axis_size("groups")
    a = lax.axis_index("adapter")
    token_refs, rest = refs[:groups], refs[groups:]
    blocks, (bases, folded, mask, numbers, base) = rest[: len(bits)], rest[len(bits) :]
    columns = blocks[0].shape[1]
    total = bases[0]
    for k in range(1, bases.shape[0]):
        total = total + bases[k]
    base[...] = total
    adapter = adapters(rows, columns)
    for n, tokens in enumerate(token_refs):
        owner, slot = id_columns(tokens, rows, rows)
        if n == 0:
            numbers[...] = owner * (columns // ADAPTER_RANK) + slot
        right = adapter == slot
        picked = jnp.zeros((rows, columns), jnp.float32)
        for bit, block in zip(bits, blocks):
            wide = jnp.dot(tokens[:rows, :], block[...], preferred_element_type=jnp.float32)
            picked = jnp.where(owner == (a ^ bit).astype(jnp.float32), wide, picked)
        folded[n] = fold(jnp.where(right, picked, 0.0))
        mask[n] = jnp.where(owner == (a ^ 2).astype(jnp.float32), right.astype(jnp.float32), 0.0)


def last_body(part, rows, capacity, *refs):
    groups = lax.axis_size("groups")
    a = lax.axis_index("adapter")
    token_refs, rest = refs[:groups], refs[groups:]
    hops, rest = rest[:groups], rest[groups:]
    folded, mask, inside, outside = rest[:4]
    lows, hop_lows = rest[4 : 4 + groups], rest[4 + groups :]
    columns = inside.shape[1]

    def finish(block):
        for n, tokens in enumerate(token_refs):
            wide = jnp.dot(tokens[:rows, :], block[...], preferred_element_type=jnp.float32)
            kept = fold(jnp.where(mask[n] > 0, wide, 0.0))
            lows[n][...] = low_rank(folded[n] + kept)

    middle = (a == 1) | (a == 2)

    @pl.when(middle)
    def _():
        finish(inside)
        adapter = adapters(capacity, columns)
        for hop, out in zip(hops, hop_lows):
            _, slot = id_columns(hop, capacity, capacity)
            wide = jnp.dot(hop[:capacity, :], inside[...], preferred_element_type=jnp.float32)
            kept = fold(jnp.where(adapter == slot, wide, 0.0))
            rest_rows = -capacity % LANES
            kept = jnp.concatenate([kept, jnp.zeros((rest_rows, LANES), jnp.float32)], axis=0)
            out[...] = low_rank(kept)[:, :capacity]

    @pl.when(jnp.logical_not(middle))
    def _():
        finish(outside)
        for out in hop_lows:
            out[...] = jnp.zeros(out.shape, jnp.float32)


def merge_body(low, near, places, *refs):
    hops, out = refs[:-1], refs[-1]
    back = hops[0][...]
    for hop in hops[1:]:
        back = back + hop[...]
    spread = jnp.zeros(low.shape, jnp.float32)
    for _ in range(3):
        piece = back.astype(jnp.bfloat16)
        back = back - piece.astype(jnp.float32)
        spread = spread + jnp.dot(piece, places[...], preferred_element_type=jnp.float32)
    out[...] = low[...] + near[...] + spread


def ups_body(mine, other, out):
    g = lax.axis_index("groups")
    owners, height, wide = mine.shape
    keys = out.shape[1]
    count = wide // keys
    for block, half in ((mine, g), (other, 1 - g)):
        for i in range(owners):
            for k in range(count):
                start = pl.multiple_of(((2 * i + half) * count + k) * height, height)
                out[pl.ds(start, height), :] = block[i][:, k * keys : (k + 1) * keys]


def finish_body(near, far, base, numbers, ups, out):
    rows = out.shape[0]
    columns = ups.shape[0] // OWNERS
    column = lax.broadcasted_iota(jnp.int32, (ADAPTER_RANK, columns), 1)
    row = lax.broadcasted_iota(jnp.int32, (ADAPTER_RANK, columns), 0)
    repeat = (lax.rem(column, ADAPTER_RANK) == row).astype(jnp.bfloat16)
    shrunk = (near[...] + far[...]).astype(jnp.bfloat16)
    spread = lax.dot_general(shrunk, repeat, TN, preferred_element_type=jnp.float32)
    adapter = adapters(rows, columns)
    updates = jnp.zeros(out.shape, jnp.float32)
    for i in range(OWNERS):
        wanted = numbers[...] - float(i * (columns // ADAPTER_RANK))
        chosen = jnp.where(adapter == wanted, spread, 0.0).astype(jnp.bfloat16)
        up = ups[i * columns : (i + 1) * columns, :]
        updates = updates + jnp.dot(chosen, up, preferred_element_type=jnp.float32)
    updates = updates.astype(jnp.bfloat16).astype(jnp.float32)
    out[...] = (base[...] + ADAPTER_SCALE * updates).astype(jnp.bfloat16)


def gather(
    tokens,
    base_key_weight,
    stacked_down_weight,
    stacked_up_weight,
    request_adapter_owner,
    request_adapter_slot,
):
    rows, features = tokens.shape
    groups, owners, shares = (lax.axis_size(name) for name in AXES)
    columns = stacked_down_weight.shape[1]
    keys = stacked_up_weight.shape[1]
    part = features // groups
    half = columns // keys
    capacity = -(-row_limit(rows) // ID_ROWS) * ID_ROWS
    up_rows = columns // half // groups

    def narrow(*dims):
        return jax.ShapeDtypeStruct(dims, jnp.bfloat16)

    def wide(*dims):
        return jax.ShapeDtypeStruct(dims, jnp.float32)

    own, up_own = kernel(
        pack_body,
        [narrow(part, columns), narrow(owners, up_rows, columns)],
        (stacked_down_weight, stacked_up_weight),
        (pltpu.HBM, pltpu.HBM),
        [pltpu.SemaphoreType.DMA((1 + half * owners,))],
    )
    beside = exchange(own, 0, 0, BESIDE)
    mirror = exchange(own, 0, 0, MIDDLE)

    slot = request_adapter_slot.reshape(1, rows)
    tok_own, tok_away = kernel(
        split_body,
        [narrow(rows + ID_ROWS, part)] * groups,
        (tokens, request_adapter_owner.reshape(1, rows), after(slot, own)),
        (pltpu.HBM, None, None),
        [pltpu.SemaphoreType.DMA((groups,))],
    )
    token_parts = [tok_own, exchange(tok_away, 1, 0, SAME)]
    hop_own, hop_away, places = kernel(
        functools.partial(hop_body, rows, capacity),
        [narrow(capacity + ID_ROWS, part)] * groups + [narrow(capacity, rows)],
        (tok_own, tok_away),
    )

    up_half = lax.all_to_all(up_own, "adapter", 0, 0, tiled=True)
    up_other = exchange(after(up_half, token_parts[1]), 1, 0, SAME)
    ups = kernel(ups_body, narrow(owners * columns, keys), (up_half, up_other))

    bases = kernel(
        functools.partial(base_body, keys), wide(shares, rows, keys), (tokens, base_key_weight)
    )
    bases = lax.all_to_all(bases, "mp", 0, 0, tiled=True)

    inside = exchange(after(beside, places), 0, 0, MIDDLE)
    outside = exchange(mirror, 0, 0, OUTWARD)
    hops = [
        exchange(hop_own, 0, 0, INWARD),
        exchange(hop_away, 1, 0, INWARD),
    ]

    folded, mask, numbers, base = kernel(
        functools.partial(early_body, (0, 1, 3), part, rows),
        [wide(groups, rows, LANES), wide(groups, rows, columns), wide(rows, 1), wide(rows, keys)],
        (*token_parts, after(own, up_half), beside, mirror, bases),
    )
    low, low_away, back, back_away = kernel(
        functools.partial(last_body, part, rows, capacity),
        [wide(ADAPTER_RANK, rows)] * groups + [wide(ADAPTER_RANK, capacity)] * groups,
        (*token_parts, *hops, after(folded, ups), mask, inside, outside),
    )

    near = exchange(low_away, 1, 0, SAME)
    back = exchange(back, 0, 0, OUTWARD)
    back_away = exchange(back_away, 1, 0, OUTWARD)
    low = kernel(merge_body, wide(ADAPTER_RANK, rows), (low, near, places, back, back_away))
    bit = shares // 2
    while bit > 1:
        low = low + exchange(low, 0, bit, SAME)
        bit //= 2
    low_far = exchange(low, 0, 1, SAME)
    return kernel(finish_body, narrow(rows, keys), (low, low_far, base, numbers, ups))


def row_limit(rows):
    return max(2, 3 * rows // (2 * lax.axis_size("adapter")))


def local(*args):
    rows, columns = args[0].shape[0], args[2].shape[1]
    groups, owners, shares = (lax.axis_size(name) for name in AXES)
    fits = owners == OWNERS and groups == 2 and shares > 1 and shares & (shares - 1) == 0
    travels = fits and columns <= groups * row_limit(rows)
    return (gather if travels else dispatch)(*args)


def solution(mesh):
    placed = (
        P(("groups", "adapter"), "mp"),
        P("mp", None),
        P("mp", "adapter"),
        P("adapter", "mp"),
        P(("groups", "adapter"), None),
        P(("groups", "adapter")),
    )
    return jax.shard_map(
        local, mesh=mesh, in_specs=placed, out_specs=P(("groups", "adapter"), "mp"), check_vma=False
    )
```

```python
import functools

import jax
import jax.numpy as jnp
from jax import lax
from jax.experimental import pallas as pl
from jax.experimental.pallas import tpu as pltpu
from jax.sharding import PartitionSpec as P

ADAPTER_RANK = 16


ADAPTER_SCALE = 2.0


def dispatch(
    tokens,
    base_key_weight,
    stacked_down_weight,
    stacked_up_weight,
    request_adapter_owner,
    request_adapter_slot,
):
    rows_here = tokens.shape[0]
    feature_share = tokens.shape[1]
    owner_count = lax.axis_size("adapter")
    capacity = max(2, 3 * rows_here // (2 * owner_count))
    local_adapters = stacked_down_weight.shape[1] // ADAPTER_RANK
    key_output_share = stacked_up_weight.shape[1]
    owners = request_adapter_owner.reshape(-1)
    onehot = (owners[:, None] == jnp.arange(owner_count, dtype=jnp.int32)[None, :]).astype(
        jnp.int32
    )
    before = jnp.sum((jnp.cumsum(onehot, axis=0) - onehot) * onehot, axis=1)
    places = owners * capacity + before
    send_rows = (
        jnp.zeros((owner_count * capacity, feature_share), jnp.bfloat16).at[places].set(tokens)
    )
    send_rows = send_rows.reshape(owner_count, capacity, feature_share)
    send_slots = (
        jnp.full((owner_count * capacity,), -1, jnp.int32).at[places].set(request_adapter_slot)
    )
    send_slots = send_slots.reshape(owner_count, capacity)
    input_rows = lax.all_to_all(send_rows, "adapter", split_axis=0, concat_axis=0, tiled=True)
    slots_in = lax.all_to_all(send_slots, "adapter", split_axis=0, concat_axis=0, tiled=True)
    key_projection_output = jnp.einsum(
        "rzq,qt->rzt", input_rows, stacked_down_weight, preferred_element_type=jnp.float32
    )
    key_projection_output = key_projection_output.reshape(
        input_rows.shape[0], input_rows.shape[1], local_adapters, ADAPTER_RANK
    )
    chosen = slots_in[:, :, None] == jnp.arange(local_adapters, dtype=jnp.int32)[None, None, :]
    partial_low = jnp.sum(jnp.where(chosen[:, :, :, None], key_projection_output, 0.0), axis=2)
    shrunk = lax.psum(partial_low, "mp")
    shrunk_bf = shrunk.astype(jnp.bfloat16)
    returned = lax.all_to_all(shrunk_bf, "adapter", split_axis=0, concat_axis=0, tiled=True)
    low_rows = returned.reshape(owner_count * capacity, ADAPTER_RANK)[places]
    gathered_up_weight = lax.all_gather(stacked_up_weight, "adapter", axis=0, tiled=True)
    adapter_ids = owners * local_adapters + request_adapter_slot
    up_taken = gathered_up_weight.reshape(-1, ADAPTER_RANK, key_output_share)[adapter_ids]
    adapter_updates = jnp.einsum(
        "tr,trk->tk", low_rows, up_taken, preferred_element_type=jnp.float32
    ).astype(jnp.bfloat16)
    base_output_share = lax.psum_scatter(
        lax.dot_general(
            base_key_weight, tokens, (((0,), (1,)), ((), ())), preferred_element_type=jnp.float32
        ),
        "mp",
        scatter_dimension=0,
        tiled=True,
    )
    return (base_output_share.T + ADAPTER_SCALE * adapter_updates.astype(jnp.float32)).astype(
        jnp.bfloat16
    )


AXES = ("groups", "adapter", "mp")
ID_ROWS = 16
OWNERS = 4
LANES = 128


def exchange(x, group_bits, share_bits, owners):
    groups, count, shares = (lax.axis_size(name) for name in AXES)

    def number(g, a, m):
        return (g * count + a) * shares + m

    pairs = [
        (number(g, a, m), number(g ^ group_bits, b, m ^ share_bits))
        for g in range(groups)
        for a, b in owners
        for m in range(shares)
    ]
    return lax.ppermute(x, AXES, pairs)


SAME = tuple((a, a) for a in range(OWNERS))
BESIDE = ((0, 1), (1, 0), (2, 3), (3, 2))
MIDDLE = ((1, 2), (2, 1))
ENDS = ((0, 3), (3, 0))
OUTWARD = ((1, 0), (2, 3))
INWARD = ((0, 1), (3, 2))


def after(x, *others):
    return lax.optimization_barrier((x, *others))[0]


def kernel(body, outs, operands, flops=0, spaces=None, scratch=()):
    inner = pl.BlockSpec(memory_space=pltpu.VMEM)
    specs = [inner if s is None else pl.BlockSpec(memory_space=s) for s in spaces or ()]
    touched = sum(x.size * x.dtype.itemsize for x in jax.tree.leaves((operands, outs)))
    return pl.pallas_call(
        body,
        out_shape=outs,
        in_specs=specs or [inner] * len(operands),
        out_specs=jax.tree.map(lambda _: inner, outs),
        scratch_shapes=scratch,
        compiler_params=pltpu.CompilerParams(vmem_limit_bytes=16 * 1024 * 1024),
        cost_estimate=pl.CostEstimate(flops=flops, bytes_accessed=touched, transcendentals=0),
    )(*operands)


def copy_all(copies):
    for copy in copies:
        copy.start()
    for copy in copies:
        copy.wait()


def pack_body(down, up, out, sems):
    g = lax.axis_index("groups")
    columns, keys = down.shape[1], up.shape[1]
    count = columns // keys
    size = up.shape[0] // count
    part = out.shape[0] - size
    mine = down.at[pl.ds(pl.multiple_of(g * part, part), part), :]
    copies = [pltpu.make_async_copy(mine, out.at[pl.ds(0, part), :], sems.at[count])]
    for k in range(count):
        copies.append(
            pltpu.make_async_copy(
                up.at[pl.ds(k * size, size), :],
                out.at[pl.ds(part, size), pl.ds(k * keys, keys)],
                sems.at[k],
            )
        )
    copy_all(copies)


def split_body(tokens, owner, slot, own, away, sems):
    g = lax.axis_index("groups")
    rows, part = tokens.shape[0], own.shape[1]
    copies = []
    for n, (out, half) in enumerate(((own, g), (away, 1 - g))):
        taken = tokens.at[:, pl.ds(pl.multiple_of(half * part, part), part)]
        copies.append(pltpu.make_async_copy(taken, out.at[pl.ds(0, rows), :], sems.at[n]))
    for copy in copies:
        copy.start()
    row = lax.broadcasted_iota(jnp.int32, (ID_ROWS, rows), 0)
    ids = jnp.where(row == 0, owner[...], jnp.where(row == 1, slot[...], 0))
    ids = ids.astype(jnp.float32).astype(jnp.bfloat16)
    for out in (own, away):
        out[rows:, :rows] = ids
        out[rows:, rows:] = jnp.zeros((ID_ROWS, part - rows), jnp.bfloat16)
    for copy in copies:
        copy.wait()


def hop_body(rows, capacity, own, away, own_out, away_out, places):
    a = lax.axis_index("adapter")
    part = own.shape[1]
    ids = own[rows:, :rows]
    match = (ids.astype(jnp.float32) == (OWNERS - 1 - a).astype(jnp.float32)).astype(jnp.bfloat16)
    earlier = lax.broadcasted_iota(jnp.int32, (rows, rows), 0) < lax.broadcasted_iota(
        jnp.int32, (rows, rows), 1
    )
    rank = jnp.dot(match, earlier.astype(jnp.bfloat16), preferred_element_type=jnp.float32)
    place = lax.broadcasted_iota(jnp.int32, (capacity, rows), 0).astype(jnp.float32)
    taken = (place == rank[0:1]) & (match[0:1].astype(jnp.float32) > 0)
    chosen = taken.astype(jnp.bfloat16)
    places[...] = chosen
    kept = lax.dot_general(ids, chosen, NT, preferred_element_type=jnp.float32)
    for tokens, out in ((own, own_out), (away, away_out)):
        packed = jnp.dot(chosen, tokens[:rows, :], preferred_element_type=jnp.float32)
        out[:capacity, :] = packed.astype(jnp.bfloat16)
        out[capacity:, :] = jnp.zeros((ID_ROWS, part), jnp.bfloat16)
        out[capacity:, :capacity] = kept.astype(jnp.bfloat16)


NT = (((1,), (1,)), ((), ()))
TN = (((0,), (0,)), ((), ()))


def base_body(keys, tokens, weights, out):
    wide = jnp.dot(tokens[...], weights[...], preferred_element_type=jnp.float32)
    for k in range(out.shape[0]):
        out[k] = wide[:, k * keys : (k + 1) * keys]


def id_columns(rows_ref, start, count):
    eye = (
        lax.broadcasted_iota(jnp.int32, (ID_ROWS, ID_ROWS), 0)
        == lax.broadcasted_iota(jnp.int32, (ID_ROWS, ID_ROWS), 1)
    ).astype(jnp.bfloat16)
    ids = lax.dot_general(
        rows_ref[start : start + ID_ROWS, :count], eye, TN, preferred_element_type=jnp.float32
    )
    return ids[:, 0:1], ids[:, 1:2]


def adapters(rows, columns):
    column = lax.broadcasted_iota(jnp.int32, (rows, columns), 1)
    return (column // ADAPTER_RANK).astype(jnp.float32)


def fold(wide):
    folded = wide[:, :LANES]
    for k in range(1, wide.shape[1] // LANES):
        folded = folded + wide[:, k * LANES : (k + 1) * LANES]
    return folded


def low_rank(folded):
    turned = folded.T
    low = turned[:ADAPTER_RANK]
    for k in range(1, LANES // ADAPTER_RANK):
        low = low + turned[k * ADAPTER_RANK : (k + 1) * ADAPTER_RANK]
    return low


def early_body(bits, part, rows, *refs):
    groups = lax.axis_size("groups")
    a = lax.axis_index("adapter")
    token_refs, rest = refs[:groups], refs[groups:]
    blocks, (bases, folded, mask, numbers, base) = rest[: len(bits)], rest[len(bits) :]
    columns = blocks[0].shape[1]
    total = bases[0]
    for k in range(1, bases.shape[0]):
        total = total + bases[k]
    base[...] = total
    adapter = adapters(rows, columns)
    for n, tokens in enumerate(token_refs):
        owner, slot = id_columns(tokens, rows, rows)
        if n == 0:
            numbers[...] = owner * (columns // ADAPTER_RANK) + slot
        right = adapter == slot
        picked = jnp.zeros((rows, columns), jnp.float32)
        for bit, block in zip(bits, blocks):
            wide = jnp.dot(tokens[:rows, :], block[:part, :], preferred_element_type=jnp.float32)
            picked = jnp.where(owner == (a ^ bit).astype(jnp.float32), wide, picked)
        folded[n] = fold(jnp.where(right, picked, 0.0))
        mask[n] = jnp.where(owner == (a ^ 2).astype(jnp.float32), right.astype(jnp.float32), 0.0)


def last_body(part, rows, capacity, *refs):
    groups = lax.axis_size("groups")
    a = lax.axis_index("adapter")
    token_refs, rest = refs[:groups], refs[groups:]
    hops, rest = rest[:groups], rest[groups:]
    folded, mask, inside, outside = rest[:4]
    lows, hop_lows = rest[4 : 4 + groups], rest[4 + groups :]
    columns = inside.shape[1]

    def finish(block):
        for n, tokens in enumerate(token_refs):
            wide = jnp.dot(tokens[:rows, :], block[:part, :], preferred_element_type=jnp.float32)
            kept = fold(jnp.where(mask[n] > 0, wide, 0.0))
            lows[n][...] = low_rank(folded[n] + kept)

    middle = (a == 1) | (a == 2)

    @pl.when(middle)
    def _():
        finish(inside)
        adapter = adapters(capacity, columns)
        for hop, out in zip(hops, hop_lows):
            _, slot = id_columns(hop, capacity, capacity)
            wide = jnp.dot(hop[:capacity, :], inside[:part, :], preferred_element_type=jnp.float32)
            kept = fold(jnp.where(adapter == slot, wide, 0.0))
            rest_rows = -capacity % LANES
            kept = jnp.concatenate([kept, jnp.zeros((rest_rows, LANES), jnp.float32)], axis=0)
            out[...] = low_rank(kept)[:, :capacity]

    @pl.when(jnp.logical_not(middle))
    def _():
        finish(outside)
        for out in hop_lows:
            out[...] = jnp.zeros(out.shape, jnp.float32)


def merge_body(low, near, places, *refs):
    hops, out = refs[:-1], refs[-1]
    back = hops[0][...]
    for hop in hops[1:]:
        back = back + hop[...]
    spread = jnp.zeros(low.shape, jnp.float32)
    for _ in range(3):
        piece = back.astype(jnp.bfloat16)
        back = back - piece.astype(jnp.float32)
        spread = spread + jnp.dot(piece, places[...], preferred_element_type=jnp.float32)
    out[...] = low[...] + near[...] + spread


def ups_body(part, own, beside, mirror, inside, outside, distant, out):
    a = lax.axis_index("adapter")
    columns, keys = distant.shape
    count = columns // keys
    size = columns // count

    def place(number, block):
        for k in range(count):
            start = number * columns + k * size
            out[start : start + size, :] = block[part:, k * keys : (k + 1) * keys]

    place(0, own)
    place(1, beside)
    middle = (a == 1) | (a == 2)

    @pl.when(middle)
    def _():
        place(2, inside)
        place(3, mirror)

    @pl.when(jnp.logical_not(middle))
    def _():
        place(2, outside)
        out[3 * columns :, :] = distant[...]


def finish_body(near, far, base, numbers, ups, out):
    a = lax.axis_index("adapter")
    rows = out.shape[0]
    columns = ups.shape[0] // OWNERS
    column = lax.broadcasted_iota(jnp.int32, (ADAPTER_RANK, columns), 1)
    row = lax.broadcasted_iota(jnp.int32, (ADAPTER_RANK, columns), 0)
    repeat = (lax.rem(column, ADAPTER_RANK) == row).astype(jnp.bfloat16)
    shrunk = (near[...] + far[...]).astype(jnp.bfloat16)
    spread = lax.dot_general(shrunk, repeat, TN, preferred_element_type=jnp.float32)
    adapter = adapters(rows, columns)
    updates = jnp.zeros(out.shape, jnp.float32)
    for i in range(OWNERS):
        wanted = numbers[...] - ((a ^ i) * (columns // ADAPTER_RANK)).astype(jnp.float32)
        chosen = jnp.where(adapter == wanted, spread, 0.0).astype(jnp.bfloat16)
        up = ups[i * columns : (i + 1) * columns, :]
        updates = updates + jnp.dot(chosen, up, preferred_element_type=jnp.float32)
    updates = updates.astype(jnp.bfloat16).astype(jnp.float32)
    out[...] = (base[...] + ADAPTER_SCALE * updates).astype(jnp.bfloat16)


def gather(
    tokens,
    base_key_weight,
    stacked_down_weight,
    stacked_up_weight,
    request_adapter_owner,
    request_adapter_slot,
):
    rows, features = tokens.shape
    groups, owners, shares = (lax.axis_size(name) for name in AXES)
    columns = stacked_down_weight.shape[1]
    keys = stacked_up_weight.shape[1]
    part = features // groups
    half = columns // keys
    capacity = -(-row_limit(rows) // ID_ROWS) * ID_ROWS

    def narrow(*dims):
        return jax.ShapeDtypeStruct(dims, jnp.bfloat16)

    def wide(*dims):
        return jax.ShapeDtypeStruct(dims, jnp.float32)

    own = kernel(
        pack_body,
        narrow(part + columns // half, columns),
        (stacked_down_weight, stacked_up_weight),
        0,
        (pltpu.HBM, pltpu.HBM),
        [pltpu.SemaphoreType.DMA((1 + half,))],
    )
    beside = exchange(own, 0, 0, BESIDE)
    mirror = exchange(own, 0, 0, MIDDLE)
    distant = exchange(after(stacked_up_weight, own), 0, 0, ENDS)

    slot = request_adapter_slot.reshape(1, rows)
    tok_own, tok_away = kernel(
        split_body,
        [narrow(rows + ID_ROWS, part)] * groups,
        (tokens, request_adapter_owner.reshape(1, rows), after(slot, own)),
        0,
        (pltpu.HBM, None, None),
        [pltpu.SemaphoreType.DMA((groups,))],
    )
    token_parts = [tok_own, exchange(tok_away, 1, 0, SAME)]
    hop_own, hop_away, places = kernel(
        functools.partial(hop_body, rows, capacity),
        [narrow(capacity + ID_ROWS, part)] * groups + [narrow(capacity, rows)],
        (tok_own, tok_away),
        2 * capacity * rows * features,
    )

    bases = kernel(
        functools.partial(base_body, keys), wide(shares, rows, keys), (tokens, base_key_weight),
        2 * rows * features * shares * keys,
    )
    bases = lax.all_to_all(bases, "mp", 0, 0, tiled=True)

    inside = exchange(after(beside, places), 0, 0, MIDDLE)
    outside = exchange(mirror, 0, 0, OUTWARD)
    hops = [
        exchange(hop_own, 0, 0, INWARD),
        exchange(hop_away, 1, 0, INWARD),
    ]

    folded, mask, numbers, base = kernel(
        functools.partial(early_body, (0, 1, 3), part, rows),
        [wide(groups, rows, LANES), wide(groups, rows, columns), wide(rows, 1), wide(rows, keys)],
        (*token_parts, own, beside, mirror, after(bases, distant)),
        6 * groups * rows * part * columns,
    )
    low, low_away, back, back_away = kernel(
        functools.partial(last_body, part, rows, capacity),
        [wide(ADAPTER_RANK, rows)] * groups + [wide(ADAPTER_RANK, capacity)] * groups,
        (*token_parts, *hops, folded, mask, inside, outside),
        2 * groups * (rows + capacity) * part * columns,
    )

    near = exchange(low_away, 1, 0, SAME)
    back = exchange(back, 0, 0, OUTWARD)
    back_away = exchange(back_away, 1, 0, OUTWARD)
    low = kernel(merge_body, wide(ADAPTER_RANK, rows), (low, near, places, back, back_away))
    bit = shares // 2
    while bit > 1:
        low = low + exchange(low, 0, bit, SAME)
        bit //= 2
    low_far = exchange(low, 0, 1, SAME)
    ups = kernel(
        functools.partial(ups_body, part),
        narrow(owners * columns, keys),
        (own, beside, mirror, inside, outside, distant),
    )
    return kernel(finish_body, narrow(rows, keys), (low, low_far, base, numbers, ups))


def row_limit(rows):
    return max(2, 3 * rows // (2 * lax.axis_size("adapter")))


def local(*args):
    rows, columns = args[0].shape[0], args[2].shape[1]
    groups, owners, shares = (lax.axis_size(name) for name in AXES)
    fits = owners == OWNERS and groups == 2 and shares > 1 and shares & (shares - 1) == 0
    travels = fits and columns <= groups * row_limit(rows)
    return (gather if travels else dispatch)(*args)


def solution(mesh):
    placed = (
        P(("groups", "adapter"), "mp"),
        P("mp", None),
        P("mp", "adapter"),
        P("adapter", "mp"),
        P(("groups", "adapter"), None),
        P(("groups", "adapter")),
    )
    return jax.shard_map(
        local, mesh=mesh, in_specs=placed, out_specs=P(("groups", "adapter"), "mp"), check_vma=False
    )
```

```python
import functools

import jax
import jax.numpy as jnp
from jax import lax
from jax.experimental import pallas as pl
from jax.experimental.pallas import tpu as pltpu
from jax.sharding import PartitionSpec as P

ADAPTER_RANK = 16


ADAPTER_SCALE = 2.0


def dispatch(
    tokens,
    base_key_weight,
    stacked_down_weight,
    stacked_up_weight,
    request_adapter_owner,
    request_adapter_slot,
):
    rows_here = tokens.shape[0]
    feature_share = tokens.shape[1]
    owner_count = lax.axis_size("adapter")
    capacity = max(2, 3 * rows_here // (2 * owner_count))
    local_adapters = stacked_down_weight.shape[1] // ADAPTER_RANK
    key_output_share = stacked_up_weight.shape[1]
    owners = request_adapter_owner.reshape(-1)
    onehot = (owners[:, None] == jnp.arange(owner_count, dtype=jnp.int32)[None, :]).astype(
        jnp.int32
    )
    before = jnp.sum((jnp.cumsum(onehot, axis=0) - onehot) * onehot, axis=1)
    places = owners * capacity + before
    send_rows = (
        jnp.zeros((owner_count * capacity, feature_share), jnp.bfloat16).at[places].set(tokens)
    )
    send_rows = send_rows.reshape(owner_count, capacity, feature_share)
    send_slots = (
        jnp.full((owner_count * capacity,), -1, jnp.int32).at[places].set(request_adapter_slot)
    )
    send_slots = send_slots.reshape(owner_count, capacity)
    input_rows = lax.all_to_all(send_rows, "adapter", split_axis=0, concat_axis=0, tiled=True)
    slots_in = lax.all_to_all(send_slots, "adapter", split_axis=0, concat_axis=0, tiled=True)
    key_projection_output = jnp.einsum(
        "rzq,qt->rzt", input_rows, stacked_down_weight, preferred_element_type=jnp.float32
    )
    key_projection_output = key_projection_output.reshape(
        input_rows.shape[0], input_rows.shape[1], local_adapters, ADAPTER_RANK
    )
    chosen = slots_in[:, :, None] == jnp.arange(local_adapters, dtype=jnp.int32)[None, None, :]
    partial_low = jnp.sum(jnp.where(chosen[:, :, :, None], key_projection_output, 0.0), axis=2)
    shrunk = lax.psum(partial_low, "mp")
    shrunk_bf = shrunk.astype(jnp.bfloat16)
    returned = lax.all_to_all(shrunk_bf, "adapter", split_axis=0, concat_axis=0, tiled=True)
    low_rows = returned.reshape(owner_count * capacity, ADAPTER_RANK)[places]
    gathered_up_weight = lax.all_gather(stacked_up_weight, "adapter", axis=0, tiled=True)
    adapter_ids = owners * local_adapters + request_adapter_slot
    up_taken = gathered_up_weight.reshape(-1, ADAPTER_RANK, key_output_share)[adapter_ids]
    adapter_updates = jnp.einsum(
        "tr,trk->tk", low_rows, up_taken, preferred_element_type=jnp.float32
    ).astype(jnp.bfloat16)
    base_output_share = lax.psum_scatter(
        lax.dot_general(
            base_key_weight, tokens, (((0,), (1,)), ((), ())), preferred_element_type=jnp.float32
        ),
        "mp",
        scatter_dimension=0,
        tiled=True,
    )
    return (base_output_share.T + ADAPTER_SCALE * adapter_updates.astype(jnp.float32)).astype(
        jnp.bfloat16
    )


AXES = ("groups", "adapter", "mp")
ID_ROWS = 16
OWNERS = 4
LANES = 128


def exchange(x, group_bits, share_bits, owners):
    groups, count, shares = (lax.axis_size(name) for name in AXES)

    def number(g, a, m):
        return (g * count + a) * shares + m

    pairs = [
        (number(g, a, m), number(g ^ group_bits, b, m ^ share_bits))
        for g in range(groups)
        for a, b in owners
        for m in range(shares)
    ]
    return lax.ppermute(x, AXES, pairs)


SAME = tuple((a, a) for a in range(OWNERS))
BESIDE = ((0, 1), (1, 0), (2, 3), (3, 2))
MIDDLE = ((1, 2), (2, 1))
OUTWARD = ((1, 0), (2, 3))
INWARD = ((0, 1), (3, 2))


def after(x, *others):
    return lax.optimization_barrier((x, *others))[0]


def kernel(body, outs, operands, flops=0, spaces=None, scratch=()):
    inner = pl.BlockSpec(memory_space=pltpu.VMEM)
    specs = [inner if s is None else pl.BlockSpec(memory_space=s) for s in spaces or ()]
    touched = sum(x.size * x.dtype.itemsize for x in jax.tree.leaves((operands, outs)))
    return pl.pallas_call(
        body,
        out_shape=outs,
        in_specs=specs or [inner] * len(operands),
        out_specs=jax.tree.map(lambda _: inner, outs),
        scratch_shapes=scratch,
        compiler_params=pltpu.CompilerParams(vmem_limit_bytes=16 * 1024 * 1024),
        cost_estimate=pl.CostEstimate(flops=flops, bytes_accessed=touched, transcendentals=0),
    )(*operands)


def copy_all(copies):
    for copy in copies:
        copy.start()
    for copy in copies:
        copy.wait()


def pack_body(down, up, out, sems):
    g = lax.axis_index("groups")
    columns, keys = down.shape[1], up.shape[1]
    count = columns // keys
    size = up.shape[0] // count
    part = out.shape[0] - size
    mine = down.at[pl.ds(pl.multiple_of(g * part, part), part), :]
    copies = [pltpu.make_async_copy(mine, out.at[pl.ds(0, part), :], sems.at[count])]
    for k in range(count):
        copies.append(
            pltpu.make_async_copy(
                up.at[pl.ds(k * size, size), :],
                out.at[pl.ds(part, size), pl.ds(k * keys, keys)],
                sems.at[k],
            )
        )
    copy_all(copies)


def split_body(tokens, owner, slot, own, away, sems):
    g = lax.axis_index("groups")
    rows, part = tokens.shape[0], own.shape[1]
    copies = []
    for n, (out, half) in enumerate(((own, g), (away, 1 - g))):
        taken = tokens.at[:, pl.ds(pl.multiple_of(half * part, part), part)]
        copies.append(pltpu.make_async_copy(taken, out.at[pl.ds(0, rows), :], sems.at[n]))
    for copy in copies:
        copy.start()
    row = lax.broadcasted_iota(jnp.int32, (ID_ROWS, rows), 0)
    ids = jnp.where(row == 0, owner[...], jnp.where(row == 1, slot[...].reshape(1, rows), 0))
    ids = ids.astype(jnp.float32).astype(jnp.bfloat16)
    for out in (own, away):
        out[rows:, :rows] = ids
        out[rows:, rows:] = jnp.zeros((ID_ROWS, part - rows), jnp.bfloat16)
    for copy in copies:
        copy.wait()


def hop_body(rows, capacity, own, away, weights, own_out, away_out, places, bases):
    a, g = lax.axis_index("adapter"), lax.axis_index("groups")
    part = own.shape[1]
    ids = own[rows:, :rows]
    match = (ids.astype(jnp.float32) == (OWNERS - 1 - a).astype(jnp.float32)).astype(jnp.bfloat16)
    earlier = lax.broadcasted_iota(jnp.int32, (rows, rows), 0) < lax.broadcasted_iota(
        jnp.int32, (rows, rows), 1
    )
    rank = jnp.dot(match, earlier.astype(jnp.bfloat16), preferred_element_type=jnp.float32)
    place = lax.broadcasted_iota(jnp.int32, (capacity, rows), 0).astype(jnp.float32)
    taken = (place == rank[0:1]) & (match[0:1].astype(jnp.float32) > 0)
    chosen = taken.astype(jnp.bfloat16)
    places[...] = chosen
    kept = lax.dot_general(ids, chosen, NT, preferred_element_type=jnp.float32)
    for tokens, out in ((own, own_out), (away, away_out)):
        packed = jnp.dot(chosen, tokens[:rows, :], preferred_element_type=jnp.float32)
        out[:capacity, :] = packed.astype(jnp.bfloat16)
        out[capacity:, :] = jnp.zeros((ID_ROWS, part), jnp.bfloat16)
        out[capacity:, :capacity] = kept.astype(jnp.bfloat16)
    base = jnp.zeros((rows, weights.shape[1]), jnp.float32)
    for tokens, half in ((own, g), (away, 1 - g)):
        part_weights = weights[pl.ds(pl.multiple_of(half * part, part), part), :]
        base = base + jnp.dot(tokens[:rows, :], part_weights, preferred_element_type=jnp.float32)
    keys = bases.shape[2]
    for k in range(bases.shape[0]):
        bases[k] = base[:, k * keys : (k + 1) * keys]


NT = (((1,), (1,)), ((), ()))
TN = (((0,), (0,)), ((), ()))


def id_columns(rows_ref, start, count):
    eye = (
        lax.broadcasted_iota(jnp.int32, (ID_ROWS, ID_ROWS), 0)
        == lax.broadcasted_iota(jnp.int32, (ID_ROWS, ID_ROWS), 1)
    ).astype(jnp.bfloat16)
    ids = lax.dot_general(
        rows_ref[start : start + ID_ROWS, :count], eye, TN, preferred_element_type=jnp.float32
    )
    return ids[:, 0:1], ids[:, 1:2]


def adapters(rows, columns):
    column = lax.broadcasted_iota(jnp.int32, (rows, columns), 1)
    return (column // ADAPTER_RANK).astype(jnp.float32)


def fold(wide):
    folded = wide[:, :LANES]
    for k in range(1, wide.shape[1] // LANES):
        folded = folded + wide[:, k * LANES : (k + 1) * LANES]
    return folded


def low_rank(folded):
    turned = folded.T
    low = turned[:ADAPTER_RANK]
    for k in range(1, LANES // ADAPTER_RANK):
        low = low + turned[k * ADAPTER_RANK : (k + 1) * ADAPTER_RANK]
    return low


def early_body(bits, part, rows, *refs):
    groups = lax.axis_size("groups")
    a = lax.axis_index("adapter")
    token_refs, rest = refs[:groups], refs[groups:]
    blocks, (bases, folded, mask, numbers, base) = rest[: len(bits)], rest[len(bits) :]
    columns = blocks[0].shape[1]
    total = bases[0]
    for k in range(1, bases.shape[0]):
        total = total + bases[k]
    base[...] = total
    adapter = adapters(rows, columns)
    for n, tokens in enumerate(token_refs):
        owner, slot = id_columns(tokens, rows, rows)
        if n == 0:
            numbers[...] = owner * (columns // ADAPTER_RANK) + slot
        right = adapter == slot
        picked = jnp.zeros((rows, columns), jnp.float32)
        for bit, block in zip(bits, blocks):
            wide = jnp.dot(tokens[:rows, :], block[:part, :], preferred_element_type=jnp.float32)
            picked = jnp.where(owner == (a ^ bit).astype(jnp.float32), wide, picked)
        folded[n] = fold(jnp.where(right, picked, 0.0))
        mask[n] = jnp.where(owner == (a ^ 2).astype(jnp.float32), right.astype(jnp.float32), 0.0)


def hop_mask_body(capacity, *refs):
    hops, out = refs[:-1], refs[-1]
    adapter = adapters(capacity, out.shape[2])
    for n, hop in enumerate(hops):
        _, slot = id_columns(hop, capacity, capacity)
        out[n] = (adapter == slot).astype(jnp.float32)


def last_body(part, rows, capacity, *refs):
    groups = lax.axis_size("groups")
    a = lax.axis_index("adapter")
    token_refs, rest = refs[:groups], refs[groups:]
    hops, rest = rest[:groups], rest[groups:]
    hop_mask, folded, mask, inside, outside = rest[:5]
    lows, hop_lows, far_ups = rest[5 : 5 + groups], rest[5 + groups : -1], rest[-1]
    columns = inside.shape[1]

    def finish(block):
        for n, tokens in enumerate(token_refs):
            wide = jnp.dot(tokens[:rows, :], block[:part, :], preferred_element_type=jnp.float32)
            kept = fold(jnp.where(mask[n] > 0, wide, 0.0))
            lows[n][...] = low_rank(folded[n] + kept)

    middle = (a == 1) | (a == 2)

    @pl.when(middle)
    def _():
        finish(inside)
        far_ups[...] = inside[part:, :]
        for n, (hop, out) in enumerate(zip(hops, hop_lows)):
            wide = jnp.dot(hop[:capacity, :], inside[:part, :], preferred_element_type=jnp.float32)
            kept = fold(jnp.where(hop_mask[n] > 0, wide, 0.0))
            rest_rows = -capacity % LANES
            kept = jnp.concatenate([kept, jnp.zeros((rest_rows, LANES), jnp.float32)], axis=0)
            out[...] = low_rank(kept)[:, :capacity]

    @pl.when(jnp.logical_not(middle))
    def _():
        finish(outside)
        far_ups[...] = outside[part:, :]
        for out in hop_lows:
            out[...] = jnp.zeros(out.shape, jnp.float32)


def merge_body(low, near, places, *refs):
    hops, out = refs[:-1], refs[-1]
    back = hops[0][...]
    for hop in hops[1:]:
        back = back + hop[...]
    spread = jnp.zeros(low.shape, jnp.float32)
    for _ in range(3):
        piece = back.astype(jnp.bfloat16)
        back = back - piece.astype(jnp.float32)
        spread = spread + jnp.dot(piece, places[...], preferred_element_type=jnp.float32)
    out[...] = low[...] + near[...] + spread


def ups_body(keys, part, own, beside, mirror, inside, outside, distant, out):
    a = lax.axis_index("adapter")
    columns = own.shape[1]
    count = columns // keys
    size = columns // count

    def place(number, block, first=part):
        for k in range(count):
            start = number * columns + k * size
            out[start : start + size, :] = block[first:, k * keys : (k + 1) * keys]

    place(0, own)
    place(1, beside)
    middle = (a == 1) | (a == 2)

    @pl.when(middle)
    def _():
        place(2, inside)
        place(3, mirror)

    @pl.when(jnp.logical_not(middle))
    def _():
        place(2, outside)
        place(3, distant, 0)


def finish_body(near, far, base, numbers, ups, out):
    a = lax.axis_index("adapter")
    rows = out.shape[0]
    columns = ups.shape[0] // OWNERS
    column = lax.broadcasted_iota(jnp.int32, (ADAPTER_RANK, columns), 1)
    row = lax.broadcasted_iota(jnp.int32, (ADAPTER_RANK, columns), 0)
    repeat = (lax.rem(column, ADAPTER_RANK) == row).astype(jnp.bfloat16)
    shrunk = (near[...] + far[...]).astype(jnp.bfloat16)
    spread = lax.dot_general(shrunk, repeat, TN, preferred_element_type=jnp.float32)
    adapter = adapters(rows, columns)
    updates = jnp.zeros(out.shape, jnp.float32)
    for i in range(OWNERS):
        wanted = numbers[...] - ((a ^ i) * (columns // ADAPTER_RANK)).astype(jnp.float32)
        chosen = jnp.where(adapter == wanted, spread, 0.0).astype(jnp.bfloat16)
        up = ups[i * columns : (i + 1) * columns, :]
        updates = updates + jnp.dot(chosen, up, preferred_element_type=jnp.float32)
    updates = updates.astype(jnp.bfloat16).astype(jnp.float32)
    out[...] = (base[...] + ADAPTER_SCALE * updates).astype(jnp.bfloat16)


def gather(
    tokens,
    base_key_weight,
    stacked_down_weight,
    stacked_up_weight,
    request_adapter_owner,
    request_adapter_slot,
):
    rows, features = tokens.shape
    groups, owners, shares = (lax.axis_size(name) for name in AXES)
    columns = stacked_down_weight.shape[1]
    keys = stacked_up_weight.shape[1]
    part = features // groups
    half = columns // keys
    capacity = -(-row_limit(rows) // ID_ROWS) * ID_ROWS

    def narrow(*dims):
        return jax.ShapeDtypeStruct(dims, jnp.bfloat16)

    def wide(*dims):
        return jax.ShapeDtypeStruct(dims, jnp.float32)

    own = kernel(
        pack_body,
        narrow(part + columns // half, columns),
        (stacked_down_weight, stacked_up_weight),
        0,
        (pltpu.HBM, pltpu.HBM),
        [pltpu.SemaphoreType.DMA((1 + half,))],
    )
    mirror = exchange(own, 0, 0, MIDDLE)
    beside = exchange(own, 0, 0, BESIDE)

    tok_own, tok_away = kernel(
        split_body,
        [narrow(rows + ID_ROWS, part)] * groups,
        (tokens, request_adapter_owner.reshape(1, rows), after(request_adapter_slot, own)),
        0,
        (pltpu.HBM, None, None),
        [pltpu.SemaphoreType.DMA((groups,))],
    )
    token_parts = [tok_own, exchange(tok_away, 1, 0, SAME)]
    hop_own, hop_away, places, bases = kernel(
        functools.partial(hop_body, rows, capacity),
        [narrow(capacity + ID_ROWS, part)] * groups
        + [narrow(capacity, rows), wide(shares, rows, keys)],
        (tok_own, tok_away, base_key_weight),
        2 * rows * features * (capacity + shares * keys),
    )
    bases = lax.all_to_all(bases, "mp", 0, 0, tiled=True)

    inside = exchange(after(beside, places), 0, 0, MIDDLE)
    outside = exchange(mirror, 0, 0, OUTWARD)
    hops = [
        exchange(hop_own, 0, 0, INWARD),
        exchange(hop_away, 1, 0, INWARD),
    ]

    folded, mask, numbers, base = kernel(
        functools.partial(early_body, (0, 1, 3), part, rows),
        [wide(groups, rows, LANES), wide(groups, rows, columns), wide(rows, 1), wide(rows, keys)],
        (*token_parts, own, beside, mirror, bases),
        6 * groups * rows * part * columns,
    )
    hop_mask = kernel(
        functools.partial(hop_mask_body, capacity), wide(groups, capacity, columns), (hops[0], after(hops[1], folded))
    )
    low, low_away, back, back_away, far_ups = kernel(
        functools.partial(last_body, part, rows, capacity),
        [wide(ADAPTER_RANK, rows)] * groups
        + [wide(ADAPTER_RANK, capacity)] * groups
        + [narrow(columns // half, columns)],
        (*token_parts, *hops, hop_mask, folded, mask, inside, outside),
        2 * groups * (rows + capacity) * part * columns,
    )

    near = exchange(low_away, 1, 0, SAME)
    back = exchange(back, 0, 0, OUTWARD)
    back_away = exchange(back_away, 1, 0, OUTWARD)
    distant = exchange(far_ups, 0, 0, OUTWARD)
    low = kernel(merge_body, wide(ADAPTER_RANK, rows), (low, near, places, back, back_away))
    bit = shares // 2
    while bit > 1:
        low = low + exchange(low, 0, bit, SAME)
        bit //= 2
    low_far = exchange(low, 0, 1, SAME)
    ups = kernel(
        functools.partial(ups_body, keys, part),
        narrow(owners * columns, keys),
        (own, beside, mirror, inside, outside, distant),
    )
    return kernel(finish_body, narrow(rows, keys), (low, low_far, base, numbers, ups))


def row_limit(rows):
    return max(2, 3 * rows // (2 * lax.axis_size("adapter")))


def local(*args):
    rows, columns = args[0].shape[0], args[2].shape[1]
    groups, owners, shares = (lax.axis_size(name) for name in AXES)
    fits = owners == OWNERS and groups == 2 and shares > 1 and shares & (shares - 1) == 0
    travels = fits and columns <= groups * row_limit(rows)
    return (gather if travels else dispatch)(*args)


def solution(mesh):
    placed = (
        P(("groups", "adapter"), "mp"),
        P("mp", None),
        P("mp", "adapter"),
        P("adapter", "mp"),
        P(("groups", "adapter"), None),
        P(("groups", "adapter")),
    )
    return jax.shard_map(
        local, mesh=mesh, in_specs=placed, out_specs=P(("groups", "adapter"), "mp"), check_vma=False
    )
```

```python
import functools

import jax
import jax.numpy as jnp
from jax import lax
from jax.experimental import pallas as pl
from jax.experimental.pallas import tpu as pltpu
from jax.sharding import PartitionSpec as P

ADAPTER_RANK = 16


ADAPTER_SCALE = 2.0


def dispatch(
    tokens,
    base_key_weight,
    stacked_down_weight,
    stacked_up_weight,
    request_adapter_owner,
    request_adapter_slot,
):
    rows_here = tokens.shape[0]
    feature_share = tokens.shape[1]
    owner_count = lax.axis_size("adapter")
    capacity = max(2, 3 * rows_here // (2 * owner_count))
    local_adapters = stacked_down_weight.shape[1] // ADAPTER_RANK
    key_output_share = stacked_up_weight.shape[1]
    owners = request_adapter_owner.reshape(-1)
    onehot = (owners[:, None] == jnp.arange(owner_count, dtype=jnp.int32)[None, :]).astype(
        jnp.int32
    )
    before = jnp.sum((jnp.cumsum(onehot, axis=0) - onehot) * onehot, axis=1)
    places = owners * capacity + before
    send_rows = (
        jnp.zeros((owner_count * capacity, feature_share), jnp.bfloat16).at[places].set(tokens)
    )
    send_rows = send_rows.reshape(owner_count, capacity, feature_share)
    send_slots = (
        jnp.full((owner_count * capacity,), -1, jnp.int32).at[places].set(request_adapter_slot)
    )
    send_slots = send_slots.reshape(owner_count, capacity)
    input_rows = lax.all_to_all(send_rows, "adapter", split_axis=0, concat_axis=0, tiled=True)
    slots_in = lax.all_to_all(send_slots, "adapter", split_axis=0, concat_axis=0, tiled=True)
    key_projection_output = jnp.einsum(
        "rzq,qt->rzt", input_rows, stacked_down_weight, preferred_element_type=jnp.float32
    )
    key_projection_output = key_projection_output.reshape(
        input_rows.shape[0], input_rows.shape[1], local_adapters, ADAPTER_RANK
    )
    chosen = slots_in[:, :, None] == jnp.arange(local_adapters, dtype=jnp.int32)[None, None, :]
    partial_low = jnp.sum(jnp.where(chosen[:, :, :, None], key_projection_output, 0.0), axis=2)
    shrunk = lax.psum(partial_low, "mp")
    shrunk_bf = shrunk.astype(jnp.bfloat16)
    returned = lax.all_to_all(shrunk_bf, "adapter", split_axis=0, concat_axis=0, tiled=True)
    low_rows = returned.reshape(owner_count * capacity, ADAPTER_RANK)[places]
    gathered_up_weight = lax.all_gather(stacked_up_weight, "adapter", axis=0, tiled=True)
    adapter_ids = owners * local_adapters + request_adapter_slot
    up_taken = gathered_up_weight.reshape(-1, ADAPTER_RANK, key_output_share)[adapter_ids]
    adapter_updates = jnp.einsum(
        "tr,trk->tk", low_rows, up_taken, preferred_element_type=jnp.float32
    ).astype(jnp.bfloat16)
    base_output_share = lax.psum_scatter(
        lax.dot_general(
            base_key_weight, tokens, (((0,), (1,)), ((), ())), preferred_element_type=jnp.float32
        ),
        "mp",
        scatter_dimension=0,
        tiled=True,
    )
    return (base_output_share.T + ADAPTER_SCALE * adapter_updates.astype(jnp.float32)).astype(
        jnp.bfloat16
    )


AXES = ("groups", "adapter", "mp")
ID_ROWS = 16
HOP_URGENCY = 12 * 10**9
OWNERS = 4
LANES = 128


def exchange(x, group_bits, share_bits, owners):
    groups, count, shares = (lax.axis_size(name) for name in AXES)

    def number(g, a, m):
        return (g * count + a) * shares + m

    pairs = [
        (number(g, a, m), number(g ^ group_bits, b, m ^ share_bits))
        for g in range(groups)
        for a, b in owners
        for m in range(shares)
    ]
    return lax.ppermute(x, AXES, pairs)


SAME = tuple((a, a) for a in range(OWNERS))
BESIDE = ((0, 1), (1, 0), (2, 3), (3, 2))
MIDDLE = ((1, 2), (2, 1))
ENDS = ((0, 3), (3, 0))
OUTWARD = ((1, 0), (2, 3))
INWARD = ((0, 1), (3, 2))


def after(x, *others):
    return lax.optimization_barrier((x, *others))[0]


def kernel(body, outs, operands, flops=0, spaces=None, scratch=()):
    inner = pl.BlockSpec(memory_space=pltpu.VMEM)
    specs = [inner if s is None else pl.BlockSpec(memory_space=s) for s in spaces or ()]
    touched = sum(x.size * x.dtype.itemsize for x in jax.tree.leaves((operands, outs)))
    return pl.pallas_call(
        body,
        out_shape=outs,
        in_specs=specs or [inner] * len(operands),
        out_specs=jax.tree.map(lambda _: inner, outs),
        scratch_shapes=scratch,
        compiler_params=pltpu.CompilerParams(vmem_limit_bytes=16 * 1024 * 1024),
        cost_estimate=pl.CostEstimate(flops=flops, bytes_accessed=touched, transcendentals=0),
    )(*operands)


def copy_all(copies):
    for copy in copies:
        copy.start()
    for copy in copies:
        copy.wait()


def pack_body(down, up, out, sems):
    g = lax.axis_index("groups")
    columns, keys = down.shape[1], up.shape[1]
    count = columns // keys
    size = up.shape[0] // count
    part = out.shape[0] - size
    mine = down.at[pl.ds(pl.multiple_of(g * part, part), part), :]
    copies = [pltpu.make_async_copy(mine, out.at[pl.ds(0, part), :], sems.at[count])]
    for k in range(count):
        copies.append(
            pltpu.make_async_copy(
                up.at[pl.ds(k * size, size), :],
                out.at[pl.ds(part, size), pl.ds(k * keys, keys)],
                sems.at[k],
            )
        )
    copy_all(copies)


def split_body(tokens, owner, slot, own, away, sems):
    g = lax.axis_index("groups")
    rows, part = tokens.shape[0], own.shape[1]
    copies = []
    for n, (out, half) in enumerate(((own, g), (away, 1 - g))):
        taken = tokens.at[:, pl.ds(pl.multiple_of(half * part, part), part)]
        copies.append(pltpu.make_async_copy(taken, out.at[pl.ds(0, rows), :], sems.at[n]))
    for copy in copies:
        copy.start()
    row = lax.broadcasted_iota(jnp.int32, (ID_ROWS, rows), 0)
    ids = jnp.where(row == 0, owner[...], jnp.where(row == 1, slot[...].reshape(1, rows), 0))
    ids = ids.astype(jnp.float32).astype(jnp.bfloat16)
    for out in (own, away):
        out[rows:, :rows] = ids
        out[rows:, rows:] = jnp.zeros((ID_ROWS, part - rows), jnp.bfloat16)
    for copy in copies:
        copy.wait()


def hop_body(rows, capacity, own, away, weights, own_out, away_out, places, bases):
    a, g = lax.axis_index("adapter"), lax.axis_index("groups")
    part = own.shape[1]
    ids = own[rows:, :rows]
    match = (ids.astype(jnp.float32) == (OWNERS - 1 - a).astype(jnp.float32)).astype(jnp.bfloat16)
    earlier = lax.broadcasted_iota(jnp.int32, (rows, rows), 0) < lax.broadcasted_iota(
        jnp.int32, (rows, rows), 1
    )
    rank = jnp.dot(match, earlier.astype(jnp.bfloat16), preferred_element_type=jnp.float32)
    place = lax.broadcasted_iota(jnp.int32, (capacity, rows), 0).astype(jnp.float32)
    taken = (place == rank[0:1]) & (match[0:1].astype(jnp.float32) > 0)
    chosen = taken.astype(jnp.bfloat16)
    places[...] = chosen
    kept = lax.dot_general(ids, chosen, NT, preferred_element_type=jnp.float32)
    for tokens, out in ((own, own_out), (away, away_out)):
        packed = jnp.dot(chosen, tokens[:rows, :], preferred_element_type=jnp.float32)
        out[:capacity, :] = packed.astype(jnp.bfloat16)
        out[capacity:, :] = jnp.zeros((ID_ROWS, part), jnp.bfloat16)
        out[capacity:, :capacity] = kept.astype(jnp.bfloat16)
    base = jnp.zeros((rows, weights.shape[1]), jnp.float32)
    for tokens, half in ((own, g), (away, 1 - g)):
        part_weights = weights[pl.ds(pl.multiple_of(half * part, part), part), :]
        base = base + jnp.dot(tokens[:rows, :], part_weights, preferred_element_type=jnp.float32)
    keys = bases.shape[2]
    for k in range(bases.shape[0]):
        bases[k] = base[:, k * keys : (k + 1) * keys]


NT = (((1,), (1,)), ((), ()))
TN = (((0,), (0,)), ((), ()))


def id_columns(rows_ref, start, count):
    eye = (
        lax.broadcasted_iota(jnp.int32, (ID_ROWS, ID_ROWS), 0)
        == lax.broadcasted_iota(jnp.int32, (ID_ROWS, ID_ROWS), 1)
    ).astype(jnp.bfloat16)
    ids = lax.dot_general(
        rows_ref[start : start + ID_ROWS, :count], eye, TN, preferred_element_type=jnp.float32
    )
    return ids[:, 0:1], ids[:, 1:2]


def adapters(rows, columns):
    column = lax.broadcasted_iota(jnp.int32, (rows, columns), 1)
    return (column // ADAPTER_RANK).astype(jnp.float32)


def fold(wide):
    folded = wide[:, :LANES]
    for k in range(1, wide.shape[1] // LANES):
        folded = folded + wide[:, k * LANES : (k + 1) * LANES]
    return folded


def low_rank(folded):
    turned = folded.T
    low = turned[:ADAPTER_RANK]
    for k in range(1, LANES // ADAPTER_RANK):
        low = low + turned[k * ADAPTER_RANK : (k + 1) * ADAPTER_RANK]
    return low


def stacked(wide, keys):
    return jnp.concatenate([wide[:, k : k + keys] for k in range(0, wide.shape[1], keys)], axis=0)


def early_body(bits, part, rows, *refs):
    groups = lax.axis_size("groups")
    a = lax.axis_index("adapter")
    token_refs, rest = refs[:groups], refs[groups:]
    blocks, (bases, folded, mask, numbers, base, ups) = rest[: len(bits)], rest[len(bits) :]
    columns = blocks[0].shape[1]
    for n, block in enumerate(blocks):
        ups[n] = stacked(block[part:, :], ups.shape[2])
    total = bases[0]
    for k in range(1, bases.shape[0]):
        total = total + bases[k]
    base[...] = total
    adapter = adapters(rows, columns)
    for n, tokens in enumerate(token_refs):
        owner, slot = id_columns(tokens, rows, rows)
        if n == 0:
            numbers[...] = owner * (columns // ADAPTER_RANK) + slot
        right = adapter == slot
        picked = jnp.zeros((rows, columns), jnp.float32)
        for bit, block in zip(bits, blocks):
            wide = jnp.dot(tokens[:rows, :], block[:part, :], preferred_element_type=jnp.float32)
            picked = jnp.where(owner == (a ^ bit).astype(jnp.float32), wide, picked)
        folded[n] = fold(jnp.where(right, picked, 0.0))
        mask[n] = jnp.where(owner == (a ^ 2).astype(jnp.float32), right.astype(jnp.float32), 0.0)


def hop_mask_body(capacity, *refs):
    hops, out = refs[:-1], refs[-1]
    adapter = adapters(capacity, out.shape[2])
    for n, hop in enumerate(hops):
        _, slot = id_columns(hop, capacity, capacity)
        out[n] = (adapter == slot).astype(jnp.float32)


def last_body(part, rows, capacity, *refs):
    groups = lax.axis_size("groups")
    a = lax.axis_index("adapter")
    token_refs, rest = refs[:groups], refs[groups:]
    hops, rest = rest[:groups], rest[groups:]
    hop_mask, folded, mask, outside, inside = rest[:5]
    lows, hop_lows, last_up = rest[5 : 5 + groups], rest[5 + groups : -1], rest[-1]
    columns = inside.shape[1]

    def finish(block):
        for n, tokens in enumerate(token_refs):
            wide = jnp.dot(tokens[:rows, :], block[:part, :], preferred_element_type=jnp.float32)
            kept = fold(jnp.where(mask[n] > 0, wide, 0.0))
            lows[n][...] = low_rank(folded[n] + kept)

    middle = (a == 1) | (a == 2)

    @pl.when(middle)
    def _():
        finish(inside)
        last_up[...] = stacked(inside[part:, :], last_up.shape[1])
        for n, (hop, out) in enumerate(zip(hops, hop_lows)):
            wide = jnp.dot(hop[:capacity, :], inside[:part, :], preferred_element_type=jnp.float32)
            kept = fold(jnp.where(hop_mask[n] > 0, wide, 0.0))
            rest_rows = -capacity % LANES
            kept = jnp.concatenate([kept, jnp.zeros((rest_rows, LANES), jnp.float32)], axis=0)
            out[...] = low_rank(kept)[:, :capacity]

    @pl.when(jnp.logical_not(middle))
    def _():
        finish(outside)
        last_up[...] = stacked(outside[part:, :], last_up.shape[1])
        for out in hop_lows:
            out[...] = jnp.zeros(out.shape, jnp.float32)


def merge_body(low, near, places, *refs):
    hops, out = refs[:-1], refs[-1]
    back = hops[0][...]
    for hop in hops[1:]:
        back = back + hop[...]
    spread = jnp.zeros(low.shape, jnp.float32)
    for _ in range(3):
        piece = back.astype(jnp.bfloat16)
        back = back - piece.astype(jnp.float32)
        spread = spread + jnp.dot(piece, places[...], preferred_element_type=jnp.float32)
    out[...] = low[...] + near[...] + spread


def finish_body(near, far, base, numbers, ups, last_up, distant, out):
    a = lax.axis_index("adapter")
    rows = out.shape[0]
    columns = last_up.shape[0]
    column = lax.broadcasted_iota(jnp.int32, (ADAPTER_RANK, columns), 1)
    row = lax.broadcasted_iota(jnp.int32, (ADAPTER_RANK, columns), 0)
    repeat = (lax.rem(column, ADAPTER_RANK) == row).astype(jnp.bfloat16)
    shrunk = (near[...] + far[...]).astype(jnp.bfloat16)
    spread = lax.dot_general(shrunk, repeat, TN, preferred_element_type=jnp.float32)
    adapter = adapters(rows, columns)
    middle = (a == 1) | (a == 2)
    mirrored = jnp.where(middle, ups[1].astype(jnp.float32), distant[...].astype(jnp.float32))
    blocks = ((0, ups[0]), (1, ups[2]), (2, last_up[...]), (3, mirrored.astype(jnp.bfloat16)))
    updates = jnp.zeros(out.shape, jnp.float32)
    for bit, up in blocks:
        wanted = numbers[...] - ((a ^ bit) * (columns // ADAPTER_RANK)).astype(jnp.float32)
        chosen = jnp.where(adapter == wanted, spread, 0.0).astype(jnp.bfloat16)
        updates = updates + jnp.dot(chosen, up, preferred_element_type=jnp.float32)
    updates = updates.astype(jnp.bfloat16).astype(jnp.float32)
    out[...] = (base[...] + ADAPTER_SCALE * updates).astype(jnp.bfloat16)


def gather(
    tokens,
    base_key_weight,
    stacked_down_weight,
    stacked_up_weight,
    request_adapter_owner,
    request_adapter_slot,
):
    rows, features = tokens.shape
    groups, owners, shares = (lax.axis_size(name) for name in AXES)
    columns = stacked_down_weight.shape[1]
    keys = stacked_up_weight.shape[1]
    part = features // groups
    half = columns // keys
    capacity = -(-row_limit(rows) // ID_ROWS) * ID_ROWS

    def narrow(*dims):
        return jax.ShapeDtypeStruct(dims, jnp.bfloat16)

    def wide(*dims):
        return jax.ShapeDtypeStruct(dims, jnp.float32)

    own = kernel(
        pack_body,
        narrow(part + columns // half, columns),
        (stacked_down_weight, stacked_up_weight),
        0,
        (pltpu.HBM, pltpu.HBM),
        [pltpu.SemaphoreType.DMA((1 + half,))],
    )
    mirror = exchange(own, 0, 0, MIDDLE)
    beside = exchange(own, 0, 0, BESIDE)

    tok_own, tok_away = kernel(
        split_body,
        [narrow(rows + ID_ROWS, part)] * groups,
        (tokens, request_adapter_owner.reshape(1, rows), after(request_adapter_slot, own)),
        0,
        (pltpu.HBM, None, None),
        [pltpu.SemaphoreType.DMA((groups,))],
    )
    token_parts = [tok_own, exchange(tok_away, 1, 0, SAME)]
    hop_own, hop_away, places, bases = kernel(
        functools.partial(hop_body, rows, capacity),
        [narrow(capacity + ID_ROWS, part)] * groups
        + [narrow(capacity, rows), wide(shares, rows, keys)],
        (tok_own, tok_away, base_key_weight),
        2 * rows * features * (capacity + shares * keys),
    )
    bases = lax.all_to_all(bases, "mp", 0, 0, tiled=True)

    inside = exchange(after(beside, places), 0, 0, MIDDLE)
    outside = exchange(mirror, 0, 0, OUTWARD)
    hops = [
        exchange(hop_own, 0, 0, INWARD),
        exchange(hop_away, 1, 0, INWARD),
    ]

    folded, mask, numbers, base, ups = kernel(
        functools.partial(early_body, (0, 3, 1), part, rows),
        [wide(groups, rows, LANES), wide(groups, rows, columns), wide(rows, 1), wide(rows, keys), narrow(3, columns, keys)],
        (*token_parts, own, mirror, beside, bases),
        6 * groups * rows * part * columns,
    )
    distant = exchange(after(stacked_up_weight, folded), 0, 0, ENDS)
    hop_mask = kernel(
        functools.partial(hop_mask_body, capacity),
        wide(groups, capacity, columns),
        (hops[0], after(hops[1], folded)),
        HOP_URGENCY,
    )
    low, low_away, back, back_away, last_up = kernel(
        functools.partial(last_body, part, rows, capacity),
        [wide(ADAPTER_RANK, rows)] * groups
        + [wide(ADAPTER_RANK, capacity)] * groups
        + [narrow(columns, keys)],
        (*token_parts, *hops, hop_mask, after(folded, distant), mask, outside, inside),
        2 * groups * (rows + capacity) * part * columns,
    )

    near = exchange(low_away, 1, 0, SAME)
    back = exchange(back, 0, 0, OUTWARD)
    back_away = exchange(back_away, 1, 0, OUTWARD)
    low = kernel(merge_body, wide(ADAPTER_RANK, rows), (low, near, places, back, back_away))
    bit = shares // 2
    while bit > 1:
        low = low + exchange(low, 0, bit, SAME)
        bit //= 2
    low_far = exchange(low, 0, 1, SAME)
    return kernel(
        finish_body, narrow(rows, keys), (low, low_far, base, numbers, ups, last_up, distant)
    )


def row_limit(rows):
    return max(2, 3 * rows // (2 * lax.axis_size("adapter")))


def local(*args):
    rows, columns = args[0].shape[0], args[2].shape[1]
    groups, owners, shares = (lax.axis_size(name) for name in AXES)
    fits = owners == OWNERS and groups == 2 and shares > 1 and shares & (shares - 1) == 0
    travels = fits and columns <= groups * row_limit(rows)
    return (gather if travels else dispatch)(*args)


def solution(mesh):
    placed = (
        P(("groups", "adapter"), "mp"),
        P("mp", None),
        P("mp", "adapter"),
        P("adapter", "mp"),
        P(("groups", "adapter"), None),
        P(("groups", "adapter")),
    )
    return jax.shard_map(
        local, mesh=mesh, in_specs=placed, out_specs=P(("groups", "adapter"), "mp"), check_vma=False
    )
```

```python
import functools

import jax
import jax.numpy as jnp
from jax import lax
from jax.experimental import pallas as pl
from jax.experimental.pallas import tpu as pltpu
from jax.sharding import PartitionSpec as P

ADAPTER_RANK = 16


ADAPTER_SCALE = 2.0


def dispatch(
    tokens,
    base_key_weight,
    stacked_down_weight,
    stacked_up_weight,
    request_adapter_owner,
    request_adapter_slot,
):
    rows_here = tokens.shape[0]
    feature_share = tokens.shape[1]
    owner_count = lax.axis_size("adapter")
    capacity = max(2, 3 * rows_here // (2 * owner_count))
    local_adapters = stacked_down_weight.shape[1] // ADAPTER_RANK
    key_output_share = stacked_up_weight.shape[1]
    owners = request_adapter_owner.reshape(-1)
    onehot = (owners[:, None] == jnp.arange(owner_count, dtype=jnp.int32)[None, :]).astype(
        jnp.int32
    )
    before = jnp.sum((jnp.cumsum(onehot, axis=0) - onehot) * onehot, axis=1)
    places = owners * capacity + before
    send_rows = (
        jnp.zeros((owner_count * capacity, feature_share), jnp.bfloat16).at[places].set(tokens)
    )
    send_rows = send_rows.reshape(owner_count, capacity, feature_share)
    send_slots = (
        jnp.full((owner_count * capacity,), -1, jnp.int32).at[places].set(request_adapter_slot)
    )
    send_slots = send_slots.reshape(owner_count, capacity)
    input_rows = lax.all_to_all(send_rows, "adapter", split_axis=0, concat_axis=0, tiled=True)
    slots_in = lax.all_to_all(send_slots, "adapter", split_axis=0, concat_axis=0, tiled=True)
    key_projection_output = jnp.einsum(
        "rzq,qt->rzt", input_rows, stacked_down_weight, preferred_element_type=jnp.float32
    )
    key_projection_output = key_projection_output.reshape(
        input_rows.shape[0], input_rows.shape[1], local_adapters, ADAPTER_RANK
    )
    chosen = slots_in[:, :, None] == jnp.arange(local_adapters, dtype=jnp.int32)[None, None, :]
    partial_low = jnp.sum(jnp.where(chosen[:, :, :, None], key_projection_output, 0.0), axis=2)
    shrunk = lax.psum(partial_low, "mp")
    shrunk_bf = shrunk.astype(jnp.bfloat16)
    returned = lax.all_to_all(shrunk_bf, "adapter", split_axis=0, concat_axis=0, tiled=True)
    low_rows = returned.reshape(owner_count * capacity, ADAPTER_RANK)[places]
    gathered_up_weight = lax.all_gather(stacked_up_weight, "adapter", axis=0, tiled=True)
    adapter_ids = owners * local_adapters + request_adapter_slot
    up_taken = gathered_up_weight.reshape(-1, ADAPTER_RANK, key_output_share)[adapter_ids]
    adapter_updates = jnp.einsum(
        "tr,trk->tk", low_rows, up_taken, preferred_element_type=jnp.float32
    ).astype(jnp.bfloat16)
    base_output_share = lax.psum_scatter(
        lax.dot_general(
            base_key_weight, tokens, (((0,), (1,)), ((), ())), preferred_element_type=jnp.float32
        ),
        "mp",
        scatter_dimension=0,
        tiled=True,
    )
    return (base_output_share.T + ADAPTER_SCALE * adapter_updates.astype(jnp.float32)).astype(
        jnp.bfloat16
    )


AXES = ("groups", "adapter", "mp")
ID_ROWS = 16
HOP_URGENCY = 4 * 10**9
OWNERS = 4
LANES = 128


def exchange(x, group_bits, share_bits, owners):
    groups, count, shares = (lax.axis_size(name) for name in AXES)

    def number(g, a, m):
        return (g * count + a) * shares + m

    pairs = [
        (number(g, a, m), number(g ^ group_bits, b, m ^ share_bits))
        for g in range(groups)
        for a, b in owners
        for m in range(shares)
    ]
    return lax.ppermute(x, AXES, pairs)


SAME = tuple((a, a) for a in range(OWNERS))
BESIDE = ((0, 1), (1, 0), (2, 3), (3, 2))
MIDDLE = ((1, 2), (2, 1))
ENDS = ((0, 3), (3, 0))
OUTWARD = ((1, 0), (2, 3))
INWARD = ((0, 1), (3, 2))


def after(x, *others):
    return lax.optimization_barrier((x, *others))[0]


def kernel(body, outs, operands, flops=0, spaces=None, scratch=()):
    inner = pl.BlockSpec(memory_space=pltpu.VMEM)
    specs = [inner if s is None else pl.BlockSpec(memory_space=s) for s in spaces or ()]
    touched = sum(x.size * x.dtype.itemsize for x in jax.tree.leaves((operands, outs)))
    return pl.pallas_call(
        body,
        out_shape=outs,
        in_specs=specs or [inner] * len(operands),
        out_specs=jax.tree.map(lambda _: inner, outs),
        scratch_shapes=scratch,
        compiler_params=pltpu.CompilerParams(vmem_limit_bytes=16 * 1024 * 1024),
        cost_estimate=pl.CostEstimate(flops=flops, bytes_accessed=touched, transcendentals=0),
    )(*operands)


def copy_all(copies):
    for copy in copies:
        copy.start()
    for copy in copies:
        copy.wait()


def pack_body(down, up, out, sems):
    g = lax.axis_index("groups")
    columns, keys = down.shape[1], up.shape[1]
    count = columns // keys
    size = up.shape[0] // count
    part = out.shape[0] - size
    mine = down.at[pl.ds(pl.multiple_of(g * part, part), part), :]
    copies = [pltpu.make_async_copy(mine, out.at[pl.ds(0, part), :], sems.at[count])]
    for k in range(count):
        copies.append(
            pltpu.make_async_copy(
                up.at[pl.ds(k * size, size), :],
                out.at[pl.ds(part, size), pl.ds(k * keys, keys)],
                sems.at[k],
            )
        )
    copy_all(copies)


def split_body(tokens, owner, slot, own, away, sems):
    g = lax.axis_index("groups")
    rows, part = tokens.shape[0], own.shape[1]
    copies = []
    for n, (out, half) in enumerate(((own, g), (away, 1 - g))):
        taken = tokens.at[:, pl.ds(pl.multiple_of(half * part, part), part)]
        copies.append(pltpu.make_async_copy(taken, out.at[pl.ds(0, rows), :], sems.at[n]))
    for copy in copies:
        copy.start()
    row = lax.broadcasted_iota(jnp.int32, (ID_ROWS, rows), 0)
    ids = jnp.where(row == 0, owner[...], jnp.where(row == 1, slot[...].reshape(1, rows), 0))
    ids = ids.astype(jnp.float32).astype(jnp.bfloat16)
    for out in (own, away):
        out[rows:, :rows] = ids
        out[rows:, rows:] = jnp.zeros((ID_ROWS, part - rows), jnp.bfloat16)
    for copy in copies:
        copy.wait()


def hop_body(rows, capacity, own, away, weights, own_out, away_out, places, bases):
    a, g = lax.axis_index("adapter"), lax.axis_index("groups")
    part = own.shape[1]
    ids = own[rows:, :rows]
    match = (ids.astype(jnp.float32) == (OWNERS - 1 - a).astype(jnp.float32)).astype(jnp.bfloat16)
    earlier = lax.broadcasted_iota(jnp.int32, (rows, rows), 0) < lax.broadcasted_iota(
        jnp.int32, (rows, rows), 1
    )
    rank = jnp.dot(match, earlier.astype(jnp.bfloat16), preferred_element_type=jnp.float32)
    place = lax.broadcasted_iota(jnp.int32, (capacity, rows), 0).astype(jnp.float32)
    taken = (place == rank[0:1]) & (match[0:1].astype(jnp.float32) > 0)
    chosen = taken.astype(jnp.bfloat16)
    places[...] = chosen
    kept = lax.dot_general(ids, chosen, NT, preferred_element_type=jnp.float32)
    for tokens, out in ((own, own_out), (away, away_out)):
        packed = jnp.dot(chosen, tokens[:rows, :], preferred_element_type=jnp.float32)
        out[:capacity, :] = packed.astype(jnp.bfloat16)
        out[capacity:, :] = jnp.zeros((ID_ROWS, part), jnp.bfloat16)
        out[capacity:, :capacity] = kept.astype(jnp.bfloat16)
    base = jnp.zeros((rows, weights.shape[1]), jnp.float32)
    for tokens, half in ((own, g), (away, 1 - g)):
        part_weights = weights[pl.ds(pl.multiple_of(half * part, part), part), :]
        base = base + jnp.dot(tokens[:rows, :], part_weights, preferred_element_type=jnp.float32)
    keys = bases.shape[2]
    for k in range(bases.shape[0]):
        bases[k] = base[:, k * keys : (k + 1) * keys]


NT = (((1,), (1,)), ((), ()))
TN = (((0,), (0,)), ((), ()))


def id_columns(rows_ref, start, count):
    eye = (
        lax.broadcasted_iota(jnp.int32, (ID_ROWS, ID_ROWS), 0)
        == lax.broadcasted_iota(jnp.int32, (ID_ROWS, ID_ROWS), 1)
    ).astype(jnp.bfloat16)
    ids = lax.dot_general(
        rows_ref[start : start + ID_ROWS, :count], eye, TN, preferred_element_type=jnp.float32
    )
    return ids[:, 0:1], ids[:, 1:2]


def adapters(rows, columns):
    column = lax.broadcasted_iota(jnp.int32, (rows, columns), 1)
    return (column // ADAPTER_RANK).astype(jnp.float32)


def fold(wide):
    folded = wide[:, :LANES]
    for k in range(1, wide.shape[1] // LANES):
        folded = folded + wide[:, k * LANES : (k + 1) * LANES]
    return folded


def low_rank(folded):
    turned = folded.T
    low = turned[:ADAPTER_RANK]
    for k in range(1, LANES // ADAPTER_RANK):
        low = low + turned[k * ADAPTER_RANK : (k + 1) * ADAPTER_RANK]
    return low


def stacked(wide, keys):
    return jnp.concatenate([wide[:, k : k + keys] for k in range(0, wide.shape[1], keys)], axis=0)


def early_body(bits, part, rows, *refs):
    groups = lax.axis_size("groups")
    a = lax.axis_index("adapter")
    token_refs, rest = refs[:groups], refs[groups:]
    blocks, (folded, mask, numbers, ups) = rest[: len(bits)], rest[len(bits) :]
    columns = blocks[0].shape[1]
    for n, block in enumerate(blocks):
        ups[n] = stacked(block[part:, :], ups.shape[2])
    adapter = adapters(rows, columns)
    for n, tokens in enumerate(token_refs):
        owner, slot = id_columns(tokens, rows, rows)
        if n == 0:
            numbers[...] = owner * (columns // ADAPTER_RANK) + slot
        right = adapter == slot
        picked = jnp.zeros((rows, columns), jnp.float32)
        for bit, block in zip(bits, blocks):
            wide = jnp.dot(tokens[:rows, :], block[:part, :], preferred_element_type=jnp.float32)
            picked = jnp.where(owner == (a ^ bit).astype(jnp.float32), wide, picked)
        folded[n] = fold(jnp.where(right, picked, 0.0))
        mask[n] = jnp.where(owner == (a ^ 2).astype(jnp.float32), right.astype(jnp.float32), 0.0)


def hop_mask_body(capacity, *refs):
    hops, out = refs[:-1], refs[-1]
    adapter = adapters(capacity, out.shape[2])
    for n, hop in enumerate(hops):
        _, slot = id_columns(hop, capacity, capacity)
        out[n] = (adapter == slot).astype(jnp.float32)


def last_body(part, rows, capacity, *refs):
    groups = lax.axis_size("groups")
    a = lax.axis_index("adapter")
    token_refs, rest = refs[:groups], refs[groups:]
    hops, rest = rest[:groups], rest[groups:]
    hop_mask, folded, mask, outside, inside = rest[:5]
    lows, hop_lows, last_up = rest[5 : 5 + groups], rest[5 + groups : -1], rest[-1]
    columns = inside.shape[1]

    def finish(block):
        for n, tokens in enumerate(token_refs):
            wide = jnp.dot(tokens[:rows, :], block[:part, :], preferred_element_type=jnp.float32)
            kept = fold(jnp.where(mask[n] > 0, wide, 0.0))
            lows[n][...] = low_rank(folded[n] + kept)

    middle = (a == 1) | (a == 2)

    @pl.when(middle)
    def _():
        finish(inside)
        last_up[...] = stacked(inside[part:, :], last_up.shape[1])
        for n, (hop, out) in enumerate(zip(hops, hop_lows)):
            wide = jnp.dot(hop[:capacity, :], inside[:part, :], preferred_element_type=jnp.float32)
            kept = fold(jnp.where(hop_mask[n] > 0, wide, 0.0))
            rest_rows = -capacity % LANES
            kept = jnp.concatenate([kept, jnp.zeros((rest_rows, LANES), jnp.float32)], axis=0)
            out[...] = low_rank(kept)[:, :capacity]

    @pl.when(jnp.logical_not(middle))
    def _():
        finish(outside)
        last_up[...] = stacked(outside[part:, :], last_up.shape[1])
        for out in hop_lows:
            out[...] = jnp.zeros(out.shape, jnp.float32)


def merge_body(low, near, places, *refs):
    hops, out = refs[:-1], refs[-1]
    back = hops[0][...]
    for hop in hops[1:]:
        back = back + hop[...]
    spread = jnp.zeros(low.shape, jnp.float32)
    for _ in range(3):
        piece = back.astype(jnp.bfloat16)
        back = back - piece.astype(jnp.float32)
        spread = spread + jnp.dot(piece, places[...], preferred_element_type=jnp.float32)
    out[...] = low[...] + near[...] + spread


def sum_body(parts, out):
    total = parts[0]
    for k in range(1, parts.shape[0]):
        total = total + parts[k]
    out[...] = total


def finish_body(near, far, base, numbers, ups, last_up, distant, out):
    a = lax.axis_index("adapter")
    rows = out.shape[0]
    columns = last_up.shape[0]
    column = lax.broadcasted_iota(jnp.int32, (ADAPTER_RANK, columns), 1)
    row = lax.broadcasted_iota(jnp.int32, (ADAPTER_RANK, columns), 0)
    repeat = (lax.rem(column, ADAPTER_RANK) == row).astype(jnp.bfloat16)
    shrunk = (near[...] + far[...]).astype(jnp.bfloat16)
    spread = lax.dot_general(shrunk, repeat, TN, preferred_element_type=jnp.float32)
    adapter = adapters(rows, columns)
    middle = (a == 1) | (a == 2)
    mirrored = jnp.where(middle, ups[1].astype(jnp.float32), distant[...].astype(jnp.float32))
    blocks = ((0, ups[0]), (1, ups[2]), (2, last_up[...]), (3, mirrored.astype(jnp.bfloat16)))
    updates = jnp.zeros(out.shape, jnp.float32)
    for bit, up in blocks:
        wanted = numbers[...] - ((a ^ bit) * (columns // ADAPTER_RANK)).astype(jnp.float32)
        chosen = jnp.where(adapter == wanted, spread, 0.0).astype(jnp.bfloat16)
        updates = updates + jnp.dot(chosen, up, preferred_element_type=jnp.float32)
    updates = updates.astype(jnp.bfloat16).astype(jnp.float32)
    out[...] = (base[...] + ADAPTER_SCALE * updates).astype(jnp.bfloat16)


def gather(
    tokens,
    base_key_weight,
    stacked_down_weight,
    stacked_up_weight,
    request_adapter_owner,
    request_adapter_slot,
):
    rows, features = tokens.shape
    groups, owners, shares = (lax.axis_size(name) for name in AXES)
    columns = stacked_down_weight.shape[1]
    keys = stacked_up_weight.shape[1]
    part = features // groups
    half = columns // keys
    capacity = -(-row_limit(rows) // ID_ROWS) * ID_ROWS

    def narrow(*dims):
        return jax.ShapeDtypeStruct(dims, jnp.bfloat16)

    def wide(*dims):
        return jax.ShapeDtypeStruct(dims, jnp.float32)

    own = kernel(
        pack_body,
        narrow(part + columns // half, columns),
        (stacked_down_weight, stacked_up_weight),
        0,
        (pltpu.HBM, pltpu.HBM),
        [pltpu.SemaphoreType.DMA((1 + half,))],
    )
    mirror = exchange(own, 0, 0, MIDDLE)
    beside = exchange(own, 0, 0, BESIDE)

    tok_own, tok_away = kernel(
        split_body,
        [narrow(rows + ID_ROWS, part)] * groups,
        (tokens, request_adapter_owner.reshape(1, rows), after(request_adapter_slot, own)),
        0,
        (pltpu.HBM, None, None),
        [pltpu.SemaphoreType.DMA((groups,))],
    )
    token_parts = [tok_own, exchange(tok_away, 1, 0, SAME)]
    hop_own, hop_away, places, bases = kernel(
        functools.partial(hop_body, rows, capacity),
        [narrow(capacity + ID_ROWS, part)] * groups
        + [narrow(capacity, rows), wide(shares, rows, keys)],
        (tok_own, tok_away, base_key_weight),
        2 * rows * features * (capacity + shares * keys),
    )
    bases = lax.all_to_all(bases, "mp", 0, 0, tiled=True)

    inside = exchange(after(beside, places), 0, 0, MIDDLE)
    outside = exchange(mirror, 0, 0, OUTWARD)
    hops = [
        exchange(hop_own, 0, 0, INWARD),
        exchange(hop_away, 1, 0, INWARD),
    ]

    folded, mask, numbers, ups = kernel(
        functools.partial(early_body, (0, 3, 1), part, rows),
        [wide(groups, rows, LANES), wide(groups, rows, columns), wide(rows, 1), narrow(3, columns, keys)],
        (*token_parts, own, mirror, beside),
        6 * groups * rows * part * columns,
    )
    distant = exchange(after(stacked_up_weight, folded), 0, 0, ENDS)
    hop_mask = kernel(
        functools.partial(hop_mask_body, capacity),
        wide(groups, capacity, columns),
        (hops[0], after(hops[1], folded)),
        HOP_URGENCY,
    )
    low, low_away, back, back_away, last_up = kernel(
        functools.partial(last_body, part, rows, capacity),
        [wide(ADAPTER_RANK, rows)] * groups
        + [wide(ADAPTER_RANK, capacity)] * groups
        + [narrow(columns, keys)],
        (*token_parts, *hops, hop_mask, after(folded, distant), mask, outside, inside),
        2 * groups * (rows + capacity) * part * columns,
    )

    near = exchange(low_away, 1, 0, SAME)
    back = exchange(back, 0, 0, OUTWARD)
    back_away = exchange(back_away, 1, 0, OUTWARD)
    low = kernel(merge_body, wide(ADAPTER_RANK, rows), (low, near, places, back, back_away))
    base = kernel(sum_body, wide(rows, keys), (after(bases, low),))
    bit = shares // 2
    while bit > 1:
        low = low + exchange(low, 0, bit, SAME)
        bit //= 2
    low_far = exchange(low, 0, 1, SAME)
    return kernel(
        finish_body, narrow(rows, keys), (low, low_far, base, numbers, ups, last_up, distant)
    )


def row_limit(rows):
    return max(2, 3 * rows // (2 * lax.axis_size("adapter")))


def local(*args):
    rows, columns = args[0].shape[0], args[2].shape[1]
    groups, owners, shares = (lax.axis_size(name) for name in AXES)
    fits = owners == OWNERS and groups == 2 and shares > 1 and shares & (shares - 1) == 0
    travels = fits and columns <= groups * row_limit(rows)
    return (gather if travels else dispatch)(*args)


def solution(mesh):
    placed = (
        P(("groups", "adapter"), "mp"),
        P("mp", None),
        P("mp", "adapter"),
        P("adapter", "mp"),
        P(("groups", "adapter"), None),
        P(("groups", "adapter")),
    )
    return jax.shard_map(
        local, mesh=mesh, in_specs=placed, out_specs=P(("groups", "adapter"), "mp"), check_vma=False
    )
```

```python
import functools

import jax
import jax.numpy as jnp
from jax import lax
from jax.experimental import pallas as pl
from jax.experimental.pallas import tpu as pltpu
from jax.sharding import PartitionSpec as P

ADAPTER_RANK = 16


ADAPTER_SCALE = 2.0


def dispatch(
    tokens,
    base_key_weight,
    stacked_down_weight,
    stacked_up_weight,
    request_adapter_owner,
    request_adapter_slot,
):
    rows_here = tokens.shape[0]
    feature_share = tokens.shape[1]
    owner_count = lax.axis_size("adapter")
    capacity = max(2, 3 * rows_here // (2 * owner_count))
    local_adapters = stacked_down_weight.shape[1] // ADAPTER_RANK
    key_output_share = stacked_up_weight.shape[1]
    owners = request_adapter_owner.reshape(-1)
    onehot = (owners[:, None] == jnp.arange(owner_count, dtype=jnp.int32)[None, :]).astype(
        jnp.int32
    )
    before = jnp.sum((jnp.cumsum(onehot, axis=0) - onehot) * onehot, axis=1)
    places = owners * capacity + before
    send_rows = (
        jnp.zeros((owner_count * capacity, feature_share), jnp.bfloat16).at[places].set(tokens)
    )
    send_rows = send_rows.reshape(owner_count, capacity, feature_share)
    send_slots = (
        jnp.full((owner_count * capacity,), -1, jnp.int32).at[places].set(request_adapter_slot)
    )
    send_slots = send_slots.reshape(owner_count, capacity)
    input_rows = lax.all_to_all(send_rows, "adapter", split_axis=0, concat_axis=0, tiled=True)
    slots_in = lax.all_to_all(send_slots, "adapter", split_axis=0, concat_axis=0, tiled=True)
    key_projection_output = jnp.einsum(
        "rzq,qt->rzt", input_rows, stacked_down_weight, preferred_element_type=jnp.float32
    )
    key_projection_output = key_projection_output.reshape(
        input_rows.shape[0], input_rows.shape[1], local_adapters, ADAPTER_RANK
    )
    chosen = slots_in[:, :, None] == jnp.arange(local_adapters, dtype=jnp.int32)[None, None, :]
    partial_low = jnp.sum(jnp.where(chosen[:, :, :, None], key_projection_output, 0.0), axis=2)
    shrunk = lax.psum(partial_low, "mp")
    shrunk_bf = shrunk.astype(jnp.bfloat16)
    returned = lax.all_to_all(shrunk_bf, "adapter", split_axis=0, concat_axis=0, tiled=True)
    low_rows = returned.reshape(owner_count * capacity, ADAPTER_RANK)[places]
    gathered_up_weight = lax.all_gather(stacked_up_weight, "adapter", axis=0, tiled=True)
    adapter_ids = owners * local_adapters + request_adapter_slot
    up_taken = gathered_up_weight.reshape(-1, ADAPTER_RANK, key_output_share)[adapter_ids]
    adapter_updates = jnp.einsum(
        "tr,trk->tk", low_rows, up_taken, preferred_element_type=jnp.float32
    ).astype(jnp.bfloat16)
    base_output_share = lax.psum_scatter(
        lax.dot_general(
            base_key_weight, tokens, (((0,), (1,)), ((), ())), preferred_element_type=jnp.float32
        ),
        "mp",
        scatter_dimension=0,
        tiled=True,
    )
    return (base_output_share.T + ADAPTER_SCALE * adapter_updates.astype(jnp.float32)).astype(
        jnp.bfloat16
    )


AXES = ("groups", "adapter", "mp")
ID_ROWS = 16
OWNERS = 4
LANES = 128
NT = (((1,), (1,)), ((), ()))
TN = (((0,), (0,)), ((), ()))


def exchange(x, group_bits, share_bits, owners):
    groups, count, shares = (lax.axis_size(name) for name in AXES)

    def number(g, a, m):
        return (g * count + a) * shares + m

    pairs = [
        (number(g, a, m), number(g ^ group_bits, b, m ^ share_bits))
        for g in range(groups)
        for a, b in owners
        for m in range(shares)
    ]
    return lax.ppermute(x, AXES, pairs)


SAME = tuple((a, a) for a in range(OWNERS))
BESIDE = ((0, 1), (1, 0), (2, 3), (3, 2))
MIDDLE = ((1, 2), (2, 1))
ENDS = ((0, 3), (3, 0))
OUTWARD = ((1, 0), (2, 3))
INWARD = ((0, 1), (3, 2))


def after(x, *others):
    return lax.optimization_barrier((x, *others))[0]


def kernel(body, outs, operands, flops=0, spaces=None, scratch=(), light=False):
    inner = pl.BlockSpec(memory_space=pltpu.VMEM)
    specs = [inner if s is None else pl.BlockSpec(memory_space=s) for s in spaces or ()]
    touched = sum(x.size * x.dtype.itemsize for x in jax.tree.leaves((operands, outs)))
    return pl.pallas_call(
        body,
        out_shape=outs,
        in_specs=specs or [inner] * len(operands),
        out_specs=jax.tree.map(lambda _: inner, outs),
        scratch_shapes=scratch,
        compiler_params=pltpu.CompilerParams(vmem_limit_bytes=16 * 1024 * 1024),
        cost_estimate=pl.CostEstimate(
            flops=flops, bytes_accessed=0 if light else touched, transcendentals=0
        ),
    )(*operands)


def copy_all(copies):
    for copy in copies:
        copy.start()
    for copy in copies:
        copy.wait()


def pack_body(down, up, out, sems):
    g = lax.axis_index("groups")
    columns, keys = down.shape[1], up.shape[1]
    count = columns // keys
    size = up.shape[0] // count
    part = out.shape[0] - size
    mine = down.at[pl.ds(pl.multiple_of(g * part, part), part), :]
    copies = [pltpu.make_async_copy(mine, out.at[pl.ds(0, part), :], sems.at[count])]
    for k in range(count):
        copies.append(
            pltpu.make_async_copy(
                up.at[pl.ds(k * size, size), :],
                out.at[pl.ds(part, size), pl.ds(k * keys, keys)],
                sems.at[k],
            )
        )
    copy_all(copies)


def split_body(tokens, owner, slot, own, away, sems):
    g = lax.axis_index("groups")
    rows, part = tokens.shape[0], own.shape[1]
    copies = []
    for n, (out, half) in enumerate(((own, g), (away, 1 - g))):
        taken = tokens.at[:, pl.ds(pl.multiple_of(half * part, part), part)]
        copies.append(pltpu.make_async_copy(taken, out.at[pl.ds(0, rows), :], sems.at[n]))
    for copy in copies:
        copy.start()
    row = lax.broadcasted_iota(jnp.int32, (ID_ROWS, rows), 0)
    ids = jnp.where(row == 0, owner[...], jnp.where(row == 1, slot[...].reshape(1, rows), 0))
    ids = ids.astype(jnp.float32).astype(jnp.bfloat16)
    for out in (own, away):
        out[rows:, :rows] = ids
        out[rows:, rows:] = jnp.zeros((ID_ROWS, part - rows), jnp.bfloat16)
    for copy in copies:
        copy.wait()


def hop_body(rows, capacity, own, away, weights, own_out, away_out, places, keep, give, base):
    a, g = lax.axis_index("adapter"), lax.axis_index("groups")
    part = own.shape[1]
    ids = own[rows:, :rows]
    match = (ids.astype(jnp.float32) == (OWNERS - 1 - a).astype(jnp.float32)).astype(jnp.bfloat16)
    earlier = lax.broadcasted_iota(jnp.int32, (rows, rows), 0) < lax.broadcasted_iota(
        jnp.int32, (rows, rows), 1
    )
    rank = jnp.dot(match, earlier.astype(jnp.bfloat16), preferred_element_type=jnp.float32)
    place = lax.broadcasted_iota(jnp.int32, (capacity, rows), 0).astype(jnp.float32)
    taken = (place == rank[0:1]) & (match[0:1].astype(jnp.float32) > 0)
    chosen = taken.astype(jnp.bfloat16)
    places[...] = chosen
    kept = lax.dot_general(ids, chosen, NT, preferred_element_type=jnp.float32)
    for tokens, out in ((own, own_out), (away, away_out)):
        packed = jnp.dot(chosen, tokens[:rows, :], preferred_element_type=jnp.float32)
        out[:capacity, :] = packed.astype(jnp.bfloat16)
        out[capacity:, :] = jnp.zeros((ID_ROWS, part), jnp.bfloat16)
        out[capacity:, :capacity] = kept.astype(jnp.bfloat16)
    total = jnp.zeros(base.shape, jnp.float32)
    for tokens, half in ((own, g), (away, 1 - g)):
        part_weights = weights[pl.ds(pl.multiple_of(half * part, part), part), :]
        total = total + jnp.dot(tokens[:rows, :], part_weights, preferred_element_type=jnp.float32)
    base[...] = total
    halves(base, lax.axis_size("mp") // 2, keep, give)


def halves(base, bit, keep, give):
    m = lax.axis_index("mp")
    width = keep.shape[1]
    side = (m // bit) % 2
    keep[...] = base[:, pl.ds(pl.multiple_of(side * width, width), width)]
    give[...] = base[:, pl.ds(pl.multiple_of((1 - side) * width, width), width)]


def id_columns(rows_ref, start, count):
    eye = (
        lax.broadcasted_iota(jnp.int32, (ID_ROWS, ID_ROWS), 0)
        == lax.broadcasted_iota(jnp.int32, (ID_ROWS, ID_ROWS), 1)
    ).astype(jnp.bfloat16)
    ids = lax.dot_general(
        rows_ref[start : start + ID_ROWS, :count], eye, TN, preferred_element_type=jnp.float32
    )
    return ids[:, 0:1], ids[:, 1:2]


def adapters(rows, columns):
    column = lax.broadcasted_iota(jnp.int32, (rows, columns), 1)
    return (column // ADAPTER_RANK).astype(jnp.float32)


def fold(wide):
    folded = wide[:, :LANES]
    for k in range(1, wide.shape[1] // LANES):
        folded = folded + wide[:, k * LANES : (k + 1) * LANES]
    return folded


def low_rank(folded):
    turned = folded.T
    low = turned[:ADAPTER_RANK]
    for k in range(1, LANES // ADAPTER_RANK):
        low = low + turned[k * ADAPTER_RANK : (k + 1) * ADAPTER_RANK]
    return low


def stacked(wide, keys):
    return jnp.concatenate([wide[:, k : k + keys] for k in range(0, wide.shape[1], keys)], axis=0)


def early_body(bits, part, rows, *refs):
    groups = lax.axis_size("groups")
    a = lax.axis_index("adapter")
    token_refs, rest = refs[:groups], refs[groups:]
    blocks, (folded, mask, numbers, ups) = rest[: len(bits)], rest[len(bits) :]
    columns = blocks[0].shape[1]
    for n, block in enumerate(blocks):
        ups[n] = stacked(block[part:, :], ups.shape[2])
    adapter = adapters(rows, columns)
    for n, tokens in enumerate(token_refs):
        owner, slot = id_columns(tokens, rows, rows)
        if n == 0:
            numbers[...] = owner * (columns // ADAPTER_RANK) + slot
        right = adapter == slot
        picked = jnp.zeros((rows, columns), jnp.float32)
        for bit, block in zip(bits, blocks):
            wide = jnp.dot(tokens[:rows, :], block[:part, :], preferred_element_type=jnp.float32)
            picked = jnp.where(owner == (a ^ bit).astype(jnp.float32), wide, picked)
        folded[n] = fold(jnp.where(right, picked, 0.0))
        mask[n] = jnp.where(owner == (a ^ 2).astype(jnp.float32), right.astype(jnp.float32), 0.0)


def hop_mask_body(capacity, *refs):
    hops, out = refs[:-1], refs[-1]
    adapter = adapters(capacity, out.shape[2])
    for n, hop in enumerate(hops):
        _, slot = id_columns(hop, capacity, capacity)
        out[n] = (adapter == slot).astype(jnp.float32)


def last_body(part, rows, capacity, *refs):
    groups = lax.axis_size("groups")
    a = lax.axis_index("adapter")
    token_refs, rest = refs[:groups], refs[groups:]
    hops, rest = rest[:groups], rest[groups:]
    hop_mask, folded, mask, outside, inside = rest[:5]
    lows, hop_lows, last_up = rest[5 : 5 + groups], rest[5 + groups : -1], rest[-1]
    columns = inside.shape[1]

    def finish(block):
        for n, tokens in enumerate(token_refs):
            wide = jnp.dot(tokens[:rows, :], block[:part, :], preferred_element_type=jnp.float32)
            kept = fold(jnp.where(mask[n] > 0, wide, 0.0))
            lows[n][...] = low_rank(folded[n] + kept)

    middle = (a == 1) | (a == 2)

    @pl.when(middle)
    def _():
        finish(inside)
        last_up[...] = stacked(inside[part:, :], last_up.shape[1])
        for n, (hop, out) in enumerate(zip(hops, hop_lows)):
            wide = jnp.dot(hop[:capacity, :], inside[:part, :], preferred_element_type=jnp.float32)
            kept = fold(jnp.where(hop_mask[n] > 0, wide, 0.0))
            rest_rows = -capacity % LANES
            kept = jnp.concatenate([kept, jnp.zeros((rest_rows, LANES), jnp.float32)], axis=0)
            out[...] = low_rank(kept)[:, :capacity]

    @pl.when(jnp.logical_not(middle))
    def _():
        finish(outside)
        last_up[...] = stacked(outside[part:, :], last_up.shape[1])
        for out in hop_lows:
            out[...] = jnp.zeros(out.shape, jnp.float32)


def merge_body(bit, low, near, places, kept, got, *refs):
    hops, (out, keep, give, base) = refs[:-4], refs[-4:]
    back = hops[0][...]
    for hop in hops[1:]:
        back = back + hop[...]
    spread = jnp.zeros(low.shape, jnp.float32)
    for _ in range(3):
        piece = back.astype(jnp.bfloat16)
        back = back - piece.astype(jnp.float32)
        spread = spread + jnp.dot(piece, places[...], preferred_element_type=jnp.float32)
    out[...] = low[...] + near[...] + spread
    base[...] = kept[...] + got[...]
    halves(base, bit, keep, give)


def finish_body(near, far, keep, got, numbers, ups, last_up, distant, out):
    a = lax.axis_index("adapter")
    rows = out.shape[0]
    columns = last_up.shape[0]
    column = lax.broadcasted_iota(jnp.int32, (ADAPTER_RANK, columns), 1)
    row = lax.broadcasted_iota(jnp.int32, (ADAPTER_RANK, columns), 0)
    repeat = (lax.rem(column, ADAPTER_RANK) == row).astype(jnp.bfloat16)
    shrunk = (near[...] + far[...]).astype(jnp.bfloat16)
    spread = lax.dot_general(shrunk, repeat, TN, preferred_element_type=jnp.float32)
    adapter = adapters(rows, columns)
    middle = (a == 1) | (a == 2)
    mirrored = jnp.where(middle, ups[1].astype(jnp.float32), distant[...].astype(jnp.float32))
    blocks = ((0, ups[0]), (1, ups[2]), (2, last_up[...]), (3, mirrored.astype(jnp.bfloat16)))
    updates = jnp.zeros(out.shape, jnp.float32)
    for bit, up in blocks:
        wanted = numbers[...] - ((a ^ bit) * (columns // ADAPTER_RANK)).astype(jnp.float32)
        chosen = jnp.where(adapter == wanted, spread, 0.0).astype(jnp.bfloat16)
        updates = updates + jnp.dot(chosen, up, preferred_element_type=jnp.float32)
    updates = updates.astype(jnp.bfloat16).astype(jnp.float32)
    base = keep[...] + got[...]
    out[...] = (base + ADAPTER_SCALE * updates).astype(jnp.bfloat16)


def gather(
    tokens,
    base_key_weight,
    stacked_down_weight,
    stacked_up_weight,
    request_adapter_owner,
    request_adapter_slot,
):
    rows, features = tokens.shape
    groups, owners, shares = (lax.axis_size(name) for name in AXES)
    columns = stacked_down_weight.shape[1]
    keys = stacked_up_weight.shape[1]
    part = features // groups
    half = columns // keys
    capacity = -(-row_limit(rows) // ID_ROWS) * ID_ROWS

    def narrow(*dims):
        return jax.ShapeDtypeStruct(dims, jnp.bfloat16)

    def wide(*dims):
        return jax.ShapeDtypeStruct(dims, jnp.float32)

    own = kernel(
        pack_body,
        narrow(part + columns // half, columns),
        (stacked_down_weight, stacked_up_weight),
        0,
        (pltpu.HBM, pltpu.HBM),
        [pltpu.SemaphoreType.DMA((1 + half,))],
    )
    mirror = exchange(own, 0, 0, MIDDLE)
    beside = exchange(own, 0, 0, BESIDE)

    tok_own, tok_away = kernel(
        split_body,
        [narrow(rows + ID_ROWS, part)] * groups,
        (tokens, request_adapter_owner.reshape(1, rows), after(request_adapter_slot, own)),
        0,
        (pltpu.HBM, None, None),
        [pltpu.SemaphoreType.DMA((groups,))],
    )
    token_parts = [tok_own, exchange(tok_away, 1, 0, SAME)]
    hop_own, hop_away, places, keep, give = kernel(
        functools.partial(hop_body, rows, capacity),
        [narrow(capacity + ID_ROWS, part)] * groups
        + [narrow(capacity, rows)]
        + [wide(rows, shares * keys // 2)] * 2,
        (tok_own, tok_away, base_key_weight),
        2 * rows * features * (capacity + shares * keys),
        scratch=[pltpu.VMEM((rows, shares * keys), jnp.float32)],
    )

    inside = exchange(after(beside, places), 0, 0, MIDDLE)
    outside = exchange(mirror, 0, 0, OUTWARD)
    hops = [
        exchange(hop_own, 0, 0, INWARD),
        exchange(hop_away, 1, 0, INWARD),
    ]

    folded, mask, numbers, ups = kernel(
        functools.partial(early_body, (0, 3, 1), part, rows),
        [wide(groups, rows, LANES), wide(groups, rows, columns), wide(rows, 1), narrow(3, columns, keys)],
        (*token_parts, own, mirror, beside),
        light=True,
    )
    distant = exchange(after(stacked_up_weight, folded), 0, 0, ENDS)
    hop_mask = kernel(
        functools.partial(hop_mask_body, capacity),
        wide(groups, capacity, columns),
        (hops[0], after(hops[1], folded)),
    )
    bits = (2, 1)
    got = exchange(after(give, hop_mask), 0, bits[0], SAME)

    low, low_away, back, back_away, last_up = kernel(
        functools.partial(last_body, part, rows, capacity),
        [wide(ADAPTER_RANK, rows)] * groups
        + [wide(ADAPTER_RANK, capacity)] * groups
        + [narrow(columns, keys)],
        (*token_parts, *hops, hop_mask, after(folded, distant), mask, outside, inside),
        2 * groups * (rows + capacity) * part * columns,
    )

    near = exchange(low_away, 1, 0, SAME)
    back = exchange(back, 0, 0, OUTWARD)
    back_away = exchange(back_away, 1, 0, OUTWARD)
    low, keep, give = kernel(
        functools.partial(merge_body, bits[1]),
        [wide(ADAPTER_RANK, rows)] + [wide(rows, bits[1] * keys)] * 2,
        (low, near, places, keep, got, back, back_away),
        scratch=[pltpu.VMEM((rows, bits[0] * keys), jnp.float32)],
    )
    got = exchange(give, 0, bits[1], SAME)
    low = low + exchange(low, 0, bits[0], SAME)
    low_far = exchange(low, 0, bits[1], SAME)
    return kernel(
        finish_body, narrow(rows, keys), (low, low_far, keep, got, numbers, ups, last_up, distant)
    )


def row_limit(rows):
    return max(2, 3 * rows // (2 * lax.axis_size("adapter")))


def local(*args):
    rows, columns = args[0].shape[0], args[2].shape[1]
    groups, owners, shares = (lax.axis_size(name) for name in AXES)
    fits = owners == OWNERS and groups == 2 and shares == 4
    travels = fits and columns <= groups * row_limit(rows)
    return (gather if travels else dispatch)(*args)


def solution(mesh):
    placed = (
        P(("groups", "adapter"), "mp"),
        P("mp", None),
        P("mp", "adapter"),
        P("adapter", "mp"),
        P(("groups", "adapter"), None),
        P(("groups", "adapter")),
    )
    return jax.shard_map(
        local, mesh=mesh, in_specs=placed, out_specs=P(("groups", "adapter"), "mp"), check_vma=False
    )
```

```python
import functools

import jax
import jax.numpy as jnp
from jax import lax
from jax.experimental import pallas as pl
from jax.experimental.pallas import tpu as pltpu
from jax.sharding import PartitionSpec as P

ADAPTER_RANK = 16


ADAPTER_SCALE = 2.0


def dispatch(
    tokens,
    base_key_weight,
    stacked_down_weight,
    stacked_up_weight,
    request_adapter_owner,
    request_adapter_slot,
):
    rows_here = tokens.shape[0]
    feature_share = tokens.shape[1]
    owner_count = lax.axis_size("adapter")
    capacity = max(2, 3 * rows_here // (2 * owner_count))
    local_adapters = stacked_down_weight.shape[1] // ADAPTER_RANK
    key_output_share = stacked_up_weight.shape[1]
    owners = request_adapter_owner.reshape(-1)
    onehot = (owners[:, None] == jnp.arange(owner_count, dtype=jnp.int32)[None, :]).astype(
        jnp.int32
    )
    before = jnp.sum((jnp.cumsum(onehot, axis=0) - onehot) * onehot, axis=1)
    places = owners * capacity + before
    send_rows = (
        jnp.zeros((owner_count * capacity, feature_share), jnp.bfloat16).at[places].set(tokens)
    )
    send_rows = send_rows.reshape(owner_count, capacity, feature_share)
    send_slots = (
        jnp.full((owner_count * capacity,), -1, jnp.int32).at[places].set(request_adapter_slot)
    )
    send_slots = send_slots.reshape(owner_count, capacity)
    input_rows = lax.all_to_all(send_rows, "adapter", split_axis=0, concat_axis=0, tiled=True)
    slots_in = lax.all_to_all(send_slots, "adapter", split_axis=0, concat_axis=0, tiled=True)
    key_projection_output = jnp.einsum(
        "rzq,qt->rzt", input_rows, stacked_down_weight, preferred_element_type=jnp.float32
    )
    key_projection_output = key_projection_output.reshape(
        input_rows.shape[0], input_rows.shape[1], local_adapters, ADAPTER_RANK
    )
    chosen = slots_in[:, :, None] == jnp.arange(local_adapters, dtype=jnp.int32)[None, None, :]
    partial_low = jnp.sum(jnp.where(chosen[:, :, :, None], key_projection_output, 0.0), axis=2)
    shrunk = lax.psum(partial_low, "mp")
    shrunk_bf = shrunk.astype(jnp.bfloat16)
    returned = lax.all_to_all(shrunk_bf, "adapter", split_axis=0, concat_axis=0, tiled=True)
    low_rows = returned.reshape(owner_count * capacity, ADAPTER_RANK)[places]
    gathered_up_weight = lax.all_gather(stacked_up_weight, "adapter", axis=0, tiled=True)
    adapter_ids = owners * local_adapters + request_adapter_slot
    up_taken = gathered_up_weight.reshape(-1, ADAPTER_RANK, key_output_share)[adapter_ids]
    adapter_updates = jnp.einsum(
        "tr,trk->tk", low_rows, up_taken, preferred_element_type=jnp.float32
    ).astype(jnp.bfloat16)
    base_output_share = lax.psum_scatter(
        lax.dot_general(
            base_key_weight, tokens, (((0,), (1,)), ((), ())), preferred_element_type=jnp.float32
        ),
        "mp",
        scatter_dimension=0,
        tiled=True,
    )
    return (base_output_share.T + ADAPTER_SCALE * adapter_updates.astype(jnp.float32)).astype(
        jnp.bfloat16
    )


AXES = ("groups", "adapter", "mp")
ID_ROWS = 16
HOP_URGENCY = 3 * 10**9
OWNERS = 4
LANES = 128
NT = (((1,), (1,)), ((), ()))
TN = (((0,), (0,)), ((), ()))


def exchange(x, group_bits, share_bits, owners):
    groups, count, shares = (lax.axis_size(name) for name in AXES)

    def number(g, a, m):
        return (g * count + a) * shares + m

    pairs = [
        (number(g, a, m), number(g ^ group_bits, b, m ^ share_bits))
        for g in range(groups)
        for a, b in owners
        for m in range(shares)
    ]
    return lax.ppermute(x, AXES, pairs)


SAME = tuple((a, a) for a in range(OWNERS))
BESIDE = ((0, 1), (1, 0), (2, 3), (3, 2))
MIDDLE = ((1, 2), (2, 1))
ENDS = ((0, 3), (3, 0))
OUTWARD = ((1, 0), (2, 3))
INWARD = ((0, 1), (3, 2))


def after(x, *others):
    return lax.optimization_barrier((x, *others))[0]


def kernel(body, outs, operands, flops=0, spaces=None, scratch=(), light=False):
    inner = pl.BlockSpec(memory_space=pltpu.VMEM)
    specs = [inner if s is None else pl.BlockSpec(memory_space=s) for s in spaces or ()]
    touched = sum(x.size * x.dtype.itemsize for x in jax.tree.leaves((operands, outs)))
    return pl.pallas_call(
        body,
        out_shape=outs,
        in_specs=specs or [inner] * len(operands),
        out_specs=jax.tree.map(lambda _: inner, outs),
        scratch_shapes=scratch,
        compiler_params=pltpu.CompilerParams(vmem_limit_bytes=16 * 1024 * 1024),
        cost_estimate=pl.CostEstimate(
            flops=flops, bytes_accessed=0 if light else touched, transcendentals=0
        ),
    )(*operands)


def copy_all(copies):
    for copy in copies:
        copy.start()
    for copy in copies:
        copy.wait()


def pack_body(down, up, out, sems):
    g = lax.axis_index("groups")
    columns, keys = down.shape[1], up.shape[1]
    count = columns // keys
    size = up.shape[0] // count
    part = out.shape[0] - size
    mine = down.at[pl.ds(pl.multiple_of(g * part, part), part), :]
    copies = [pltpu.make_async_copy(mine, out.at[pl.ds(0, part), :], sems.at[count])]
    for k in range(count):
        copies.append(
            pltpu.make_async_copy(
                up.at[pl.ds(k * size, size), :],
                out.at[pl.ds(part, size), pl.ds(k * keys, keys)],
                sems.at[k],
            )
        )
    copy_all(copies)


def split_body(tokens, owner, slot, _, own, away, sems):
    g = lax.axis_index("groups")
    rows, part = tokens.shape[0], own.shape[1]
    copies = []
    for n, (out, half) in enumerate(((own, g), (away, 1 - g))):
        taken = tokens.at[:, pl.ds(pl.multiple_of(half * part, part), part)]
        copies.append(pltpu.make_async_copy(taken, out.at[pl.ds(0, rows), :], sems.at[n]))
    for copy in copies:
        copy.start()
    row = lax.broadcasted_iota(jnp.int32, (ID_ROWS, rows), 0)
    ids = jnp.where(row == 0, owner[...], jnp.where(row == 1, slot[...].reshape(1, rows), 0))
    ids = ids.astype(jnp.float32).astype(jnp.bfloat16)
    for out in (own, away):
        out[rows:, :rows] = ids
        out[rows:, rows:] = jnp.zeros((ID_ROWS, part - rows), jnp.bfloat16)
    for copy in copies:
        copy.wait()


def hop_body(rows, capacity, own, away, own_out, away_out, places):
    a = lax.axis_index("adapter")
    part = own.shape[1]
    ids = own[rows:, :rows]
    match = (ids.astype(jnp.float32) == (OWNERS - 1 - a).astype(jnp.float32)).astype(jnp.bfloat16)
    earlier = lax.broadcasted_iota(jnp.int32, (rows, rows), 0) < lax.broadcasted_iota(
        jnp.int32, (rows, rows), 1
    )
    rank = jnp.dot(match, earlier.astype(jnp.bfloat16), preferred_element_type=jnp.float32)
    place = lax.broadcasted_iota(jnp.int32, (capacity, rows), 0).astype(jnp.float32)
    taken = (place == rank[0:1]) & (match[0:1].astype(jnp.float32) > 0)
    chosen = taken.astype(jnp.bfloat16)
    places[...] = chosen
    kept = lax.dot_general(ids, chosen, NT, preferred_element_type=jnp.float32)
    for tokens, out in ((own, own_out), (away, away_out)):
        packed = jnp.dot(chosen, tokens[:rows, :], preferred_element_type=jnp.float32)
        out[:capacity, :] = packed.astype(jnp.bfloat16)
        out[capacity:, :] = jnp.zeros((ID_ROWS, part), jnp.bfloat16)
        out[capacity:, :capacity] = kept.astype(jnp.bfloat16)


def base_body(bit, rows, own, away, weights, _, keep, give, base):
    g = lax.axis_index("groups")
    part = own.shape[1]
    total = jnp.zeros(base.shape, jnp.float32)
    for tokens, half in ((own, g), (away, 1 - g)):
        part_weights = weights[pl.ds(pl.multiple_of(half * part, part), part), :]
        total = total + jnp.dot(tokens[:rows, :], part_weights, preferred_element_type=jnp.float32)
    base[...] = total
    halves(base, bit, keep, give)


def halves(base, bit, keep, give):
    m = lax.axis_index("mp")
    width = keep.shape[1]
    side = (m // bit) % 2
    keep[...] = base[:, pl.ds(pl.multiple_of(side * width, width), width)]
    give[...] = base[:, pl.ds(pl.multiple_of((1 - side) * width, width), width)]


def id_columns(rows_ref, start, count):
    eye = (
        lax.broadcasted_iota(jnp.int32, (ID_ROWS, ID_ROWS), 0)
        == lax.broadcasted_iota(jnp.int32, (ID_ROWS, ID_ROWS), 1)
    ).astype(jnp.bfloat16)
    ids = lax.dot_general(
        rows_ref[start : start + ID_ROWS, :count], eye, TN, preferred_element_type=jnp.float32
    )
    return ids[:, 0:1], ids[:, 1:2]


def adapters(rows, columns):
    column = lax.broadcasted_iota(jnp.int32, (rows, columns), 1)
    return (column // ADAPTER_RANK).astype(jnp.float32)


def fold(wide):
    folded = wide[:, :LANES]
    for k in range(1, wide.shape[1] // LANES):
        folded = folded + wide[:, k * LANES : (k + 1) * LANES]
    return folded


def low_rank(folded):
    turned = folded.T
    low = turned[:ADAPTER_RANK]
    for k in range(1, LANES // ADAPTER_RANK):
        low = low + turned[k * ADAPTER_RANK : (k + 1) * ADAPTER_RANK]
    return low


def stacked(wide, keys):
    return jnp.concatenate([wide[:, k : k + keys] for k in range(0, wide.shape[1], keys)], axis=0)


def early_body(bits, part, rows, *refs):
    groups = lax.axis_size("groups")
    a = lax.axis_index("adapter")
    token_refs, rest = refs[:groups], refs[groups:]
    blocks, (folded, mask, numbers, ups) = rest[: len(bits)], rest[len(bits) :]
    columns = blocks[0].shape[1]
    for n, block in enumerate(blocks):
        ups[n] = stacked(block[part:, :], ups.shape[2])
    adapter = adapters(rows, columns)
    for n, tokens in enumerate(token_refs):
        owner, slot = id_columns(tokens, rows, rows)
        if n == 0:
            numbers[...] = owner * (columns // ADAPTER_RANK) + slot
        right = adapter == slot
        picked = jnp.zeros((rows, columns), jnp.float32)
        for bit, block in zip(bits, blocks):
            wide = jnp.dot(tokens[:rows, :], block[:part, :], preferred_element_type=jnp.float32)
            picked = jnp.where(owner == (a ^ bit).astype(jnp.float32), wide, picked)
        folded[n] = fold(jnp.where(right, picked, 0.0))
        mask[n] = jnp.where(owner == (a ^ 2).astype(jnp.float32), right.astype(jnp.float32), 0.0)


def hop_mask_body(capacity, *refs):
    hops, out = refs[:-1], refs[-1]
    adapter = adapters(capacity, out.shape[2])
    for n, hop in enumerate(hops):
        _, slot = id_columns(hop, capacity, capacity)
        out[n] = (adapter == slot).astype(jnp.float32)


def last_body(part, rows, capacity, *refs):
    groups = lax.axis_size("groups")
    a = lax.axis_index("adapter")
    token_refs, rest = refs[:groups], refs[groups:]
    hops, rest = rest[:groups], rest[groups:]
    hop_mask, folded, mask, outside, inside = rest[:5]
    lows, hop_lows, last_up = rest[5 : 5 + groups], rest[5 + groups : -1], rest[-1]
    columns = inside.shape[1]

    def finish(block):
        for n, tokens in enumerate(token_refs):
            wide = jnp.dot(tokens[:rows, :], block[:part, :], preferred_element_type=jnp.float32)
            kept = fold(jnp.where(mask[n] > 0, wide, 0.0))
            lows[n][...] = low_rank(folded[n] + kept)

    middle = (a == 1) | (a == 2)

    @pl.when(middle)
    def _():
        finish(inside)
        last_up[...] = stacked(inside[part:, :], last_up.shape[1])
        for n, (hop, out) in enumerate(zip(hops, hop_lows)):
            wide = jnp.dot(hop[:capacity, :], inside[:part, :], preferred_element_type=jnp.float32)
            kept = fold(jnp.where(hop_mask[n] > 0, wide, 0.0))
            rest_rows = -capacity % LANES
            kept = jnp.concatenate([kept, jnp.zeros((rest_rows, LANES), jnp.float32)], axis=0)
            out[...] = low_rank(kept)[:, :capacity]

    @pl.when(jnp.logical_not(middle))
    def _():
        finish(outside)
        last_up[...] = stacked(outside[part:, :], last_up.shape[1])
        for out in hop_lows:
            out[...] = jnp.zeros(out.shape, jnp.float32)


def merge_body(bit, low, near, places, kept, got, *refs):
    hops, (out, keep, give, base) = refs[:-4], refs[-4:]
    back = hops[0][...]
    for hop in hops[1:]:
        back = back + hop[...]
    spread = jnp.zeros(low.shape, jnp.float32)
    for _ in range(3):
        piece = back.astype(jnp.bfloat16)
        back = back - piece.astype(jnp.float32)
        spread = spread + jnp.dot(piece, places[...], preferred_element_type=jnp.float32)
    out[...] = low[...] + near[...] + spread
    base[...] = kept[...] + got[...]
    halves(base, bit, keep, give)


def finish_body(near, far, keep, got, numbers, ups, last_up, distant, out):
    a = lax.axis_index("adapter")
    rows = out.shape[0]
    columns = last_up.shape[0]
    column = lax.broadcasted_iota(jnp.int32, (ADAPTER_RANK, columns), 1)
    row = lax.broadcasted_iota(jnp.int32, (ADAPTER_RANK, columns), 0)
    repeat = (lax.rem(column, ADAPTER_RANK) == row).astype(jnp.bfloat16)
    shrunk = (near[...] + far[...]).astype(jnp.bfloat16)
    spread = lax.dot_general(shrunk, repeat, TN, preferred_element_type=jnp.float32)
    adapter = adapters(rows, columns)
    middle = (a == 1) | (a == 2)
    mirrored = jnp.where(middle, ups[1].astype(jnp.float32), distant[...].astype(jnp.float32))
    blocks = ((0, ups[0]), (1, ups[2]), (2, last_up[...]), (3, mirrored.astype(jnp.bfloat16)))
    updates = jnp.zeros(out.shape, jnp.float32)
    for bit, up in blocks:
        wanted = numbers[...] - ((a ^ bit) * (columns // ADAPTER_RANK)).astype(jnp.float32)
        chosen = jnp.where(adapter == wanted, spread, 0.0).astype(jnp.bfloat16)
        updates = updates + jnp.dot(chosen, up, preferred_element_type=jnp.float32)
    updates = updates.astype(jnp.bfloat16).astype(jnp.float32)
    base = keep[...] + got[...]
    out[...] = (base + ADAPTER_SCALE * updates).astype(jnp.bfloat16)


def gather(
    tokens,
    base_key_weight,
    stacked_down_weight,
    stacked_up_weight,
    request_adapter_owner,
    request_adapter_slot,
):
    rows, features = tokens.shape
    groups, owners, shares = (lax.axis_size(name) for name in AXES)
    columns = stacked_down_weight.shape[1]
    keys = stacked_up_weight.shape[1]
    part = features // groups
    half = columns // keys
    capacity = -(-row_limit(rows) // ID_ROWS) * ID_ROWS

    def narrow(*dims):
        return jax.ShapeDtypeStruct(dims, jnp.bfloat16)

    def wide(*dims):
        return jax.ShapeDtypeStruct(dims, jnp.float32)

    own = kernel(
        pack_body,
        narrow(part + columns // half, columns),
        (stacked_down_weight, stacked_up_weight),
        0,
        (pltpu.HBM, pltpu.HBM),
        [pltpu.SemaphoreType.DMA((1 + half,))],
    )
    mirror = exchange(own, 0, 0, MIDDLE)
    beside = exchange(own, 0, 0, BESIDE)

    tok_own, tok_away = kernel(
        split_body,
        [narrow(rows + ID_ROWS, part)] * groups,
        (tokens, request_adapter_owner.reshape(1, rows), request_adapter_slot, own),
        0,
        (pltpu.HBM, None, None, pl.ANY),
        [pltpu.SemaphoreType.DMA((groups,))],
    )
    token_parts = [tok_own, exchange(tok_away, 1, 0, SAME)]
    hop_own, hop_away, places = kernel(
        functools.partial(hop_body, rows, capacity),
        [narrow(capacity + ID_ROWS, part)] * groups
        + [narrow(capacity, rows)],
        (tok_own, tok_away),
        2 * rows * features * capacity,
    )

    inside = exchange(beside, 0, 0, MIDDLE)
    outside = exchange(mirror, 0, 0, OUTWARD)
    hops = [
        exchange(hop_own, 0, 0, INWARD),
        exchange(hop_away, 1, 0, INWARD),
    ]

    folded, mask, numbers, ups = kernel(
        functools.partial(early_body, (0, 3, 1), part, rows),
        [wide(groups, rows, LANES), wide(groups, rows, columns), wide(rows, 1), narrow(3, columns, keys)],
        (*token_parts, own, mirror, beside),
        light=True,
    )
    distant = exchange(after(stacked_up_weight, folded), 0, 0, ENDS)
    hop_mask = kernel(
        functools.partial(hop_mask_body, capacity),
        wide(groups, capacity, columns),
        (hops[0], after(hops[1], folded)),
        HOP_URGENCY,
    )
    bits = (2, 1)
    keep, give = kernel(
        functools.partial(base_body, bits[0], rows),
        [wide(rows, shares * keys // 2)] * 2,
        (tok_own, tok_away, base_key_weight, places),
        2 * rows * features * shares * keys,
        (None, None, None, pl.ANY),
        [pltpu.VMEM((rows, shares * keys), jnp.float32)],
    )
    got = exchange(give, 0, bits[0], SAME)

    low, low_away, back, back_away, last_up = kernel(
        functools.partial(last_body, part, rows, capacity),
        [wide(ADAPTER_RANK, rows)] * groups
        + [wide(ADAPTER_RANK, capacity)] * groups
        + [narrow(columns, keys)],
        (*token_parts, *hops, hop_mask, after(folded, distant), mask, outside, inside),
        2 * groups * (rows + capacity) * part * columns,
    )

    near = exchange(low_away, 1, 0, SAME)
    back = exchange(back, 0, 0, OUTWARD)
    back_away = exchange(back_away, 1, 0, OUTWARD)
    low, keep, give = kernel(
        functools.partial(merge_body, bits[1]),
        [wide(ADAPTER_RANK, rows)] + [wide(rows, bits[1] * keys)] * 2,
        (low, near, places, keep, got, back, back_away),
        scratch=[pltpu.VMEM((rows, bits[0] * keys), jnp.float32)],
    )
    got = exchange(give, 0, bits[1], SAME)
    low = low + exchange(low, 0, bits[0], SAME)
    low_far = exchange(low, 0, bits[1], SAME)
    return kernel(
        finish_body, narrow(rows, keys), (low, low_far, keep, got, numbers, ups, last_up, distant)
    )


def row_limit(rows):
    return max(2, 3 * rows // (2 * lax.axis_size("adapter")))


def local(*args):
    rows, columns = args[0].shape[0], args[2].shape[1]
    groups, owners, shares = (lax.axis_size(name) for name in AXES)
    fits = owners == OWNERS and groups == 2 and shares == 4
    travels = fits and columns <= groups * row_limit(rows)
    return (gather if travels else dispatch)(*args)


def solution(mesh):
    placed = (
        P(("groups", "adapter"), "mp"),
        P("mp", None),
        P("mp", "adapter"),
        P("adapter", "mp"),
        P(("groups", "adapter"), None),
        P(("groups", "adapter")),
    )
    return jax.shard_map(
        local, mesh=mesh, in_specs=placed, out_specs=P(("groups", "adapter"), "mp"), check_vma=False
    )
```

```python
import functools

import jax
import jax.numpy as jnp
from jax import lax
from jax.experimental import pallas as pl
from jax.experimental.pallas import tpu as pltpu
from jax.sharding import PartitionSpec as P

ADAPTER_RANK = 16


ADAPTER_SCALE = 2.0


def dispatch(
    tokens,
    base_key_weight,
    stacked_down_weight,
    stacked_up_weight,
    request_adapter_owner,
    request_adapter_slot,
):
    rows_here = tokens.shape[0]
    feature_share = tokens.shape[1]
    owner_count = lax.axis_size("adapter")
    capacity = max(2, 3 * rows_here // (2 * owner_count))
    local_adapters = stacked_down_weight.shape[1] // ADAPTER_RANK
    key_output_share = stacked_up_weight.shape[1]
    owners = request_adapter_owner.reshape(-1)
    onehot = (owners[:, None] == jnp.arange(owner_count, dtype=jnp.int32)[None, :]).astype(
        jnp.int32
    )
    before = jnp.sum((jnp.cumsum(onehot, axis=0) - onehot) * onehot, axis=1)
    places = owners * capacity + before
    send_rows = (
        jnp.zeros((owner_count * capacity, feature_share), jnp.bfloat16).at[places].set(tokens)
    )
    send_rows = send_rows.reshape(owner_count, capacity, feature_share)
    send_slots = (
        jnp.full((owner_count * capacity,), -1, jnp.int32).at[places].set(request_adapter_slot)
    )
    send_slots = send_slots.reshape(owner_count, capacity)
    input_rows = lax.all_to_all(send_rows, "adapter", split_axis=0, concat_axis=0, tiled=True)
    slots_in = lax.all_to_all(send_slots, "adapter", split_axis=0, concat_axis=0, tiled=True)
    key_projection_output = jnp.einsum(
        "rzq,qt->rzt", input_rows, stacked_down_weight, preferred_element_type=jnp.float32
    )
    key_projection_output = key_projection_output.reshape(
        input_rows.shape[0], input_rows.shape[1], local_adapters, ADAPTER_RANK
    )
    chosen = slots_in[:, :, None] == jnp.arange(local_adapters, dtype=jnp.int32)[None, None, :]
    partial_low = jnp.sum(jnp.where(chosen[:, :, :, None], key_projection_output, 0.0), axis=2)
    shrunk = lax.psum(partial_low, "mp")
    shrunk_bf = shrunk.astype(jnp.bfloat16)
    returned = lax.all_to_all(shrunk_bf, "adapter", split_axis=0, concat_axis=0, tiled=True)
    low_rows = returned.reshape(owner_count * capacity, ADAPTER_RANK)[places]
    gathered_up_weight = lax.all_gather(stacked_up_weight, "adapter", axis=0, tiled=True)
    adapter_ids = owners * local_adapters + request_adapter_slot
    up_taken = gathered_up_weight.reshape(-1, ADAPTER_RANK, key_output_share)[adapter_ids]
    adapter_updates = jnp.einsum(
        "tr,trk->tk", low_rows, up_taken, preferred_element_type=jnp.float32
    ).astype(jnp.bfloat16)
    base_output_share = lax.psum_scatter(
        lax.dot_general(
            base_key_weight, tokens, (((0,), (1,)), ((), ())), preferred_element_type=jnp.float32
        ),
        "mp",
        scatter_dimension=0,
        tiled=True,
    )
    return (base_output_share.T + ADAPTER_SCALE * adapter_updates.astype(jnp.float32)).astype(
        jnp.bfloat16
    )


AXES = ("groups", "adapter", "mp")
ID_ROWS = 16
HOP_URGENCY = (30 * 10**8, 0)
OWNERS = 4
LANES = 128
NT = (((1,), (1,)), ((), ()))
TN = (((0,), (0,)), ((), ()))


def exchange(x, group_bits, share_bits, owners):
    groups, count, shares = (lax.axis_size(name) for name in AXES)

    def number(g, a, m):
        return (g * count + a) * shares + m

    pairs = [
        (number(g, a, m), number(g ^ group_bits, b, m ^ share_bits))
        for g in range(groups)
        for a, b in owners
        for m in range(shares)
    ]
    return lax.ppermute(x, AXES, pairs)


SAME = tuple((a, a) for a in range(OWNERS))
BESIDE = ((0, 1), (1, 0), (2, 3), (3, 2))
MIDDLE = ((1, 2), (2, 1))
ENDS = ((0, 3), (3, 0))
OUTWARD = ((1, 0), (2, 3))
INWARD = ((0, 1), (3, 2))


def after(x, *others):
    return lax.optimization_barrier((x, *others))[0]


def kernel(body, outs, operands, flops=0, spaces=None, scratch=(), light=False):
    inner = pl.BlockSpec(memory_space=pltpu.VMEM)
    specs = [inner if s is None else pl.BlockSpec(memory_space=s) for s in spaces or ()]
    touched = sum(x.size * x.dtype.itemsize for x in jax.tree.leaves((operands, outs)))
    return pl.pallas_call(
        body,
        out_shape=outs,
        in_specs=specs or [inner] * len(operands),
        out_specs=jax.tree.map(lambda _: inner, outs),
        scratch_shapes=scratch,
        compiler_params=pltpu.CompilerParams(vmem_limit_bytes=16 * 1024 * 1024),
        cost_estimate=pl.CostEstimate(
            flops=flops, bytes_accessed=0 if light else touched, transcendentals=0
        ),
    )(*operands)


def pack_body(down, up, owner, slot, out, ids, sems):
    g = lax.axis_index("groups")
    columns, keys = down.shape[1], up.shape[1]
    count = columns // keys
    size = up.shape[0] // count
    part = out.shape[0] - size
    mine = down.at[pl.ds(pl.multiple_of(g * part, part), part), :]
    copies = [pltpu.make_async_copy(mine, out.at[pl.ds(0, part), :], sems.at[count])]
    for k in range(count):
        copies.append(
            pltpu.make_async_copy(
                up.at[pl.ds(k * size, size), :],
                out.at[pl.ds(part, size), pl.ds(k * keys, keys)],
                sems.at[k],
            )
        )
    for copy in copies:
        copy.start()
    row = lax.broadcasted_iota(jnp.int32, ids.shape, 0)
    value = jnp.where(row == 0, owner[...], jnp.where(row == 1, slot[...].reshape(1, -1), 0))
    ids[...] = value.astype(jnp.float32).astype(jnp.bfloat16)
    for copy in copies:
        copy.wait()


def split_body(tokens, ids, own, away, sems):
    g = lax.axis_index("groups")
    rows, part = tokens.shape[0], own.shape[1]
    copies = []
    for n, (out, half) in enumerate(((own, g), (away, 1 - g))):
        taken = tokens.at[:, pl.ds(pl.multiple_of(half * part, part), part)]
        copies.append(pltpu.make_async_copy(taken, out.at[pl.ds(0, rows), :], sems.at[n]))
    for copy in copies:
        copy.start()
    for out in (own, away):
        out[rows:, :rows] = ids[...]
        out[rows:, rows:] = jnp.zeros((ID_ROWS, part - rows), jnp.bfloat16)
    for copy in copies:
        copy.wait()


def hop_body(rows, capacity, own, away, own_out, away_out, places):
    a = lax.axis_index("adapter")
    part = own.shape[1]
    ids = own[rows:, :rows]
    match = (ids.astype(jnp.float32) == (OWNERS - 1 - a).astype(jnp.float32)).astype(jnp.bfloat16)
    earlier = lax.broadcasted_iota(jnp.int32, (rows, rows), 0) < lax.broadcasted_iota(
        jnp.int32, (rows, rows), 1
    )
    rank = jnp.dot(match, earlier.astype(jnp.bfloat16), preferred_element_type=jnp.float32)
    place = lax.broadcasted_iota(jnp.int32, (capacity, rows), 0).astype(jnp.float32)
    taken = (place == rank[0:1]) & (match[0:1].astype(jnp.float32) > 0)
    chosen = taken.astype(jnp.bfloat16)
    places[...] = chosen
    kept = lax.dot_general(ids, chosen, NT, preferred_element_type=jnp.float32)
    for tokens, out in ((own, own_out), (away, away_out)):
        packed = jnp.dot(chosen, tokens[:rows, :], preferred_element_type=jnp.float32)
        out[:capacity, :] = packed.astype(jnp.bfloat16)
        out[capacity:, :] = jnp.zeros((ID_ROWS, part), jnp.bfloat16)
        out[capacity:, :capacity] = kept.astype(jnp.bfloat16)


def base_body(bit, rows, own, away, weights, _, keep, give, base):
    g = lax.axis_index("groups")
    part = own.shape[1]
    total = jnp.zeros(base.shape, jnp.float32)
    for tokens, half in ((own, g), (away, 1 - g)):
        part_weights = weights[pl.ds(pl.multiple_of(half * part, part), part), :]
        total = total + jnp.dot(tokens[:rows, :], part_weights, preferred_element_type=jnp.float32)
    base[...] = total
    halves(base, bit, keep, give)


def halves(base, bit, keep, give):
    m = lax.axis_index("mp")
    width = keep.shape[1]
    side = (m // bit) % 2
    keep[...] = base[:, pl.ds(pl.multiple_of(side * width, width), width)]
    give[...] = base[:, pl.ds(pl.multiple_of((1 - side) * width, width), width)]


def id_columns(rows_ref, start, count):
    eye = (
        lax.broadcasted_iota(jnp.int32, (ID_ROWS, ID_ROWS), 0)
        == lax.broadcasted_iota(jnp.int32, (ID_ROWS, ID_ROWS), 1)
    ).astype(jnp.bfloat16)
    ids = lax.dot_general(
        rows_ref[start : start + ID_ROWS, :count], eye, TN, preferred_element_type=jnp.float32
    )
    return ids[:, 0:1], ids[:, 1:2]


def adapters(rows, columns):
    column = lax.broadcasted_iota(jnp.int32, (rows, columns), 1)
    return (column // ADAPTER_RANK).astype(jnp.float32)


def fold(wide):
    folded = wide[:, :LANES]
    for k in range(1, wide.shape[1] // LANES):
        folded = folded + wide[:, k * LANES : (k + 1) * LANES]
    return folded


def low_rank(folded):
    turned = folded.T
    low = turned[:ADAPTER_RANK]
    for k in range(1, LANES // ADAPTER_RANK):
        low = low + turned[k * ADAPTER_RANK : (k + 1) * ADAPTER_RANK]
    return low


def stacked(wide, keys):
    return jnp.concatenate([wide[:, k : k + keys] for k in range(0, wide.shape[1], keys)], axis=0)


def early_body(bits, part, rows, *refs):
    groups = lax.axis_size("groups")
    a = lax.axis_index("adapter")
    token_refs, rest = refs[:groups], refs[groups:]
    blocks, (folded, mask, numbers, ups) = rest[: len(bits)], rest[len(bits) :]
    columns = blocks[0].shape[1]
    for n, block in enumerate(blocks):
        ups[n] = stacked(block[part:, :], ups.shape[2])
    adapter = adapters(rows, columns)
    for n, tokens in enumerate(token_refs):
        owner, slot = id_columns(tokens, rows, rows)
        if n == 0:
            numbers[...] = owner * (columns // ADAPTER_RANK) + slot
        right = adapter == slot
        picked = jnp.zeros((rows, columns), jnp.float32)
        for bit, block in zip(bits, blocks):
            wide = jnp.dot(tokens[:rows, :], block[:part, :], preferred_element_type=jnp.float32)
            picked = jnp.where(owner == (a ^ bit).astype(jnp.float32), wide, picked)
        folded[n] = fold(jnp.where(right, picked, 0.0))
        mask[n] = jnp.where(owner == (a ^ 2).astype(jnp.float32), right.astype(jnp.float32), 0.0)


def hop_mask_body(capacity, hop, _, out):
    _, slot = id_columns(hop, capacity, capacity)
    out[...] = (adapters(capacity, out.shape[1]) == slot).astype(jnp.float32)


def last_body(part, rows, capacity, *refs):
    groups = lax.axis_size("groups")
    a = lax.axis_index("adapter")
    token_refs, rest = refs[:groups], refs[groups:]
    hops, rest = rest[:groups], rest[groups:]
    hop_masks, rest = rest[:groups], rest[groups:]
    folded, mask, outside, inside, low, hop_low, away, last_up = rest
    columns = inside.shape[1]

    def finish(block):
        for n, tokens in enumerate(token_refs):
            wide = jnp.dot(tokens[:rows, :], block[:part, :], preferred_element_type=jnp.float32)
            kept = fold(jnp.where(mask[n] > 0, wide, 0.0))
            if n:
                away[:, :rows] = low_rank(folded[n] + kept)
            else:
                low[...] = low_rank(folded[n] + kept)

    middle = (a == 1) | (a == 2)

    @pl.when(middle)
    def _():
        finish(inside)
        last_up[...] = stacked(inside[part:, :], last_up.shape[1])
        for n, (hop, hop_mask) in enumerate(zip(hops, hop_masks)):
            wide = jnp.dot(hop[:capacity, :], inside[:part, :], preferred_element_type=jnp.float32)
            kept = fold(jnp.where(hop_mask[...] > 0, wide, 0.0))
            rest_rows = -capacity % LANES
            kept = jnp.concatenate([kept, jnp.zeros((rest_rows, LANES), jnp.float32)], axis=0)
            if n:
                away[:, rows:] = low_rank(kept)[:, :capacity]
            else:
                hop_low[...] = low_rank(kept)[:, :capacity]

    @pl.when(jnp.logical_not(middle))
    def _():
        finish(outside)
        last_up[...] = stacked(outside[part:, :], last_up.shape[1])
        hop_low[...] = jnp.zeros(hop_low.shape, jnp.float32)
        away[:, rows:] = jnp.zeros(hop_low.shape, jnp.float32)


def near_body(low, hop_low, near, low_out, hop_out):
    rows = low.shape[1]
    low_out[...] = low[...] + near[:, :rows]
    hop_out[...] = hop_low[...] + near[:, rows:]


def merge_body(bit, low, places, kept, got, hop, out, keep, give, base):
    back = hop[...]
    spread = jnp.zeros(low.shape, jnp.float32)
    for _ in range(3):
        piece = back.astype(jnp.bfloat16)
        back = back - piece.astype(jnp.float32)
        spread = spread + jnp.dot(piece, places[...], preferred_element_type=jnp.float32)
    out[...] = low[...] + spread
    base[...] = kept[...] + got[...]
    halves(base, bit, keep, give)


def finish_body(near, far, keep, got, numbers, ups, last_up, distant, out):
    a = lax.axis_index("adapter")
    rows = out.shape[0]
    columns = last_up.shape[0]
    column = lax.broadcasted_iota(jnp.int32, (ADAPTER_RANK, columns), 1)
    row = lax.broadcasted_iota(jnp.int32, (ADAPTER_RANK, columns), 0)
    repeat = (lax.rem(column, ADAPTER_RANK) == row).astype(jnp.bfloat16)
    shrunk = (near[...] + far[...]).astype(jnp.bfloat16)
    spread = lax.dot_general(shrunk, repeat, TN, preferred_element_type=jnp.float32)
    adapter = adapters(rows, columns)
    middle = (a == 1) | (a == 2)
    mirrored = jnp.where(middle, ups[1].astype(jnp.float32), distant[...].astype(jnp.float32))
    blocks = ((0, ups[0]), (1, ups[2]), (2, last_up[...]), (3, mirrored.astype(jnp.bfloat16)))
    updates = jnp.zeros(out.shape, jnp.float32)
    for bit, up in blocks:
        wanted = numbers[...] - ((a ^ bit) * (columns // ADAPTER_RANK)).astype(jnp.float32)
        chosen = jnp.where(adapter == wanted, spread, 0.0).astype(jnp.bfloat16)
        updates = updates + jnp.dot(chosen, up, preferred_element_type=jnp.float32)
    updates = updates.astype(jnp.bfloat16).astype(jnp.float32)
    base = keep[...] + got[...]
    out[...] = (base + ADAPTER_SCALE * updates).astype(jnp.bfloat16)


def gather(
    tokens,
    base_key_weight,
    stacked_down_weight,
    stacked_up_weight,
    request_adapter_owner,
    request_adapter_slot,
):
    rows, features = tokens.shape
    groups, owners, shares = (lax.axis_size(name) for name in AXES)
    columns = stacked_down_weight.shape[1]
    keys = stacked_up_weight.shape[1]
    part = features // groups
    half = columns // keys
    capacity = -(-row_limit(rows) // ID_ROWS) * ID_ROWS

    def narrow(*dims):
        return jax.ShapeDtypeStruct(dims, jnp.bfloat16)

    def wide(*dims):
        return jax.ShapeDtypeStruct(dims, jnp.float32)

    own, ids = kernel(
        pack_body,
        [narrow(part + columns // half, columns), narrow(ID_ROWS, rows)],
        (
            stacked_down_weight,
            stacked_up_weight,
            request_adapter_owner.reshape(1, rows),
            request_adapter_slot,
        ),
        0,
        (pl.ANY, pl.ANY, None, None),
        [pltpu.SemaphoreType.DMA((1 + half,))],
    )
    mirror = exchange(own, 0, 0, MIDDLE)
    beside = exchange(own, 0, 0, BESIDE)

    tok_own, tok_away = kernel(
        split_body,
        [narrow(rows + ID_ROWS, part)] * groups,
        (tokens, ids),
        0,
        (pl.ANY, None),
        [pltpu.SemaphoreType.DMA((groups,))],
    )
    token_parts = [tok_own, exchange(tok_away, 1, 0, SAME)]
    hop_own, hop_away, places = kernel(
        functools.partial(hop_body, rows, capacity),
        [narrow(capacity + ID_ROWS, part)] * groups
        + [narrow(capacity, rows)],
        (tok_own, tok_away),
        2 * rows * features * capacity,
    )

    inside = exchange(beside, 0, 0, MIDDLE)
    outside = exchange(mirror, 0, 0, OUTWARD)
    hops = [
        exchange(hop_own, 0, 0, INWARD),
        exchange(hop_away, 1, 0, INWARD),
    ]

    folded, mask, numbers, ups = kernel(
        functools.partial(early_body, (0, 3, 1), part, rows),
        [wide(groups, rows, LANES), wide(groups, rows, columns), wide(rows, 1), narrow(3, columns, keys)],
        (*token_parts, own, mirror, beside),
        light=True,
    )
    distant = exchange(after(stacked_up_weight, folded), 0, 0, ENDS)
    hop_masks, latest = [], folded
    for hop, urgency in zip(hops, HOP_URGENCY):
        latest = kernel(
            functools.partial(hop_mask_body, capacity),
            wide(capacity, columns),
            (hop, latest),
            urgency,
            (None, pl.ANY),
        )
        hop_masks.append(latest)
    bits = (2, 1)
    keep, give = kernel(
        functools.partial(base_body, bits[0], rows),
        [wide(rows, shares * keys // 2)] * 2,
        (tok_own, tok_away, base_key_weight, places),
        2 * rows * features * shares * keys,
        (None, None, None, pl.ANY),
        [pltpu.VMEM((rows, shares * keys), jnp.float32)],
    )
    got = exchange(after(give, folded), 0, bits[0], SAME)

    low, hop_low, away, last_up = kernel(
        functools.partial(last_body, part, rows, capacity),
        [
            wide(ADAPTER_RANK, rows),
            wide(ADAPTER_RANK, capacity),
            wide(ADAPTER_RANK, rows + capacity),
            narrow(columns, keys),
        ],
        (*token_parts, *hops, *hop_masks, after(folded, distant), mask, outside, inside),
        2 * groups * (rows + capacity) * part * columns,
    )

    near = exchange(away, 1, 0, SAME)
    low, hop_low = kernel(
        near_body, [wide(ADAPTER_RANK, rows), wide(ADAPTER_RANK, capacity)], (low, hop_low, near)
    )
    back = exchange(hop_low, 0, 0, OUTWARD)
    low, keep, give = kernel(
        functools.partial(merge_body, bits[1]),
        [wide(ADAPTER_RANK, rows)] + [wide(rows, bits[1] * keys)] * 2,
        (low, places, keep, got, back),
        scratch=[pltpu.VMEM((rows, bits[0] * keys), jnp.float32)],
    )
    got = exchange(give, 0, bits[1], SAME)
    low = low + exchange(low, 0, bits[0], SAME)
    low_far = exchange(low, 0, bits[1], SAME)
    return kernel(
        finish_body, narrow(rows, keys), (low, low_far, keep, got, numbers, ups, last_up, distant)
    )


def row_limit(rows):
    return max(2, 3 * rows // (2 * lax.axis_size("adapter")))


def local(*args):
    rows, columns = args[0].shape[0], args[2].shape[1]
    groups, owners, shares = (lax.axis_size(name) for name in AXES)
    fits = owners == OWNERS and groups == 2 and shares == 4
    travels = fits and columns <= groups * row_limit(rows)
    return (gather if travels else dispatch)(*args)


def solution(mesh):
    placed = (
        P(("groups", "adapter"), "mp"),
        P("mp", None),
        P("mp", "adapter"),
        P("adapter", "mp"),
        P(("groups", "adapter"), None),
        P(("groups", "adapter")),
    )
    return jax.shard_map(
        local, mesh=mesh, in_specs=placed, out_specs=P(("groups", "adapter"), "mp"), check_vma=False
    )
```

```python
import functools

import jax
import jax.numpy as jnp
from jax import lax
from jax.experimental import pallas as pl
from jax.experimental.pallas import tpu as pltpu
from jax.sharding import PartitionSpec as P

ADAPTER_RANK = 16


ADAPTER_SCALE = 2.0


def dispatch(
    tokens,
    base_key_weight,
    stacked_down_weight,
    stacked_up_weight,
    request_adapter_owner,
    request_adapter_slot,
):
    rows_here = tokens.shape[0]
    feature_share = tokens.shape[1]
    owner_count = lax.axis_size("adapter")
    capacity = max(2, 3 * rows_here // (2 * owner_count))
    local_adapters = stacked_down_weight.shape[1] // ADAPTER_RANK
    key_output_share = stacked_up_weight.shape[1]
    owners = request_adapter_owner.reshape(-1)
    onehot = (owners[:, None] == jnp.arange(owner_count, dtype=jnp.int32)[None, :]).astype(
        jnp.int32
    )
    before = jnp.sum((jnp.cumsum(onehot, axis=0) - onehot) * onehot, axis=1)
    places = owners * capacity + before
    send_rows = (
        jnp.zeros((owner_count * capacity, feature_share), jnp.bfloat16).at[places].set(tokens)
    )
    send_rows = send_rows.reshape(owner_count, capacity, feature_share)
    send_slots = (
        jnp.full((owner_count * capacity,), -1, jnp.int32).at[places].set(request_adapter_slot)
    )
    send_slots = send_slots.reshape(owner_count, capacity)
    input_rows = lax.all_to_all(send_rows, "adapter", split_axis=0, concat_axis=0, tiled=True)
    slots_in = lax.all_to_all(send_slots, "adapter", split_axis=0, concat_axis=0, tiled=True)
    key_projection_output = jnp.einsum(
        "rzq,qt->rzt", input_rows, stacked_down_weight, preferred_element_type=jnp.float32
    )
    key_projection_output = key_projection_output.reshape(
        input_rows.shape[0], input_rows.shape[1], local_adapters, ADAPTER_RANK
    )
    chosen = slots_in[:, :, None] == jnp.arange(local_adapters, dtype=jnp.int32)[None, None, :]
    partial_low = jnp.sum(jnp.where(chosen[:, :, :, None], key_projection_output, 0.0), axis=2)
    shrunk = lax.psum(partial_low, "mp")
    shrunk_bf = shrunk.astype(jnp.bfloat16)
    returned = lax.all_to_all(shrunk_bf, "adapter", split_axis=0, concat_axis=0, tiled=True)
    low_rows = returned.reshape(owner_count * capacity, ADAPTER_RANK)[places]
    gathered_up_weight = lax.all_gather(stacked_up_weight, "adapter", axis=0, tiled=True)
    adapter_ids = owners * local_adapters + request_adapter_slot
    up_taken = gathered_up_weight.reshape(-1, ADAPTER_RANK, key_output_share)[adapter_ids]
    adapter_updates = jnp.einsum(
        "tr,trk->tk", low_rows, up_taken, preferred_element_type=jnp.float32
    ).astype(jnp.bfloat16)
    base_output_share = lax.psum_scatter(
        lax.dot_general(
            base_key_weight, tokens, (((0,), (1,)), ((), ())), preferred_element_type=jnp.float32
        ),
        "mp",
        scatter_dimension=0,
        tiled=True,
    )
    return (base_output_share.T + ADAPTER_SCALE * adapter_updates.astype(jnp.float32)).astype(
        jnp.bfloat16
    )


AXES = ("groups", "adapter", "mp")
ID_ROWS = 16
HOP_URGENCY = (30 * 10**8, 0)
OWNERS = 4
LANES = 128
NT = (((1,), (1,)), ((), ()))
TN = (((0,), (0,)), ((), ()))


def exchange(x, group_bits, share_bits, owners):
    groups, count, shares = (lax.axis_size(name) for name in AXES)

    def number(g, a, m):
        return (g * count + a) * shares + m

    pairs = [
        (number(g, a, m), number(g ^ group_bits, b, m ^ share_bits))
        for g in range(groups)
        for a, b in owners
        for m in range(shares)
    ]
    return lax.ppermute(x, AXES, pairs)


SAME = tuple((a, a) for a in range(OWNERS))
BESIDE = ((0, 1), (1, 0), (2, 3), (3, 2))
MIDDLE = ((1, 2), (2, 1))
ENDS = ((0, 3), (3, 0))
OUTWARD = ((1, 0), (2, 3))
INWARD = ((0, 1), (3, 2))


def after(x, *others):
    return lax.optimization_barrier((x, *others))[0]


def in_hbm(x):
    return pltpu.with_memory_space_constraint(x, pltpu.HBM)


def kernel(body, outs, operands, flops=0, spaces=None, scratch=(), light=False):
    inner = pl.BlockSpec(memory_space=pltpu.VMEM)
    specs = [inner if s is None else pl.BlockSpec(memory_space=s) for s in spaces or ()]
    touched = sum(x.size * x.dtype.itemsize for x in jax.tree.leaves((operands, outs)))
    return pl.pallas_call(
        body,
        out_shape=outs,
        in_specs=specs or [inner] * len(operands),
        out_specs=jax.tree.map(lambda _: inner, outs),
        scratch_shapes=scratch,
        compiler_params=pltpu.CompilerParams(vmem_limit_bytes=16 * 1024 * 1024),
        cost_estimate=pl.CostEstimate(
            flops=flops, bytes_accessed=0 if light else touched, transcendentals=0
        ),
    )(*operands)


def pack_body(down, up, out, sems):
    g = lax.axis_index("groups")
    columns, keys = down.shape[1], up.shape[1]
    count = columns // keys
    size = up.shape[0] // count
    part = out.shape[0] - size
    mine = down.at[pl.ds(pl.multiple_of(g * part, part), part), :]
    copies = [pltpu.make_async_copy(mine, out.at[pl.ds(0, part), :], sems.at[count])]
    for k in range(count):
        copies.append(
            pltpu.make_async_copy(
                up.at[pl.ds(k * size, size), :],
                out.at[pl.ds(part, size), pl.ds(k * keys, keys)],
                sems.at[k],
            )
        )
    for copy in copies:
        copy.start()
    for copy in copies:
        copy.wait()


def split_body(tokens, owner, slot, _, own, away, sems):
    g = lax.axis_index("groups")
    rows, part = tokens.shape[0], own.shape[1]
    copies = []
    for n, (out, half) in enumerate(((own, g), (away, 1 - g))):
        taken = tokens.at[:, pl.ds(pl.multiple_of(half * part, part), part)]
        copies.append(pltpu.make_async_copy(taken, out.at[pl.ds(0, rows), :], sems.at[n]))
    for copy in copies:
        copy.start()
    row = lax.broadcasted_iota(jnp.int32, (ID_ROWS, rows), 0)
    ids = jnp.where(row == 0, owner[...], jnp.where(row == 1, slot[...].reshape(1, rows), 0))
    ids = ids.astype(jnp.float32).astype(jnp.bfloat16)
    for out in (own, away):
        out[rows:, :rows] = ids
        out[rows:, rows:] = jnp.zeros((ID_ROWS, part - rows), jnp.bfloat16)
    for copy in copies:
        copy.wait()


def hop_body(rows, capacity, own, away, own_out, away_out, places):
    a = lax.axis_index("adapter")
    part = own.shape[1]
    ids = own[rows:, :rows]
    match = (ids.astype(jnp.float32) == (OWNERS - 1 - a).astype(jnp.float32)).astype(jnp.bfloat16)
    earlier = lax.broadcasted_iota(jnp.int32, (rows, rows), 0) < lax.broadcasted_iota(
        jnp.int32, (rows, rows), 1
    )
    rank = jnp.dot(match, earlier.astype(jnp.bfloat16), preferred_element_type=jnp.float32)
    place = lax.broadcasted_iota(jnp.int32, (capacity, rows), 0).astype(jnp.float32)
    taken = (place == rank[0:1]) & (match[0:1].astype(jnp.float32) > 0)
    chosen = taken.astype(jnp.bfloat16)
    places[...] = chosen
    kept = lax.dot_general(ids, chosen, NT, preferred_element_type=jnp.float32)
    for tokens, out in ((own, own_out), (away, away_out)):
        packed = jnp.dot(chosen, tokens[:rows, :], preferred_element_type=jnp.float32)
        out[:capacity, :] = packed.astype(jnp.bfloat16)
        out[capacity:, :] = jnp.zeros((ID_ROWS, part), jnp.bfloat16)
        out[capacity:, :capacity] = kept.astype(jnp.bfloat16)


def base_body(bit, rows, own, away, weights, _, keep, give, base):
    g = lax.axis_index("groups")
    part = own.shape[1]
    total = jnp.zeros(base.shape, jnp.float32)
    for tokens, half in ((own, g), (away, 1 - g)):
        part_weights = weights[pl.ds(pl.multiple_of(half * part, part), part), :]
        total = total + jnp.dot(tokens[:rows, :], part_weights, preferred_element_type=jnp.float32)
    base[...] = total
    halves(base, bit, keep, give)


def halves(base, bit, keep, give):
    m = lax.axis_index("mp")
    width = keep.shape[1]
    side = (m // bit) % 2
    keep[...] = base[:, pl.ds(pl.multiple_of(side * width, width), width)]
    give[...] = base[:, pl.ds(pl.multiple_of((1 - side) * width, width), width)]


def id_columns(rows_ref, start, count):
    eye = (
        lax.broadcasted_iota(jnp.int32, (ID_ROWS, ID_ROWS), 0)
        == lax.broadcasted_iota(jnp.int32, (ID_ROWS, ID_ROWS), 1)
    ).astype(jnp.bfloat16)
    ids = lax.dot_general(
        rows_ref[start : start + ID_ROWS, :count], eye, TN, preferred_element_type=jnp.float32
    )
    return ids[:, 0:1], ids[:, 1:2]


def adapters(rows, columns):
    column = lax.broadcasted_iota(jnp.int32, (rows, columns), 1)
    return (column // ADAPTER_RANK).astype(jnp.float32)


def fold(wide):
    folded = wide[:, :LANES]
    for k in range(1, wide.shape[1] // LANES):
        folded = folded + wide[:, k * LANES : (k + 1) * LANES]
    return folded


def low_rank(folded):
    turned = folded.T
    low = turned[:ADAPTER_RANK]
    for k in range(1, LANES // ADAPTER_RANK):
        low = low + turned[k * ADAPTER_RANK : (k + 1) * ADAPTER_RANK]
    return low


def stacked(wide, keys):
    return jnp.concatenate([wide[:, k : k + keys] for k in range(0, wide.shape[1], keys)], axis=0)


def early_body(bits, part, rows, *refs):
    groups = lax.axis_size("groups")
    a = lax.axis_index("adapter")
    token_refs, rest = refs[:groups], refs[groups:]
    blocks, (folded, mask, numbers, ups) = rest[: len(bits)], rest[len(bits) :]
    columns = blocks[0].shape[1]
    for n, block in enumerate(blocks):
        ups[n] = stacked(block[part:, :], ups.shape[2])
    adapter = adapters(rows, columns)
    for n, tokens in enumerate(token_refs):
        owner, slot = id_columns(tokens, rows, rows)
        if n == 0:
            numbers[...] = owner * (columns // ADAPTER_RANK) + slot
        right = adapter == slot
        picked = jnp.zeros((rows, columns), jnp.float32)
        for bit, block in zip(bits, blocks):
            wide = jnp.dot(tokens[:rows, :], block[:part, :], preferred_element_type=jnp.float32)
            picked = jnp.where(owner == (a ^ bit).astype(jnp.float32), wide, picked)
        folded[n] = fold(jnp.where(right, picked, 0.0))
        mask[n] = jnp.where(owner == (a ^ 2).astype(jnp.float32), right.astype(jnp.float32), 0.0)


def hop_mask_body(capacity, hop, _, out):
    _, slot = id_columns(hop, capacity, capacity)
    out[...] = (adapters(capacity, out.shape[1]) == slot).astype(jnp.float32)


def last_body(part, rows, capacity, *refs):
    groups = lax.axis_size("groups")
    a = lax.axis_index("adapter")
    token_refs, rest = refs[:groups], refs[groups:]
    hops, rest = rest[:groups], rest[groups:]
    hop_masks, rest = rest[:groups], rest[groups:]
    folded, mask, outside, inside, low, hop_low, away, last_up = rest
    columns = inside.shape[1]

    def finish(block):
        for n, tokens in enumerate(token_refs):
            wide = jnp.dot(tokens[:rows, :], block[:part, :], preferred_element_type=jnp.float32)
            kept = fold(jnp.where(mask[n] > 0, wide, 0.0))
            if n:
                away[:, :rows] = low_rank(folded[n] + kept)
            else:
                low[...] = low_rank(folded[n] + kept)

    middle = (a == 1) | (a == 2)

    @pl.when(middle)
    def _():
        finish(inside)
        last_up[...] = stacked(inside[part:, :], last_up.shape[1])
        for n, (hop, hop_mask) in enumerate(zip(hops, hop_masks)):
            wide = jnp.dot(hop[:capacity, :], inside[:part, :], preferred_element_type=jnp.float32)
            kept = fold(jnp.where(hop_mask[...] > 0, wide, 0.0))
            rest_rows = -capacity % LANES
            kept = jnp.concatenate([kept, jnp.zeros((rest_rows, LANES), jnp.float32)], axis=0)
            if n:
                away[:, rows:] = low_rank(kept)[:, :capacity]
            else:
                hop_low[...] = low_rank(kept)[:, :capacity]

    @pl.when(jnp.logical_not(middle))
    def _():
        finish(outside)
        last_up[...] = stacked(outside[part:, :], last_up.shape[1])
        hop_low[...] = jnp.zeros(hop_low.shape, jnp.float32)
        away[:, rows:] = jnp.zeros(hop_low.shape, jnp.float32)


def near_body(low, hop_low, near, low_out, hop_out):
    rows = low.shape[1]
    low_out[...] = low[...] + near[:, :rows]
    hop_out[...] = hop_low[...] + near[:, rows:]


def merge_body(bit, low, places, kept, got, hop, out, keep, give, base):
    back = hop[...]
    spread = jnp.zeros(low.shape, jnp.float32)
    for _ in range(3):
        piece = back.astype(jnp.bfloat16)
        back = back - piece.astype(jnp.float32)
        spread = spread + jnp.dot(piece, places[...], preferred_element_type=jnp.float32)
    out[...] = low[...] + spread
    base[...] = kept[...] + got[...]
    halves(base, bit, keep, give)


def finish_body(near, far, keep, got, numbers, ups, last_up, distant, out):
    a = lax.axis_index("adapter")
    rows = out.shape[0]
    columns = last_up.shape[0]
    column = lax.broadcasted_iota(jnp.int32, (ADAPTER_RANK, columns), 1)
    row = lax.broadcasted_iota(jnp.int32, (ADAPTER_RANK, columns), 0)
    repeat = (lax.rem(column, ADAPTER_RANK) == row).astype(jnp.bfloat16)
    shrunk = (near[...] + far[...]).astype(jnp.bfloat16)
    spread = lax.dot_general(shrunk, repeat, TN, preferred_element_type=jnp.float32)
    adapter = adapters(rows, columns)
    middle = (a == 1) | (a == 2)
    mirrored = jnp.where(middle, ups[1].astype(jnp.float32), distant[...].astype(jnp.float32))
    blocks = ((0, ups[0]), (1, ups[2]), (2, last_up[...]), (3, mirrored.astype(jnp.bfloat16)))
    updates = jnp.zeros(out.shape, jnp.float32)
    for bit, up in blocks:
        wanted = numbers[...] - ((a ^ bit) * (columns // ADAPTER_RANK)).astype(jnp.float32)
        chosen = jnp.where(adapter == wanted, spread, 0.0).astype(jnp.bfloat16)
        updates = updates + jnp.dot(chosen, up, preferred_element_type=jnp.float32)
    updates = updates.astype(jnp.bfloat16).astype(jnp.float32)
    base = keep[...] + got[...]
    out[...] = (base + ADAPTER_SCALE * updates).astype(jnp.bfloat16)


def gather(
    tokens,
    base_key_weight,
    stacked_down_weight,
    stacked_up_weight,
    request_adapter_owner,
    request_adapter_slot,
):
    rows, features = tokens.shape
    groups, owners, shares = (lax.axis_size(name) for name in AXES)
    columns = stacked_down_weight.shape[1]
    keys = stacked_up_weight.shape[1]
    part = features // groups
    half = columns // keys
    capacity = -(-row_limit(rows) // ID_ROWS) * ID_ROWS

    def narrow(*dims):
        return jax.ShapeDtypeStruct(dims, jnp.bfloat16)

    def wide(*dims):
        return jax.ShapeDtypeStruct(dims, jnp.float32)

    own = kernel(
        pack_body,
        narrow(part + columns // half, columns),
        (in_hbm(stacked_down_weight), in_hbm(stacked_up_weight)),
        0,
        (pl.ANY, pl.ANY),
        [pltpu.SemaphoreType.DMA((1 + half,))],
    )
    mirror = exchange(own, 0, 0, MIDDLE)
    beside = exchange(own, 0, 0, BESIDE)

    tok_own, tok_away = kernel(
        split_body,
        [narrow(rows + ID_ROWS, part)] * groups,
        (in_hbm(tokens), request_adapter_owner.reshape(1, rows), request_adapter_slot, own),
        0,
        (pl.ANY, None, None, pl.ANY),
        [pltpu.SemaphoreType.DMA((groups,))],
    )
    token_parts = [tok_own, exchange(tok_away, 1, 0, SAME)]
    hop_own, hop_away, places = kernel(
        functools.partial(hop_body, rows, capacity),
        [narrow(capacity + ID_ROWS, part)] * groups
        + [narrow(capacity, rows)],
        (tok_own, tok_away),
        2 * rows * features * capacity,
    )

    inside = exchange(beside, 0, 0, MIDDLE)
    outside = exchange(mirror, 0, 0, OUTWARD)
    hops = [
        exchange(after(hop_own, beside), 0, 0, INWARD),
        exchange(hop_away, 1, 0, INWARD),
    ]

    folded, mask, numbers, ups = kernel(
        functools.partial(early_body, (0, 3, 1), part, rows),
        [wide(groups, rows, LANES), wide(groups, rows, columns), wide(rows, 1), narrow(3, columns, keys)],
        (*token_parts, own, mirror, beside),
        light=True,
    )
    hop_masks, latest = [], folded
    for hop, urgency in zip(hops, HOP_URGENCY):
        latest = kernel(
            functools.partial(hop_mask_body, capacity),
            wide(capacity, columns),
            (hop, latest),
            urgency,
            (None, pl.ANY),
        )
        hop_masks.append(latest)
    bits = (2, 1)
    keep, give = kernel(
        functools.partial(base_body, bits[0], rows),
        [wide(rows, shares * keys // 2)] * 2,
        (tok_own, tok_away, base_key_weight, places),
        2 * rows * features * shares * keys,
        (None, None, None, pl.ANY),
        [pltpu.VMEM((rows, shares * keys), jnp.float32)],
    )
    got = exchange(after(give, folded), 0, bits[0], SAME)

    low, hop_low, away, last_up = kernel(
        functools.partial(last_body, part, rows, capacity),
        [
            wide(ADAPTER_RANK, rows),
            wide(ADAPTER_RANK, capacity),
            wide(ADAPTER_RANK, rows + capacity),
            narrow(columns, keys),
        ],
        (*token_parts, *hops, *hop_masks, folded, mask, outside, inside),
        2 * groups * (rows + capacity) * part * columns,
    )

    near = exchange(away, 1, 0, SAME)
    distant = exchange(after(stacked_up_weight, folded), 0, 0, ENDS)
    low, hop_low = kernel(
        near_body, [wide(ADAPTER_RANK, rows), wide(ADAPTER_RANK, capacity)], (low, hop_low, near)
    )
    back = exchange(hop_low, 0, 0, OUTWARD)
    low, keep, give = kernel(
        functools.partial(merge_body, bits[1]),
        [wide(ADAPTER_RANK, rows)] + [wide(rows, bits[1] * keys)] * 2,
        (after(low, distant), places, keep, got, back),
        scratch=[pltpu.VMEM((rows, bits[0] * keys), jnp.float32)],
    )
    got = exchange(give, 0, bits[1], SAME)
    low = low + exchange(low, 0, bits[0], SAME)
    low_far = exchange(low, 0, bits[1], SAME)
    return kernel(
        finish_body, narrow(rows, keys), (low, low_far, keep, got, numbers, ups, last_up, distant)
    )


def row_limit(rows):
    return max(2, 3 * rows // (2 * lax.axis_size("adapter")))


def local(*args):
    rows, columns = args[0].shape[0], args[2].shape[1]
    groups, owners, shares = (lax.axis_size(name) for name in AXES)
    fits = owners == OWNERS and groups == 2 and shares == 4
    travels = fits and columns <= groups * row_limit(rows)
    return (gather if travels else dispatch)(*args)


def solution(mesh):
    placed = (
        P(("groups", "adapter"), "mp"),
        P("mp", None),
        P("mp", "adapter"),
        P("adapter", "mp"),
        P(("groups", "adapter"), None),
        P(("groups", "adapter")),
    )
    return jax.shard_map(
        local, mesh=mesh, in_specs=placed, out_specs=P(("groups", "adapter"), "mp"), check_vma=False
    )
```

```python
import functools

import jax
import jax.numpy as jnp
from jax import lax
from jax.experimental import pallas as pl
from jax.experimental.pallas import tpu as pltpu
from jax.sharding import PartitionSpec as P

ADAPTER_RANK = 16


ADAPTER_SCALE = 2.0


def dispatch(
    tokens,
    base_key_weight,
    stacked_down_weight,
    stacked_up_weight,
    request_adapter_owner,
    request_adapter_slot,
):
    rows_here = tokens.shape[0]
    feature_share = tokens.shape[1]
    owner_count = lax.axis_size("adapter")
    capacity = max(2, 3 * rows_here // (2 * owner_count))
    local_adapters = stacked_down_weight.shape[1] // ADAPTER_RANK
    key_output_share = stacked_up_weight.shape[1]
    owners = request_adapter_owner.reshape(-1)
    onehot = (owners[:, None] == jnp.arange(owner_count, dtype=jnp.int32)[None, :]).astype(
        jnp.int32
    )
    before = jnp.sum((jnp.cumsum(onehot, axis=0) - onehot) * onehot, axis=1)
    places = owners * capacity + before
    send_rows = (
        jnp.zeros((owner_count * capacity, feature_share), jnp.bfloat16).at[places].set(tokens)
    )
    send_rows = send_rows.reshape(owner_count, capacity, feature_share)
    send_slots = (
        jnp.full((owner_count * capacity,), -1, jnp.int32).at[places].set(request_adapter_slot)
    )
    send_slots = send_slots.reshape(owner_count, capacity)
    input_rows = lax.all_to_all(send_rows, "adapter", split_axis=0, concat_axis=0, tiled=True)
    slots_in = lax.all_to_all(send_slots, "adapter", split_axis=0, concat_axis=0, tiled=True)
    key_projection_output = jnp.einsum(
        "rzq,qt->rzt", input_rows, stacked_down_weight, preferred_element_type=jnp.float32
    )
    key_projection_output = key_projection_output.reshape(
        input_rows.shape[0], input_rows.shape[1], local_adapters, ADAPTER_RANK
    )
    chosen = slots_in[:, :, None] == jnp.arange(local_adapters, dtype=jnp.int32)[None, None, :]
    partial_low = jnp.sum(jnp.where(chosen[:, :, :, None], key_projection_output, 0.0), axis=2)
    shrunk = lax.psum(partial_low, "mp")
    shrunk_bf = shrunk.astype(jnp.bfloat16)
    returned = lax.all_to_all(shrunk_bf, "adapter", split_axis=0, concat_axis=0, tiled=True)
    low_rows = returned.reshape(owner_count * capacity, ADAPTER_RANK)[places]
    gathered_up_weight = lax.all_gather(stacked_up_weight, "adapter", axis=0, tiled=True)
    adapter_ids = owners * local_adapters + request_adapter_slot
    up_taken = gathered_up_weight.reshape(-1, ADAPTER_RANK, key_output_share)[adapter_ids]
    adapter_updates = jnp.einsum(
        "tr,trk->tk", low_rows, up_taken, preferred_element_type=jnp.float32
    ).astype(jnp.bfloat16)
    base_output_share = lax.psum_scatter(
        lax.dot_general(
            base_key_weight, tokens, (((0,), (1,)), ((), ())), preferred_element_type=jnp.float32
        ),
        "mp",
        scatter_dimension=0,
        tiled=True,
    )
    return (base_output_share.T + ADAPTER_SCALE * adapter_updates.astype(jnp.float32)).astype(
        jnp.bfloat16
    )


AXES = ("groups", "adapter", "mp")
ID_ROWS = 16
HOP_URGENCY = (42 * 10**8, 0)
OWNERS = 4
LANES = 128
NT = (((1,), (1,)), ((), ()))
TN = (((0,), (0,)), ((), ()))


def exchange(x, group_bits, share_bits, owners):
    groups, count, shares = (lax.axis_size(name) for name in AXES)

    def number(g, a, m):
        return (g * count + a) * shares + m

    pairs = [
        (number(g, a, m), number(g ^ group_bits, b, m ^ share_bits))
        for g in range(groups)
        for a, b in owners
        for m in range(shares)
    ]
    return lax.ppermute(x, AXES, pairs)


SAME = tuple((a, a) for a in range(OWNERS))
BESIDE = ((0, 1), (1, 0), (2, 3), (3, 2))
MIDDLE = ((1, 2), (2, 1))
ENDS = ((0, 3), (3, 0))
OUTWARD = ((1, 0), (2, 3))
INWARD = ((0, 1), (3, 2))


def after(x, *others):
    return lax.optimization_barrier((x, *others))[0]


def in_hbm(x):
    return pltpu.with_memory_space_constraint(x, pltpu.HBM)


def kernel(body, outs, operands, flops=0, spaces=None, scratch=(), light=False):
    inner = pl.BlockSpec(memory_space=pltpu.VMEM)
    specs = [inner if s is None else pl.BlockSpec(memory_space=s) for s in spaces or ()]
    touched = sum(x.size * x.dtype.itemsize for x in jax.tree.leaves((operands, outs)))
    return pl.pallas_call(
        body,
        out_shape=outs,
        in_specs=specs or [inner] * len(operands),
        out_specs=jax.tree.map(lambda _: inner, outs),
        scratch_shapes=scratch,
        compiler_params=pltpu.CompilerParams(vmem_limit_bytes=16 * 1024 * 1024),
        cost_estimate=pl.CostEstimate(
            flops=flops, bytes_accessed=0 if light else touched, transcendentals=0
        ),
    )(*operands)


def pack_body(down, up, out, sems):
    g = lax.axis_index("groups")
    columns, keys = down.shape[1], up.shape[1]
    count = columns // keys
    size = up.shape[0] // count
    part = out.shape[0] - size
    mine = down.at[pl.ds(pl.multiple_of(g * part, part), part), :]
    copies = [pltpu.make_async_copy(mine, out.at[pl.ds(0, part), :], sems.at[count])]
    for k in range(count):
        copies.append(
            pltpu.make_async_copy(
                up.at[pl.ds(k * size, size), :],
                out.at[pl.ds(part, size), pl.ds(k * keys, keys)],
                sems.at[k],
            )
        )
    for copy in copies:
        copy.start()
    for copy in copies:
        copy.wait()


def split_body(tokens, owner_in, slot_in, _, own, away, owner, slot, sems):
    g = lax.axis_index("groups")
    rows, part = tokens.shape[0], own.shape[1]
    copies = []
    for n, (out, half) in enumerate(((own, g), (away, 1 - g))):
        taken = tokens.at[:, pl.ds(pl.multiple_of(half * part, part), part)]
        copies.append(pltpu.make_async_copy(taken, out.at[pl.ds(0, rows), :], sems.at[n]))
    id_copies = [
        pltpu.make_async_copy(owner_in, owner, sems.at[2]),
        pltpu.make_async_copy(slot_in, slot, sems.at[3]),
    ]
    for copy in id_copies + copies:
        copy.start()
    for copy in id_copies:
        copy.wait()
    row = lax.broadcasted_iota(jnp.int32, (ID_ROWS, rows), 0)
    ids = jnp.where(row == 0, owner[...], jnp.where(row == 1, slot[...].reshape(1, rows), 0))
    ids = ids.astype(jnp.float32).astype(jnp.bfloat16)
    for out in (own, away):
        out[rows:, :rows] = ids
        out[rows:, rows:] = jnp.zeros((ID_ROWS, part - rows), jnp.bfloat16)
    for copy in copies:
        copy.wait()


def hop_body(rows, capacity, own, away, own_out, away_out, places):
    a = lax.axis_index("adapter")
    part = own.shape[1]
    ids = own[rows:, :rows]
    match = (ids.astype(jnp.float32) == (OWNERS - 1 - a).astype(jnp.float32)).astype(jnp.bfloat16)
    earlier = lax.broadcasted_iota(jnp.int32, (rows, rows), 0) < lax.broadcasted_iota(
        jnp.int32, (rows, rows), 1
    )
    rank = jnp.dot(match, earlier.astype(jnp.bfloat16), preferred_element_type=jnp.float32)
    place = lax.broadcasted_iota(jnp.int32, (capacity, rows), 0).astype(jnp.float32)
    taken = (place == rank[0:1]) & (match[0:1].astype(jnp.float32) > 0)
    chosen = taken.astype(jnp.bfloat16)
    places[...] = chosen
    kept = lax.dot_general(ids, chosen, NT, preferred_element_type=jnp.float32)
    for tokens, out in ((own, own_out), (away, away_out)):
        packed = jnp.dot(chosen, tokens[:rows, :], preferred_element_type=jnp.float32)
        out[:capacity, :] = packed.astype(jnp.bfloat16)
        out[capacity:, :] = jnp.zeros((ID_ROWS, part), jnp.bfloat16)
        out[capacity:, :capacity] = kept.astype(jnp.bfloat16)


def base_body(bit, rows, own, away, weights, _, keep, give, base):
    g = lax.axis_index("groups")
    part = own.shape[1]
    total = jnp.zeros(base.shape, jnp.float32)
    for tokens, half in ((own, g), (away, 1 - g)):
        part_weights = weights[pl.ds(pl.multiple_of(half * part, part), part), :]
        total = total + jnp.dot(tokens[:rows, :], part_weights, preferred_element_type=jnp.float32)
    base[...] = total
    halves(base, bit, keep, give)


def halves(base, bit, keep, give):
    m = lax.axis_index("mp")
    width = keep.shape[1]
    side = (m // bit) % 2
    keep[...] = base[:, pl.ds(pl.multiple_of(side * width, width), width)]
    give[...] = base[:, pl.ds(pl.multiple_of((1 - side) * width, width), width)]


def id_columns(rows_ref, start, count):
    eye = (
        lax.broadcasted_iota(jnp.int32, (ID_ROWS, ID_ROWS), 0)
        == lax.broadcasted_iota(jnp.int32, (ID_ROWS, ID_ROWS), 1)
    ).astype(jnp.bfloat16)
    ids = lax.dot_general(
        rows_ref[start : start + ID_ROWS, :count], eye, TN, preferred_element_type=jnp.float32
    )
    return ids[:, 0:1], ids[:, 1:2]


def adapters(rows, columns):
    column = lax.broadcasted_iota(jnp.int32, (rows, columns), 1)
    return (column // ADAPTER_RANK).astype(jnp.float32)


def fold(wide):
    folded = wide[:, :LANES]
    for k in range(1, wide.shape[1] // LANES):
        folded = folded + wide[:, k * LANES : (k + 1) * LANES]
    return folded


def low_rank(folded):
    turned = folded.T
    low = turned[:ADAPTER_RANK]
    for k in range(1, LANES // ADAPTER_RANK):
        low = low + turned[k * ADAPTER_RANK : (k + 1) * ADAPTER_RANK]
    return low


def stacked(wide, keys):
    return jnp.concatenate([wide[:, k : k + keys] for k in range(0, wide.shape[1], keys)], axis=0)


def early_body(bits, part, rows, *refs):
    groups = lax.axis_size("groups")
    a = lax.axis_index("adapter")
    token_refs, rest = refs[:groups], refs[groups:]
    blocks, (folded, mask, numbers, ups) = rest[: len(bits)], rest[len(bits) :]
    columns = blocks[0].shape[1]
    for n, block in enumerate(blocks):
        ups[n] = stacked(block[part:, :], ups.shape[2])
    adapter = adapters(rows, columns)
    for n, tokens in enumerate(token_refs):
        owner, slot = id_columns(tokens, rows, rows)
        if n == 0:
            numbers[...] = owner * (columns // ADAPTER_RANK) + slot
        right = adapter == slot
        picked = jnp.zeros((rows, columns), jnp.float32)
        for bit, block in zip(bits, blocks):
            wide = jnp.dot(tokens[:rows, :], block[:part, :], preferred_element_type=jnp.float32)
            picked = jnp.where(owner == (a ^ bit).astype(jnp.float32), wide, picked)
        folded[n] = fold(jnp.where(right, picked, 0.0))
        mask[n] = jnp.where(owner == (a ^ 2).astype(jnp.float32), right.astype(jnp.float32), 0.0)


def hop_mask_body(capacity, hop, _, out):
    _, slot = id_columns(hop, capacity, capacity)
    out[...] = (adapters(capacity, out.shape[1]) == slot).astype(jnp.float32)


def last_body(part, rows, capacity, *refs):
    groups = lax.axis_size("groups")
    a = lax.axis_index("adapter")
    token_refs, rest = refs[:groups], refs[groups:]
    hops, rest = rest[:groups], rest[groups:]
    hop_masks, rest = rest[:groups], rest[groups:]
    folded, mask, outside, inside, low, hop_low, away, last_up = rest
    columns = inside.shape[1]

    def finish(block):
        for n, tokens in enumerate(token_refs):
            wide = jnp.dot(tokens[:rows, :], block[:part, :], preferred_element_type=jnp.float32)
            kept = fold(jnp.where(mask[n] > 0, wide, 0.0))
            if n:
                away[:, :rows] = low_rank(folded[n] + kept)
            else:
                low[...] = low_rank(folded[n] + kept)

    middle = (a == 1) | (a == 2)

    @pl.when(middle)
    def _():
        finish(inside)
        last_up[...] = stacked(inside[part:, :], last_up.shape[1])
        for n, (hop, hop_mask) in enumerate(zip(hops, hop_masks)):
            wide = jnp.dot(hop[:capacity, :], inside[:part, :], preferred_element_type=jnp.float32)
            kept = fold(jnp.where(hop_mask[...] > 0, wide, 0.0))
            rest_rows = -capacity % LANES
            kept = jnp.concatenate([kept, jnp.zeros((rest_rows, LANES), jnp.float32)], axis=0)
            if n:
                away[:, rows:] = low_rank(kept)[:, :capacity]
            else:
                hop_low[...] = low_rank(kept)[:, :capacity]

    @pl.when(jnp.logical_not(middle))
    def _():
        finish(outside)
        last_up[...] = stacked(outside[part:, :], last_up.shape[1])
        hop_low[...] = jnp.zeros(hop_low.shape, jnp.float32)
        away[:, rows:] = jnp.zeros(hop_low.shape, jnp.float32)


def near_body(low, hop_low, near, low_out, hop_out):
    rows = low.shape[1]
    low_out[...] = low[...] + near[:, :rows]
    hop_out[...] = hop_low[...] + near[:, rows:]


def merge_body(bit, low, places, kept, got, hop, out, keep, give, base):
    back = hop[...]
    spread = jnp.zeros(low.shape, jnp.float32)
    for _ in range(3):
        piece = back.astype(jnp.bfloat16)
        back = back - piece.astype(jnp.float32)
        spread = spread + jnp.dot(piece, places[...], preferred_element_type=jnp.float32)
    out[...] = low[...] + spread
    base[...] = kept[...] + got[...]
    halves(base, bit, keep, give)


def finish_body(near, far, keep, got, numbers, ups, last_up, distant, out):
    a = lax.axis_index("adapter")
    rows = out.shape[0]
    columns = last_up.shape[0]
    column = lax.broadcasted_iota(jnp.int32, (ADAPTER_RANK, columns), 1)
    row = lax.broadcasted_iota(jnp.int32, (ADAPTER_RANK, columns), 0)
    repeat = (lax.rem(column, ADAPTER_RANK) == row).astype(jnp.bfloat16)
    shrunk = (near[...] + far[...]).astype(jnp.bfloat16)
    spread = lax.dot_general(shrunk, repeat, TN, preferred_element_type=jnp.float32)
    adapter = adapters(rows, columns)
    middle = (a == 1) | (a == 2)
    mirrored = jnp.where(middle, ups[1].astype(jnp.float32), distant[...].astype(jnp.float32))
    blocks = ((0, ups[0]), (1, ups[2]), (2, last_up[...]), (3, mirrored.astype(jnp.bfloat16)))
    updates = jnp.zeros(out.shape, jnp.float32)
    for bit, up in blocks:
        wanted = numbers[...] - ((a ^ bit) * (columns // ADAPTER_RANK)).astype(jnp.float32)
        chosen = jnp.where(adapter == wanted, spread, 0.0).astype(jnp.bfloat16)
        updates = updates + jnp.dot(chosen, up, preferred_element_type=jnp.float32)
    updates = updates.astype(jnp.bfloat16).astype(jnp.float32)
    base = keep[...] + got[...]
    out[...] = (base + ADAPTER_SCALE * updates).astype(jnp.bfloat16)


def gather(
    tokens,
    base_key_weight,
    stacked_down_weight,
    stacked_up_weight,
    request_adapter_owner,
    request_adapter_slot,
):
    rows, features = tokens.shape
    groups, owners, shares = (lax.axis_size(name) for name in AXES)
    columns = stacked_down_weight.shape[1]
    keys = stacked_up_weight.shape[1]
    part = features // groups
    half = columns // keys
    capacity = -(-row_limit(rows) // ID_ROWS) * ID_ROWS

    def narrow(*dims):
        return jax.ShapeDtypeStruct(dims, jnp.bfloat16)

    def wide(*dims):
        return jax.ShapeDtypeStruct(dims, jnp.float32)

    own = kernel(
        pack_body,
        narrow(part + columns // half, columns),
        (in_hbm(stacked_down_weight), in_hbm(stacked_up_weight)),
        0,
        (pl.ANY, pl.ANY),
        [pltpu.SemaphoreType.DMA((1 + half,))],
    )
    mirror = exchange(own, 0, 0, MIDDLE)
    beside = exchange(own, 0, 0, BESIDE)

    tok_own, tok_away = kernel(
        split_body,
        [narrow(rows + ID_ROWS, part)] * groups,
        (
            in_hbm(tokens),
            in_hbm(request_adapter_owner.reshape(1, rows)),
            in_hbm(request_adapter_slot),
            own,
        ),
        0,
        (pl.ANY, pl.ANY, pl.ANY, pl.ANY),
        [
            pltpu.VMEM((1, rows), jnp.int32),
            pltpu.VMEM((rows,), jnp.int32),
            pltpu.SemaphoreType.DMA((4,)),
        ],
    )
    token_parts = [tok_own, exchange(tok_away, 1, 0, SAME)]
    hop_own, hop_away, places = kernel(
        functools.partial(hop_body, rows, capacity),
        [narrow(capacity + ID_ROWS, part)] * groups
        + [narrow(capacity, rows)],
        (tok_own, tok_away),
        2 * rows * features * capacity,
    )

    inside = exchange(beside, 0, 0, MIDDLE)
    outside = exchange(mirror, 0, 0, OUTWARD)
    hops = [
        exchange(after(hop_own, beside), 0, 0, INWARD),
        exchange(hop_away, 1, 0, INWARD),
    ]

    folded, mask, numbers, ups = kernel(
        functools.partial(early_body, (0, 3, 1), part, rows),
        [wide(groups, rows, LANES), wide(groups, rows, columns), wide(rows, 1), narrow(3, columns, keys)],
        (*token_parts, own, mirror, beside),
        light=True,
    )
    hop_masks, latest = [], folded
    for hop, urgency in zip(hops, HOP_URGENCY):
        latest = kernel(
            functools.partial(hop_mask_body, capacity),
            wide(capacity, columns),
            (hop, latest),
            urgency,
            (None, pl.ANY),
        )
        hop_masks.append(latest)
    bits = (2, 1)
    keep, give = kernel(
        functools.partial(base_body, bits[0], rows),
        [wide(rows, shares * keys // 2)] * 2,
        (tok_own, tok_away, base_key_weight, places),
        2 * rows * features * shares * keys,
        (None, None, None, pl.ANY),
        [pltpu.VMEM((rows, shares * keys), jnp.float32)],
    )
    got = exchange(after(give, folded), 0, bits[0], SAME)

    low, hop_low, away, last_up = kernel(
        functools.partial(last_body, part, rows, capacity),
        [
            wide(ADAPTER_RANK, rows),
            wide(ADAPTER_RANK, capacity),
            wide(ADAPTER_RANK, rows + capacity),
            narrow(columns, keys),
        ],
        (*token_parts, *hops, *hop_masks, folded, mask, outside, inside),
        2 * groups * (rows + capacity) * part * columns,
    )

    near = exchange(away, 1, 0, SAME)
    distant = exchange(after(stacked_up_weight, folded), 0, 0, ENDS)
    low, hop_low = kernel(
        near_body, [wide(ADAPTER_RANK, rows), wide(ADAPTER_RANK, capacity)], (low, hop_low, near)
    )
    back = exchange(hop_low, 0, 0, OUTWARD)
    low, keep, give = kernel(
        functools.partial(merge_body, bits[1]),
        [wide(ADAPTER_RANK, rows)] + [wide(rows, bits[1] * keys)] * 2,
        (after(low, distant), places, keep, got, back),
        scratch=[pltpu.VMEM((rows, bits[0] * keys), jnp.float32)],
    )
    got = exchange(give, 0, bits[1], SAME)
    low = low + exchange(low, 0, bits[0], SAME)
    low_far = exchange(low, 0, bits[1], SAME)
    return kernel(
        finish_body, narrow(rows, keys), (low, low_far, keep, got, numbers, ups, last_up, distant)
    )


def row_limit(rows):
    return max(2, 3 * rows // (2 * lax.axis_size("adapter")))


def local(*args):
    rows, columns = args[0].shape[0], args[2].shape[1]
    groups, owners, shares = (lax.axis_size(name) for name in AXES)
    fits = owners == OWNERS and groups == 2 and shares == 4
    travels = fits and columns <= groups * row_limit(rows)
    return (gather if travels else dispatch)(*args)


def solution(mesh):
    placed = (
        P(("groups", "adapter"), "mp"),
        P("mp", None),
        P("mp", "adapter"),
        P("adapter", "mp"),
        P(("groups", "adapter"), None),
        P(("groups", "adapter")),
    )
    return jax.shard_map(
        local, mesh=mesh, in_specs=placed, out_specs=P(("groups", "adapter"), "mp"), check_vma=False
    )
```

```python
import functools

import jax
import jax.numpy as jnp
from jax import lax
from jax.experimental import pallas as pl
from jax.experimental.pallas import tpu as pltpu
from jax.sharding import PartitionSpec as P

ADAPTER_RANK = 16


ADAPTER_SCALE = 2.0


def dispatch(
    tokens,
    base_key_weight,
    stacked_down_weight,
    stacked_up_weight,
    request_adapter_owner,
    request_adapter_slot,
):
    rows_here = tokens.shape[0]
    feature_share = tokens.shape[1]
    owner_count = lax.axis_size("adapter")
    capacity = max(2, 3 * rows_here // (2 * owner_count))
    local_adapters = stacked_down_weight.shape[1] // ADAPTER_RANK
    key_output_share = stacked_up_weight.shape[1]
    owners = request_adapter_owner.reshape(-1)
    onehot = (owners[:, None] == jnp.arange(owner_count, dtype=jnp.int32)[None, :]).astype(
        jnp.int32
    )
    before = jnp.sum((jnp.cumsum(onehot, axis=0) - onehot) * onehot, axis=1)
    places = owners * capacity + before
    send_rows = (
        jnp.zeros((owner_count * capacity, feature_share), jnp.bfloat16).at[places].set(tokens)
    )
    send_rows = send_rows.reshape(owner_count, capacity, feature_share)
    send_slots = (
        jnp.full((owner_count * capacity,), -1, jnp.int32).at[places].set(request_adapter_slot)
    )
    send_slots = send_slots.reshape(owner_count, capacity)
    input_rows = lax.all_to_all(send_rows, "adapter", split_axis=0, concat_axis=0, tiled=True)
    slots_in = lax.all_to_all(send_slots, "adapter", split_axis=0, concat_axis=0, tiled=True)
    key_projection_output = jnp.einsum(
        "rzq,qt->rzt", input_rows, stacked_down_weight, preferred_element_type=jnp.float32
    )
    key_projection_output = key_projection_output.reshape(
        input_rows.shape[0], input_rows.shape[1], local_adapters, ADAPTER_RANK
    )
    chosen = slots_in[:, :, None] == jnp.arange(local_adapters, dtype=jnp.int32)[None, None, :]
    partial_low = jnp.sum(jnp.where(chosen[:, :, :, None], key_projection_output, 0.0), axis=2)
    shrunk = lax.psum(partial_low, "mp")
    shrunk_bf = shrunk.astype(jnp.bfloat16)
    returned = lax.all_to_all(shrunk_bf, "adapter", split_axis=0, concat_axis=0, tiled=True)
    low_rows = returned.reshape(owner_count * capacity, ADAPTER_RANK)[places]
    gathered_up_weight = lax.all_gather(stacked_up_weight, "adapter", axis=0, tiled=True)
    adapter_ids = owners * local_adapters + request_adapter_slot
    up_taken = gathered_up_weight.reshape(-1, ADAPTER_RANK, key_output_share)[adapter_ids]
    adapter_updates = jnp.einsum(
        "tr,trk->tk", low_rows, up_taken, preferred_element_type=jnp.float32
    ).astype(jnp.bfloat16)
    base_output_share = lax.psum_scatter(
        lax.dot_general(
            base_key_weight, tokens, (((0,), (1,)), ((), ())), preferred_element_type=jnp.float32
        ),
        "mp",
        scatter_dimension=0,
        tiled=True,
    )
    return (base_output_share.T + ADAPTER_SCALE * adapter_updates.astype(jnp.float32)).astype(
        jnp.bfloat16
    )


AXES = ("groups", "adapter", "mp")
ID_ROWS = 16
HOP_URGENCY = (36 * 10**8, 0)
OWNERS = 4
LANES = 128
NT = (((1,), (1,)), ((), ()))
TN = (((0,), (0,)), ((), ()))


def exchange(x, group_bits, share_bits, owners):
    groups, count, shares = (lax.axis_size(name) for name in AXES)

    def number(g, a, m):
        return (g * count + a) * shares + m

    pairs = [
        (number(g, a, m), number(g ^ group_bits, b, m ^ share_bits))
        for g in range(groups)
        for a, b in owners
        for m in range(shares)
    ]
    return lax.ppermute(x, AXES, pairs)


SAME = tuple((a, a) for a in range(OWNERS))
BESIDE = ((0, 1), (1, 0), (2, 3), (3, 2))
MIDDLE = ((0, 0), (1, 2), (2, 1), (3, 3))
ENDS = ((0, 3), (1, 1), (2, 2), (3, 0))
OUTWARD = ((1, 0), (2, 3))
INWARD = ((0, 1), (3, 2))


def after(x, *others):
    return lax.optimization_barrier((x, *others))[0]


def in_hbm(x):
    return pltpu.with_memory_space_constraint(x, pltpu.HBM)


def kernel(body, outs, operands, flops=0, spaces=None, scratch=(), light=False):
    inner = pl.BlockSpec(memory_space=pltpu.VMEM)
    specs = [inner if s is None else pl.BlockSpec(memory_space=s) for s in spaces or ()]
    touched = sum(x.size * x.dtype.itemsize for x in jax.tree.leaves((operands, outs)))
    return pl.pallas_call(
        body,
        out_shape=outs,
        in_specs=specs or [inner] * len(operands),
        out_specs=jax.tree.map(lambda _: inner, outs),
        scratch_shapes=scratch,
        compiler_params=pltpu.CompilerParams(vmem_limit_bytes=16 * 1024 * 1024),
        cost_estimate=pl.CostEstimate(
            flops=flops, bytes_accessed=0 if light else touched, transcendentals=0
        ),
    )(*operands)


def pack_body(down, up, out, sems):
    g = lax.axis_index("groups")
    columns, keys = down.shape[1], up.shape[1]
    count = columns // keys
    size = up.shape[0] // count
    part = out.shape[0] - size
    mine = down.at[pl.ds(pl.multiple_of(g * part, part), part), :]
    copies = [pltpu.make_async_copy(mine, out.at[pl.ds(0, part), :], sems.at[count])]
    for k in range(count):
        copies.append(
            pltpu.make_async_copy(
                up.at[pl.ds(k * size, size), :],
                out.at[pl.ds(part, size), pl.ds(k * keys, keys)],
                sems.at[k],
            )
        )
    for copy in copies:
        copy.start()
    for copy in copies:
        copy.wait()


def split_body(tokens, owner_in, slot_in, _, own, away, owner, slot, sems):
    g = lax.axis_index("groups")
    rows, part = tokens.shape[0], own.shape[1]
    copies = []
    for n, (out, half) in enumerate(((own, g), (away, 1 - g))):
        taken = tokens.at[:, pl.ds(pl.multiple_of(half * part, part), part)]
        copies.append(pltpu.make_async_copy(taken, out.at[pl.ds(0, rows), :], sems.at[n]))
    id_copies = [
        pltpu.make_async_copy(owner_in, owner, sems.at[2]),
        pltpu.make_async_copy(slot_in, slot, sems.at[3]),
    ]
    for copy in id_copies + copies:
        copy.start()
    for copy in id_copies:
        copy.wait()
    row = lax.broadcasted_iota(jnp.int32, (ID_ROWS, rows), 0)
    ids = jnp.where(row == 0, owner[...], jnp.where(row == 1, slot[...].reshape(1, rows), 0))
    ids = ids.astype(jnp.float32).astype(jnp.bfloat16)
    for out in (own, away):
        out[rows:, :rows] = ids
        out[rows:, rows:] = jnp.zeros((ID_ROWS, part - rows), jnp.bfloat16)
    for copy in copies:
        copy.wait()


def hop_body(rows, capacity, own, away, own_out, away_out, places):
    a = lax.axis_index("adapter")
    part = own.shape[1]
    ids = own[rows:, :rows]
    match = (ids.astype(jnp.float32) == (OWNERS - 1 - a).astype(jnp.float32)).astype(jnp.bfloat16)
    earlier = lax.broadcasted_iota(jnp.int32, (rows, rows), 0) < lax.broadcasted_iota(
        jnp.int32, (rows, rows), 1
    )
    rank = jnp.dot(match, earlier.astype(jnp.bfloat16), preferred_element_type=jnp.float32)
    place = lax.broadcasted_iota(jnp.int32, (capacity, rows), 0).astype(jnp.float32)
    taken = (place == rank[0:1]) & (match[0:1].astype(jnp.float32) > 0)
    chosen = taken.astype(jnp.bfloat16)
    places[...] = chosen
    kept = lax.dot_general(ids, chosen, NT, preferred_element_type=jnp.float32)
    for tokens, out in ((own, own_out), (away, away_out)):
        packed = jnp.dot(chosen, tokens[:rows, :], preferred_element_type=jnp.float32)
        out[:capacity, :] = packed.astype(jnp.bfloat16)
        out[capacity:, :] = jnp.zeros((ID_ROWS, part), jnp.bfloat16)
        out[capacity:, :capacity] = kept.astype(jnp.bfloat16)


def base_body(bit, rows, own, away, weights, _, keep, give, base):
    g = lax.axis_index("groups")
    part = own.shape[1]
    total = jnp.zeros(base.shape, jnp.float32)
    for tokens, half in ((own, g), (away, 1 - g)):
        part_weights = weights[pl.ds(pl.multiple_of(half * part, part), part), :]
        total = total + jnp.dot(tokens[:rows, :], part_weights, preferred_element_type=jnp.float32)
    base[...] = total
    halves(base, bit, keep, give)


def halves(base, bit, keep, give):
    m = lax.axis_index("mp")
    width = keep.shape[1]
    side = (m // bit) % 2
    keep[...] = base[:, pl.ds(pl.multiple_of(side * width, width), width)]
    give[...] = base[:, pl.ds(pl.multiple_of((1 - side) * width, width), width)]


def id_columns(rows_ref, start, count):
    eye = (
        lax.broadcasted_iota(jnp.int32, (ID_ROWS, ID_ROWS), 0)
        == lax.broadcasted_iota(jnp.int32, (ID_ROWS, ID_ROWS), 1)
    ).astype(jnp.bfloat16)
    ids = lax.dot_general(
        rows_ref[start : start + ID_ROWS, :count], eye, TN, preferred_element_type=jnp.float32
    )
    return ids[:, 0:1], ids[:, 1:2]


def adapters(rows, columns):
    column = lax.broadcasted_iota(jnp.int32, (rows, columns), 1)
    return (column // ADAPTER_RANK).astype(jnp.float32)


def fold(wide):
    folded = wide[:, :LANES]
    for k in range(1, wide.shape[1] // LANES):
        folded = folded + wide[:, k * LANES : (k + 1) * LANES]
    return folded


def low_rank(folded):
    turned = folded.T
    low = turned[:ADAPTER_RANK]
    for k in range(1, LANES // ADAPTER_RANK):
        low = low + turned[k * ADAPTER_RANK : (k + 1) * ADAPTER_RANK]
    return low


def stacked(wide, keys):
    return jnp.concatenate([wide[:, k : k + keys] for k in range(0, wide.shape[1], keys)], axis=0)


def early_body(bits, part, rows, *refs):
    groups = lax.axis_size("groups")
    a = lax.axis_index("adapter")
    token_refs, rest = refs[:groups], refs[groups:]
    blocks, (folded, mask, numbers, ups) = rest[: len(bits)], rest[len(bits) :]
    columns = blocks[0].shape[1]
    for n, block in enumerate(blocks):
        ups[n] = stacked(block[part:, :], ups.shape[2])
    adapter = adapters(rows, columns)
    for n, tokens in enumerate(token_refs):
        owner, slot = id_columns(tokens, rows, rows)
        if n == 0:
            numbers[...] = owner * (columns // ADAPTER_RANK) + slot
        right = adapter == slot
        picked = jnp.zeros((rows, columns), jnp.float32)
        for bit, block in zip(bits, blocks):
            wide = jnp.dot(tokens[:rows, :], block[:part, :], preferred_element_type=jnp.float32)
            number = jnp.where((bit != 3) | (a == 1) | (a == 2), a ^ bit, -1)
            picked = jnp.where(owner == number.astype(jnp.float32), wide, picked)
        folded[n] = fold(jnp.where(right, picked, 0.0))
        mask[n] = jnp.where(owner == (a ^ 2).astype(jnp.float32), right.astype(jnp.float32), 0.0)


def hop_mask_body(capacity, hop, _, out):
    _, slot = id_columns(hop, capacity, capacity)
    out[...] = (adapters(capacity, out.shape[1]) == slot).astype(jnp.float32)


def last_body(part, rows, capacity, *refs):
    groups = lax.axis_size("groups")
    a = lax.axis_index("adapter")
    token_refs, rest = refs[:groups], refs[groups:]
    hops, rest = rest[:groups], rest[groups:]
    hop_masks, rest = rest[:groups], rest[groups:]
    folded, mask, outside, inside, low, hop_low, away, last_up = rest
    columns = inside.shape[1]

    def finish(block):
        for n, tokens in enumerate(token_refs):
            wide = jnp.dot(tokens[:rows, :], block[:part, :], preferred_element_type=jnp.float32)
            kept = fold(jnp.where(mask[n] > 0, wide, 0.0))
            if n:
                away[:, :rows] = low_rank(folded[n] + kept)
            else:
                low[...] = low_rank(folded[n] + kept)

    middle = (a == 1) | (a == 2)

    @pl.when(middle)
    def _():
        finish(inside)
        last_up[...] = stacked(inside[part:, :], last_up.shape[1])
        for n, (hop, hop_mask) in enumerate(zip(hops, hop_masks)):
            wide = jnp.dot(hop[:capacity, :], inside[:part, :], preferred_element_type=jnp.float32)
            kept = fold(jnp.where(hop_mask[...] > 0, wide, 0.0))
            rest_rows = -capacity % LANES
            kept = jnp.concatenate([kept, jnp.zeros((rest_rows, LANES), jnp.float32)], axis=0)
            if n:
                away[:, rows:] = low_rank(kept)[:, :capacity]
            else:
                hop_low[...] = low_rank(kept)[:, :capacity]

    @pl.when(jnp.logical_not(middle))
    def _():
        finish(outside)
        last_up[...] = stacked(outside[part:, :], last_up.shape[1])
        hop_low[...] = jnp.zeros(hop_low.shape, jnp.float32)
        away[:, rows:] = jnp.zeros(hop_low.shape, jnp.float32)


def near_body(low, hop_low, near, low_out, hop_out):
    rows = low.shape[1]
    low_out[...] = low[...] + near[:, :rows]
    hop_out[...] = hop_low[...] + near[:, rows:]


def merge_body(bit, low, places, kept, got, hop, out, keep, give, base):
    back = hop[...]
    spread = jnp.zeros(low.shape, jnp.float32)
    for _ in range(3):
        piece = back.astype(jnp.bfloat16)
        back = back - piece.astype(jnp.float32)
        spread = spread + jnp.dot(piece, places[...], preferred_element_type=jnp.float32)
    out[...] = low[...] + spread
    base[...] = kept[...] + got[...]
    halves(base, bit, keep, give)


def finish_body(near, far, keep, got, numbers, ups, last_up, distant, out):
    a = lax.axis_index("adapter")
    rows = out.shape[0]
    columns = last_up.shape[0]
    column = lax.broadcasted_iota(jnp.int32, (ADAPTER_RANK, columns), 1)
    row = lax.broadcasted_iota(jnp.int32, (ADAPTER_RANK, columns), 0)
    repeat = (lax.rem(column, ADAPTER_RANK) == row).astype(jnp.bfloat16)
    shrunk = (near[...] + far[...]).astype(jnp.bfloat16)
    spread = lax.dot_general(shrunk, repeat, TN, preferred_element_type=jnp.float32)
    adapter = adapters(rows, columns)
    middle = (a == 1) | (a == 2)
    mirrored = jnp.where(middle, ups[1].astype(jnp.float32), distant[...].astype(jnp.float32))
    blocks = ((0, ups[0]), (1, ups[2]), (2, last_up[...]), (3, mirrored.astype(jnp.bfloat16)))
    updates = jnp.zeros(out.shape, jnp.float32)
    for bit, up in blocks:
        wanted = numbers[...] - ((a ^ bit) * (columns // ADAPTER_RANK)).astype(jnp.float32)
        chosen = jnp.where(adapter == wanted, spread, 0.0).astype(jnp.bfloat16)
        updates = updates + jnp.dot(chosen, up, preferred_element_type=jnp.float32)
    updates = updates.astype(jnp.bfloat16).astype(jnp.float32)
    base = keep[...] + got[...]
    out[...] = (base + ADAPTER_SCALE * updates).astype(jnp.bfloat16)


def gather(
    tokens,
    base_key_weight,
    stacked_down_weight,
    stacked_up_weight,
    request_adapter_owner,
    request_adapter_slot,
):
    rows, features = tokens.shape
    groups, owners, shares = (lax.axis_size(name) for name in AXES)
    columns = stacked_down_weight.shape[1]
    keys = stacked_up_weight.shape[1]
    part = features // groups
    half = columns // keys
    capacity = -(-row_limit(rows) // ID_ROWS) * ID_ROWS

    def narrow(*dims):
        return jax.ShapeDtypeStruct(dims, jnp.bfloat16)

    def wide(*dims):
        return jax.ShapeDtypeStruct(dims, jnp.float32)

    own = kernel(
        pack_body,
        narrow(part + columns // half, columns),
        (in_hbm(stacked_down_weight), in_hbm(stacked_up_weight)),
        0,
        (pl.ANY, pl.ANY),
        [pltpu.SemaphoreType.DMA((1 + half,))],
    )
    beside = exchange(own, 0, 0, BESIDE)

    tok_own, tok_away = kernel(
        split_body,
        [narrow(rows + ID_ROWS, part)] * groups,
        (
            in_hbm(tokens),
            in_hbm(request_adapter_owner.reshape(1, rows)),
            in_hbm(request_adapter_slot),
            own,
        ),
        0,
        (pl.ANY, pl.ANY, pl.ANY, pl.ANY),
        [
            pltpu.VMEM((1, rows), jnp.int32),
            pltpu.VMEM((rows,), jnp.int32),
            pltpu.SemaphoreType.DMA((4,)),
        ],
    )
    token_parts = [tok_own, exchange(tok_away, 1, 0, SAME)]
    mirror = exchange(after(own, tok_own), 0, 0, MIDDLE)
    hop_own, hop_away, places = kernel(
        functools.partial(hop_body, rows, capacity),
        [narrow(capacity + ID_ROWS, part)] * groups
        + [narrow(capacity, rows)],
        (tok_own, tok_away),
        2 * rows * features * capacity,
    )

    inside = exchange(after(beside, places), 0, 0, MIDDLE)
    outside = exchange(mirror, 0, 0, OUTWARD)
    hops = [
        exchange(after(hop_own, beside), 0, 0, INWARD),
        exchange(hop_away, 1, 0, INWARD),
    ]

    folded, mask, numbers, ups = kernel(
        functools.partial(early_body, (0, 3, 1), part, rows),
        [wide(groups, rows, LANES), wide(groups, rows, columns), wide(rows, 1), narrow(3, columns, keys)],
        (*token_parts, own, mirror, beside),
        light=True,
    )
    hop_masks, latest = [], folded
    for hop, urgency in zip(hops, HOP_URGENCY):
        latest = kernel(
            functools.partial(hop_mask_body, capacity),
            wide(capacity, columns),
            (hop, latest),
            urgency,
            (None, pl.ANY),
        )
        hop_masks.append(latest)
    bits = (2, 1)
    keep, give = kernel(
        functools.partial(base_body, bits[0], rows),
        [wide(rows, shares * keys // 2)] * 2,
        (tok_own, tok_away, base_key_weight, places),
        2 * rows * features * shares * keys,
        (None, None, None, pl.ANY),
        [pltpu.VMEM((rows, shares * keys), jnp.float32)],
    )
    got = exchange(after(give, folded), 0, bits[0], SAME)

    low, hop_low, away, last_up = kernel(
        functools.partial(last_body, part, rows, capacity),
        [
            wide(ADAPTER_RANK, rows),
            wide(ADAPTER_RANK, capacity),
            wide(ADAPTER_RANK, rows + capacity),
            narrow(columns, keys),
        ],
        (*token_parts, *hops, *hop_masks, folded, mask, outside, inside),
        2 * groups * (rows + capacity) * part * columns,
    )

    near = exchange(away, 1, 0, SAME)
    distant = exchange(after(stacked_up_weight, folded), 0, 0, ENDS)
    low, hop_low = kernel(
        near_body, [wide(ADAPTER_RANK, rows), wide(ADAPTER_RANK, capacity)], (low, hop_low, near)
    )
    back = exchange(hop_low, 0, 0, BESIDE)
    low, keep, give = kernel(
        functools.partial(merge_body, bits[1]),
        [wide(ADAPTER_RANK, rows)] + [wide(rows, bits[1] * keys)] * 2,
        (after(low, distant), places, keep, got, back),
        scratch=[pltpu.VMEM((rows, bits[0] * keys), jnp.float32)],
    )
    got = exchange(give, 0, bits[1], SAME)
    low = low + exchange(low, 0, bits[0], SAME)
    low_far = exchange(low, 0, bits[1], SAME)
    return kernel(
        finish_body, narrow(rows, keys), (low, low_far, keep, got, numbers, ups, last_up, distant)
    )


def row_limit(rows):
    return max(2, 3 * rows // (2 * lax.axis_size("adapter")))


def local(*args):
    rows, columns = args[0].shape[0], args[2].shape[1]
    groups, owners, shares = (lax.axis_size(name) for name in AXES)
    fits = owners == OWNERS and groups == 2 and shares == 4
    travels = fits and columns <= groups * row_limit(rows)
    return (gather if travels else dispatch)(*args)


def solution(mesh):
    placed = (
        P(("groups", "adapter"), "mp"),
        P("mp", None),
        P("mp", "adapter"),
        P("adapter", "mp"),
        P(("groups", "adapter"), None),
        P(("groups", "adapter")),
    )
    return jax.shard_map(
        local, mesh=mesh, in_specs=placed, out_specs=P(("groups", "adapter"), "mp"), check_vma=False
    )
```

```python
import functools

import jax
import jax.numpy as jnp
from jax import lax
from jax.experimental import pallas as pl
from jax.experimental.pallas import tpu as pltpu
from jax.sharding import PartitionSpec as P

ADAPTER_RANK = 16


ADAPTER_SCALE = 2.0


def dispatch(
    tokens,
    base_key_weight,
    stacked_down_weight,
    stacked_up_weight,
    request_adapter_owner,
    request_adapter_slot,
):
    rows_here = tokens.shape[0]
    feature_share = tokens.shape[1]
    owner_count = lax.axis_size("adapter")
    capacity = max(2, 3 * rows_here // (2 * owner_count))
    local_adapters = stacked_down_weight.shape[1] // ADAPTER_RANK
    key_output_share = stacked_up_weight.shape[1]
    owners = request_adapter_owner.reshape(-1)
    onehot = (owners[:, None] == jnp.arange(owner_count, dtype=jnp.int32)[None, :]).astype(
        jnp.int32
    )
    before = jnp.sum((jnp.cumsum(onehot, axis=0) - onehot) * onehot, axis=1)
    places = owners * capacity + before
    send_rows = (
        jnp.zeros((owner_count * capacity, feature_share), jnp.bfloat16).at[places].set(tokens)
    )
    send_rows = send_rows.reshape(owner_count, capacity, feature_share)
    send_slots = (
        jnp.full((owner_count * capacity,), -1, jnp.int32).at[places].set(request_adapter_slot)
    )
    send_slots = send_slots.reshape(owner_count, capacity)
    input_rows = lax.all_to_all(send_rows, "adapter", split_axis=0, concat_axis=0, tiled=True)
    slots_in = lax.all_to_all(send_slots, "adapter", split_axis=0, concat_axis=0, tiled=True)
    key_projection_output = jnp.einsum(
        "rzq,qt->rzt", input_rows, stacked_down_weight, preferred_element_type=jnp.float32
    )
    key_projection_output = key_projection_output.reshape(
        input_rows.shape[0], input_rows.shape[1], local_adapters, ADAPTER_RANK
    )
    chosen = slots_in[:, :, None] == jnp.arange(local_adapters, dtype=jnp.int32)[None, None, :]
    partial_low = jnp.sum(jnp.where(chosen[:, :, :, None], key_projection_output, 0.0), axis=2)
    shrunk = lax.psum(partial_low, "mp")
    shrunk_bf = shrunk.astype(jnp.bfloat16)
    returned = lax.all_to_all(shrunk_bf, "adapter", split_axis=0, concat_axis=0, tiled=True)
    low_rows = returned.reshape(owner_count * capacity, ADAPTER_RANK)[places]
    gathered_up_weight = lax.all_gather(stacked_up_weight, "adapter", axis=0, tiled=True)
    adapter_ids = owners * local_adapters + request_adapter_slot
    up_taken = gathered_up_weight.reshape(-1, ADAPTER_RANK, key_output_share)[adapter_ids]
    adapter_updates = jnp.einsum(
        "tr,trk->tk", low_rows, up_taken, preferred_element_type=jnp.float32
    ).astype(jnp.bfloat16)
    base_output_share = lax.psum_scatter(
        lax.dot_general(
            base_key_weight, tokens, (((0,), (1,)), ((), ())), preferred_element_type=jnp.float32
        ),
        "mp",
        scatter_dimension=0,
        tiled=True,
    )
    return (base_output_share.T + ADAPTER_SCALE * adapter_updates.astype(jnp.float32)).astype(
        jnp.bfloat16
    )


AXES = ("groups", "adapter", "mp")
ID_ROWS = 16
HOP_URGENCY = (30 * 10**8, 0)
OWNERS = 4
LANES = 128
NT = (((1,), (1,)), ((), ()))
TN = (((0,), (0,)), ((), ()))


def exchange(x, group_bits, share_bits, owners):
    groups, count, shares = (lax.axis_size(name) for name in AXES)

    def number(g, a, m):
        return (g * count + a) * shares + m

    pairs = [
        (number(g, a, m), number(g ^ group_bits, b, m ^ share_bits))
        for g in range(groups)
        for a, b in owners
        for m in range(shares)
    ]
    return lax.ppermute(x, AXES, pairs)


SAME = tuple((a, a) for a in range(OWNERS))
BESIDE = ((0, 1), (1, 0), (2, 3), (3, 2))
MIDDLE = ((0, 0), (1, 2), (2, 1), (3, 3))
ENDS = ((0, 3), (1, 1), (2, 2), (3, 0))
OUTWARD = ((1, 0), (2, 3))
INWARD = ((0, 1), (3, 2))


def after(x, *others):
    return lax.optimization_barrier((x, *others))[0]


def in_hbm(x):
    return pltpu.with_memory_space_constraint(x, pltpu.HBM)


def kernel(body, outs, operands, flops=0, spaces=None, scratch=(), light=False):
    inner = pl.BlockSpec(memory_space=pltpu.VMEM)
    specs = [inner if s is None else pl.BlockSpec(memory_space=s) for s in spaces or ()]
    touched = sum(x.size * x.dtype.itemsize for x in jax.tree.leaves((operands, outs)))
    return pl.pallas_call(
        body,
        out_shape=outs,
        in_specs=specs or [inner] * len(operands),
        out_specs=jax.tree.map(lambda _: inner, outs),
        scratch_shapes=scratch,
        compiler_params=pltpu.CompilerParams(vmem_limit_bytes=16 * 1024 * 1024),
        cost_estimate=pl.CostEstimate(
            flops=flops, bytes_accessed=0 if light else touched, transcendentals=0
        ),
    )(*operands)


def pack_body(down, up, out, sems):
    g = lax.axis_index("groups")
    columns, keys = down.shape[1], up.shape[1]
    count = columns // keys
    size = up.shape[0] // count
    part = out.shape[0] - size
    mine = down.at[pl.ds(pl.multiple_of(g * part, part), part), :]
    copies = [pltpu.make_async_copy(mine, out.at[pl.ds(0, part), :], sems.at[count])]
    for k in range(count):
        copies.append(
            pltpu.make_async_copy(
                up.at[pl.ds(k * size, size), :],
                out.at[pl.ds(part, size), pl.ds(k * keys, keys)],
                sems.at[k],
            )
        )
    for copy in copies:
        copy.start()
    for copy in copies:
        copy.wait()


def split_body(tokens, owner_in, slot_in, _, own, away, owner, slot, sems):
    g = lax.axis_index("groups")
    rows, part = tokens.shape[0], own.shape[1]
    copies = []
    for n, (out, half) in enumerate(((own, g), (away, 1 - g))):
        taken = tokens.at[:, pl.ds(pl.multiple_of(half * part, part), part)]
        copies.append(pltpu.make_async_copy(taken, out.at[pl.ds(0, rows), :], sems.at[n]))
    id_copies = [
        pltpu.make_async_copy(owner_in, owner, sems.at[2]),
        pltpu.make_async_copy(slot_in, slot, sems.at[3]),
    ]
    for copy in id_copies + copies:
        copy.start()
    for copy in id_copies:
        copy.wait()
    row = lax.broadcasted_iota(jnp.int32, (ID_ROWS, rows), 0)
    ids = jnp.where(row == 0, owner[...], jnp.where(row == 1, slot[...].reshape(1, rows), 0))
    ids = ids.astype(jnp.float32).astype(jnp.bfloat16)
    for out in (own, away):
        out[rows:, :rows] = ids
        out[rows:, rows:] = jnp.zeros((ID_ROWS, part - rows), jnp.bfloat16)
    for copy in copies:
        copy.wait()


def hop_body(rows, capacity, own, away, own_out, away_out, places):
    a = lax.axis_index("adapter")
    part = own.shape[1]
    ids = own[rows:, :rows]
    match = (ids.astype(jnp.float32) == (OWNERS - 1 - a).astype(jnp.float32)).astype(jnp.bfloat16)
    earlier = lax.broadcasted_iota(jnp.int32, (rows, rows), 0) < lax.broadcasted_iota(
        jnp.int32, (rows, rows), 1
    )
    rank = jnp.dot(match, earlier.astype(jnp.bfloat16), preferred_element_type=jnp.float32)
    place = lax.broadcasted_iota(jnp.int32, (capacity, rows), 0).astype(jnp.float32)
    taken = (place == rank[0:1]) & (match[0:1].astype(jnp.float32) > 0)
    chosen = taken.astype(jnp.bfloat16)
    places[...] = chosen
    kept = lax.dot_general(ids, chosen, NT, preferred_element_type=jnp.float32)
    for tokens, out in ((own, own_out), (away, away_out)):
        packed = jnp.dot(chosen, tokens[:rows, :], preferred_element_type=jnp.float32)
        out[:capacity, :] = packed.astype(jnp.bfloat16)
        out[capacity:, :] = jnp.zeros((ID_ROWS, part), jnp.bfloat16)
        out[capacity:, :capacity] = kept.astype(jnp.bfloat16)


def base_body(bit, rows, own, away, weights, _, keep, give, base):
    g = lax.axis_index("groups")
    part = own.shape[1]
    total = jnp.zeros(base.shape, jnp.float32)
    for tokens, half in ((own, g), (away, 1 - g)):
        part_weights = weights[pl.ds(pl.multiple_of(half * part, part), part), :]
        total = total + jnp.dot(tokens[:rows, :], part_weights, preferred_element_type=jnp.float32)
    base[...] = total
    halves(base, bit, keep, give)


def halves(base, bit, keep, give):
    m = lax.axis_index("mp")
    width = keep.shape[1]
    side = (m // bit) % 2
    keep[...] = base[:, pl.ds(pl.multiple_of(side * width, width), width)]
    give[...] = base[:, pl.ds(pl.multiple_of((1 - side) * width, width), width)]


def id_columns(rows_ref, start, count):
    eye = (
        lax.broadcasted_iota(jnp.int32, (ID_ROWS, ID_ROWS), 0)
        == lax.broadcasted_iota(jnp.int32, (ID_ROWS, ID_ROWS), 1)
    ).astype(jnp.bfloat16)
    ids = lax.dot_general(
        rows_ref[start : start + ID_ROWS, :count], eye, TN, preferred_element_type=jnp.float32
    )
    return ids[:, 0:1], ids[:, 1:2]


def adapters(rows, columns):
    column = lax.broadcasted_iota(jnp.int32, (rows, columns), 1)
    return (column // ADAPTER_RANK).astype(jnp.float32)


def fold(wide):
    folded = wide[:, :LANES]
    for k in range(1, wide.shape[1] // LANES):
        folded = folded + wide[:, k * LANES : (k + 1) * LANES]
    return folded


def low_rank(folded):
    turned = folded.T
    low = turned[:ADAPTER_RANK]
    for k in range(1, LANES // ADAPTER_RANK):
        low = low + turned[k * ADAPTER_RANK : (k + 1) * ADAPTER_RANK]
    return low


def stacked(wide, keys):
    return jnp.concatenate([wide[:, k : k + keys] for k in range(0, wide.shape[1], keys)], axis=0)


def early_body(bits, part, rows, *refs):
    groups = lax.axis_size("groups")
    a = lax.axis_index("adapter")
    token_refs, rest = refs[:groups], refs[groups:]
    blocks, rest = rest[: len(bits)], rest[len(bits) :]
    kept, got, folded, mask, numbers, ups, keep, give, base = rest
    base[...] = kept[...] + got[...]
    halves(base, 1, keep, give)
    columns = blocks[0].shape[1]
    for n, block in enumerate(blocks):
        ups[n] = stacked(block[part:, :], ups.shape[2])
    adapter = adapters(rows, columns)
    for n, tokens in enumerate(token_refs):
        owner, slot = id_columns(tokens, rows, rows)
        if n == 0:
            numbers[...] = owner * (columns // ADAPTER_RANK) + slot
        right = adapter == slot
        picked = jnp.zeros((rows, columns), jnp.float32)
        for bit, block in zip(bits, blocks):
            wide = jnp.dot(tokens[:rows, :], block[:part, :], preferred_element_type=jnp.float32)
            number = jnp.where((bit != 3) | (a == 1) | (a == 2), a ^ bit, -1)
            picked = jnp.where(owner == number.astype(jnp.float32), wide, picked)
        folded[n] = fold(jnp.where(right, picked, 0.0))
        mask[n] = jnp.where(owner == (a ^ 2).astype(jnp.float32), right.astype(jnp.float32), 0.0)


def hop_mask_body(capacity, hop, _, out):
    _, slot = id_columns(hop, capacity, capacity)
    out[...] = (adapters(capacity, out.shape[1]) == slot).astype(jnp.float32)


def last_body(part, rows, capacity, *refs):
    groups = lax.axis_size("groups")
    a = lax.axis_index("adapter")
    token_refs, rest = refs[:groups], refs[groups:]
    hops, rest = rest[:groups], rest[groups:]
    hop_masks, rest = rest[:groups], rest[groups:]
    folded, mask, inside, outside, low, hop_low, away, last_up = rest
    columns = inside.shape[1]

    def finish(block):
        for n, tokens in enumerate(token_refs):
            wide = jnp.dot(tokens[:rows, :], block[:part, :], preferred_element_type=jnp.float32)
            kept = fold(jnp.where(mask[n] > 0, wide, 0.0))
            if n:
                away[:, :rows] = low_rank(folded[n] + kept)
            else:
                low[...] = low_rank(folded[n] + kept)

    middle = (a == 1) | (a == 2)

    @pl.when(middle)
    def _():
        finish(inside)
        last_up[...] = stacked(inside[part:, :], last_up.shape[1])
        for n, (hop, hop_mask) in enumerate(zip(hops, hop_masks)):
            wide = jnp.dot(hop[:capacity, :], inside[:part, :], preferred_element_type=jnp.float32)
            kept = fold(jnp.where(hop_mask[...] > 0, wide, 0.0))
            rest_rows = -capacity % LANES
            kept = jnp.concatenate([kept, jnp.zeros((rest_rows, LANES), jnp.float32)], axis=0)
            if n:
                away[:, rows:] = low_rank(kept)[:, :capacity]
            else:
                hop_low[...] = low_rank(kept)[:, :capacity]

    @pl.when(jnp.logical_not(middle))
    def _():
        finish(outside)
        last_up[...] = stacked(outside[part:, :], last_up.shape[1])
        hop_low[...] = jnp.zeros(hop_low.shape, jnp.float32)
        away[:, rows:] = jnp.zeros(hop_low.shape, jnp.float32)


def near_body(low, hop_low, near, low_out, hop_out):
    rows = low.shape[1]
    low_out[...] = low[...] + near[:, :rows]
    hop_out[...] = hop_low[...] + near[:, rows:]


def merge_body(low, far, places, hop, hop_far, _, out):
    back = hop[...] + hop_far[...]
    spread = jnp.zeros(low.shape, jnp.float32)
    for _ in range(3):
        piece = back.astype(jnp.bfloat16)
        back = back - piece.astype(jnp.float32)
        spread = spread + jnp.dot(piece, places[...], preferred_element_type=jnp.float32)
    out[...] = low[...] + far[...] + spread


def finish_body(near, far, keep, got, numbers, ups, last_up, distant, out):
    a = lax.axis_index("adapter")
    rows = out.shape[0]
    columns = last_up.shape[0]
    column = lax.broadcasted_iota(jnp.int32, (ADAPTER_RANK, columns), 1)
    row = lax.broadcasted_iota(jnp.int32, (ADAPTER_RANK, columns), 0)
    repeat = (lax.rem(column, ADAPTER_RANK) == row).astype(jnp.bfloat16)
    shrunk = (near[...] + far[...]).astype(jnp.bfloat16)
    spread = lax.dot_general(shrunk, repeat, TN, preferred_element_type=jnp.float32)
    adapter = adapters(rows, columns)
    middle = (a == 1) | (a == 2)
    mirrored = jnp.where(middle, ups[1].astype(jnp.float32), distant[...].astype(jnp.float32))
    blocks = ((0, ups[0]), (1, ups[2]), (2, last_up[...]), (3, mirrored.astype(jnp.bfloat16)))
    updates = jnp.zeros(out.shape, jnp.float32)
    for bit, up in blocks:
        wanted = numbers[...] - ((a ^ bit) * (columns // ADAPTER_RANK)).astype(jnp.float32)
        chosen = jnp.where(adapter == wanted, spread, 0.0).astype(jnp.bfloat16)
        updates = updates + jnp.dot(chosen, up, preferred_element_type=jnp.float32)
    updates = updates.astype(jnp.bfloat16).astype(jnp.float32)
    base = keep[...] + got[...]
    out[...] = (base + ADAPTER_SCALE * updates).astype(jnp.bfloat16)


def gather(
    tokens,
    base_key_weight,
    stacked_down_weight,
    stacked_up_weight,
    request_adapter_owner,
    request_adapter_slot,
):
    rows, features = tokens.shape
    groups, owners, shares = (lax.axis_size(name) for name in AXES)
    columns = stacked_down_weight.shape[1]
    keys = stacked_up_weight.shape[1]
    part = features // groups
    half = columns // keys
    capacity = -(-row_limit(rows) // ID_ROWS) * ID_ROWS

    def narrow(*dims):
        return jax.ShapeDtypeStruct(dims, jnp.bfloat16)

    def wide(*dims):
        return jax.ShapeDtypeStruct(dims, jnp.float32)

    own = kernel(
        pack_body,
        narrow(part + columns // half, columns),
        (in_hbm(stacked_down_weight), in_hbm(stacked_up_weight)),
        0,
        (pl.ANY, pl.ANY),
        [pltpu.SemaphoreType.DMA((1 + half,))],
    )
    beside = exchange(own, 0, 0, BESIDE)

    tok_own, tok_away = kernel(
        split_body,
        [narrow(rows + ID_ROWS, part)] * groups,
        (
            in_hbm(tokens),
            in_hbm(request_adapter_owner.reshape(1, rows)),
            in_hbm(request_adapter_slot),
            own,
        ),
        0,
        (pl.ANY, pl.ANY, pl.ANY, pl.ANY),
        [
            pltpu.VMEM((1, rows), jnp.int32),
            pltpu.VMEM((rows,), jnp.int32),
            pltpu.SemaphoreType.DMA((4,)),
        ],
    )
    token_parts = [tok_own, exchange(tok_away, 1, 0, SAME)]
    mirror = exchange(after(own, tok_own), 0, 0, MIDDLE)
    hop_own, hop_away, places = kernel(
        functools.partial(hop_body, rows, capacity),
        [narrow(capacity + ID_ROWS, part)] * groups
        + [narrow(capacity, rows)],
        (tok_own, tok_away),
        2 * rows * features * capacity,
    )

    keep, give = kernel(
        functools.partial(base_body, 2, rows),
        [wide(rows, shares * keys // 2)] * 2,
        (tok_own, tok_away, base_key_weight, places),
        2 * rows * features * shares * keys,
        (None, None, None, pl.ANY),
        [pltpu.VMEM((rows, shares * keys), jnp.float32)],
    )
    got = exchange(give, 0, 2, SAME)

    inside = exchange(after(beside, places), 0, 0, MIDDLE)
    outside = exchange(mirror, 0, 0, OUTWARD)
    hops = [
        exchange(after(hop_own, beside), 0, 0, INWARD),
        exchange(hop_away, 1, 0, INWARD),
    ]

    folded, mask, numbers, ups, keep, give = kernel(
        functools.partial(early_body, (0, 3, 1), part, rows),
        [
            wide(groups, rows, LANES),
            wide(groups, rows, columns),
            wide(rows, 1),
            narrow(3, columns, keys),
            wide(rows, keys),
            wide(rows, keys),
        ],
        (*token_parts, own, mirror, beside, keep, got),
        scratch=[pltpu.VMEM((rows, 2 * keys), jnp.float32)],
        light=True,
    )
    hop_masks, latest = [], folded
    for hop, urgency in zip(hops, HOP_URGENCY):
        latest = kernel(
            functools.partial(hop_mask_body, capacity),
            wide(capacity, columns),
            (hop, latest),
            urgency,
            (None, pl.ANY),
        )
        hop_masks.append(latest)
    low, hop_low, away, last_up = kernel(
        functools.partial(last_body, part, rows, capacity),
        [
            wide(ADAPTER_RANK, rows),
            wide(ADAPTER_RANK, capacity),
            wide(ADAPTER_RANK, rows + capacity),
            narrow(columns, keys),
        ],
        (*token_parts, *hops, *hop_masks, folded, mask, inside, outside),
        2 * groups * (rows + capacity) * part * columns,
    )

    near = exchange(away, 1, 0, SAME)
    distant = exchange(after(stacked_up_weight, folded), 0, 0, ENDS)
    low, hop_low = kernel(
        near_body, [wide(ADAPTER_RANK, rows), wide(ADAPTER_RANK, capacity)], (low, hop_low, near)
    )
    back = exchange(hop_low, 0, 0, BESIDE)
    back_far = exchange(hop_low, 0, 2, BESIDE)
    low_far = exchange(low, 0, 2, SAME)
    low = kernel(
        merge_body,
        wide(ADAPTER_RANK, rows),
        (low, low_far, places, back, back_far, distant),
        0,
        (None, None, None, None, None, pl.ANY),
    )
    got = exchange(give, 0, 1, SAME)
    low_far = exchange(low, 0, 1, SAME)
    return kernel(
        finish_body, narrow(rows, keys), (low, low_far, keep, got, numbers, ups, last_up, distant)
    )


def row_limit(rows):
    return max(2, 3 * rows // (2 * lax.axis_size("adapter")))


def local(*args):
    rows, columns = args[0].shape[0], args[2].shape[1]
    groups, owners, shares = (lax.axis_size(name) for name in AXES)
    fits = owners == OWNERS and groups == 2 and shares == 4
    travels = fits and columns <= groups * row_limit(rows)
    return (gather if travels else dispatch)(*args)


def solution(mesh):
    placed = (
        P(("groups", "adapter"), "mp"),
        P("mp", None),
        P("mp", "adapter"),
        P("adapter", "mp"),
        P(("groups", "adapter"), None),
        P(("groups", "adapter")),
    )
    return jax.shard_map(
        local, mesh=mesh, in_specs=placed, out_specs=P(("groups", "adapter"), "mp"), check_vma=False
    )
```

```python
import functools

import jax
import jax.numpy as jnp
from jax import lax
from jax.experimental import pallas as pl
from jax.experimental.pallas import tpu as pltpu
from jax.sharding import PartitionSpec as P

ADAPTER_RANK = 16


ADAPTER_SCALE = 2.0


def dispatch(
    tokens,
    base_key_weight,
    stacked_down_weight,
    stacked_up_weight,
    request_adapter_owner,
    request_adapter_slot,
):
    rows_here = tokens.shape[0]
    feature_share = tokens.shape[1]
    owner_count = lax.axis_size("adapter")
    capacity = max(2, 3 * rows_here // (2 * owner_count))
    local_adapters = stacked_down_weight.shape[1] // ADAPTER_RANK
    key_output_share = stacked_up_weight.shape[1]
    owners = request_adapter_owner.reshape(-1)
    onehot = (owners[:, None] == jnp.arange(owner_count, dtype=jnp.int32)[None, :]).astype(
        jnp.int32
    )
    before = jnp.sum((jnp.cumsum(onehot, axis=0) - onehot) * onehot, axis=1)
    places = owners * capacity + before
    send_rows = (
        jnp.zeros((owner_count * capacity, feature_share), jnp.bfloat16).at[places].set(tokens)
    )
    send_rows = send_rows.reshape(owner_count, capacity, feature_share)
    send_slots = (
        jnp.full((owner_count * capacity,), -1, jnp.int32).at[places].set(request_adapter_slot)
    )
    send_slots = send_slots.reshape(owner_count, capacity)
    input_rows = lax.all_to_all(send_rows, "adapter", split_axis=0, concat_axis=0, tiled=True)
    slots_in = lax.all_to_all(send_slots, "adapter", split_axis=0, concat_axis=0, tiled=True)
    key_projection_output = jnp.einsum(
        "rzq,qt->rzt", input_rows, stacked_down_weight, preferred_element_type=jnp.float32
    )
    key_projection_output = key_projection_output.reshape(
        input_rows.shape[0], input_rows.shape[1], local_adapters, ADAPTER_RANK
    )
    chosen = slots_in[:, :, None] == jnp.arange(local_adapters, dtype=jnp.int32)[None, None, :]
    partial_low = jnp.sum(jnp.where(chosen[:, :, :, None], key_projection_output, 0.0), axis=2)
    shrunk = lax.psum(partial_low, "mp")
    shrunk_bf = shrunk.astype(jnp.bfloat16)
    returned = lax.all_to_all(shrunk_bf, "adapter", split_axis=0, concat_axis=0, tiled=True)
    low_rows = returned.reshape(owner_count * capacity, ADAPTER_RANK)[places]
    gathered_up_weight = lax.all_gather(stacked_up_weight, "adapter", axis=0, tiled=True)
    adapter_ids = owners * local_adapters + request_adapter_slot
    up_taken = gathered_up_weight.reshape(-1, ADAPTER_RANK, key_output_share)[adapter_ids]
    adapter_updates = jnp.einsum(
        "tr,trk->tk", low_rows, up_taken, preferred_element_type=jnp.float32
    ).astype(jnp.bfloat16)
    base_output_share = lax.psum_scatter(
        lax.dot_general(
            base_key_weight, tokens, (((0,), (1,)), ((), ())), preferred_element_type=jnp.float32
        ),
        "mp",
        scatter_dimension=0,
        tiled=True,
    )
    return (base_output_share.T + ADAPTER_SCALE * adapter_updates.astype(jnp.float32)).astype(
        jnp.bfloat16
    )


AXES = ("groups", "adapter", "mp")
ID_ROWS = 16
HOP_URGENCY = (30 * 10**8, 0)
OWNERS = 4
LANES = 128
NT = (((1,), (1,)), ((), ()))
TN = (((0,), (0,)), ((), ()))


def exchange(x, group_bits, share_bits, owners):
    groups, count, shares = (lax.axis_size(name) for name in AXES)

    def number(g, a, m):
        return (g * count + a) * shares + m

    pairs = [
        (number(g, a, m), number(g ^ group_bits, b, m ^ share_bits))
        for g in range(groups)
        for a, b in owners
        for m in range(shares)
    ]
    return lax.ppermute(x, AXES, pairs)


SAME = tuple((a, a) for a in range(OWNERS))
BESIDE = ((0, 1), (1, 0), (2, 3), (3, 2))
MIDDLE = ((0, 0), (1, 2), (2, 1), (3, 3))
ENDS = ((0, 3), (1, 1), (2, 2), (3, 0))
OUTWARD = ((1, 0), (2, 3))
INWARD = ((0, 1), (3, 2))


def after(x, *others):
    return lax.optimization_barrier((x, *others))[0]


def in_hbm(x):
    return pltpu.with_memory_space_constraint(x, pltpu.HBM)


def kernel(body, outs, operands, flops=0, spaces=None, scratch=(), light=False):
    inner = pl.BlockSpec(memory_space=pltpu.VMEM)
    specs = [inner if s is None else pl.BlockSpec(memory_space=s) for s in spaces or ()]
    touched = sum(x.size * x.dtype.itemsize for x in jax.tree.leaves((operands, outs)))
    return pl.pallas_call(
        body,
        out_shape=outs,
        in_specs=specs or [inner] * len(operands),
        out_specs=jax.tree.map(lambda _: inner, outs),
        scratch_shapes=scratch,
        compiler_params=pltpu.CompilerParams(vmem_limit_bytes=16 * 1024 * 1024),
        cost_estimate=pl.CostEstimate(
            flops=flops, bytes_accessed=0 if light else touched, transcendentals=0
        ),
    )(*operands)


def pack_body(down, up, out, sems):
    g = lax.axis_index("groups")
    columns, keys = down.shape[1], up.shape[1]
    count = columns // keys
    size = up.shape[0] // count
    part = out.shape[0] - size
    mine = down.at[pl.ds(pl.multiple_of(g * part, part), part), :]
    copies = [pltpu.make_async_copy(mine, out.at[pl.ds(0, part), :], sems.at[count])]
    for k in range(count):
        copies.append(
            pltpu.make_async_copy(
                up.at[pl.ds(k * size, size), :],
                out.at[pl.ds(part, size), pl.ds(k * keys, keys)],
                sems.at[k],
            )
        )
    for copy in copies:
        copy.start()
    for copy in copies:
        copy.wait()


def split_body(tokens, owner_in, slot_in, _, own, away, owner, slot, sems):
    g = lax.axis_index("groups")
    rows, part = tokens.shape[0], own.shape[1]
    copies = []
    for n, (out, half) in enumerate(((own, g), (away, 1 - g))):
        taken = tokens.at[:, pl.ds(pl.multiple_of(half * part, part), part)]
        copies.append(pltpu.make_async_copy(taken, out.at[pl.ds(0, rows), :], sems.at[n]))
    id_copies = [
        pltpu.make_async_copy(owner_in, owner, sems.at[2]),
        pltpu.make_async_copy(slot_in, slot, sems.at[3]),
    ]
    for copy in id_copies + copies:
        copy.start()
    for copy in id_copies:
        copy.wait()
    row = lax.broadcasted_iota(jnp.int32, (ID_ROWS, rows), 0)
    ids = jnp.where(row == 0, owner[...], jnp.where(row == 1, slot[...].reshape(1, rows), 0))
    ids = ids.astype(jnp.float32).astype(jnp.bfloat16)
    for out in (own, away):
        out[rows:, :rows] = ids
        out[rows:, rows:] = jnp.zeros((ID_ROWS, part - rows), jnp.bfloat16)
    for copy in copies:
        copy.wait()


def hop_body(rows, capacity, own, away, own_out, away_out, places):
    a = lax.axis_index("adapter")
    part = own.shape[1]
    ids = own[rows:, :rows]
    match = (ids.astype(jnp.float32) == (OWNERS - 1 - a).astype(jnp.float32)).astype(jnp.bfloat16)
    earlier = lax.broadcasted_iota(jnp.int32, (rows, rows), 0) < lax.broadcasted_iota(
        jnp.int32, (rows, rows), 1
    )
    rank = jnp.dot(match, earlier.astype(jnp.bfloat16), preferred_element_type=jnp.float32)
    place = lax.broadcasted_iota(jnp.int32, (capacity, rows), 0).astype(jnp.float32)
    taken = (place == rank[0:1]) & (match[0:1].astype(jnp.float32) > 0)
    chosen = taken.astype(jnp.bfloat16)
    places[...] = chosen
    kept = lax.dot_general(ids, chosen, NT, preferred_element_type=jnp.float32)
    for tokens, out in ((own, own_out), (away, away_out)):
        packed = jnp.dot(chosen, tokens[:rows, :], preferred_element_type=jnp.float32)
        out[:capacity, :] = packed.astype(jnp.bfloat16)
        out[capacity:, :] = jnp.zeros((ID_ROWS, part), jnp.bfloat16)
        out[capacity:, :capacity] = kept.astype(jnp.bfloat16)


def base_body(bit, rows, own, away, weights, _, keep, give, base):
    g = lax.axis_index("groups")
    part = own.shape[1]
    total = jnp.zeros(base.shape, jnp.float32)
    for tokens, half in ((own, g), (away, 1 - g)):
        part_weights = weights[pl.ds(pl.multiple_of(half * part, part), part), :]
        total = total + jnp.dot(tokens[:rows, :], part_weights, preferred_element_type=jnp.float32)
    base[...] = total
    halves(base, bit, keep, give)


def halves(base, bit, keep, give):
    m = lax.axis_index("mp")
    width = keep.shape[1]
    side = (m // bit) % 2
    keep[...] = base[:, pl.ds(pl.multiple_of(side * width, width), width)]
    give[...] = base[:, pl.ds(pl.multiple_of((1 - side) * width, width), width)]


def id_columns(rows_ref, start, count):
    eye = (
        lax.broadcasted_iota(jnp.int32, (ID_ROWS, ID_ROWS), 0)
        == lax.broadcasted_iota(jnp.int32, (ID_ROWS, ID_ROWS), 1)
    ).astype(jnp.bfloat16)
    ids = lax.dot_general(
        rows_ref[start : start + ID_ROWS, :count], eye, TN, preferred_element_type=jnp.float32
    )
    return ids[:, 0:1], ids[:, 1:2]


def adapters(rows, columns):
    column = lax.broadcasted_iota(jnp.int32, (rows, columns), 1)
    return (column // ADAPTER_RANK).astype(jnp.float32)


def fold(wide):
    folded = wide[:, :LANES]
    for k in range(1, wide.shape[1] // LANES):
        folded = folded + wide[:, k * LANES : (k + 1) * LANES]
    return folded


def low_rank(folded):
    turned = folded.T
    low = turned[:ADAPTER_RANK]
    for k in range(1, LANES // ADAPTER_RANK):
        low = low + turned[k * ADAPTER_RANK : (k + 1) * ADAPTER_RANK]
    return low


def stacked(wide, keys):
    return jnp.concatenate([wide[:, k : k + keys] for k in range(0, wide.shape[1], keys)], axis=0)


def early_body(bits, part, rows, *refs):
    groups = lax.axis_size("groups")
    a = lax.axis_index("adapter")
    token_refs, rest = refs[:groups], refs[groups:]
    blocks, rest = rest[: len(bits)], rest[len(bits) :]
    kept, got, folded, mask, numbers, ups, keep, give, base = rest
    base[...] = kept[...] + got[...]
    halves(base, 1, keep, give)
    columns = blocks[0].shape[1]
    for n, block in enumerate(blocks):
        ups[n] = stacked(block[part:, :], ups.shape[2])
    adapter = adapters(rows, columns)
    for n, tokens in enumerate(token_refs):
        owner, slot = id_columns(tokens, rows, rows)
        if n == 0:
            numbers[...] = owner * (columns // ADAPTER_RANK) + slot
        right = adapter == slot
        picked = jnp.zeros((rows, columns), jnp.float32)
        for bit, block in zip(bits, blocks):
            wide = jnp.dot(tokens[:rows, :], block[:part, :], preferred_element_type=jnp.float32)
            number = jnp.where((bit != 3) | (a == 1) | (a == 2), a ^ bit, -1)
            picked = jnp.where(owner == number.astype(jnp.float32), wide, picked)
        folded[n] = fold(jnp.where(right, picked, 0.0))
        mask[n] = jnp.where(owner == (a ^ 2).astype(jnp.float32), right.astype(jnp.float32), 0.0)


def hop_mask_body(capacity, hop, _, out):
    _, slot = id_columns(hop, capacity, capacity)
    out[...] = (adapters(capacity, out.shape[1]) == slot).astype(jnp.float32)


def last_body(part, rows, capacity, *refs):
    groups = lax.axis_size("groups")
    a = lax.axis_index("adapter")
    token_refs, rest = refs[:groups], refs[groups:]
    hops, rest = rest[:groups], rest[groups:]
    hop_masks, rest = rest[:groups], rest[groups:]
    folded, mask, inside, outside, low, hop_low, away, last_up = rest
    columns = inside.shape[1]

    def finish(block):
        for n, tokens in enumerate(token_refs):
            wide = jnp.dot(tokens[:rows, :], block[:part, :], preferred_element_type=jnp.float32)
            kept = fold(jnp.where(mask[n] > 0, wide, 0.0))
            if n:
                away[:, :rows] = low_rank(folded[n] + kept)
            else:
                low[...] = low_rank(folded[n] + kept)

    middle = (a == 1) | (a == 2)

    @pl.when(middle)
    def _():
        finish(inside)
        last_up[...] = stacked(inside[part:, :], last_up.shape[1])
        for n, (hop, hop_mask) in enumerate(zip(hops, hop_masks)):
            wide = jnp.dot(hop[:capacity, :], inside[:part, :], preferred_element_type=jnp.float32)
            kept = fold(jnp.where(hop_mask[...] > 0, wide, 0.0))
            rest_rows = -capacity % LANES
            kept = jnp.concatenate([kept, jnp.zeros((rest_rows, LANES), jnp.float32)], axis=0)
            if n:
                away[:, rows:] = low_rank(kept)[:, :capacity]
            else:
                hop_low[...] = low_rank(kept)[:, :capacity]

    @pl.when(jnp.logical_not(middle))
    def _():
        finish(outside)
        last_up[...] = stacked(outside[part:, :], last_up.shape[1])
        hop_low[...] = jnp.zeros(hop_low.shape, jnp.float32)
        away[:, rows:] = jnp.zeros(hop_low.shape, jnp.float32)


def near_body(low, hop_low, near, low_out, hop_out):
    rows = low.shape[1]
    capacity = hop_low.shape[1]
    low_out[...] = low[...] + near[:, :rows]
    hop_out[...] = jnp.zeros(hop_out.shape, jnp.float32)
    hop_out[:, :capacity] = hop_low[...] + near[:, rows:]


def merge_body(low, far, places, hop_far, hop, _, out):
    capacity = places.shape[0]
    back = hop[:, :capacity] + hop_far[:, :capacity]
    spread = jnp.zeros(low.shape, jnp.float32)
    for _ in range(3):
        piece = back.astype(jnp.bfloat16)
        back = back - piece.astype(jnp.float32)
        spread = spread + jnp.dot(piece, places[...], preferred_element_type=jnp.float32)
    out[...] = low[...] + far[...] + spread


def finish_body(near, far, keep, got, numbers, ups, last_up, distant, out):
    a = lax.axis_index("adapter")
    rows = out.shape[0]
    columns = last_up.shape[0]
    column = lax.broadcasted_iota(jnp.int32, (ADAPTER_RANK, columns), 1)
    row = lax.broadcasted_iota(jnp.int32, (ADAPTER_RANK, columns), 0)
    repeat = (lax.rem(column, ADAPTER_RANK) == row).astype(jnp.bfloat16)
    shrunk = (near[...] + far[...]).astype(jnp.bfloat16)
    spread = lax.dot_general(shrunk, repeat, TN, preferred_element_type=jnp.float32)
    adapter = adapters(rows, columns)
    middle = (a == 1) | (a == 2)
    mirrored = jnp.where(middle, ups[1].astype(jnp.float32), distant[...].astype(jnp.float32))
    blocks = ((0, ups[0]), (1, ups[2]), (2, last_up[...]), (3, mirrored.astype(jnp.bfloat16)))
    updates = jnp.zeros(out.shape, jnp.float32)
    for bit, up in blocks:
        wanted = numbers[...] - ((a ^ bit) * (columns // ADAPTER_RANK)).astype(jnp.float32)
        chosen = jnp.where(adapter == wanted, spread, 0.0).astype(jnp.bfloat16)
        updates = updates + jnp.dot(chosen, up, preferred_element_type=jnp.float32)
    updates = updates.astype(jnp.bfloat16).astype(jnp.float32)
    base = keep[...] + got[...]
    out[...] = (base + ADAPTER_SCALE * updates).astype(jnp.bfloat16)


def gather(
    tokens,
    base_key_weight,
    stacked_down_weight,
    stacked_up_weight,
    request_adapter_owner,
    request_adapter_slot,
):
    rows, features = tokens.shape
    groups, owners, shares = (lax.axis_size(name) for name in AXES)
    columns = stacked_down_weight.shape[1]
    keys = stacked_up_weight.shape[1]
    part = features // groups
    half = columns // keys
    capacity = -(-row_limit(rows) // ID_ROWS) * ID_ROWS

    def narrow(*dims):
        return jax.ShapeDtypeStruct(dims, jnp.bfloat16)

    def wide(*dims):
        return jax.ShapeDtypeStruct(dims, jnp.float32)

    own = kernel(
        pack_body,
        narrow(part + columns // half, columns),
        (in_hbm(stacked_down_weight), in_hbm(stacked_up_weight)),
        0,
        (pl.ANY, pl.ANY),
        [pltpu.SemaphoreType.DMA((1 + half,))],
    )
    beside = exchange(own, 0, 0, BESIDE)

    tok_own, tok_away = kernel(
        split_body,
        [narrow(rows + ID_ROWS, part)] * groups,
        (
            in_hbm(tokens),
            in_hbm(request_adapter_owner.reshape(1, rows)),
            in_hbm(request_adapter_slot),
            own,
        ),
        0,
        (pl.ANY, pl.ANY, pl.ANY, pl.ANY),
        [
            pltpu.VMEM((1, rows), jnp.int32),
            pltpu.VMEM((rows,), jnp.int32),
            pltpu.SemaphoreType.DMA((4,)),
        ],
    )
    token_parts = [tok_own, exchange(tok_away, 1, 0, SAME)]
    mirror = exchange(after(own, tok_own), 0, 0, MIDDLE)
    hop_own, hop_away, places = kernel(
        functools.partial(hop_body, rows, capacity),
        [narrow(capacity + ID_ROWS, part)] * groups
        + [narrow(capacity, rows)],
        (tok_own, tok_away),
        2 * rows * features * capacity,
    )

    keep, give = kernel(
        functools.partial(base_body, 2, rows),
        [wide(rows, shares * keys // 2)] * 2,
        (tok_own, tok_away, base_key_weight, places),
        2 * rows * features * shares * keys,
        (None, None, None, pl.ANY),
        [pltpu.VMEM((rows, shares * keys), jnp.float32)],
    )
    got = exchange(give, 0, 2, SAME)

    inside = exchange(after(beside, places), 0, 0, MIDDLE)
    outside = exchange(mirror, 0, 0, OUTWARD)
    hops = [
        exchange(after(hop_own, beside), 0, 0, INWARD),
        exchange(hop_away, 1, 0, INWARD),
    ]

    folded, mask, numbers, ups, keep, give = kernel(
        functools.partial(early_body, (0, 3, 1), part, rows),
        [
            wide(groups, rows, LANES),
            wide(groups, rows, columns),
            wide(rows, 1),
            narrow(3, columns, keys),
            wide(rows, keys),
            wide(rows, keys),
        ],
        (*token_parts, own, mirror, beside, keep, got),
        scratch=[pltpu.VMEM((rows, 2 * keys), jnp.float32)],
        light=True,
    )
    hop_masks, latest = [], folded
    for hop, urgency in zip(hops, HOP_URGENCY):
        latest = kernel(
            functools.partial(hop_mask_body, capacity),
            wide(capacity, columns),
            (hop, latest),
            urgency,
            (None, pl.ANY),
        )
        hop_masks.append(latest)
    low, hop_low, away, last_up = kernel(
        functools.partial(last_body, part, rows, capacity),
        [
            wide(ADAPTER_RANK, rows),
            wide(ADAPTER_RANK, capacity),
            wide(ADAPTER_RANK, rows + capacity),
            narrow(columns, keys),
        ],
        (*token_parts, *hops, *hop_masks, folded, mask, inside, outside),
        2 * groups * (rows + capacity) * part * columns,
    )

    near = exchange(away, 1, 0, SAME)
    distant = exchange(after(stacked_up_weight, folded), 0, 0, ENDS)
    low, hop_low = kernel(
        near_body,
        [wide(ADAPTER_RANK, rows), wide(ADAPTER_RANK, rows + LANES)],
        (low, hop_low, near),
    )
    back = exchange(hop_low, 0, 0, BESIDE)
    back_far = exchange(hop_low, 0, 2, BESIDE)
    low_far = exchange(low, 0, 2, SAME)
    low = kernel(
        merge_body,
        wide(ADAPTER_RANK, rows),
        (low, low_far, places, back_far, back, distant),
        0,
        (None, None, None, None, None, pl.ANY),
    )
    got = exchange(give, 0, 1, SAME)
    low_far = exchange(low, 0, 1, SAME)
    return kernel(
        finish_body, narrow(rows, keys), (low, low_far, keep, got, numbers, ups, last_up, distant)
    )


def row_limit(rows):
    return max(2, 3 * rows // (2 * lax.axis_size("adapter")))


def local(*args):
    rows, columns = args[0].shape[0], args[2].shape[1]
    groups, owners, shares = (lax.axis_size(name) for name in AXES)
    fits = owners == OWNERS and groups == 2 and shares == 4
    travels = fits and columns <= groups * row_limit(rows)
    return (gather if travels else dispatch)(*args)


def solution(mesh):
    placed = (
        P(("groups", "adapter"), "mp"),
        P("mp", None),
        P("mp", "adapter"),
        P("adapter", "mp"),
        P(("groups", "adapter"), None),
        P(("groups", "adapter")),
    )
    return jax.shard_map(
        local, mesh=mesh, in_specs=placed, out_specs=P(("groups", "adapter"), "mp"), check_vma=False
    )
```

```python
import functools

import jax
import jax.numpy as jnp
from jax import lax
from jax.experimental import pallas as pl
from jax.experimental.pallas import tpu as pltpu
from jax.sharding import PartitionSpec as P

ADAPTER_RANK = 16


ADAPTER_SCALE = 2.0


def dispatch(
    tokens,
    base_key_weight,
    stacked_down_weight,
    stacked_up_weight,
    request_adapter_owner,
    request_adapter_slot,
):
    rows_here = tokens.shape[0]
    feature_share = tokens.shape[1]
    owner_count = lax.axis_size("adapter")
    capacity = max(2, 3 * rows_here // (2 * owner_count))
    local_adapters = stacked_down_weight.shape[1] // ADAPTER_RANK
    key_output_share = stacked_up_weight.shape[1]
    owners = request_adapter_owner.reshape(-1)
    onehot = (owners[:, None] == jnp.arange(owner_count, dtype=jnp.int32)[None, :]).astype(
        jnp.int32
    )
    before = jnp.sum((jnp.cumsum(onehot, axis=0) - onehot) * onehot, axis=1)
    places = owners * capacity + before
    send_rows = (
        jnp.zeros((owner_count * capacity, feature_share), jnp.bfloat16).at[places].set(tokens)
    )
    send_rows = send_rows.reshape(owner_count, capacity, feature_share)
    send_slots = (
        jnp.full((owner_count * capacity,), -1, jnp.int32).at[places].set(request_adapter_slot)
    )
    send_slots = send_slots.reshape(owner_count, capacity)
    input_rows = lax.all_to_all(send_rows, "adapter", split_axis=0, concat_axis=0, tiled=True)
    slots_in = lax.all_to_all(send_slots, "adapter", split_axis=0, concat_axis=0, tiled=True)
    key_projection_output = jnp.einsum(
        "rzq,qt->rzt", input_rows, stacked_down_weight, preferred_element_type=jnp.float32
    )
    key_projection_output = key_projection_output.reshape(
        input_rows.shape[0], input_rows.shape[1], local_adapters, ADAPTER_RANK
    )
    chosen = slots_in[:, :, None] == jnp.arange(local_adapters, dtype=jnp.int32)[None, None, :]
    partial_low = jnp.sum(jnp.where(chosen[:, :, :, None], key_projection_output, 0.0), axis=2)
    shrunk = lax.psum(partial_low, "mp")
    shrunk_bf = shrunk.astype(jnp.bfloat16)
    returned = lax.all_to_all(shrunk_bf, "adapter", split_axis=0, concat_axis=0, tiled=True)
    low_rows = returned.reshape(owner_count * capacity, ADAPTER_RANK)[places]
    gathered_up_weight = lax.all_gather(stacked_up_weight, "adapter", axis=0, tiled=True)
    adapter_ids = owners * local_adapters + request_adapter_slot
    up_taken = gathered_up_weight.reshape(-1, ADAPTER_RANK, key_output_share)[adapter_ids]
    adapter_updates = jnp.einsum(
        "tr,trk->tk", low_rows, up_taken, preferred_element_type=jnp.float32
    ).astype(jnp.bfloat16)
    base_output_share = lax.psum_scatter(
        lax.dot_general(
            base_key_weight, tokens, (((0,), (1,)), ((), ())), preferred_element_type=jnp.float32
        ),
        "mp",
        scatter_dimension=0,
        tiled=True,
    )
    return (base_output_share.T + ADAPTER_SCALE * adapter_updates.astype(jnp.float32)).astype(
        jnp.bfloat16
    )


AXES = ("groups", "adapter", "mp")
ID_ROWS = 16
HOP_URGENCY = (30 * 10**8, 0)
OWNERS = 4
LANES = 128
NT = (((1,), (1,)), ((), ()))
TN = (((0,), (0,)), ((), ()))


def exchange(x, group_bits, share_bits, owners):
    groups, count, shares = (lax.axis_size(name) for name in AXES)

    def number(g, a, m):
        return (g * count + a) * shares + m

    pairs = [
        (number(g, a, m), number(g ^ group_bits, b, m ^ share_bits))
        for g in range(groups)
        for a, b in owners
        for m in range(shares)
    ]
    return lax.ppermute(x, AXES, pairs)


SAME = tuple((a, a) for a in range(OWNERS))
BESIDE = ((0, 1), (1, 0), (2, 3), (3, 2))
MIDDLE = ((0, 0), (1, 2), (2, 1), (3, 3))
ENDS = ((0, 3), (1, 1), (2, 2), (3, 0))
OUTWARD = ((1, 0), (2, 3))
INWARD = ((0, 1), (3, 2))


def after(x, *others):
    return lax.optimization_barrier((x, *others))[0]


def in_hbm(x):
    return pltpu.with_memory_space_constraint(x, pltpu.HBM)


def kernel(body, outs, operands, flops=0, spaces=None, scratch=(), light=False):
    inner = pl.BlockSpec(memory_space=pltpu.VMEM)
    specs = [inner if s is None else pl.BlockSpec(memory_space=s) for s in spaces or ()]
    touched = sum(x.size * x.dtype.itemsize for x in jax.tree.leaves((operands, outs)))
    return pl.pallas_call(
        body,
        out_shape=outs,
        in_specs=specs or [inner] * len(operands),
        out_specs=jax.tree.map(lambda _: inner, outs),
        scratch_shapes=scratch,
        compiler_params=pltpu.CompilerParams(vmem_limit_bytes=16 * 1024 * 1024),
        cost_estimate=pl.CostEstimate(
            flops=flops, bytes_accessed=0 if light else touched, transcendentals=0
        ),
    )(*operands)


def pack_body(down, up, out, sems):
    g = lax.axis_index("groups")
    columns, keys = down.shape[1], up.shape[1]
    count = columns // keys
    size = up.shape[0] // count
    part = out.shape[0] - size
    mine = down.at[pl.ds(pl.multiple_of(g * part, part), part), :]
    copies = [pltpu.make_async_copy(mine, out.at[pl.ds(0, part), :], sems.at[count])]
    for k in range(count):
        copies.append(
            pltpu.make_async_copy(
                up.at[pl.ds(k * size, size), :],
                out.at[pl.ds(part, size), pl.ds(k * keys, keys)],
                sems.at[k],
            )
        )
    for copy in copies:
        copy.start()
    for copy in copies:
        copy.wait()


def split_body(tokens, owner_in, slot_in, _, own, away, owner, slot, sems):
    g = lax.axis_index("groups")
    rows, part = tokens.shape[0], own.shape[1]
    copies = []
    for n, (out, half) in enumerate(((own, g), (away, 1 - g))):
        taken = tokens.at[:, pl.ds(pl.multiple_of(half * part, part), part)]
        copies.append(pltpu.make_async_copy(taken, out.at[pl.ds(0, rows), :], sems.at[n]))
    id_copies = [
        pltpu.make_async_copy(owner_in, owner, sems.at[2]),
        pltpu.make_async_copy(slot_in, slot, sems.at[3]),
    ]
    for copy in id_copies + copies:
        copy.start()
    for copy in id_copies:
        copy.wait()
    row = lax.broadcasted_iota(jnp.int32, (ID_ROWS, rows), 0)
    ids = jnp.where(row == 0, owner[...], jnp.where(row == 1, slot[...].reshape(1, rows), 0))
    ids = ids.astype(jnp.float32).astype(jnp.bfloat16)
    for out in (own, away):
        out[rows:, :rows] = ids
        out[rows:, rows:] = jnp.zeros((ID_ROWS, part - rows), jnp.bfloat16)
    for copy in copies:
        copy.wait()


def hop_body(rows, capacity, own, away, own_out, away_out, places):
    a = lax.axis_index("adapter")
    part = own.shape[1]
    ids = own[rows:, :rows]
    match = (ids.astype(jnp.float32) == (OWNERS - 1 - a).astype(jnp.float32)).astype(jnp.bfloat16)
    earlier = lax.broadcasted_iota(jnp.int32, (rows, rows), 0) < lax.broadcasted_iota(
        jnp.int32, (rows, rows), 1
    )
    rank = jnp.dot(match, earlier.astype(jnp.bfloat16), preferred_element_type=jnp.float32)
    place = lax.broadcasted_iota(jnp.int32, (capacity, rows), 0).astype(jnp.float32)
    taken = (place == rank[0:1]) & (match[0:1].astype(jnp.float32) > 0)
    chosen = taken.astype(jnp.bfloat16)
    places[...] = chosen
    kept = lax.dot_general(ids, chosen, NT, preferred_element_type=jnp.float32)
    for tokens, out in ((own, own_out), (away, away_out)):
        packed = jnp.dot(chosen, tokens[:rows, :], preferred_element_type=jnp.float32)
        out[:capacity, :] = packed.astype(jnp.bfloat16)
        out[capacity:, :] = jnp.zeros((ID_ROWS, part), jnp.bfloat16)
        out[capacity:, :capacity] = kept.astype(jnp.bfloat16)


def base_body(bit, rows, own, away, weights, _, keep, give, base):
    g = lax.axis_index("groups")
    part = own.shape[1]
    total = jnp.zeros(base.shape, jnp.float32)
    for tokens, half in ((own, g), (away, 1 - g)):
        part_weights = weights[pl.ds(pl.multiple_of(half * part, part), part), :]
        total = total + jnp.dot(tokens[:rows, :], part_weights, preferred_element_type=jnp.float32)
    base[...] = total
    halves(base, bit, keep, give)


def halves(base, bit, keep, give):
    m = lax.axis_index("mp")
    width = keep.shape[1]
    side = (m // bit) % 2
    keep[...] = base[:, pl.ds(pl.multiple_of(side * width, width), width)]
    give[...] = base[:, pl.ds(pl.multiple_of((1 - side) * width, width), width)]


def id_columns(rows_ref, start, count):
    eye = (
        lax.broadcasted_iota(jnp.int32, (ID_ROWS, ID_ROWS), 0)
        == lax.broadcasted_iota(jnp.int32, (ID_ROWS, ID_ROWS), 1)
    ).astype(jnp.bfloat16)
    ids = lax.dot_general(
        rows_ref[start : start + ID_ROWS, :count], eye, TN, preferred_element_type=jnp.float32
    )
    return ids[:, 0:1], ids[:, 1:2]


def adapters(rows, columns):
    column = lax.broadcasted_iota(jnp.int32, (rows, columns), 1)
    return (column // ADAPTER_RANK).astype(jnp.float32)


def fold(wide):
    folded = wide[:, :LANES]
    for k in range(1, wide.shape[1] // LANES):
        folded = folded + wide[:, k * LANES : (k + 1) * LANES]
    return folded


def low_rank(folded):
    turned = folded.T
    low = turned[:ADAPTER_RANK]
    for k in range(1, LANES // ADAPTER_RANK):
        low = low + turned[k * ADAPTER_RANK : (k + 1) * ADAPTER_RANK]
    return low


def stacked(wide, keys):
    return jnp.concatenate([wide[:, k : k + keys] for k in range(0, wide.shape[1], keys)], axis=0)


def early_body(bits, part, rows, *refs):
    groups = lax.axis_size("groups")
    a = lax.axis_index("adapter")
    token_refs, rest = refs[:groups], refs[groups:]
    blocks, rest = rest[: len(bits)], rest[len(bits) :]
    kept, got, folded, mask, numbers, ups, keep, give, base = rest
    base[...] = kept[...] + got[...]
    halves(base, 1, keep, give)
    columns = blocks[0].shape[1]
    for n, block in enumerate(blocks):
        ups[n] = stacked(block[part:, :], ups.shape[2])
    adapter = adapters(rows, columns)
    for n, tokens in enumerate(token_refs):
        owner, slot = id_columns(tokens, rows, rows)
        if n == 0:
            numbers[...] = owner * (columns // ADAPTER_RANK) + slot
        right = adapter == slot
        picked = jnp.zeros((rows, columns), jnp.float32)
        for bit, block in zip(bits, blocks):
            wide = jnp.dot(tokens[:rows, :], block[:part, :], preferred_element_type=jnp.float32)
            number = jnp.where((bit != 3) | (a == 1) | (a == 2), a ^ bit, -1)
            picked = jnp.where(owner == number.astype(jnp.float32), wide, picked)
        folded[n] = fold(jnp.where(right, picked, 0.0))
        mask[n] = jnp.where(owner == (a ^ 2).astype(jnp.float32), right.astype(jnp.float32), 0.0)


def hop_mask_body(capacity, hop, _, out):
    _, slot = id_columns(hop, capacity, capacity)
    out[...] = (adapters(capacity, out.shape[1]) == slot).astype(jnp.float32)


def last_body(part, rows, capacity, *refs):
    groups = lax.axis_size("groups")
    a = lax.axis_index("adapter")
    token_refs, rest = refs[:groups], refs[groups:]
    hops, rest = rest[:groups], rest[groups:]
    hop_masks, rest = rest[:groups], rest[groups:]
    folded, mask, inside, outside, low, hop_low, away, last_up = rest
    columns = inside.shape[1]

    def finish(block):
        for n, tokens in enumerate(token_refs):
            wide = jnp.dot(tokens[:rows, :], block[:part, :], preferred_element_type=jnp.float32)
            kept = fold(jnp.where(mask[n] > 0, wide, 0.0))
            if n:
                away[:, :rows] = low_rank(folded[n] + kept)
            else:
                low[...] = low_rank(folded[n] + kept)

    middle = (a == 1) | (a == 2)

    @pl.when(middle)
    def _():
        finish(inside)
        last_up[...] = stacked(inside[part:, :], last_up.shape[1])
        for n, (hop, hop_mask) in enumerate(zip(hops, hop_masks)):
            wide = jnp.dot(hop[:capacity, :], inside[:part, :], preferred_element_type=jnp.float32)
            kept = fold(jnp.where(hop_mask[...] > 0, wide, 0.0))
            rest_rows = -capacity % LANES
            kept = jnp.concatenate([kept, jnp.zeros((rest_rows, LANES), jnp.float32)], axis=0)
            if n:
                away[:, rows:] = low_rank(kept)[:, :capacity]
            else:
                hop_low[...] = low_rank(kept)[:, :capacity]

    @pl.when(jnp.logical_not(middle))
    def _():
        finish(outside)
        last_up[...] = stacked(outside[part:, :], last_up.shape[1])
        hop_low[...] = jnp.zeros(hop_low.shape, jnp.float32)
        away[:, rows:] = jnp.zeros(hop_low.shape, jnp.float32)


def near_body(low, hop_low, near, low_out, hop_out):
    rows = low.shape[1]
    capacity = hop_low.shape[1]
    low_out[...] = low[...] + near[:, :rows]
    hop_out[...] = jnp.zeros(hop_out.shape, jnp.float32)
    hop_out[:, :capacity] = hop_low[...] + near[:, rows:]


def merge_body(low, far, places, hop_far, hop, out):
    capacity = places.shape[0]
    back = hop[:, :capacity] + hop_far[:, :capacity]
    spread = jnp.zeros(low.shape, jnp.float32)
    for _ in range(3):
        piece = back.astype(jnp.bfloat16)
        back = back - piece.astype(jnp.float32)
        spread = spread + jnp.dot(piece, places[...], preferred_element_type=jnp.float32)
    out[...] = low[...] + far[...] + spread


def finish_body(near, far, keep, got, numbers, ups, last_up, distant, out):
    a = lax.axis_index("adapter")
    rows = out.shape[0]
    columns = last_up.shape[0]
    column = lax.broadcasted_iota(jnp.int32, (ADAPTER_RANK, columns), 1)
    row = lax.broadcasted_iota(jnp.int32, (ADAPTER_RANK, columns), 0)
    repeat = (lax.rem(column, ADAPTER_RANK) == row).astype(jnp.bfloat16)
    shrunk = (near[...] + far[...]).astype(jnp.bfloat16)
    spread = lax.dot_general(shrunk, repeat, TN, preferred_element_type=jnp.float32)
    adapter = adapters(rows, columns)
    middle = (a == 1) | (a == 2)
    mirrored = jnp.where(middle, ups[1].astype(jnp.float32), distant[...].astype(jnp.float32))
    blocks = ((0, ups[0]), (1, ups[2]), (2, last_up[...]), (3, mirrored.astype(jnp.bfloat16)))
    updates = jnp.zeros(out.shape, jnp.float32)
    for bit, up in blocks:
        wanted = numbers[...] - ((a ^ bit) * (columns // ADAPTER_RANK)).astype(jnp.float32)
        chosen = jnp.where(adapter == wanted, spread, 0.0).astype(jnp.bfloat16)
        updates = updates + jnp.dot(chosen, up, preferred_element_type=jnp.float32)
    updates = updates.astype(jnp.bfloat16).astype(jnp.float32)
    base = keep[...] + got[...]
    out[...] = (base + ADAPTER_SCALE * updates).astype(jnp.bfloat16)


def gather(
    tokens,
    base_key_weight,
    stacked_down_weight,
    stacked_up_weight,
    request_adapter_owner,
    request_adapter_slot,
):
    rows, features = tokens.shape
    groups, owners, shares = (lax.axis_size(name) for name in AXES)
    columns = stacked_down_weight.shape[1]
    keys = stacked_up_weight.shape[1]
    part = features // groups
    half = columns // keys
    capacity = -(-row_limit(rows) // ID_ROWS) * ID_ROWS

    def narrow(*dims):
        return jax.ShapeDtypeStruct(dims, jnp.bfloat16)

    def wide(*dims):
        return jax.ShapeDtypeStruct(dims, jnp.float32)

    own = kernel(
        pack_body,
        narrow(part + columns // half, columns),
        (in_hbm(stacked_down_weight), in_hbm(stacked_up_weight)),
        0,
        (pl.ANY, pl.ANY),
        [pltpu.SemaphoreType.DMA((1 + half,))],
    )
    beside = exchange(own, 0, 0, BESIDE)

    tok_own, tok_away = kernel(
        split_body,
        [narrow(rows + ID_ROWS, part)] * groups,
        (
            in_hbm(tokens),
            in_hbm(request_adapter_owner.reshape(1, rows)),
            in_hbm(request_adapter_slot),
            own,
        ),
        0,
        (pl.ANY, pl.ANY, pl.ANY, pl.ANY),
        [
            pltpu.VMEM((1, rows), jnp.int32),
            pltpu.VMEM((rows,), jnp.int32),
            pltpu.SemaphoreType.DMA((4,)),
        ],
    )
    token_parts = [tok_own, exchange(tok_away, 1, 0, SAME)]
    mirror = exchange(after(own, tok_own), 0, 0, MIDDLE)
    hop_own, hop_away, places = kernel(
        functools.partial(hop_body, rows, capacity),
        [narrow(capacity + ID_ROWS, part)] * groups
        + [narrow(capacity, rows)],
        (tok_own, tok_away),
        2 * rows * features * capacity,
    )

    keep, give = kernel(
        functools.partial(base_body, 2, rows),
        [wide(rows, shares * keys // 2)] * 2,
        (tok_own, tok_away, base_key_weight, places),
        2 * rows * features * shares * keys,
        (None, None, None, pl.ANY),
        [pltpu.VMEM((rows, shares * keys), jnp.float32)],
    )
    got = exchange(give, 0, 2, SAME)

    inside = exchange(after(beside, places), 0, 0, MIDDLE)
    outside = exchange(mirror, 0, 0, OUTWARD)
    hops = [
        exchange(after(hop_own, beside), 0, 0, INWARD),
        exchange(hop_away, 1, 0, INWARD),
    ]

    folded, mask, numbers, ups, keep, give = kernel(
        functools.partial(early_body, (0, 3, 1), part, rows),
        [
            wide(groups, rows, LANES),
            wide(groups, rows, columns),
            wide(rows, 1),
            narrow(3, columns, keys),
            wide(rows, keys),
            wide(rows, keys),
        ],
        (*token_parts, own, mirror, beside, keep, got),
        scratch=[pltpu.VMEM((rows, 2 * keys), jnp.float32)],
        light=True,
    )
    distant = exchange(after(stacked_up_weight, folded), 0, 0, ENDS)
    hop_masks, latest = [], folded
    for hop, urgency in zip(hops, HOP_URGENCY):
        latest = kernel(
            functools.partial(hop_mask_body, capacity),
            wide(capacity, columns),
            (hop, latest),
            urgency,
            (None, pl.ANY),
        )
        hop_masks.append(latest)
    low, hop_low, away, last_up = kernel(
        functools.partial(last_body, part, rows, capacity),
        [
            wide(ADAPTER_RANK, rows),
            wide(ADAPTER_RANK, capacity),
            wide(ADAPTER_RANK, rows + capacity),
            narrow(columns, keys),
        ],
        (*token_parts, *hops, *hop_masks, folded, mask, inside, outside),
        2 * groups * (rows + capacity) * part * columns,
    )

    near = exchange(away, 1, 0, SAME)
    low, hop_low = kernel(
        near_body,
        [wide(ADAPTER_RANK, rows), wide(ADAPTER_RANK, rows + LANES)],
        (low, hop_low, after(near, distant)),
    )
    back = exchange(hop_low, 0, 0, BESIDE)
    back_far = exchange(hop_low, 0, 2, BESIDE)
    low_far = exchange(low, 0, 2, SAME)
    low = kernel(
        merge_body,
        wide(ADAPTER_RANK, rows),
        (low, low_far, places, back_far, back),
    )
    got = exchange(give, 0, 1, SAME)
    low_far = exchange(low, 0, 1, SAME)
    return kernel(
        finish_body, narrow(rows, keys), (low, low_far, keep, got, numbers, ups, last_up, distant)
    )


def row_limit(rows):
    return max(2, 3 * rows // (2 * lax.axis_size("adapter")))


def local(*args):
    rows, columns = args[0].shape[0], args[2].shape[1]
    groups, owners, shares = (lax.axis_size(name) for name in AXES)
    fits = owners == OWNERS and groups == 2 and shares == 4
    travels = fits and columns <= groups * row_limit(rows)
    return (gather if travels else dispatch)(*args)


def solution(mesh):
    placed = (
        P(("groups", "adapter"), "mp"),
        P("mp", None),
        P("mp", "adapter"),
        P("adapter", "mp"),
        P(("groups", "adapter"), None),
        P(("groups", "adapter")),
    )
    return jax.shard_map(
        local, mesh=mesh, in_specs=placed, out_specs=P(("groups", "adapter"), "mp"), check_vma=False
    )
```

```python
import functools

import jax
import jax.numpy as jnp
from jax import lax
from jax.experimental import pallas as pl
from jax.experimental.pallas import tpu as pltpu
from jax.sharding import PartitionSpec as P

ADAPTER_RANK = 16


ADAPTER_SCALE = 2.0


def dispatch(
    tokens,
    base_key_weight,
    stacked_down_weight,
    stacked_up_weight,
    request_adapter_owner,
    request_adapter_slot,
):
    rows_here = tokens.shape[0]
    feature_share = tokens.shape[1]
    owner_count = lax.axis_size("adapter")
    capacity = max(2, 3 * rows_here // (2 * owner_count))
    local_adapters = stacked_down_weight.shape[1] // ADAPTER_RANK
    key_output_share = stacked_up_weight.shape[1]
    owners = request_adapter_owner.reshape(-1)
    onehot = (owners[:, None] == jnp.arange(owner_count, dtype=jnp.int32)[None, :]).astype(
        jnp.int32
    )
    before = jnp.sum((jnp.cumsum(onehot, axis=0) - onehot) * onehot, axis=1)
    places = owners * capacity + before
    send_rows = (
        jnp.zeros((owner_count * capacity, feature_share), jnp.bfloat16).at[places].set(tokens)
    )
    send_rows = send_rows.reshape(owner_count, capacity, feature_share)
    send_slots = (
        jnp.full((owner_count * capacity,), -1, jnp.int32).at[places].set(request_adapter_slot)
    )
    send_slots = send_slots.reshape(owner_count, capacity)
    input_rows = lax.all_to_all(send_rows, "adapter", split_axis=0, concat_axis=0, tiled=True)
    slots_in = lax.all_to_all(send_slots, "adapter", split_axis=0, concat_axis=0, tiled=True)
    key_projection_output = jnp.einsum(
        "rzq,qt->rzt", input_rows, stacked_down_weight, preferred_element_type=jnp.float32
    )
    key_projection_output = key_projection_output.reshape(
        input_rows.shape[0], input_rows.shape[1], local_adapters, ADAPTER_RANK
    )
    chosen = slots_in[:, :, None] == jnp.arange(local_adapters, dtype=jnp.int32)[None, None, :]
    partial_low = jnp.sum(jnp.where(chosen[:, :, :, None], key_projection_output, 0.0), axis=2)
    shrunk = lax.psum(partial_low, "mp")
    shrunk_bf = shrunk.astype(jnp.bfloat16)
    returned = lax.all_to_all(shrunk_bf, "adapter", split_axis=0, concat_axis=0, tiled=True)
    low_rows = returned.reshape(owner_count * capacity, ADAPTER_RANK)[places]
    gathered_up_weight = lax.all_gather(stacked_up_weight, "adapter", axis=0, tiled=True)
    adapter_ids = owners * local_adapters + request_adapter_slot
    up_taken = gathered_up_weight.reshape(-1, ADAPTER_RANK, key_output_share)[adapter_ids]
    adapter_updates = jnp.einsum(
        "tr,trk->tk", low_rows, up_taken, preferred_element_type=jnp.float32
    ).astype(jnp.bfloat16)
    base_output_share = lax.psum_scatter(
        lax.dot_general(
            base_key_weight, tokens, (((0,), (1,)), ((), ())), preferred_element_type=jnp.float32
        ),
        "mp",
        scatter_dimension=0,
        tiled=True,
    )
    return (base_output_share.T + ADAPTER_SCALE * adapter_updates.astype(jnp.float32)).astype(
        jnp.bfloat16
    )


AXES = ("groups", "adapter", "mp")
ID_ROWS = 16
HOP_URGENCY = (30 * 10**8, 0)
OWNERS = 4
LANES = 128
NT = (((1,), (1,)), ((), ()))
TN = (((0,), (0,)), ((), ()))


def exchange(x, group_bits, share_bits, owners):
    groups, count, shares = (lax.axis_size(name) for name in AXES)

    def number(g, a, m):
        return (g * count + a) * shares + m

    pairs = [
        (number(g, a, m), number(g ^ group_bits, b, m ^ share_bits))
        for g in range(groups)
        for a, b in owners
        for m in range(shares)
    ]
    return lax.ppermute(x, AXES, pairs)


SAME = tuple((a, a) for a in range(OWNERS))
BESIDE = ((0, 1), (1, 0), (2, 3), (3, 2))
MIDDLE = ((0, 0), (1, 2), (2, 1), (3, 3))
OUTWARD = ((1, 0), (2, 3))
INWARD = ((0, 1), (3, 2))


def after(x, *others):
    return lax.optimization_barrier((x, *others))[0]


def in_hbm(x):
    return pltpu.with_memory_space_constraint(x, pltpu.HBM)


def kernel(body, outs, operands, flops=0, spaces=None, scratch=(), light=False):
    inner = pl.BlockSpec(memory_space=pltpu.VMEM)
    specs = [inner if s is None else pl.BlockSpec(memory_space=s) for s in spaces or ()]
    touched = sum(x.size * x.dtype.itemsize for x in jax.tree.leaves((operands, outs)))
    return pl.pallas_call(
        body,
        out_shape=outs,
        in_specs=specs or [inner] * len(operands),
        out_specs=jax.tree.map(lambda _: inner, outs),
        scratch_shapes=scratch,
        compiler_params=pltpu.CompilerParams(vmem_limit_bytes=16 * 1024 * 1024),
        cost_estimate=pl.CostEstimate(
            flops=flops, bytes_accessed=0 if light else touched, transcendentals=0
        ),
    )(*operands)


def pack_body(down, up, out, sems):
    g = lax.axis_index("groups")
    columns, keys = down.shape[1], up.shape[1]
    count = columns // keys
    size = up.shape[0] // count
    part = out.shape[0] - size
    mine = down.at[pl.ds(pl.multiple_of(g * part, part), part), :]
    copies = [pltpu.make_async_copy(mine, out.at[pl.ds(0, part), :], sems.at[count])]
    for k in range(count):
        copies.append(
            pltpu.make_async_copy(
                up.at[pl.ds(k * size, size), :],
                out.at[pl.ds(part, size), pl.ds(k * keys, keys)],
                sems.at[k],
            )
        )
    for copy in copies:
        copy.start()
    for copy in copies:
        copy.wait()


def split_body(tokens, owner_in, slot_in, _, own, away, owner, slot, sems):
    g = lax.axis_index("groups")
    rows, part = tokens.shape[0], own.shape[1]
    copies = []
    for n, (out, half) in enumerate(((own, g), (away, 1 - g))):
        taken = tokens.at[:, pl.ds(pl.multiple_of(half * part, part), part)]
        copies.append(pltpu.make_async_copy(taken, out.at[pl.ds(0, rows), :], sems.at[n]))
    id_copies = [
        pltpu.make_async_copy(owner_in, owner, sems.at[2]),
        pltpu.make_async_copy(slot_in, slot, sems.at[3]),
    ]
    for copy in id_copies + copies:
        copy.start()
    for copy in id_copies:
        copy.wait()
    row = lax.broadcasted_iota(jnp.int32, (ID_ROWS, rows), 0)
    ids = jnp.where(row == 0, owner[...], jnp.where(row == 1, slot[...].reshape(1, rows), 0))
    ids = ids.astype(jnp.float32).astype(jnp.bfloat16)
    for out in (own, away):
        out[rows:, :rows] = ids
        out[rows:, rows:] = jnp.zeros((ID_ROWS, part - rows), jnp.bfloat16)
    for copy in copies:
        copy.wait()


def hop_body(rows, capacity, own, away, own_out, away_out, places):
    a = lax.axis_index("adapter")
    part = own.shape[1]
    ids = own[rows:, :rows]
    match = (ids.astype(jnp.float32) == (OWNERS - 1 - a).astype(jnp.float32)).astype(jnp.bfloat16)
    earlier = lax.broadcasted_iota(jnp.int32, (rows, rows), 0) < lax.broadcasted_iota(
        jnp.int32, (rows, rows), 1
    )
    rank = jnp.dot(match, earlier.astype(jnp.bfloat16), preferred_element_type=jnp.float32)
    place = lax.broadcasted_iota(jnp.int32, (capacity, rows), 0).astype(jnp.float32)
    taken = (place == rank[0:1]) & (match[0:1].astype(jnp.float32) > 0)
    chosen = taken.astype(jnp.bfloat16)
    places[...] = chosen
    kept = lax.dot_general(ids, chosen, NT, preferred_element_type=jnp.float32)
    for tokens, out in ((own, own_out), (away, away_out)):
        packed = jnp.dot(chosen, tokens[:rows, :], preferred_element_type=jnp.float32)
        out[:capacity, :] = packed.astype(jnp.bfloat16)
        out[capacity:, :] = jnp.zeros((ID_ROWS, part), jnp.bfloat16)
        out[capacity:, :capacity] = kept.astype(jnp.bfloat16)


def base_body(bit, rows, own, away, weights, _, keep, give, base):
    g = lax.axis_index("groups")
    part = own.shape[1]
    total = jnp.zeros(base.shape, jnp.float32)
    for tokens, half in ((own, g), (away, 1 - g)):
        part_weights = weights[pl.ds(pl.multiple_of(half * part, part), part), :]
        total = total + jnp.dot(tokens[:rows, :], part_weights, preferred_element_type=jnp.float32)
    base[...] = total
    halves(base, bit, keep, give)


def halves(base, bit, keep, give):
    m = lax.axis_index("mp")
    width = keep.shape[1]
    side = (m // bit) % 2
    keep[...] = base[:, pl.ds(pl.multiple_of(side * width, width), width)]
    give[...] = base[:, pl.ds(pl.multiple_of((1 - side) * width, width), width)]


def id_columns(rows_ref, start, count):
    eye = (
        lax.broadcasted_iota(jnp.int32, (ID_ROWS, ID_ROWS), 0)
        == lax.broadcasted_iota(jnp.int32, (ID_ROWS, ID_ROWS), 1)
    ).astype(jnp.bfloat16)
    ids = lax.dot_general(
        rows_ref[start : start + ID_ROWS, :count], eye, TN, preferred_element_type=jnp.float32
    )
    return ids[:, 0:1], ids[:, 1:2]


def adapters(rows, columns):
    column = lax.broadcasted_iota(jnp.int32, (rows, columns), 1)
    return (column // ADAPTER_RANK).astype(jnp.float32)


def fold(wide):
    folded = wide[:, :LANES]
    for k in range(1, wide.shape[1] // LANES):
        folded = folded + wide[:, k * LANES : (k + 1) * LANES]
    return folded


def low_rank(folded):
    turned = folded.T
    low = turned[:ADAPTER_RANK]
    for k in range(1, LANES // ADAPTER_RANK):
        low = low + turned[k * ADAPTER_RANK : (k + 1) * ADAPTER_RANK]
    return low


def stacked(wide, keys):
    return jnp.concatenate([wide[:, k : k + keys] for k in range(0, wide.shape[1], keys)], axis=0)


def early_body(bits, part, rows, *refs):
    groups = lax.axis_size("groups")
    a = lax.axis_index("adapter")
    token_refs, rest = refs[:groups], refs[groups:]
    blocks, rest = rest[: len(bits)], rest[len(bits) :]
    kept, got, folded, mask, numbers, ups, keep, give, base = rest
    base[...] = kept[...] + got[...]
    halves(base, 1, keep, give)
    columns = blocks[0].shape[1]
    for n, block in enumerate(blocks):
        ups[n] = stacked(block[part:, :], ups.shape[2])
    adapter = adapters(rows, columns)
    for n, tokens in enumerate(token_refs):
        owner, slot = id_columns(tokens, rows, rows)
        if n == 0:
            numbers[...] = owner * (columns // ADAPTER_RANK) + slot
        right = adapter == slot
        picked = jnp.zeros((rows, columns), jnp.float32)
        for bit, block in zip(bits, blocks):
            wide = jnp.dot(tokens[:rows, :], block[:part, :], preferred_element_type=jnp.float32)
            number = jnp.where((bit != 3) | (a == 1) | (a == 2), a ^ bit, -1)
            picked = jnp.where(owner == number.astype(jnp.float32), wide, picked)
        folded[n] = fold(jnp.where(right, picked, 0.0))
        mask[n] = jnp.where(owner == (a ^ 2).astype(jnp.float32), right.astype(jnp.float32), 0.0)


def hop_mask_body(capacity, hop, _, out):
    _, slot = id_columns(hop, capacity, capacity)
    out[...] = (adapters(capacity, out.shape[1]) == slot).astype(jnp.float32)


def last_body(part, rows, capacity, *refs):
    groups = lax.axis_size("groups")
    a = lax.axis_index("adapter")
    token_refs, rest = refs[:groups], refs[groups:]
    hops, rest = rest[:groups], rest[groups:]
    hop_masks, rest = rest[:groups], rest[groups:]
    folded, mask, inside, outside, low, hop_low, away, last_up = rest
    columns = inside.shape[1]

    def finish(block):
        for n, tokens in enumerate(token_refs):
            wide = jnp.dot(tokens[:rows, :], block[:part, :], preferred_element_type=jnp.float32)
            kept = fold(jnp.where(mask[n] > 0, wide, 0.0))
            if n:
                away[:, :rows] = low_rank(folded[n] + kept)
            else:
                low[...] = low_rank(folded[n] + kept)

    middle = (a == 1) | (a == 2)

    @pl.when(middle)
    def _():
        finish(inside)
        last_up[...] = stacked(inside[part:, :], last_up.shape[1])
        for n, (hop, hop_mask) in enumerate(zip(hops, hop_masks)):
            wide = jnp.dot(hop[:capacity, :], inside[:part, :], preferred_element_type=jnp.float32)
            kept = fold(jnp.where(hop_mask[...] > 0, wide, 0.0))
            rest_rows = -capacity % LANES
            kept = jnp.concatenate([kept, jnp.zeros((rest_rows, LANES), jnp.float32)], axis=0)
            if n:
                away[:, rows:] = low_rank(kept)[:, :capacity]
            else:
                hop_low[...] = low_rank(kept)[:, :capacity]

    @pl.when(jnp.logical_not(middle))
    def _():
        finish(outside)
        last_up[...] = stacked(outside[part:, :], last_up.shape[1])
        hop_low[...] = jnp.zeros(hop_low.shape, jnp.float32)
        away[:, rows:] = jnp.zeros(hop_low.shape, jnp.float32)


def near_body(low, hop_low, near, low_out, hop_out):
    rows = low.shape[1]
    capacity = hop_low.shape[1]
    low_out[...] = low[...] + near[:, :rows]
    hop_out[...] = jnp.zeros(hop_out.shape, jnp.float32)
    hop_out[:, :capacity] = hop_low[...] + near[:, rows:]


def merge_body(low, far, places, hop_far, hop, out):
    capacity = places.shape[0]
    back = hop[:, :capacity] + hop_far[:, :capacity]
    spread = jnp.zeros(low.shape, jnp.float32)
    for _ in range(3):
        piece = back.astype(jnp.bfloat16)
        back = back - piece.astype(jnp.float32)
        spread = spread + jnp.dot(piece, places[...], preferred_element_type=jnp.float32)
    out[...] = low[...] + far[...] + spread


def finish_body(near, far, keep, got, numbers, ups, last_up, distant, out):
    a = lax.axis_index("adapter")
    rows = out.shape[0]
    columns = last_up.shape[0]
    column = lax.broadcasted_iota(jnp.int32, (ADAPTER_RANK, columns), 1)
    row = lax.broadcasted_iota(jnp.int32, (ADAPTER_RANK, columns), 0)
    repeat = (lax.rem(column, ADAPTER_RANK) == row).astype(jnp.bfloat16)
    shrunk = (near[...] + far[...]).astype(jnp.bfloat16)
    spread = lax.dot_general(shrunk, repeat, TN, preferred_element_type=jnp.float32)
    adapter = adapters(rows, columns)
    middle = (a == 1) | (a == 2)
    mirrored = jnp.where(middle, ups[1].astype(jnp.float32), distant[...].astype(jnp.float32))
    blocks = ((0, ups[0]), (1, ups[2]), (2, last_up[...]), (3, mirrored.astype(jnp.bfloat16)))
    updates = jnp.zeros(out.shape, jnp.float32)
    for bit, up in blocks:
        wanted = numbers[...] - ((a ^ bit) * (columns // ADAPTER_RANK)).astype(jnp.float32)
        chosen = jnp.where(adapter == wanted, spread, 0.0).astype(jnp.bfloat16)
        updates = updates + jnp.dot(chosen, up, preferred_element_type=jnp.float32)
    updates = updates.astype(jnp.bfloat16).astype(jnp.float32)
    base = keep[...] + got[...]
    out[...] = (base + ADAPTER_SCALE * updates).astype(jnp.bfloat16)


def gather(
    tokens,
    base_key_weight,
    stacked_down_weight,
    stacked_up_weight,
    request_adapter_owner,
    request_adapter_slot,
):
    rows, features = tokens.shape
    groups, owners, shares = (lax.axis_size(name) for name in AXES)
    columns = stacked_down_weight.shape[1]
    keys = stacked_up_weight.shape[1]
    part = features // groups
    half = columns // keys
    capacity = -(-row_limit(rows) // ID_ROWS) * ID_ROWS

    def narrow(*dims):
        return jax.ShapeDtypeStruct(dims, jnp.bfloat16)

    def wide(*dims):
        return jax.ShapeDtypeStruct(dims, jnp.float32)

    own = kernel(
        pack_body,
        narrow(part + columns // half, columns),
        (in_hbm(stacked_down_weight), in_hbm(stacked_up_weight)),
        0,
        (pl.ANY, pl.ANY),
        [pltpu.SemaphoreType.DMA((1 + half,))],
    )
    beside = exchange(own, 0, 0, BESIDE)

    tok_own, tok_away = kernel(
        split_body,
        [narrow(rows + ID_ROWS, part)] * groups,
        (
            in_hbm(tokens),
            in_hbm(request_adapter_owner.reshape(1, rows)),
            in_hbm(request_adapter_slot),
            own,
        ),
        0,
        (pl.ANY, pl.ANY, pl.ANY, pl.ANY),
        [
            pltpu.VMEM((1, rows), jnp.int32),
            pltpu.VMEM((rows,), jnp.int32),
            pltpu.SemaphoreType.DMA((4,)),
        ],
    )
    token_parts = [tok_own, exchange(tok_away, 1, 0, SAME)]
    mirror = exchange(after(own, tok_own), 0, 0, MIDDLE)
    hop_own, hop_away, places = kernel(
        functools.partial(hop_body, rows, capacity),
        [narrow(capacity + ID_ROWS, part)] * groups
        + [narrow(capacity, rows)],
        (tok_own, tok_away),
        2 * rows * features * capacity,
    )

    keep, give = kernel(
        functools.partial(base_body, 2, rows),
        [wide(rows, shares * keys // 2)] * 2,
        (tok_own, tok_away, base_key_weight, places),
        2 * rows * features * shares * keys,
        (None, None, None, pl.ANY),
        [pltpu.VMEM((rows, shares * keys), jnp.float32)],
    )
    got = exchange(give, 0, 2, SAME)

    inside = exchange(after(beside, places), 0, 0, MIDDLE)
    outside = exchange(mirror, 0, 0, OUTWARD)
    hops = [
        exchange(after(hop_own, beside), 0, 0, INWARD),
        exchange(hop_away, 1, 0, INWARD),
    ]

    folded, mask, numbers, ups, keep, give = kernel(
        functools.partial(early_body, (0, 3, 1), part, rows),
        [
            wide(groups, rows, LANES),
            wide(groups, rows, columns),
            wide(rows, 1),
            narrow(3, columns, keys),
            wide(rows, keys),
            wide(rows, keys),
        ],
        (*token_parts, own, mirror, beside, keep, got),
        scratch=[pltpu.VMEM((rows, 2 * keys), jnp.float32)],
        light=True,
    )
    hop_masks, latest = [], folded
    for hop, urgency in zip(hops, HOP_URGENCY):
        latest = kernel(
            functools.partial(hop_mask_body, capacity),
            wide(capacity, columns),
            (hop, latest),
            urgency,
            (None, pl.ANY),
        )
        hop_masks.append(latest)
    low, hop_low, away, last_up = kernel(
        functools.partial(last_body, part, rows, capacity),
        [
            wide(ADAPTER_RANK, rows),
            wide(ADAPTER_RANK, capacity),
            wide(ADAPTER_RANK, rows + capacity),
            narrow(columns, keys),
        ],
        (*token_parts, *hops, *hop_masks, folded, mask, inside, outside),
        2 * groups * (rows + capacity) * part * columns,
    )

    near = exchange(away, 1, 0, SAME)
    distant = exchange(last_up, 0, 0, BESIDE)
    low, hop_low = kernel(
        near_body,
        [wide(ADAPTER_RANK, rows), wide(ADAPTER_RANK, rows + LANES)],
        (low, hop_low, near),
    )
    back = exchange(hop_low, 0, 0, BESIDE)
    back_far = exchange(hop_low, 0, 2, BESIDE)
    low_far = exchange(low, 0, 2, SAME)
    low = kernel(
        merge_body,
        wide(ADAPTER_RANK, rows),
        (low, low_far, places, back_far, back),
    )
    got = exchange(give, 0, 1, SAME)
    low_far = exchange(low, 0, 1, SAME)
    return kernel(
        finish_body, narrow(rows, keys), (low, low_far, keep, got, numbers, ups, last_up, distant)
    )


def row_limit(rows):
    return max(2, 3 * rows // (2 * lax.axis_size("adapter")))


def local(*args):
    rows, columns = args[0].shape[0], args[2].shape[1]
    groups, owners, shares = (lax.axis_size(name) for name in AXES)
    fits = owners == OWNERS and groups == 2 and shares == 4
    travels = fits and columns <= groups * row_limit(rows)
    return (gather if travels else dispatch)(*args)


def solution(mesh):
    placed = (
        P(("groups", "adapter"), "mp"),
        P("mp", None),
        P("mp", "adapter"),
        P("adapter", "mp"),
        P(("groups", "adapter"), None),
        P(("groups", "adapter")),
    )
    return jax.shard_map(
        local, mesh=mesh, in_specs=placed, out_specs=P(("groups", "adapter"), "mp"), check_vma=False
    )
```

```python
import functools

import jax
import jax.numpy as jnp
from jax import lax
from jax.experimental import pallas as pl
from jax.experimental.pallas import tpu as pltpu
from jax.sharding import PartitionSpec as P

ADAPTER_RANK = 16


ADAPTER_SCALE = 2.0


def dispatch(
    tokens,
    base_key_weight,
    stacked_down_weight,
    stacked_up_weight,
    request_adapter_owner,
    request_adapter_slot,
):
    rows_here = tokens.shape[0]
    feature_share = tokens.shape[1]
    owner_count = lax.axis_size("adapter")
    capacity = max(2, 3 * rows_here // (2 * owner_count))
    local_adapters = stacked_down_weight.shape[1] // ADAPTER_RANK
    key_output_share = stacked_up_weight.shape[1]
    owners = request_adapter_owner.reshape(-1)
    onehot = (owners[:, None] == jnp.arange(owner_count, dtype=jnp.int32)[None, :]).astype(
        jnp.int32
    )
    before = jnp.sum((jnp.cumsum(onehot, axis=0) - onehot) * onehot, axis=1)
    places = owners * capacity + before
    send_rows = (
        jnp.zeros((owner_count * capacity, feature_share), jnp.bfloat16).at[places].set(tokens)
    )
    send_rows = send_rows.reshape(owner_count, capacity, feature_share)
    send_slots = (
        jnp.full((owner_count * capacity,), -1, jnp.int32).at[places].set(request_adapter_slot)
    )
    send_slots = send_slots.reshape(owner_count, capacity)
    input_rows = lax.all_to_all(send_rows, "adapter", split_axis=0, concat_axis=0, tiled=True)
    slots_in = lax.all_to_all(send_slots, "adapter", split_axis=0, concat_axis=0, tiled=True)
    key_projection_output = jnp.einsum(
        "rzq,qt->rzt", input_rows, stacked_down_weight, preferred_element_type=jnp.float32
    )
    key_projection_output = key_projection_output.reshape(
        input_rows.shape[0], input_rows.shape[1], local_adapters, ADAPTER_RANK
    )
    chosen = slots_in[:, :, None] == jnp.arange(local_adapters, dtype=jnp.int32)[None, None, :]
    partial_low = jnp.sum(jnp.where(chosen[:, :, :, None], key_projection_output, 0.0), axis=2)
    shrunk = lax.psum(partial_low, "mp")
    shrunk_bf = shrunk.astype(jnp.bfloat16)
    returned = lax.all_to_all(shrunk_bf, "adapter", split_axis=0, concat_axis=0, tiled=True)
    low_rows = returned.reshape(owner_count * capacity, ADAPTER_RANK)[places]
    gathered_up_weight = lax.all_gather(stacked_up_weight, "adapter", axis=0, tiled=True)
    adapter_ids = owners * local_adapters + request_adapter_slot
    up_taken = gathered_up_weight.reshape(-1, ADAPTER_RANK, key_output_share)[adapter_ids]
    adapter_updates = jnp.einsum(
        "tr,trk->tk", low_rows, up_taken, preferred_element_type=jnp.float32
    ).astype(jnp.bfloat16)
    base_output_share = lax.psum_scatter(
        lax.dot_general(
            base_key_weight, tokens, (((0,), (1,)), ((), ())), preferred_element_type=jnp.float32
        ),
        "mp",
        scatter_dimension=0,
        tiled=True,
    )
    return (base_output_share.T + ADAPTER_SCALE * adapter_updates.astype(jnp.float32)).astype(
        jnp.bfloat16
    )


AXES = ("groups", "adapter", "mp")
ID_ROWS = 16
HOP_URGENCY = (30 * 10**8, 0)
OWNERS = 4
LANES = 128
NT = (((1,), (1,)), ((), ()))
TN = (((0,), (0,)), ((), ()))


def exchange(x, group_bits, share_bits, owners):
    groups, count, shares = (lax.axis_size(name) for name in AXES)

    def number(g, a, m):
        return (g * count + a) * shares + m

    pairs = [
        (number(g, a, m), number(g ^ group_bits, b, m ^ share_bits))
        for g in range(groups)
        for a, b in owners
        for m in range(shares)
    ]
    return lax.ppermute(x, AXES, pairs)


SAME = tuple((a, a) for a in range(OWNERS))
BESIDE = ((0, 1), (1, 0), (2, 3), (3, 2))
MIDDLE = ((0, 0), (1, 2), (2, 1), (3, 3))
OUTWARD = ((1, 0), (2, 3))
INWARD = ((0, 1), (3, 2))


def after(x, *others):
    return lax.optimization_barrier((x, *others))[0]


def in_hbm(x):
    return pltpu.with_memory_space_constraint(x, pltpu.HBM)


def kernel(body, outs, operands, flops=0, spaces=None, scratch=(), light=False):
    inner = pl.BlockSpec(memory_space=pltpu.VMEM)
    specs = [inner if s is None else pl.BlockSpec(memory_space=s) for s in spaces or ()]
    touched = sum(x.size * x.dtype.itemsize for x in jax.tree.leaves((operands, outs)))
    return pl.pallas_call(
        body,
        out_shape=outs,
        in_specs=specs or [inner] * len(operands),
        out_specs=jax.tree.map(lambda _: inner, outs),
        scratch_shapes=scratch,
        compiler_params=pltpu.CompilerParams(vmem_limit_bytes=16 * 1024 * 1024),
        cost_estimate=pl.CostEstimate(
            flops=flops, bytes_accessed=0 if light else touched, transcendentals=0
        ),
    )(*operands)


def pack_body(down, up, out, sems):
    g = lax.axis_index("groups")
    columns, keys = down.shape[1], up.shape[1]
    count = columns // keys
    size = up.shape[0] // count
    part = out.shape[0] - size
    mine = down.at[pl.ds(pl.multiple_of(g * part, part), part), :]
    copies = [pltpu.make_async_copy(mine, out.at[pl.ds(0, part), :], sems.at[count])]
    for k in range(count):
        copies.append(
            pltpu.make_async_copy(
                up.at[pl.ds(k * size, size), :],
                out.at[pl.ds(part, size), pl.ds(k * keys, keys)],
                sems.at[k],
            )
        )
    for copy in copies:
        copy.start()
    for copy in copies:
        copy.wait()


def split_body(tokens, owner_in, slot_in, _, own, away, owner, slot, sems):
    g = lax.axis_index("groups")
    rows, part = tokens.shape[0], own.shape[1]
    copies = []
    for n, (out, half) in enumerate(((own, g), (away, 1 - g))):
        taken = tokens.at[:, pl.ds(pl.multiple_of(half * part, part), part)]
        copies.append(pltpu.make_async_copy(taken, out.at[pl.ds(0, rows), :], sems.at[n]))
    id_copies = [
        pltpu.make_async_copy(owner_in, owner, sems.at[2]),
        pltpu.make_async_copy(slot_in, slot, sems.at[3]),
    ]
    for copy in id_copies + copies:
        copy.start()
    for copy in id_copies:
        copy.wait()
    row = lax.broadcasted_iota(jnp.int32, (ID_ROWS, rows), 0)
    ids = jnp.where(row == 0, owner[...], jnp.where(row == 1, slot[...].reshape(1, rows), 0))
    ids = ids.astype(jnp.float32).astype(jnp.bfloat16)
    for out in (own, away):
        out[rows:, :rows] = ids
        out[rows:, rows:] = jnp.zeros((ID_ROWS, part - rows), jnp.bfloat16)
    for copy in copies:
        copy.wait()


def hop_body(rows, capacity, own, away, own_out, away_out, places):
    a = lax.axis_index("adapter")
    part = own.shape[1]
    ids = own[rows:, :rows]
    match = (ids.astype(jnp.float32) == (OWNERS - 1 - a).astype(jnp.float32)).astype(jnp.bfloat16)
    earlier = lax.broadcasted_iota(jnp.int32, (rows, rows), 0) < lax.broadcasted_iota(
        jnp.int32, (rows, rows), 1
    )
    rank = jnp.dot(match, earlier.astype(jnp.bfloat16), preferred_element_type=jnp.float32)
    place = lax.broadcasted_iota(jnp.int32, (capacity, rows), 0).astype(jnp.float32)
    taken = (place == rank[0:1]) & (match[0:1].astype(jnp.float32) > 0)
    chosen = taken.astype(jnp.bfloat16)
    places[...] = chosen
    kept = lax.dot_general(ids, chosen, NT, preferred_element_type=jnp.float32)
    for tokens, out in ((own, own_out), (away, away_out)):
        packed = jnp.dot(chosen, tokens[:rows, :], preferred_element_type=jnp.float32)
        out[:capacity, :] = packed.astype(jnp.bfloat16)
        out[capacity:, :] = jnp.zeros((ID_ROWS, part), jnp.bfloat16)
        out[capacity:, :capacity] = kept.astype(jnp.bfloat16)


def base_body(bit, rows, own, away, weights, _, keep, give, base):
    g = lax.axis_index("groups")
    part = own.shape[1]
    total = jnp.zeros(base.shape, jnp.float32)
    for tokens, half in ((own, g), (away, 1 - g)):
        part_weights = weights[pl.ds(pl.multiple_of(half * part, part), part), :]
        total = total + jnp.dot(tokens[:rows, :], part_weights, preferred_element_type=jnp.float32)
    base[...] = total
    halves(base, bit, keep, give)


def halves(base, bit, keep, give):
    m = lax.axis_index("mp")
    width = keep.shape[1]
    side = (m // bit) % 2
    keep[...] = base[:, pl.ds(pl.multiple_of(side * width, width), width)]
    give[...] = base[:, pl.ds(pl.multiple_of((1 - side) * width, width), width)]


def id_columns(rows_ref, start, count):
    eye = (
        lax.broadcasted_iota(jnp.int32, (ID_ROWS, ID_ROWS), 0)
        == lax.broadcasted_iota(jnp.int32, (ID_ROWS, ID_ROWS), 1)
    ).astype(jnp.bfloat16)
    ids = lax.dot_general(
        rows_ref[start : start + ID_ROWS, :count], eye, TN, preferred_element_type=jnp.float32
    )
    return ids[:, 0:1], ids[:, 1:2]


def adapters(rows, columns):
    column = lax.broadcasted_iota(jnp.int32, (rows, columns), 1)
    return (column // ADAPTER_RANK).astype(jnp.float32)


def fold(wide):
    folded = wide[:, :LANES]
    for k in range(1, wide.shape[1] // LANES):
        folded = folded + wide[:, k * LANES : (k + 1) * LANES]
    return folded


def low_rank(folded):
    turned = folded.T
    low = turned[:ADAPTER_RANK]
    for k in range(1, LANES // ADAPTER_RANK):
        low = low + turned[k * ADAPTER_RANK : (k + 1) * ADAPTER_RANK]
    return low


def stacked(wide, keys):
    return jnp.concatenate([wide[:, k : k + keys] for k in range(0, wide.shape[1], keys)], axis=0)


def early_body(bits, part, rows, *refs):
    groups = lax.axis_size("groups")
    a = lax.axis_index("adapter")
    token_refs, rest = refs[:groups], refs[groups:]
    blocks, rest = rest[: len(bits)], rest[len(bits) :]
    kept, got, folded, mask, numbers, ups, keep, give, base = rest
    base[...] = kept[...] + got[...]
    halves(base, 1, keep, give)
    columns = blocks[0].shape[1]
    for n, block in enumerate(blocks):
        ups[n] = stacked(block[part:, :], ups.shape[2])
    adapter = adapters(rows, columns)
    for n, tokens in enumerate(token_refs):
        owner, slot = id_columns(tokens, rows, rows)
        if n == 0:
            numbers[...] = owner * (columns // ADAPTER_RANK) + slot
        right = adapter == slot
        picked = jnp.zeros((rows, columns), jnp.float32)
        for bit, block in zip(bits, blocks):
            wide = jnp.dot(tokens[:rows, :], block[:part, :], preferred_element_type=jnp.float32)
            number = jnp.where((bit != 3) | (a == 1) | (a == 2), a ^ bit, -1)
            picked = jnp.where(owner == number.astype(jnp.float32), wide, picked)
        folded[n] = fold(jnp.where(right, picked, 0.0))
        mask[n] = jnp.where(owner == (a ^ 2).astype(jnp.float32), right.astype(jnp.float32), 0.0)


def hop_mask_body(capacity, hop, _, out):
    _, slot = id_columns(hop, capacity, capacity)
    out[...] = (adapters(capacity, out.shape[1]) == slot).astype(jnp.float32)


def last_body(part, rows, capacity, *refs):
    groups = lax.axis_size("groups")
    a = lax.axis_index("adapter")
    token_refs, rest = refs[:groups], refs[groups:]
    hops, rest = rest[:groups], rest[groups:]
    hop_mask, rest = rest[0], rest[1:]
    folded, mask, inside, outside, low, hop_low, away, last_up = rest
    columns = inside.shape[1]

    def finish(block):
        for n, tokens in enumerate(token_refs):
            wide = jnp.dot(tokens[:rows, :], block[:part, :], preferred_element_type=jnp.float32)
            kept = fold(jnp.where(mask[n] > 0, wide, 0.0))
            if n:
                away[:, :rows] = low_rank(folded[n] + kept)
            else:
                low[...] = low_rank(folded[n] + kept)

    middle = (a == 1) | (a == 2)

    @pl.when(middle)
    def _():
        finish(inside)
        last_up[...] = stacked(inside[part:, :], last_up.shape[1])
        for n, hop in enumerate(hops):
            wide = jnp.dot(hop[:capacity, :], inside[:part, :], preferred_element_type=jnp.float32)
            if n:
                _, slot = id_columns(hop, capacity, capacity)
                wanted = adapters(capacity, columns) == slot
            else:
                wanted = hop_mask[...] > 0
            kept = fold(jnp.where(wanted, wide, 0.0))
            rest_rows = -capacity % LANES
            kept = jnp.concatenate([kept, jnp.zeros((rest_rows, LANES), jnp.float32)], axis=0)
            if n:
                away[:, rows:] = low_rank(kept)[:, :capacity]
            else:
                hop_low[...] = low_rank(kept)[:, :capacity]

    @pl.when(jnp.logical_not(middle))
    def _():
        finish(outside)
        last_up[...] = stacked(outside[part:, :], last_up.shape[1])
        hop_low[...] = jnp.zeros(hop_low.shape, jnp.float32)
        away[:, rows:] = jnp.zeros(hop_low.shape, jnp.float32)


def near_body(low, hop_low, near, low_out, hop_out):
    rows = low.shape[1]
    capacity = hop_low.shape[1]
    low_out[...] = low[...] + near[:, :rows]
    hop_out[...] = jnp.zeros(hop_out.shape, jnp.float32)
    hop_out[:, :capacity] = hop_low[...] + near[:, rows:]


def merge_body(low, far, places, hop_far, hop, out):
    capacity = places.shape[0]
    back = hop[:, :capacity] + hop_far[:, :capacity]
    spread = jnp.zeros(low.shape, jnp.float32)
    for _ in range(3):
        piece = back.astype(jnp.bfloat16)
        back = back - piece.astype(jnp.float32)
        spread = spread + jnp.dot(piece, places[...], preferred_element_type=jnp.float32)
    out[...] = low[...] + far[...] + spread


def finish_body(near, far, keep, got, numbers, ups, last_up, distant, out):
    a = lax.axis_index("adapter")
    rows = out.shape[0]
    columns = last_up.shape[0]
    column = lax.broadcasted_iota(jnp.int32, (ADAPTER_RANK, columns), 1)
    row = lax.broadcasted_iota(jnp.int32, (ADAPTER_RANK, columns), 0)
    repeat = (lax.rem(column, ADAPTER_RANK) == row).astype(jnp.bfloat16)
    shrunk = (near[...] + far[...]).astype(jnp.bfloat16)
    spread = lax.dot_general(shrunk, repeat, TN, preferred_element_type=jnp.float32)
    adapter = adapters(rows, columns)
    middle = (a == 1) | (a == 2)
    mirrored = jnp.where(middle, ups[1].astype(jnp.float32), distant[...].astype(jnp.float32))
    blocks = ((0, ups[0]), (1, ups[2]), (2, last_up[...]), (3, mirrored.astype(jnp.bfloat16)))
    updates = jnp.zeros(out.shape, jnp.float32)
    for bit, up in blocks:
        wanted = numbers[...] - ((a ^ bit) * (columns // ADAPTER_RANK)).astype(jnp.float32)
        chosen = jnp.where(adapter == wanted, spread, 0.0).astype(jnp.bfloat16)
        updates = updates + jnp.dot(chosen, up, preferred_element_type=jnp.float32)
    updates = updates.astype(jnp.bfloat16).astype(jnp.float32)
    base = keep[...] + got[...]
    out[...] = (base + ADAPTER_SCALE * updates).astype(jnp.bfloat16)


def gather(
    tokens,
    base_key_weight,
    stacked_down_weight,
    stacked_up_weight,
    request_adapter_owner,
    request_adapter_slot,
):
    rows, features = tokens.shape
    groups, owners, shares = (lax.axis_size(name) for name in AXES)
    columns = stacked_down_weight.shape[1]
    keys = stacked_up_weight.shape[1]
    part = features // groups
    half = columns // keys
    capacity = -(-row_limit(rows) // ID_ROWS) * ID_ROWS

    def narrow(*dims):
        return jax.ShapeDtypeStruct(dims, jnp.bfloat16)

    def wide(*dims):
        return jax.ShapeDtypeStruct(dims, jnp.float32)

    own = kernel(
        pack_body,
        narrow(part + columns // half, columns),
        (in_hbm(stacked_down_weight), in_hbm(stacked_up_weight)),
        0,
        (pl.ANY, pl.ANY),
        [pltpu.SemaphoreType.DMA((1 + half,))],
    )
    beside = exchange(own, 0, 0, BESIDE)
    mirror = exchange(own, 0, 0, MIDDLE)

    tok_own, tok_away = kernel(
        split_body,
        [narrow(rows + ID_ROWS, part)] * groups,
        (
            in_hbm(tokens),
            in_hbm(request_adapter_owner.reshape(1, rows)),
            in_hbm(request_adapter_slot),
            own,
        ),
        0,
        (pl.ANY, pl.ANY, pl.ANY, pl.ANY),
        [
            pltpu.VMEM((1, rows), jnp.int32),
            pltpu.VMEM((rows,), jnp.int32),
            pltpu.SemaphoreType.DMA((4,)),
        ],
    )
    token_parts = [tok_own, exchange(tok_away, 1, 0, SAME)]
    hop_own, hop_away, places = kernel(
        functools.partial(hop_body, rows, capacity),
        [narrow(capacity + ID_ROWS, part)] * groups
        + [narrow(capacity, rows)],
        (tok_own, tok_away),
        2 * rows * features * capacity,
    )

    keep, give = kernel(
        functools.partial(base_body, 2, rows),
        [wide(rows, shares * keys // 2)] * 2,
        (tok_own, tok_away, base_key_weight, places),
        2 * rows * features * shares * keys,
        (None, None, None, pl.ANY),
        [pltpu.VMEM((rows, shares * keys), jnp.float32)],
    )
    got = exchange(give, 0, 2, SAME)

    inside = exchange(after(beside, places), 0, 0, MIDDLE)
    outside = exchange(mirror, 0, 0, OUTWARD)
    hops = [
        exchange(after(hop_own, beside), 0, 0, INWARD),
        exchange(hop_away, 1, 0, INWARD),
    ]

    folded, mask, numbers, ups, keep, give = kernel(
        functools.partial(early_body, (0, 3, 1), part, rows),
        [
            wide(groups, rows, LANES),
            wide(groups, rows, columns),
            wide(rows, 1),
            narrow(3, columns, keys),
            wide(rows, keys),
            wide(rows, keys),
        ],
        (*token_parts, own, mirror, beside, keep, got),
        scratch=[pltpu.VMEM((rows, 2 * keys), jnp.float32)],
        light=True,
    )
    hop_masks, latest = [], folded
    for hop, urgency in zip(hops[:1], HOP_URGENCY):
        latest = kernel(
            functools.partial(hop_mask_body, capacity),
            wide(capacity, columns),
            (hop, latest),
            urgency,
            (None, pl.ANY),
        )
        hop_masks.append(latest)
    low, hop_low, away, last_up = kernel(
        functools.partial(last_body, part, rows, capacity),
        [
            wide(ADAPTER_RANK, rows),
            wide(ADAPTER_RANK, capacity),
            wide(ADAPTER_RANK, rows + capacity),
            narrow(columns, keys),
        ],
        (*token_parts, *hops, *hop_masks, folded, mask, inside, outside),
        2 * groups * (rows + capacity) * part * columns,
    )

    near = exchange(away, 1, 0, SAME)
    distant = exchange(last_up, 0, 0, BESIDE)
    low, hop_low = kernel(
        near_body,
        [wide(ADAPTER_RANK, rows), wide(ADAPTER_RANK, rows + LANES)],
        (low, hop_low, near),
    )
    back = exchange(hop_low, 0, 0, BESIDE)
    back_far = exchange(hop_low, 0, 2, BESIDE)
    low_far = exchange(low, 0, 2, SAME)
    low = kernel(
        merge_body,
        wide(ADAPTER_RANK, rows),
        (low, low_far, places, back_far, back),
    )
    got = exchange(give, 0, 1, SAME)
    low_far = exchange(low, 0, 1, SAME)
    return kernel(
        finish_body, narrow(rows, keys), (low, low_far, keep, got, numbers, ups, last_up, distant)
    )


def row_limit(rows):
    return max(2, 3 * rows // (2 * lax.axis_size("adapter")))


def local(*args):
    rows, columns = args[0].shape[0], args[2].shape[1]
    groups, owners, shares = (lax.axis_size(name) for name in AXES)
    fits = owners == OWNERS and groups == 2 and shares == 4
    travels = fits and columns <= groups * row_limit(rows)
    return (gather if travels else dispatch)(*args)


def solution(mesh):
    placed = (
        P(("groups", "adapter"), "mp"),
        P("mp", None),
        P("mp", "adapter"),
        P("adapter", "mp"),
        P(("groups", "adapter"), None),
        P(("groups", "adapter")),
    )
    return jax.shard_map(
        local, mesh=mesh, in_specs=placed, out_specs=P(("groups", "adapter"), "mp"), check_vma=False
    )
```

```python
import functools

import jax
import jax.numpy as jnp
from jax import lax
from jax.experimental import pallas as pl
from jax.experimental.pallas import tpu as pltpu
from jax.sharding import PartitionSpec as P

ADAPTER_RANK = 16


ADAPTER_SCALE = 2.0


def dispatch(
    tokens,
    base_key_weight,
    stacked_down_weight,
    stacked_up_weight,
    request_adapter_owner,
    request_adapter_slot,
):
    rows_here = tokens.shape[0]
    feature_share = tokens.shape[1]
    owner_count = lax.axis_size("adapter")
    capacity = max(2, 3 * rows_here // (2 * owner_count))
    local_adapters = stacked_down_weight.shape[1] // ADAPTER_RANK
    key_output_share = stacked_up_weight.shape[1]
    owners = request_adapter_owner.reshape(-1)
    onehot = (owners[:, None] == jnp.arange(owner_count, dtype=jnp.int32)[None, :]).astype(
        jnp.int32
    )
    before = jnp.sum((jnp.cumsum(onehot, axis=0) - onehot) * onehot, axis=1)
    places = owners * capacity + before
    send_rows = (
        jnp.zeros((owner_count * capacity, feature_share), jnp.bfloat16).at[places].set(tokens)
    )
    send_rows = send_rows.reshape(owner_count, capacity, feature_share)
    send_slots = (
        jnp.full((owner_count * capacity,), -1, jnp.int32).at[places].set(request_adapter_slot)
    )
    send_slots = send_slots.reshape(owner_count, capacity)
    input_rows = lax.all_to_all(send_rows, "adapter", split_axis=0, concat_axis=0, tiled=True)
    slots_in = lax.all_to_all(send_slots, "adapter", split_axis=0, concat_axis=0, tiled=True)
    key_projection_output = jnp.einsum(
        "rzq,qt->rzt", input_rows, stacked_down_weight, preferred_element_type=jnp.float32
    )
    key_projection_output = key_projection_output.reshape(
        input_rows.shape[0], input_rows.shape[1], local_adapters, ADAPTER_RANK
    )
    chosen = slots_in[:, :, None] == jnp.arange(local_adapters, dtype=jnp.int32)[None, None, :]
    partial_low = jnp.sum(jnp.where(chosen[:, :, :, None], key_projection_output, 0.0), axis=2)
    shrunk = lax.psum(partial_low, "mp")
    shrunk_bf = shrunk.astype(jnp.bfloat16)
    returned = lax.all_to_all(shrunk_bf, "adapter", split_axis=0, concat_axis=0, tiled=True)
    low_rows = returned.reshape(owner_count * capacity, ADAPTER_RANK)[places]
    gathered_up_weight = lax.all_gather(stacked_up_weight, "adapter", axis=0, tiled=True)
    adapter_ids = owners * local_adapters + request_adapter_slot
    up_taken = gathered_up_weight.reshape(-1, ADAPTER_RANK, key_output_share)[adapter_ids]
    adapter_updates = jnp.einsum(
        "tr,trk->tk", low_rows, up_taken, preferred_element_type=jnp.float32
    ).astype(jnp.bfloat16)
    base_output_share = lax.psum_scatter(
        lax.dot_general(
            base_key_weight, tokens, (((0,), (1,)), ((), ())), preferred_element_type=jnp.float32
        ),
        "mp",
        scatter_dimension=0,
        tiled=True,
    )
    return (base_output_share.T + ADAPTER_SCALE * adapter_updates.astype(jnp.float32)).astype(
        jnp.bfloat16
    )


AXES = ("groups", "adapter", "mp")
ID_ROWS = 16
HOP_URGENCY = (30 * 10**8, 0)
OWNERS = 4
LANES = 128
NT = (((1,), (1,)), ((), ()))
TN = (((0,), (0,)), ((), ()))


def exchange(x, group_bits, share_bits, owners):
    groups, count, shares = (lax.axis_size(name) for name in AXES)

    def number(g, a, m):
        return (g * count + a) * shares + m

    pairs = [
        (number(g, a, m), number(g ^ group_bits, b, m ^ share_bits))
        for g in range(groups)
        for a, b in owners
        for m in range(shares)
    ]
    return lax.ppermute(x, AXES, pairs)


SAME = tuple((a, a) for a in range(OWNERS))
BESIDE = ((0, 1), (1, 0), (2, 3), (3, 2))
MIDDLE = ((0, 0), (1, 2), (2, 1), (3, 3))
OUTWARD = ((1, 0), (2, 3))
INWARD = ((0, 1), (3, 2))


def after(x, *others):
    return lax.optimization_barrier((x, *others))[0]


def in_hbm(x):
    return pltpu.with_memory_space_constraint(x, pltpu.HBM)


def kernel(body, outs, operands, flops=0, spaces=None, scratch=(), light=False):
    inner = pl.BlockSpec(memory_space=pltpu.VMEM)
    specs = [inner if s is None else pl.BlockSpec(memory_space=s) for s in spaces or ()]
    touched = sum(x.size * x.dtype.itemsize for x in jax.tree.leaves((operands, outs)))
    return pl.pallas_call(
        body,
        out_shape=outs,
        in_specs=specs or [inner] * len(operands),
        out_specs=jax.tree.map(lambda _: inner, outs),
        scratch_shapes=scratch,
        compiler_params=pltpu.CompilerParams(vmem_limit_bytes=16 * 1024 * 1024),
        cost_estimate=pl.CostEstimate(
            flops=flops, bytes_accessed=0 if light else touched, transcendentals=0
        ),
    )(*operands)


def pack_body(down, up, out, sems):
    g = lax.axis_index("groups")
    columns, keys = down.shape[1], up.shape[1]
    count = columns // keys
    size = up.shape[0] // count
    part = out.shape[0] - size
    mine = down.at[pl.ds(pl.multiple_of(g * part, part), part), :]
    copies = [pltpu.make_async_copy(mine, out.at[pl.ds(0, part), :], sems.at[count])]
    for k in range(count):
        copies.append(
            pltpu.make_async_copy(
                up.at[pl.ds(k * size, size), :],
                out.at[pl.ds(part, size), pl.ds(k * keys, keys)],
                sems.at[k],
            )
        )
    for copy in copies:
        copy.start()
    for copy in copies:
        copy.wait()


def split_body(tokens, owner_in, slot_in, _, own, away, owner, slot, sems):
    g = lax.axis_index("groups")
    rows, part = tokens.shape[0], own.shape[1]
    copies = []
    for n, (out, half) in enumerate(((own, g), (away, 1 - g))):
        taken = tokens.at[:, pl.ds(pl.multiple_of(half * part, part), part)]
        copies.append(pltpu.make_async_copy(taken, out.at[pl.ds(0, rows), :], sems.at[n]))
    id_copies = [
        pltpu.make_async_copy(owner_in, owner, sems.at[2]),
        pltpu.make_async_copy(slot_in, slot, sems.at[3]),
    ]
    for copy in id_copies + copies:
        copy.start()
    for copy in id_copies:
        copy.wait()
    row = lax.broadcasted_iota(jnp.int32, (ID_ROWS, rows), 0)
    ids = jnp.where(row == 0, owner[...], jnp.where(row == 1, slot[...].reshape(1, rows), 0))
    ids = ids.astype(jnp.float32).astype(jnp.bfloat16)
    for out in (own, away):
        out[rows:, :rows] = ids
        out[rows:, rows:] = jnp.zeros((ID_ROWS, part - rows), jnp.bfloat16)
    for copy in copies:
        copy.wait()


def hop_body(rows, capacity, own, away, own_out, away_out, places):
    a = lax.axis_index("adapter")
    part = own.shape[1]
    ids = own[rows:, :rows]
    match = (ids.astype(jnp.float32) == (OWNERS - 1 - a).astype(jnp.float32)).astype(jnp.bfloat16)
    earlier = lax.broadcasted_iota(jnp.int32, (rows, rows), 0) < lax.broadcasted_iota(
        jnp.int32, (rows, rows), 1
    )
    rank = jnp.dot(match, earlier.astype(jnp.bfloat16), preferred_element_type=jnp.float32)
    place = lax.broadcasted_iota(jnp.int32, (capacity, rows), 0).astype(jnp.float32)
    taken = (place == rank[0:1]) & (match[0:1].astype(jnp.float32) > 0)
    chosen = taken.astype(jnp.bfloat16)
    places[...] = chosen
    kept = lax.dot_general(ids, chosen, NT, preferred_element_type=jnp.float32)
    for tokens, out in ((own, own_out), (away, away_out)):
        packed = jnp.dot(chosen, tokens[:rows, :], preferred_element_type=jnp.float32)
        out[:capacity, :] = packed.astype(jnp.bfloat16)
        out[capacity:, :] = jnp.zeros((ID_ROWS, part), jnp.bfloat16)
        out[capacity:, :capacity] = kept.astype(jnp.bfloat16)


def base_body(bit, rows, own, away, weights, _, keep, give, base):
    g = lax.axis_index("groups")
    part = own.shape[1]
    total = jnp.zeros(base.shape, jnp.float32)
    for tokens, half in ((own, g), (away, 1 - g)):
        part_weights = weights[pl.ds(pl.multiple_of(half * part, part), part), :]
        total = total + jnp.dot(tokens[:rows, :], part_weights, preferred_element_type=jnp.float32)
    base[...] = total
    halves(base, bit, keep, give)


def halves(base, bit, keep, give):
    m = lax.axis_index("mp")
    width = keep.shape[1]
    side = (m // bit) % 2
    keep[...] = base[:, pl.ds(pl.multiple_of(side * width, width), width)]
    give[...] = base[:, pl.ds(pl.multiple_of((1 - side) * width, width), width)]


def id_columns(rows_ref, start, count):
    eye = (
        lax.broadcasted_iota(jnp.int32, (ID_ROWS, ID_ROWS), 0)
        == lax.broadcasted_iota(jnp.int32, (ID_ROWS, ID_ROWS), 1)
    ).astype(jnp.bfloat16)
    ids = lax.dot_general(
        rows_ref[start : start + ID_ROWS, :count], eye, TN, preferred_element_type=jnp.float32
    )
    return ids[:, 0:1], ids[:, 1:2]


def adapters(rows, columns):
    column = lax.broadcasted_iota(jnp.int32, (rows, columns), 1)
    return (column // ADAPTER_RANK).astype(jnp.float32)


def fold(wide):
    folded = wide[:, :LANES]
    for k in range(1, wide.shape[1] // LANES):
        folded = folded + wide[:, k * LANES : (k + 1) * LANES]
    return folded


def low_rank(folded):
    turned = folded.T
    low = turned[:ADAPTER_RANK]
    for k in range(1, LANES // ADAPTER_RANK):
        low = low + turned[k * ADAPTER_RANK : (k + 1) * ADAPTER_RANK]
    return low


def stacked(wide, keys):
    return jnp.concatenate([wide[:, k : k + keys] for k in range(0, wide.shape[1], keys)], axis=0)


def early_body(bits, part, rows, *refs):
    groups = lax.axis_size("groups")
    a = lax.axis_index("adapter")
    token_refs, rest = refs[:groups], refs[groups:]
    blocks, rest = rest[: len(bits)], rest[len(bits) :]
    kept, got, folded, mask, numbers, ups, keep, give, base = rest
    base[...] = kept[...] + got[...]
    halves(base, 1, keep, give)
    columns = blocks[0].shape[1]
    for n, block in enumerate(blocks):
        ups[n] = stacked(block[part:, :], ups.shape[2])
    adapter = adapters(rows, columns)
    for n, tokens in enumerate(token_refs):
        owner, slot = id_columns(tokens, rows, rows)
        if n == 0:
            numbers[...] = owner * (columns // ADAPTER_RANK) + slot
        right = adapter == slot
        picked = jnp.zeros((rows, columns), jnp.float32)
        for bit, block in zip(bits, blocks):
            wide = jnp.dot(tokens[:rows, :], block[:part, :], preferred_element_type=jnp.float32)
            number = jnp.where((bit != 3) | (a == 1) | (a == 2), a ^ bit, -1)
            picked = jnp.where(owner == number.astype(jnp.float32), wide, picked)
        folded[n] = fold(jnp.where(right, picked, 0.0))
        mask[n] = jnp.where(owner == (a ^ 2).astype(jnp.float32), right.astype(jnp.float32), 0.0)


def hop_mask_body(capacity, hop, _, out):
    _, slot = id_columns(hop, capacity, capacity)
    out[...] = (adapters(capacity, out.shape[1]) == slot).astype(jnp.float32)


def last_body(part, rows, capacity, *refs):
    groups = lax.axis_size("groups")
    a = lax.axis_index("adapter")
    token_refs, rest = refs[:groups], refs[groups:]
    hops, rest = rest[:groups], rest[groups:]
    hop_masks, rest = rest[:groups], rest[groups:]
    folded, mask, inside, outside, mine, away, last_up = rest
    sums = (mine, away)
    columns = inside.shape[1]

    def finish(block):
        for n, tokens in enumerate(token_refs):
            wide = jnp.dot(tokens[:rows, :], block[:part, :], preferred_element_type=jnp.float32)
            kept = fold(jnp.where(mask[n] > 0, wide, 0.0))
            sums[n][:, :rows] = low_rank(folded[n] + kept)

    middle = (a == 1) | (a == 2)

    @pl.when(middle)
    def _():
        finish(inside)
        last_up[...] = stacked(inside[part:, :], last_up.shape[1])
        for n, (hop, hop_mask) in enumerate(zip(hops, hop_masks)):
            wide = jnp.dot(hop[:capacity, :], inside[:part, :], preferred_element_type=jnp.float32)
            kept = fold(jnp.where(hop_mask[...] > 0, wide, 0.0))
            rest_rows = -capacity % LANES
            kept = jnp.concatenate([kept, jnp.zeros((rest_rows, LANES), jnp.float32)], axis=0)
            sums[n][:, rows:] = low_rank(kept)[:, :capacity]

    @pl.when(jnp.logical_not(middle))
    def _():
        finish(outside)
        last_up[...] = stacked(outside[part:, :], last_up.shape[1])
        for total in sums:
            total[:, rows:] = jnp.zeros((ADAPTER_RANK, capacity), jnp.float32)


def near_body(mine, near_far, near, far, low, hop):
    rows = low.shape[1]
    low[...] = (mine[:, :rows] + far[:, :rows]) + (near[:, :rows] + near_far[:, :rows])
    hop[...] = (mine[:, rows:] + far[:, rows:]) + (near[:, rows:] + near_far[:, rows:])


def merge_body(low, places, hop, out):
    back = hop[...]
    spread = jnp.zeros(low.shape, jnp.float32)
    for _ in range(3):
        piece = back.astype(jnp.bfloat16)
        back = back - piece.astype(jnp.float32)
        spread = spread + jnp.dot(piece, places[...], preferred_element_type=jnp.float32)
    out[...] = low[...] + spread


def finish_body(near, far, keep, got, numbers, ups, last_up, distant, out):
    a = lax.axis_index("adapter")
    rows = out.shape[0]
    columns = last_up.shape[0]
    column = lax.broadcasted_iota(jnp.int32, (ADAPTER_RANK, columns), 1)
    row = lax.broadcasted_iota(jnp.int32, (ADAPTER_RANK, columns), 0)
    repeat = (lax.rem(column, ADAPTER_RANK) == row).astype(jnp.bfloat16)
    shrunk = (near[...] + far[...]).astype(jnp.bfloat16)
    spread = lax.dot_general(shrunk, repeat, TN, preferred_element_type=jnp.float32)
    adapter = adapters(rows, columns)
    middle = (a == 1) | (a == 2)
    mirrored = jnp.where(middle, ups[1].astype(jnp.float32), distant[...].astype(jnp.float32))
    blocks = ((0, ups[0]), (1, ups[2]), (2, last_up[...]), (3, mirrored.astype(jnp.bfloat16)))
    updates = jnp.zeros(out.shape, jnp.float32)
    for bit, up in blocks:
        wanted = numbers[...] - ((a ^ bit) * (columns // ADAPTER_RANK)).astype(jnp.float32)
        chosen = jnp.where(adapter == wanted, spread, 0.0).astype(jnp.bfloat16)
        updates = updates + jnp.dot(chosen, up, preferred_element_type=jnp.float32)
    updates = updates.astype(jnp.bfloat16).astype(jnp.float32)
    base = keep[...] + got[...]
    out[...] = (base + ADAPTER_SCALE * updates).astype(jnp.bfloat16)


def gather(
    tokens,
    base_key_weight,
    stacked_down_weight,
    stacked_up_weight,
    request_adapter_owner,
    request_adapter_slot,
):
    rows, features = tokens.shape
    groups, owners, shares = (lax.axis_size(name) for name in AXES)
    columns = stacked_down_weight.shape[1]
    keys = stacked_up_weight.shape[1]
    part = features // groups
    half = columns // keys
    capacity = -(-row_limit(rows) // ID_ROWS) * ID_ROWS

    def narrow(*dims):
        return jax.ShapeDtypeStruct(dims, jnp.bfloat16)

    def wide(*dims):
        return jax.ShapeDtypeStruct(dims, jnp.float32)

    own = kernel(
        pack_body,
        narrow(part + columns // half, columns),
        (in_hbm(stacked_down_weight), in_hbm(stacked_up_weight)),
        0,
        (pl.ANY, pl.ANY),
        [pltpu.SemaphoreType.DMA((1 + half,))],
    )
    beside = exchange(own, 0, 0, BESIDE)

    tok_own, tok_away = kernel(
        split_body,
        [narrow(rows + ID_ROWS, part)] * groups,
        (
            in_hbm(tokens),
            in_hbm(request_adapter_owner.reshape(1, rows)),
            in_hbm(request_adapter_slot),
            own,
        ),
        0,
        (pl.ANY, pl.ANY, pl.ANY, pl.ANY),
        [
            pltpu.VMEM((1, rows), jnp.int32),
            pltpu.VMEM((rows,), jnp.int32),
            pltpu.SemaphoreType.DMA((4,)),
        ],
    )
    token_parts = [tok_own, exchange(tok_away, 1, 0, SAME)]
    mirror = exchange(after(own, tok_own), 0, 0, MIDDLE)
    hop_own, hop_away, places = kernel(
        functools.partial(hop_body, rows, capacity),
        [narrow(capacity + ID_ROWS, part)] * groups
        + [narrow(capacity, rows)],
        (tok_own, tok_away),
        2 * rows * features * capacity,
    )

    keep, give = kernel(
        functools.partial(base_body, 2, rows),
        [wide(rows, shares * keys // 2)] * 2,
        (tok_own, tok_away, base_key_weight, places),
        2 * rows * features * shares * keys,
        (None, None, None, pl.ANY),
        [pltpu.VMEM((rows, shares * keys), jnp.float32)],
    )
    got = exchange(give, 0, 2, SAME)

    inside = exchange(after(beside, places), 0, 0, MIDDLE)
    outside = exchange(mirror, 0, 0, OUTWARD)
    hops = [
        exchange(after(hop_own, beside), 0, 0, INWARD),
        exchange(hop_away, 1, 0, INWARD),
    ]

    folded, mask, numbers, ups, keep, give = kernel(
        functools.partial(early_body, (0, 3, 1), part, rows),
        [
            wide(groups, rows, LANES),
            wide(groups, rows, columns),
            wide(rows, 1),
            narrow(3, columns, keys),
            wide(rows, keys),
            wide(rows, keys),
        ],
        (*token_parts, own, mirror, beside, keep, got),
        scratch=[pltpu.VMEM((rows, 2 * keys), jnp.float32)],
        light=True,
    )
    hop_masks, latest = [], folded
    for hop, urgency in zip(hops, HOP_URGENCY):
        latest = kernel(
            functools.partial(hop_mask_body, capacity),
            wide(capacity, columns),
            (hop, latest),
            urgency,
            (None, pl.ANY),
        )
        hop_masks.append(latest)
    mine, away, last_up = kernel(
        functools.partial(last_body, part, rows, capacity),
        [wide(ADAPTER_RANK, rows + capacity)] * groups + [narrow(columns, keys)],
        (*token_parts, *hops, *hop_masks, folded, mask, inside, outside),
        2 * groups * (rows + capacity) * part * columns,
    )

    near_far = exchange(away, 1, 2, SAME)
    near = exchange(away, 1, 0, SAME)
    far = exchange(mine, 0, 2, SAME)
    distant = exchange(last_up, 0, 0, BESIDE)
    low, hop_low = kernel(
        near_body,
        [wide(ADAPTER_RANK, rows), wide(ADAPTER_RANK, capacity)],
        (mine, near_far, near, far),
    )
    back = exchange(hop_low, 0, 0, BESIDE)
    low = kernel(merge_body, wide(ADAPTER_RANK, rows), (low, places, back))
    got = exchange(give, 0, 1, SAME)
    low_far = exchange(low, 0, 1, SAME)
    return kernel(
        finish_body, narrow(rows, keys), (low, low_far, keep, got, numbers, ups, last_up, distant)
    )


def row_limit(rows):
    return max(2, 3 * rows // (2 * lax.axis_size("adapter")))


def local(*args):
    rows, columns = args[0].shape[0], args[2].shape[1]
    groups, owners, shares = (lax.axis_size(name) for name in AXES)
    fits = owners == OWNERS and groups == 2 and shares == 4
    travels = fits and columns <= groups * row_limit(rows)
    return (gather if travels else dispatch)(*args)


def solution(mesh):
    placed = (
        P(("groups", "adapter"), "mp"),
        P("mp", None),
        P("mp", "adapter"),
        P("adapter", "mp"),
        P(("groups", "adapter"), None),
        P(("groups", "adapter")),
    )
    return jax.shard_map(
        local, mesh=mesh, in_specs=placed, out_specs=P(("groups", "adapter"), "mp"), check_vma=False
    )
```

```python
import functools

import jax
import jax.numpy as jnp
from jax import lax
from jax.experimental import pallas as pl
from jax.experimental.pallas import tpu as pltpu
from jax.sharding import PartitionSpec as P

ADAPTER_RANK = 16


ADAPTER_SCALE = 2.0


def dispatch(
    tokens,
    base_key_weight,
    stacked_down_weight,
    stacked_up_weight,
    request_adapter_owner,
    request_adapter_slot,
):
    rows_here = tokens.shape[0]
    feature_share = tokens.shape[1]
    owner_count = lax.axis_size("adapter")
    capacity = max(2, 3 * rows_here // (2 * owner_count))
    local_adapters = stacked_down_weight.shape[1] // ADAPTER_RANK
    key_output_share = stacked_up_weight.shape[1]
    owners = request_adapter_owner.reshape(-1)
    onehot = (owners[:, None] == jnp.arange(owner_count, dtype=jnp.int32)[None, :]).astype(
        jnp.int32
    )
    before = jnp.sum((jnp.cumsum(onehot, axis=0) - onehot) * onehot, axis=1)
    places = owners * capacity + before
    send_rows = (
        jnp.zeros((owner_count * capacity, feature_share), jnp.bfloat16).at[places].set(tokens)
    )
    send_rows = send_rows.reshape(owner_count, capacity, feature_share)
    send_slots = (
        jnp.full((owner_count * capacity,), -1, jnp.int32).at[places].set(request_adapter_slot)
    )
    send_slots = send_slots.reshape(owner_count, capacity)
    input_rows = lax.all_to_all(send_rows, "adapter", split_axis=0, concat_axis=0, tiled=True)
    slots_in = lax.all_to_all(send_slots, "adapter", split_axis=0, concat_axis=0, tiled=True)
    key_projection_output = jnp.einsum(
        "rzq,qt->rzt", input_rows, stacked_down_weight, preferred_element_type=jnp.float32
    )
    key_projection_output = key_projection_output.reshape(
        input_rows.shape[0], input_rows.shape[1], local_adapters, ADAPTER_RANK
    )
    chosen = slots_in[:, :, None] == jnp.arange(local_adapters, dtype=jnp.int32)[None, None, :]
    partial_low = jnp.sum(jnp.where(chosen[:, :, :, None], key_projection_output, 0.0), axis=2)
    shrunk = lax.psum(partial_low, "mp")
    shrunk_bf = shrunk.astype(jnp.bfloat16)
    returned = lax.all_to_all(shrunk_bf, "adapter", split_axis=0, concat_axis=0, tiled=True)
    low_rows = returned.reshape(owner_count * capacity, ADAPTER_RANK)[places]
    gathered_up_weight = lax.all_gather(stacked_up_weight, "adapter", axis=0, tiled=True)
    adapter_ids = owners * local_adapters + request_adapter_slot
    up_taken = gathered_up_weight.reshape(-1, ADAPTER_RANK, key_output_share)[adapter_ids]
    adapter_updates = jnp.einsum(
        "tr,trk->tk", low_rows, up_taken, preferred_element_type=jnp.float32
    ).astype(jnp.bfloat16)
    base_output_share = lax.psum_scatter(
        lax.dot_general(
            base_key_weight, tokens, (((0,), (1,)), ((), ())), preferred_element_type=jnp.float32
        ),
        "mp",
        scatter_dimension=0,
        tiled=True,
    )
    return (base_output_share.T + ADAPTER_SCALE * adapter_updates.astype(jnp.float32)).astype(
        jnp.bfloat16
    )


AXES = ("groups", "adapter", "mp")
ID_ROWS = 16
HOP_URGENCY = (30 * 10**8, 0)
OWNERS = 4
LANES = 128
NT = (((1,), (1,)), ((), ()))
TN = (((0,), (0,)), ((), ()))


def exchange(x, group_bits, share_bits, owners):
    groups, count, shares = (lax.axis_size(name) for name in AXES)

    def number(g, a, m):
        return (g * count + a) * shares + m

    pairs = [
        (number(g, a, m), number(g ^ group_bits, b, m ^ share_bits))
        for g in range(groups)
        for a, b in owners
        for m in range(shares)
    ]
    return lax.ppermute(x, AXES, pairs)


SAME = tuple((a, a) for a in range(OWNERS))
BESIDE = ((0, 1), (1, 0), (2, 3), (3, 2))
MIDDLE = ((0, 0), (1, 2), (2, 1), (3, 3))
OUTWARD = ((1, 0), (2, 3))
INWARD = ((0, 1), (3, 2))


def after(x, *others):
    return lax.optimization_barrier((x, *others))[0]


def in_hbm(x):
    return pltpu.with_memory_space_constraint(x, pltpu.HBM)


def kernel(body, outs, operands, flops=0, spaces=None, scratch=(), light=False):
    inner = pl.BlockSpec(memory_space=pltpu.VMEM)
    specs = [inner if s is None else pl.BlockSpec(memory_space=s) for s in spaces or ()]
    touched = sum(x.size * x.dtype.itemsize for x in jax.tree.leaves((operands, outs)))
    return pl.pallas_call(
        body,
        out_shape=outs,
        in_specs=specs or [inner] * len(operands),
        out_specs=jax.tree.map(lambda _: inner, outs),
        scratch_shapes=scratch,
        compiler_params=pltpu.CompilerParams(vmem_limit_bytes=16 * 1024 * 1024),
        cost_estimate=pl.CostEstimate(
            flops=flops, bytes_accessed=0 if light else touched, transcendentals=0
        ),
    )(*operands)


def pack_body(down, up, out, sems):
    g = lax.axis_index("groups")
    columns, keys = down.shape[1], up.shape[1]
    count = columns // keys
    size = up.shape[0] // count
    part = out.shape[0] - size
    mine = down.at[pl.ds(pl.multiple_of(g * part, part), part), :]
    copies = [pltpu.make_async_copy(mine, out.at[pl.ds(0, part), :], sems.at[count])]
    for k in range(count):
        copies.append(
            pltpu.make_async_copy(
                up.at[pl.ds(k * size, size), :],
                out.at[pl.ds(part, size), pl.ds(k * keys, keys)],
                sems.at[k],
            )
        )
    for copy in copies:
        copy.start()
    for copy in copies:
        copy.wait()


def split_body(tokens, owner_in, slot_in, _, own, away, owner, slot, sems):
    g = lax.axis_index("groups")
    rows, part = tokens.shape[0], own.shape[1]
    copies = []
    for n, (out, half) in enumerate(((own, g), (away, 1 - g))):
        taken = tokens.at[:, pl.ds(pl.multiple_of(half * part, part), part)]
        copies.append(pltpu.make_async_copy(taken, out.at[pl.ds(0, rows), :], sems.at[n]))
    id_copies = [
        pltpu.make_async_copy(owner_in, owner, sems.at[2]),
        pltpu.make_async_copy(slot_in, slot, sems.at[3]),
    ]
    for copy in id_copies + copies:
        copy.start()
    for copy in id_copies:
        copy.wait()
    row = lax.broadcasted_iota(jnp.int32, (ID_ROWS, rows), 0)
    ids = jnp.where(row == 0, owner[...], jnp.where(row == 1, slot[...].reshape(1, rows), 0))
    ids = ids.astype(jnp.float32).astype(jnp.bfloat16)
    for out in (own, away):
        out[rows:, :rows] = ids
        out[rows:, rows:] = jnp.zeros((ID_ROWS, part - rows), jnp.bfloat16)
    for copy in copies:
        copy.wait()


def hop_body(rows, capacity, own, away, own_out, away_out, places):
    a = lax.axis_index("adapter")
    part = own.shape[1]
    ids = own[rows:, :rows]
    match = (ids.astype(jnp.float32) == (OWNERS - 1 - a).astype(jnp.float32)).astype(jnp.bfloat16)
    earlier = lax.broadcasted_iota(jnp.int32, (rows, rows), 0) < lax.broadcasted_iota(
        jnp.int32, (rows, rows), 1
    )
    rank = jnp.dot(match, earlier.astype(jnp.bfloat16), preferred_element_type=jnp.float32)
    place = lax.broadcasted_iota(jnp.int32, (capacity, rows), 0).astype(jnp.float32)
    taken = (place == rank[0:1]) & (match[0:1].astype(jnp.float32) > 0)
    chosen = taken.astype(jnp.bfloat16)
    places[...] = chosen
    kept = lax.dot_general(ids, chosen, NT, preferred_element_type=jnp.float32)
    for tokens, out in ((own, own_out), (away, away_out)):
        packed = jnp.dot(chosen, tokens[:rows, :], preferred_element_type=jnp.float32)
        out[:capacity, :] = packed.astype(jnp.bfloat16)
        out[capacity:, :] = jnp.zeros((ID_ROWS, part), jnp.bfloat16)
        out[capacity:, :capacity] = kept.astype(jnp.bfloat16)


def base_body(bit, rows, own, away, weights, _, keep, give, base):
    g = lax.axis_index("groups")
    part = own.shape[1]
    total = jnp.zeros(base.shape, jnp.float32)
    for tokens, half in ((own, g), (away, 1 - g)):
        part_weights = weights[pl.ds(pl.multiple_of(half * part, part), part), :]
        total = total + jnp.dot(tokens[:rows, :], part_weights, preferred_element_type=jnp.float32)
    base[...] = total
    halves(base, bit, keep, give)


def halves(base, bit, keep, give):
    m = lax.axis_index("mp")
    width = keep.shape[1]
    side = (m // bit) % 2
    keep[...] = base[:, pl.ds(pl.multiple_of(side * width, width), width)]
    give[...] = base[:, pl.ds(pl.multiple_of((1 - side) * width, width), width)]


def id_columns(rows_ref, start, count):
    eye = (
        lax.broadcasted_iota(jnp.int32, (ID_ROWS, ID_ROWS), 0)
        == lax.broadcasted_iota(jnp.int32, (ID_ROWS, ID_ROWS), 1)
    ).astype(jnp.bfloat16)
    ids = lax.dot_general(
        rows_ref[start : start + ID_ROWS, :count], eye, TN, preferred_element_type=jnp.float32
    )
    return ids[:, 0:1], ids[:, 1:2]


def adapters(rows, columns):
    column = lax.broadcasted_iota(jnp.int32, (rows, columns), 1)
    return (column // ADAPTER_RANK).astype(jnp.float32)


def fold(wide):
    folded = wide[:, :LANES]
    for k in range(1, wide.shape[1] // LANES):
        folded = folded + wide[:, k * LANES : (k + 1) * LANES]
    return folded


def low_rank(folded):
    turned = folded.T
    low = turned[:ADAPTER_RANK]
    for k in range(1, LANES // ADAPTER_RANK):
        low = low + turned[k * ADAPTER_RANK : (k + 1) * ADAPTER_RANK]
    return low


def stacked(wide, keys):
    return jnp.concatenate([wide[:, k : k + keys] for k in range(0, wide.shape[1], keys)], axis=0)


def early_body(bits, part, rows, *refs):
    groups = lax.axis_size("groups")
    a = lax.axis_index("adapter")
    token_refs, rest = refs[:groups], refs[groups:]
    blocks, rest = rest[: len(bits)], rest[len(bits) :]
    kept, got, folded, mask, numbers, ups, keep, give, base = rest
    base[...] = kept[...] + got[...]
    halves(base, 1, keep, give)
    columns = blocks[0].shape[1]
    for n, block in enumerate(blocks):
        ups[n] = stacked(block[part:, :], ups.shape[2])
    adapter = adapters(rows, columns)
    for n, tokens in enumerate(token_refs):
        owner, slot = id_columns(tokens, rows, rows)
        if n == 0:
            numbers[...] = owner * (columns // ADAPTER_RANK) + slot
        right = adapter == slot
        picked = jnp.zeros((rows, columns), jnp.float32)
        for bit, block in zip(bits, blocks):
            wide = jnp.dot(tokens[:rows, :], block[:part, :], preferred_element_type=jnp.float32)
            number = jnp.where((bit != 3) | (a == 1) | (a == 2), a ^ bit, -1)
            picked = jnp.where(owner == number.astype(jnp.float32), wide, picked)
        folded[n] = fold(jnp.where(right, picked, 0.0))
        mask[n] = jnp.where(owner == (a ^ 2).astype(jnp.float32), right.astype(jnp.float32), 0.0)


def hop_mask_body(capacity, hop, _, out):
    _, slot = id_columns(hop, capacity, capacity)
    out[...] = (adapters(capacity, out.shape[1]) == slot).astype(jnp.float32)


def last_body(part, rows, capacity, *refs):
    groups = lax.axis_size("groups")
    a = lax.axis_index("adapter")
    token_refs, rest = refs[:groups], refs[groups:]
    hops, rest = rest[:groups], rest[groups:]
    hop_mask, rest = rest[0], rest[1:]
    folded, mask, inside, outside, low, hop_low, away, last_up = rest
    columns = inside.shape[1]

    def finish(block):
        for n, tokens in enumerate(token_refs):
            wide = jnp.dot(tokens[:rows, :], block[:part, :], preferred_element_type=jnp.float32)
            kept = fold(jnp.where(mask[n] > 0, wide, 0.0))
            if n:
                away[:, :rows] = low_rank(folded[n] + kept)
            else:
                low[...] = low_rank(folded[n] + kept)

    middle = (a == 1) | (a == 2)

    @pl.when(middle)
    def _():
        finish(inside)
        last_up[...] = stacked(inside[part:, :], last_up.shape[1])
        for n, hop in enumerate(hops):
            wide = jnp.dot(hop[:capacity, :], inside[:part, :], preferred_element_type=jnp.float32)
            if n:
                _, slot = id_columns(hop, capacity, capacity)
                wanted = adapters(capacity, columns) == slot
            else:
                wanted = hop_mask[...] > 0
            kept = fold(jnp.where(wanted, wide, 0.0))
            rest_rows = -capacity % LANES
            kept = jnp.concatenate([kept, jnp.zeros((rest_rows, LANES), jnp.float32)], axis=0)
            if n:
                away[:, rows:] = low_rank(kept)[:, :capacity]
            else:
                hop_low[...] = low_rank(kept)[:, :capacity]

    @pl.when(jnp.logical_not(middle))
    def _():
        finish(outside)
        last_up[...] = stacked(outside[part:, :], last_up.shape[1])
        hop_low[...] = jnp.zeros(hop_low.shape, jnp.float32)
        away[:, rows:] = jnp.zeros(hop_low.shape, jnp.float32)


def near_body(low, hop_low, near, low_out, hop_out, hop_wide):
    rows = low.shape[1]
    capacity = hop_low.shape[1]
    low_out[...] = low[...] + near[:, :rows]
    hop = hop_low[...] + near[:, rows:]
    hop_out[...] = hop
    hop_wide[...] = jnp.zeros(hop_wide.shape, jnp.float32)
    hop_wide[:, :capacity] = hop


def merge_body(low, far, places, hop_far, hop, out):
    capacity = places.shape[0]
    back = hop[...] + hop_far[:, :capacity]
    spread = jnp.zeros(low.shape, jnp.float32)
    for _ in range(3):
        piece = back.astype(jnp.bfloat16)
        back = back - piece.astype(jnp.float32)
        spread = spread + jnp.dot(piece, places[...], preferred_element_type=jnp.float32)
    out[...] = low[...] + far[...] + spread


def finish_body(near, far, keep, got, numbers, ups, last_up, distant, out):
    a = lax.axis_index("adapter")
    rows = out.shape[0]
    columns = last_up.shape[0]
    column = lax.broadcasted_iota(jnp.int32, (ADAPTER_RANK, columns), 1)
    row = lax.broadcasted_iota(jnp.int32, (ADAPTER_RANK, columns), 0)
    repeat = (lax.rem(column, ADAPTER_RANK) == row).astype(jnp.bfloat16)
    shrunk = (near[...] + far[...]).astype(jnp.bfloat16)
    spread = lax.dot_general(shrunk, repeat, TN, preferred_element_type=jnp.float32)
    adapter = adapters(rows, columns)
    middle = (a == 1) | (a == 2)
    mirrored = jnp.where(middle, ups[1].astype(jnp.float32), distant[...].astype(jnp.float32))
    blocks = ((0, ups[0]), (1, ups[2]), (2, last_up[...]), (3, mirrored.astype(jnp.bfloat16)))
    updates = jnp.zeros(out.shape, jnp.float32)
    for bit, up in blocks:
        wanted = numbers[...] - ((a ^ bit) * (columns // ADAPTER_RANK)).astype(jnp.float32)
        chosen = jnp.where(adapter == wanted, spread, 0.0).astype(jnp.bfloat16)
        updates = updates + jnp.dot(chosen, up, preferred_element_type=jnp.float32)
    updates = updates.astype(jnp.bfloat16).astype(jnp.float32)
    base = keep[...] + got[...]
    out[...] = (base + ADAPTER_SCALE * updates).astype(jnp.bfloat16)


def gather(
    tokens,
    base_key_weight,
    stacked_down_weight,
    stacked_up_weight,
    request_adapter_owner,
    request_adapter_slot,
):
    rows, features = tokens.shape
    groups, owners, shares = (lax.axis_size(name) for name in AXES)
    columns = stacked_down_weight.shape[1]
    keys = stacked_up_weight.shape[1]
    part = features // groups
    half = columns // keys
    capacity = -(-row_limit(rows) // ID_ROWS) * ID_ROWS

    def narrow(*dims):
        return jax.ShapeDtypeStruct(dims, jnp.bfloat16)

    def wide(*dims):
        return jax.ShapeDtypeStruct(dims, jnp.float32)

    own = kernel(
        pack_body,
        narrow(part + columns // half, columns),
        (in_hbm(stacked_down_weight), in_hbm(stacked_up_weight)),
        0,
        (pl.ANY, pl.ANY),
        [pltpu.SemaphoreType.DMA((1 + half,))],
    )
    beside = exchange(own, 0, 0, BESIDE)
    mirror = exchange(own, 0, 0, MIDDLE)

    tok_own, tok_away = kernel(
        split_body,
        [narrow(rows + ID_ROWS, part)] * groups,
        (
            in_hbm(tokens),
            in_hbm(request_adapter_owner.reshape(1, rows)),
            in_hbm(request_adapter_slot),
            own,
        ),
        0,
        (pl.ANY, pl.ANY, pl.ANY, pl.ANY),
        [
            pltpu.VMEM((1, rows), jnp.int32),
            pltpu.VMEM((rows,), jnp.int32),
            pltpu.SemaphoreType.DMA((4,)),
        ],
    )
    token_parts = [tok_own, exchange(tok_away, 1, 0, SAME)]
    hop_own, hop_away, places = kernel(
        functools.partial(hop_body, rows, capacity),
        [narrow(capacity + ID_ROWS, part)] * groups
        + [narrow(capacity, rows)],
        (tok_own, tok_away),
        2 * rows * features * capacity,
    )

    keep, give = kernel(
        functools.partial(base_body, 2, rows),
        [wide(rows, shares * keys // 2)] * 2,
        (tok_own, tok_away, base_key_weight, places),
        2 * rows * features * shares * keys,
        (None, None, None, pl.ANY),
        [pltpu.VMEM((rows, shares * keys), jnp.float32)],
    )
    got = exchange(give, 0, 2, SAME)

    inside = exchange(after(beside, places), 0, 0, MIDDLE)
    outside = exchange(mirror, 0, 0, OUTWARD)
    hops = [
        exchange(after(hop_own, beside), 0, 0, INWARD),
        exchange(hop_away, 1, 0, INWARD),
    ]

    folded, mask, numbers, ups, keep, give = kernel(
        functools.partial(early_body, (0, 3, 1), part, rows),
        [
            wide(groups, rows, LANES),
            wide(groups, rows, columns),
            wide(rows, 1),
            narrow(3, columns, keys),
            wide(rows, keys),
            wide(rows, keys),
        ],
        (*token_parts, own, mirror, beside, keep, got),
        scratch=[pltpu.VMEM((rows, 2 * keys), jnp.float32)],
        light=True,
    )
    hop_masks, latest = [], folded
    for hop, urgency in zip(hops[:1], HOP_URGENCY):
        latest = kernel(
            functools.partial(hop_mask_body, capacity),
            wide(capacity, columns),
            (hop, latest),
            urgency,
            (None, pl.ANY),
        )
        hop_masks.append(latest)
    low, hop_low, away, last_up = kernel(
        functools.partial(last_body, part, rows, capacity),
        [
            wide(ADAPTER_RANK, rows),
            wide(ADAPTER_RANK, capacity),
            wide(ADAPTER_RANK, rows + capacity),
            narrow(columns, keys),
        ],
        (*token_parts, *hops, *hop_masks, folded, mask, inside, outside),
        2 * groups * (rows + capacity) * part * columns,
    )

    near = exchange(away, 1, 0, SAME)
    distant = exchange(last_up, 0, 0, BESIDE)
    low, hop_low, hop_wide = kernel(
        near_body,
        [
            wide(ADAPTER_RANK, rows),
            wide(ADAPTER_RANK, capacity),
            wide(ADAPTER_RANK, rows + LANES),
        ],
        (low, hop_low, near),
    )
    back = exchange(hop_low, 0, 0, BESIDE)
    back_far = exchange(hop_wide, 0, 2, BESIDE)
    low_far = exchange(low, 0, 2, SAME)
    low = kernel(
        merge_body,
        wide(ADAPTER_RANK, rows),
        (low, low_far, places, back_far, back),
    )
    got = exchange(give, 0, 1, SAME)
    low_far = exchange(low, 0, 1, SAME)
    return kernel(
        finish_body, narrow(rows, keys), (low, low_far, keep, got, numbers, ups, last_up, distant)
    )


def row_limit(rows):
    return max(2, 3 * rows // (2 * lax.axis_size("adapter")))


def local(*args):
    rows, columns = args[0].shape[0], args[2].shape[1]
    groups, owners, shares = (lax.axis_size(name) for name in AXES)
    fits = owners == OWNERS and groups == 2 and shares == 4
    travels = fits and columns <= groups * row_limit(rows)
    return (gather if travels else dispatch)(*args)


def solution(mesh):
    placed = (
        P(("groups", "adapter"), "mp"),
        P("mp", None),
        P("mp", "adapter"),
        P("adapter", "mp"),
        P(("groups", "adapter"), None),
        P(("groups", "adapter")),
    )
    return jax.shard_map(
        local, mesh=mesh, in_specs=placed, out_specs=P(("groups", "adapter"), "mp"), check_vma=False
    )
```

```python
import functools

import jax
import jax.numpy as jnp
from jax import lax
from jax.experimental import pallas as pl
from jax.experimental.pallas import tpu as pltpu
from jax.sharding import PartitionSpec as P

ADAPTER_RANK = 16


ADAPTER_SCALE = 2.0


def dispatch(
    tokens,
    base_key_weight,
    stacked_down_weight,
    stacked_up_weight,
    request_adapter_owner,
    request_adapter_slot,
):
    rows_here = tokens.shape[0]
    feature_share = tokens.shape[1]
    owner_count = lax.axis_size("adapter")
    capacity = max(2, 3 * rows_here // (2 * owner_count))
    local_adapters = stacked_down_weight.shape[1] // ADAPTER_RANK
    key_output_share = stacked_up_weight.shape[1]
    owners = request_adapter_owner.reshape(-1)
    onehot = (owners[:, None] == jnp.arange(owner_count, dtype=jnp.int32)[None, :]).astype(
        jnp.int32
    )
    before = jnp.sum((jnp.cumsum(onehot, axis=0) - onehot) * onehot, axis=1)
    places = owners * capacity + before
    send_rows = (
        jnp.zeros((owner_count * capacity, feature_share), jnp.bfloat16).at[places].set(tokens)
    )
    send_rows = send_rows.reshape(owner_count, capacity, feature_share)
    send_slots = (
        jnp.full((owner_count * capacity,), -1, jnp.int32).at[places].set(request_adapter_slot)
    )
    send_slots = send_slots.reshape(owner_count, capacity)
    input_rows = lax.all_to_all(send_rows, "adapter", split_axis=0, concat_axis=0, tiled=True)
    slots_in = lax.all_to_all(send_slots, "adapter", split_axis=0, concat_axis=0, tiled=True)
    key_projection_output = jnp.einsum(
        "rzq,qt->rzt", input_rows, stacked_down_weight, preferred_element_type=jnp.float32
    )
    key_projection_output = key_projection_output.reshape(
        input_rows.shape[0], input_rows.shape[1], local_adapters, ADAPTER_RANK
    )
    chosen = slots_in[:, :, None] == jnp.arange(local_adapters, dtype=jnp.int32)[None, None, :]
    partial_low = jnp.sum(jnp.where(chosen[:, :, :, None], key_projection_output, 0.0), axis=2)
    shrunk = lax.psum(partial_low, "mp")
    shrunk_bf = shrunk.astype(jnp.bfloat16)
    returned = lax.all_to_all(shrunk_bf, "adapter", split_axis=0, concat_axis=0, tiled=True)
    low_rows = returned.reshape(owner_count * capacity, ADAPTER_RANK)[places]
    gathered_up_weight = lax.all_gather(stacked_up_weight, "adapter", axis=0, tiled=True)
    adapter_ids = owners * local_adapters + request_adapter_slot
    up_taken = gathered_up_weight.reshape(-1, ADAPTER_RANK, key_output_share)[adapter_ids]
    adapter_updates = jnp.einsum(
        "tr,trk->tk", low_rows, up_taken, preferred_element_type=jnp.float32
    ).astype(jnp.bfloat16)
    base_output_share = lax.psum_scatter(
        lax.dot_general(
            base_key_weight, tokens, (((0,), (1,)), ((), ())), preferred_element_type=jnp.float32
        ),
        "mp",
        scatter_dimension=0,
        tiled=True,
    )
    return (base_output_share.T + ADAPTER_SCALE * adapter_updates.astype(jnp.float32)).astype(
        jnp.bfloat16
    )


AXES = ("groups", "adapter", "mp")
ID_ROWS = 16
HOP_URGENCY = (30 * 10**8, 0)
OWNERS = 4
LANES = 128
NT = (((1,), (1,)), ((), ()))
TN = (((0,), (0,)), ((), ()))


def exchange(x, group_bits, share_bits, owners):
    groups, count, shares = (lax.axis_size(name) for name in AXES)

    def number(g, a, m):
        return (g * count + a) * shares + m

    pairs = [
        (number(g, a, m), number(g ^ group_bits, b, m ^ share_bits))
        for g in range(groups)
        for a, b in owners
        for m in range(shares)
    ]
    return lax.ppermute(x, AXES, pairs)


SAME = tuple((a, a) for a in range(OWNERS))
BESIDE = ((0, 1), (1, 0), (2, 3), (3, 2))
MIDDLE = ((0, 0), (1, 2), (2, 1), (3, 3))
OUTWARD = ((1, 0), (2, 3))
INWARD = ((0, 1), (3, 2))


def after(x, *others):
    return lax.optimization_barrier((x, *others))[0]


def in_hbm(x):
    return pltpu.with_memory_space_constraint(x, pltpu.HBM)


def kernel(body, outs, operands, flops=0, spaces=None, scratch=(), light=False):
    inner = pl.BlockSpec(memory_space=pltpu.VMEM)
    specs = [inner if s is None else pl.BlockSpec(memory_space=s) for s in spaces or ()]
    touched = sum(x.size * x.dtype.itemsize for x in jax.tree.leaves((operands, outs)))
    return pl.pallas_call(
        body,
        out_shape=outs,
        in_specs=specs or [inner] * len(operands),
        out_specs=jax.tree.map(lambda _: inner, outs),
        scratch_shapes=scratch,
        compiler_params=pltpu.CompilerParams(vmem_limit_bytes=16 * 1024 * 1024),
        cost_estimate=pl.CostEstimate(
            flops=flops, bytes_accessed=0 if light else touched, transcendentals=0
        ),
    )(*operands)


def pack_body(down, up, out, sems):
    g = lax.axis_index("groups")
    columns, keys = down.shape[1], up.shape[1]
    count = columns // keys
    size = up.shape[0] // count
    part = out.shape[0] - size
    mine = down.at[pl.ds(pl.multiple_of(g * part, part), part), :]
    copies = [pltpu.make_async_copy(mine, out.at[pl.ds(0, part), :], sems.at[count])]
    for k in range(count):
        copies.append(
            pltpu.make_async_copy(
                up.at[pl.ds(k * size, size), :],
                out.at[pl.ds(part, size), pl.ds(k * keys, keys)],
                sems.at[k],
            )
        )
    for copy in copies:
        copy.start()
    for copy in copies:
        copy.wait()


def split_body(tokens, owner_in, slot_in, _, own, away, owner, slot, sems):
    g = lax.axis_index("groups")
    rows, part = tokens.shape[0], own.shape[1]
    copies = []
    for n, (out, half) in enumerate(((own, g), (away, 1 - g))):
        taken = tokens.at[:, pl.ds(pl.multiple_of(half * part, part), part)]
        copies.append(pltpu.make_async_copy(taken, out.at[pl.ds(0, rows), :], sems.at[n]))
    id_copies = [
        pltpu.make_async_copy(owner_in, owner, sems.at[2]),
        pltpu.make_async_copy(slot_in, slot, sems.at[3]),
    ]
    for copy in id_copies + copies:
        copy.start()
    for copy in id_copies:
        copy.wait()
    row = lax.broadcasted_iota(jnp.int32, (ID_ROWS, rows), 0)
    ids = jnp.where(row == 0, owner[...], jnp.where(row == 1, slot[...].reshape(1, rows), 0))
    ids = ids.astype(jnp.float32).astype(jnp.bfloat16)
    for out in (own, away):
        out[rows:, :rows] = ids
        out[rows:, rows:] = jnp.zeros((ID_ROWS, part - rows), jnp.bfloat16)
    for copy in copies:
        copy.wait()


def packed_places(ids, capacity):
    a = lax.axis_index("adapter")
    rows = ids.shape[1]
    match = (ids.astype(jnp.float32) == (OWNERS - 1 - a).astype(jnp.float32)).astype(jnp.bfloat16)
    earlier = lax.broadcasted_iota(jnp.int32, (rows, rows), 0) < lax.broadcasted_iota(
        jnp.int32, (rows, rows), 1
    )
    rank = jnp.dot(match, earlier.astype(jnp.bfloat16), preferred_element_type=jnp.float32)
    place = lax.broadcasted_iota(jnp.int32, (capacity, rows), 0).astype(jnp.float32)
    taken = (place == rank[0:1]) & (match[0:1].astype(jnp.float32) > 0)
    return taken.astype(jnp.bfloat16)


def hop_body(rows, capacity, own, away, own_out, away_out, places):
    part = own.shape[1]
    ids = own[rows:, :rows]
    chosen = packed_places(ids, capacity)
    places[...] = chosen
    kept = lax.dot_general(ids, chosen, NT, preferred_element_type=jnp.float32)
    for tokens, out in ((own, own_out), (away, away_out)):
        packed = jnp.dot(chosen, tokens[:rows, :], preferred_element_type=jnp.float32)
        out[:capacity, :] = packed.astype(jnp.bfloat16)
        out[capacity:, :] = jnp.zeros((ID_ROWS, part), jnp.bfloat16)
        out[capacity:, :capacity] = kept.astype(jnp.bfloat16)


def base_body(bit, rows, own, away, weights, _, keep, give, base):
    g = lax.axis_index("groups")
    part = own.shape[1]
    total = jnp.zeros(base.shape, jnp.float32)
    for tokens, half in ((own, g), (away, 1 - g)):
        part_weights = weights[pl.ds(pl.multiple_of(half * part, part), part), :]
        total = total + jnp.dot(tokens[:rows, :], part_weights, preferred_element_type=jnp.float32)
    base[...] = total
    halves(base, bit, keep, give)


def halves(base, bit, keep, give):
    m = lax.axis_index("mp")
    width = keep.shape[1]
    side = (m // bit) % 2
    keep[...] = base[:, pl.ds(pl.multiple_of(side * width, width), width)]
    give[...] = base[:, pl.ds(pl.multiple_of((1 - side) * width, width), width)]


def id_columns(rows_ref, start, count):
    eye = (
        lax.broadcasted_iota(jnp.int32, (ID_ROWS, ID_ROWS), 0)
        == lax.broadcasted_iota(jnp.int32, (ID_ROWS, ID_ROWS), 1)
    ).astype(jnp.bfloat16)
    ids = lax.dot_general(
        rows_ref[start : start + ID_ROWS, :count], eye, TN, preferred_element_type=jnp.float32
    )
    return ids[:, 0:1], ids[:, 1:2]


def adapters(rows, columns):
    column = lax.broadcasted_iota(jnp.int32, (rows, columns), 1)
    return (column // ADAPTER_RANK).astype(jnp.float32)


def fold(wide):
    folded = wide[:, :LANES]
    for k in range(1, wide.shape[1] // LANES):
        folded = folded + wide[:, k * LANES : (k + 1) * LANES]
    return folded


def low_rank(folded):
    turned = folded.T
    low = turned[:ADAPTER_RANK]
    for k in range(1, LANES // ADAPTER_RANK):
        low = low + turned[k * ADAPTER_RANK : (k + 1) * ADAPTER_RANK]
    return low


def stacked(wide, keys):
    return jnp.concatenate([wide[:, k : k + keys] for k in range(0, wide.shape[1], keys)], axis=0)


def early_body(bits, part, rows, *refs):
    groups = lax.axis_size("groups")
    a = lax.axis_index("adapter")
    token_refs, rest = refs[:groups], refs[groups:]
    blocks, rest = rest[: len(bits)], rest[len(bits) :]
    kept, got, folded, mask, numbers, ups, keep, give, places, base = rest
    places[...] = packed_places(token_refs[1][rows:, :rows], places.shape[0])
    base[...] = kept[...] + got[...]
    halves(base, 1, keep, give)
    columns = blocks[0].shape[1]
    for n, block in enumerate(blocks):
        ups[n] = stacked(block[part:, :], ups.shape[2])
    adapter = adapters(rows, columns)
    for n, tokens in enumerate(token_refs):
        owner, slot = id_columns(tokens, rows, rows)
        if n == 0:
            numbers[...] = owner * (columns // ADAPTER_RANK) + slot
        right = adapter == slot
        picked = jnp.zeros((rows, columns), jnp.float32)
        for bit, block in zip(bits, blocks):
            wide = jnp.dot(tokens[:rows, :], block[:part, :], preferred_element_type=jnp.float32)
            number = jnp.where((bit != 3) | (a == 1) | (a == 2), a ^ bit, -1)
            picked = jnp.where(owner == number.astype(jnp.float32), wide, picked)
        folded[n] = fold(jnp.where(right, picked, 0.0))
        mask[n] = jnp.where(owner == (a ^ 2).astype(jnp.float32), right.astype(jnp.float32), 0.0)


def hop_mask_body(capacity, hop, _, out):
    _, slot = id_columns(hop, capacity, capacity)
    out[...] = (adapters(capacity, out.shape[1]) == slot).astype(jnp.float32)


def last_body(part, rows, capacity, *refs):
    groups = lax.axis_size("groups")
    a = lax.axis_index("adapter")
    token_refs, rest = refs[:groups], refs[groups:]
    hops, rest = rest[:groups], rest[groups:]
    hop_mask, rest = rest[0], rest[1:]
    folded, mask, inside, outside, low, low_away, hop_sums, last_up = rest
    columns = inside.shape[1]

    def finish(block):
        for n, tokens in enumerate(token_refs):
            wide = jnp.dot(tokens[:rows, :], block[:part, :], preferred_element_type=jnp.float32)
            kept = fold(jnp.where(mask[n] > 0, wide, 0.0))
            (low, low_away)[n][...] = low_rank(folded[n] + kept)

    middle = (a == 1) | (a == 2)

    @pl.when(middle)
    def _():
        finish(inside)
        last_up[...] = stacked(inside[part:, :], last_up.shape[1])
        for n, hop in enumerate(hops):
            wide = jnp.dot(hop[:capacity, :], inside[:part, :], preferred_element_type=jnp.float32)
            if n:
                _, slot = id_columns(hop, capacity, capacity)
                wanted = adapters(capacity, columns) == slot
            else:
                wanted = hop_mask[...] > 0
            kept = fold(jnp.where(wanted, wide, 0.0))
            rest_rows = -capacity % LANES
            kept = jnp.concatenate([kept, jnp.zeros((rest_rows, LANES), jnp.float32)], axis=0)
            hop_sums[n] = low_rank(kept)[:, :capacity]

    @pl.when(jnp.logical_not(middle))
    def _():
        finish(outside)
        last_up[...] = stacked(outside[part:, :], last_up.shape[1])
        hop_sums[...] = jnp.zeros(hop_sums.shape, jnp.float32)


def merge_body(low, low_away, places, places_away, hop_sums, out, out_away):
    for n, (own, where, total) in enumerate(
        ((low, places, out), (low_away, places_away, out_away))
    ):
        back = hop_sums[n]
        spread = jnp.zeros(own.shape, jnp.float32)
        for _ in range(3):
            piece = back.astype(jnp.bfloat16)
            back = back - piece.astype(jnp.float32)
            spread = spread + jnp.dot(piece, where[...], preferred_element_type=jnp.float32)
        total[...] = own[...] + spread


def near_body(low, near_far, near, far, out):
    out[...] = (low[...] + far[...]) + (near[...] + near_far[...])


def finish_body(near, far, keep, got, numbers, ups, last_up, distant, out):
    a = lax.axis_index("adapter")
    rows = out.shape[0]
    columns = last_up.shape[0]
    column = lax.broadcasted_iota(jnp.int32, (ADAPTER_RANK, columns), 1)
    row = lax.broadcasted_iota(jnp.int32, (ADAPTER_RANK, columns), 0)
    repeat = (lax.rem(column, ADAPTER_RANK) == row).astype(jnp.bfloat16)
    shrunk = (near[...] + far[...]).astype(jnp.bfloat16)
    spread = lax.dot_general(shrunk, repeat, TN, preferred_element_type=jnp.float32)
    adapter = adapters(rows, columns)
    middle = (a == 1) | (a == 2)
    mirrored = jnp.where(middle, ups[1].astype(jnp.float32), distant[...].astype(jnp.float32))
    blocks = ((0, ups[0]), (1, ups[2]), (2, last_up[...]), (3, mirrored.astype(jnp.bfloat16)))
    updates = jnp.zeros(out.shape, jnp.float32)
    for bit, up in blocks:
        wanted = numbers[...] - ((a ^ bit) * (columns // ADAPTER_RANK)).astype(jnp.float32)
        chosen = jnp.where(adapter == wanted, spread, 0.0).astype(jnp.bfloat16)
        updates = updates + jnp.dot(chosen, up, preferred_element_type=jnp.float32)
    updates = updates.astype(jnp.bfloat16).astype(jnp.float32)
    base = keep[...] + got[...]
    out[...] = (base + ADAPTER_SCALE * updates).astype(jnp.bfloat16)


def gather(
    tokens,
    base_key_weight,
    stacked_down_weight,
    stacked_up_weight,
    request_adapter_owner,
    request_adapter_slot,
):
    rows, features = tokens.shape
    groups, owners, shares = (lax.axis_size(name) for name in AXES)
    columns = stacked_down_weight.shape[1]
    keys = stacked_up_weight.shape[1]
    part = features // groups
    half = columns // keys
    capacity = -(-row_limit(rows) // ID_ROWS) * ID_ROWS

    def narrow(*dims):
        return jax.ShapeDtypeStruct(dims, jnp.bfloat16)

    def wide(*dims):
        return jax.ShapeDtypeStruct(dims, jnp.float32)

    own = kernel(
        pack_body,
        narrow(part + columns // half, columns),
        (in_hbm(stacked_down_weight), in_hbm(stacked_up_weight)),
        0,
        (pl.ANY, pl.ANY),
        [pltpu.SemaphoreType.DMA((1 + half,))],
    )
    beside = exchange(own, 0, 0, BESIDE)
    mirror = exchange(own, 0, 0, MIDDLE)

    tok_own, tok_away = kernel(
        split_body,
        [narrow(rows + ID_ROWS, part)] * groups,
        (
            in_hbm(tokens),
            in_hbm(request_adapter_owner.reshape(1, rows)),
            in_hbm(request_adapter_slot),
            own,
        ),
        0,
        (pl.ANY, pl.ANY, pl.ANY, pl.ANY),
        [
            pltpu.VMEM((1, rows), jnp.int32),
            pltpu.VMEM((rows,), jnp.int32),
            pltpu.SemaphoreType.DMA((4,)),
        ],
    )
    token_parts = [tok_own, exchange(tok_away, 1, 0, SAME)]
    hop_own, hop_away, places = kernel(
        functools.partial(hop_body, rows, capacity),
        [narrow(capacity + ID_ROWS, part)] * groups
        + [narrow(capacity, rows)],
        (tok_own, tok_away),
        2 * rows * features * capacity,
    )

    keep, give = kernel(
        functools.partial(base_body, 2, rows),
        [wide(rows, shares * keys // 2)] * 2,
        (tok_own, tok_away, base_key_weight, places),
        2 * rows * features * shares * keys,
        (None, None, None, pl.ANY),
        [pltpu.VMEM((rows, shares * keys), jnp.float32)],
    )
    got = exchange(give, 0, 2, SAME)

    inside = exchange(after(beside, places), 0, 0, MIDDLE)
    outside = exchange(mirror, 0, 0, OUTWARD)
    hops = [
        exchange(after(hop_own, beside), 0, 0, INWARD),
        exchange(hop_away, 1, 0, INWARD),
    ]

    folded, mask, numbers, ups, keep, give, places_away = kernel(
        functools.partial(early_body, (0, 3, 1), part, rows),
        [
            wide(groups, rows, LANES),
            wide(groups, rows, columns),
            wide(rows, 1),
            narrow(3, columns, keys),
            wide(rows, keys),
            wide(rows, keys),
            narrow(capacity, rows),
        ],
        (*token_parts, own, mirror, beside, keep, got),
        scratch=[pltpu.VMEM((rows, 2 * keys), jnp.float32)],
        light=True,
    )
    hop_masks, latest = [], folded
    for hop, urgency in zip(hops[:1], HOP_URGENCY):
        latest = kernel(
            functools.partial(hop_mask_body, capacity),
            wide(capacity, columns),
            (hop, latest),
            urgency,
            (None, pl.ANY),
        )
        hop_masks.append(latest)
    low_shape = wide(ADAPTER_RANK, rows)
    low, low_away, hop_sums, last_up = kernel(
        functools.partial(last_body, part, rows, capacity),
        [low_shape, low_shape, wide(groups, ADAPTER_RANK, capacity), narrow(columns, keys)],
        (*token_parts, *hops, *hop_masks, folded, mask, inside, outside),
        2 * groups * (rows + capacity) * part * columns,
    )

    back = exchange(hop_sums, 0, 0, BESIDE)
    distant = exchange(last_up, 0, 0, BESIDE)
    low, low_away = kernel(
        merge_body, [low_shape, low_shape], (low, low_away, places, places_away, back)
    )

    near_far = exchange(low_away, 1, 2, SAME)
    near = exchange(low_away, 1, 0, SAME)
    far = exchange(low, 0, 2, SAME)
    low = kernel(near_body, low_shape, (low, near_far, near, far))
    got = exchange(give, 0, 1, SAME)
    low_far = exchange(low, 0, 1, SAME)
    return kernel(
        finish_body, narrow(rows, keys), (low, low_far, keep, got, numbers, ups, last_up, distant)
    )


def row_limit(rows):
    return max(2, 3 * rows // (2 * lax.axis_size("adapter")))


def local(*args):
    rows, columns = args[0].shape[0], args[2].shape[1]
    groups, owners, shares = (lax.axis_size(name) for name in AXES)
    fits = owners == OWNERS and groups == 2 and shares == 4
    travels = fits and columns <= groups * row_limit(rows)
    return (gather if travels else dispatch)(*args)


def solution(mesh):
    placed = (
        P(("groups", "adapter"), "mp"),
        P("mp", None),
        P("mp", "adapter"),
        P("adapter", "mp"),
        P(("groups", "adapter"), None),
        P(("groups", "adapter")),
    )
    return jax.shard_map(
        local, mesh=mesh, in_specs=placed, out_specs=P(("groups", "adapter"), "mp"), check_vma=False
    )
```

```python
import functools

import jax
import jax.numpy as jnp
from jax import lax
from jax.experimental import pallas as pl
from jax.experimental.pallas import tpu as pltpu
from jax.sharding import PartitionSpec as P

ADAPTER_RANK = 16


ADAPTER_SCALE = 2.0


def dispatch(
    tokens,
    base_key_weight,
    stacked_down_weight,
    stacked_up_weight,
    request_adapter_owner,
    request_adapter_slot,
):
    rows_here = tokens.shape[0]
    feature_share = tokens.shape[1]
    owner_count = lax.axis_size("adapter")
    capacity = max(2, 3 * rows_here // (2 * owner_count))
    local_adapters = stacked_down_weight.shape[1] // ADAPTER_RANK
    key_output_share = stacked_up_weight.shape[1]
    owners = request_adapter_owner.reshape(-1)
    onehot = (owners[:, None] == jnp.arange(owner_count, dtype=jnp.int32)[None, :]).astype(
        jnp.int32
    )
    before = jnp.sum((jnp.cumsum(onehot, axis=0) - onehot) * onehot, axis=1)
    places = owners * capacity + before
    send_rows = (
        jnp.zeros((owner_count * capacity, feature_share), jnp.bfloat16).at[places].set(tokens)
    )
    send_rows = send_rows.reshape(owner_count, capacity, feature_share)
    send_slots = (
        jnp.full((owner_count * capacity,), -1, jnp.int32).at[places].set(request_adapter_slot)
    )
    send_slots = send_slots.reshape(owner_count, capacity)
    input_rows = lax.all_to_all(send_rows, "adapter", split_axis=0, concat_axis=0, tiled=True)
    slots_in = lax.all_to_all(send_slots, "adapter", split_axis=0, concat_axis=0, tiled=True)
    key_projection_output = jnp.einsum(
        "rzq,qt->rzt", input_rows, stacked_down_weight, preferred_element_type=jnp.float32
    )
    key_projection_output = key_projection_output.reshape(
        input_rows.shape[0], input_rows.shape[1], local_adapters, ADAPTER_RANK
    )
    chosen = slots_in[:, :, None] == jnp.arange(local_adapters, dtype=jnp.int32)[None, None, :]
    partial_low = jnp.sum(jnp.where(chosen[:, :, :, None], key_projection_output, 0.0), axis=2)
    shrunk = lax.psum(partial_low, "mp")
    shrunk_bf = shrunk.astype(jnp.bfloat16)
    returned = lax.all_to_all(shrunk_bf, "adapter", split_axis=0, concat_axis=0, tiled=True)
    low_rows = returned.reshape(owner_count * capacity, ADAPTER_RANK)[places]
    gathered_up_weight = lax.all_gather(stacked_up_weight, "adapter", axis=0, tiled=True)
    adapter_ids = owners * local_adapters + request_adapter_slot
    up_taken = gathered_up_weight.reshape(-1, ADAPTER_RANK, key_output_share)[adapter_ids]
    adapter_updates = jnp.einsum(
        "tr,trk->tk", low_rows, up_taken, preferred_element_type=jnp.float32
    ).astype(jnp.bfloat16)
    base_output_share = lax.psum_scatter(
        lax.dot_general(
            base_key_weight, tokens, (((0,), (1,)), ((), ())), preferred_element_type=jnp.float32
        ),
        "mp",
        scatter_dimension=0,
        tiled=True,
    )
    return (base_output_share.T + ADAPTER_SCALE * adapter_updates.astype(jnp.float32)).astype(
        jnp.bfloat16
    )


AXES = ("groups", "adapter", "mp")
ID_ROWS = 16
HOP_URGENCY = (30 * 10**8, 0)
OWNERS = 4
LANES = 128
NT = (((1,), (1,)), ((), ()))
TN = (((0,), (0,)), ((), ()))


def exchange(x, group_bits, share_bits, owners):
    groups, count, shares = (lax.axis_size(name) for name in AXES)

    def number(g, a, m):
        return (g * count + a) * shares + m

    pairs = [
        (number(g, a, m), number(g ^ group_bits, b, m ^ share_bits))
        for g in range(groups)
        for a, b in owners
        for m in range(shares)
    ]
    return lax.ppermute(x, AXES, pairs)


SAME = tuple((a, a) for a in range(OWNERS))
BESIDE = ((0, 1), (1, 0), (2, 3), (3, 2))
MIDDLE = ((0, 0), (1, 2), (2, 1), (3, 3))
OUTWARD = ((1, 0), (2, 3))
INWARD = ((0, 1), (3, 2))


def after(x, *others):
    return lax.optimization_barrier((x, *others))[0]


def in_hbm(x):
    return pltpu.with_memory_space_constraint(x, pltpu.HBM)


def kernel(body, outs, operands, flops=0, spaces=None, scratch=(), light=False):
    inner = pl.BlockSpec(memory_space=pltpu.VMEM)
    specs = [inner if s is None else pl.BlockSpec(memory_space=s) for s in spaces or ()]
    touched = sum(x.size * x.dtype.itemsize for x in jax.tree.leaves((operands, outs)))
    return pl.pallas_call(
        body,
        out_shape=outs,
        in_specs=specs or [inner] * len(operands),
        out_specs=jax.tree.map(lambda _: inner, outs),
        scratch_shapes=scratch,
        compiler_params=pltpu.CompilerParams(vmem_limit_bytes=16 * 1024 * 1024),
        cost_estimate=pl.CostEstimate(
            flops=flops, bytes_accessed=0 if light else touched, transcendentals=0
        ),
    )(*operands)


def pack_body(down, up, out, sems):
    g = lax.axis_index("groups")
    columns, keys = down.shape[1], up.shape[1]
    count = columns // keys
    size = up.shape[0] // count
    part = out.shape[0] - size
    mine = down.at[pl.ds(pl.multiple_of(g * part, part), part), :]
    copies = [pltpu.make_async_copy(mine, out.at[pl.ds(0, part), :], sems.at[count])]
    for k in range(count):
        copies.append(
            pltpu.make_async_copy(
                up.at[pl.ds(k * size, size), :],
                out.at[pl.ds(part, size), pl.ds(k * keys, keys)],
                sems.at[k],
            )
        )
    for copy in copies:
        copy.start()
    for copy in copies:
        copy.wait()


def split_body(tokens, owner_in, slot_in, _, own, away, owner, slot, sems):
    g = lax.axis_index("groups")
    rows, part = tokens.shape[0], own.shape[1]
    copies = []
    for n, (out, half) in enumerate(((own, g), (away, 1 - g))):
        taken = tokens.at[:, pl.ds(pl.multiple_of(half * part, part), part)]
        copies.append(pltpu.make_async_copy(taken, out.at[pl.ds(0, rows), :], sems.at[n]))
    id_copies = [
        pltpu.make_async_copy(owner_in, owner, sems.at[2]),
        pltpu.make_async_copy(slot_in, slot, sems.at[3]),
    ]
    for copy in id_copies + copies:
        copy.start()
    for copy in id_copies:
        copy.wait()
    row = lax.broadcasted_iota(jnp.int32, (ID_ROWS, rows), 0)
    ids = jnp.where(row == 0, owner[...], jnp.where(row == 1, slot[...].reshape(1, rows), 0))
    ids = ids.astype(jnp.float32).astype(jnp.bfloat16)
    for out in (own, away):
        out[rows:, :rows] = ids
        out[rows:, rows:] = jnp.zeros((ID_ROWS, part - rows), jnp.bfloat16)
    for copy in copies:
        copy.wait()


def hop_body(rows, capacity, own, away, own_out, away_out, places):
    a = lax.axis_index("adapter")
    part = own.shape[1]
    ids = own[rows:, :rows]
    match = (ids.astype(jnp.float32) == (OWNERS - 1 - a).astype(jnp.float32)).astype(jnp.bfloat16)
    earlier = lax.broadcasted_iota(jnp.int32, (rows, rows), 0) < lax.broadcasted_iota(
        jnp.int32, (rows, rows), 1
    )
    rank = jnp.dot(match, earlier.astype(jnp.bfloat16), preferred_element_type=jnp.float32)
    place = lax.broadcasted_iota(jnp.int32, (capacity, rows), 0).astype(jnp.float32)
    taken = (place == rank[0:1]) & (match[0:1].astype(jnp.float32) > 0)
    chosen = taken.astype(jnp.bfloat16)
    places[...] = chosen
    kept = lax.dot_general(ids, chosen, NT, preferred_element_type=jnp.float32)
    for tokens, out in ((own, own_out), (away, away_out)):
        packed = jnp.dot(chosen, tokens[:rows, :], preferred_element_type=jnp.float32)
        out[:capacity, :] = packed.astype(jnp.bfloat16)
        out[capacity:, :] = jnp.zeros((ID_ROWS, part), jnp.bfloat16)
        out[capacity:, :capacity] = kept.astype(jnp.bfloat16)


def base_body(bit, rows, own, away, weights, _, keep, give, base):
    g = lax.axis_index("groups")
    part = own.shape[1]
    total = jnp.zeros(base.shape, jnp.float32)
    for tokens, half in ((own, g), (away, 1 - g)):
        part_weights = weights[pl.ds(pl.multiple_of(half * part, part), part), :]
        total = total + jnp.dot(tokens[:rows, :], part_weights, preferred_element_type=jnp.float32)
    base[...] = total
    halves(base, bit, keep, give)


def halves(base, bit, keep, give):
    m = lax.axis_index("mp")
    width = keep.shape[1]
    side = (m // bit) % 2
    keep[...] = base[:, pl.ds(pl.multiple_of(side * width, width), width)]
    give[...] = base[:, pl.ds(pl.multiple_of((1 - side) * width, width), width)]


def id_columns(rows_ref, start, count):
    eye = (
        lax.broadcasted_iota(jnp.int32, (ID_ROWS, ID_ROWS), 0)
        == lax.broadcasted_iota(jnp.int32, (ID_ROWS, ID_ROWS), 1)
    ).astype(jnp.bfloat16)
    ids = lax.dot_general(
        rows_ref[start : start + ID_ROWS, :count], eye, TN, preferred_element_type=jnp.float32
    )
    return ids[:, 0:1], ids[:, 1:2]


def adapters(rows, columns):
    column = lax.broadcasted_iota(jnp.int32, (rows, columns), 1)
    return (column // ADAPTER_RANK).astype(jnp.float32)


def fold(wide):
    folded = wide[:, :LANES]
    for k in range(1, wide.shape[1] // LANES):
        folded = folded + wide[:, k * LANES : (k + 1) * LANES]
    return folded


def low_rank(folded):
    turned = folded.T
    low = turned[:ADAPTER_RANK]
    for k in range(1, LANES // ADAPTER_RANK):
        low = low + turned[k * ADAPTER_RANK : (k + 1) * ADAPTER_RANK]
    return low


def stacked(wide, keys):
    return jnp.concatenate([wide[:, k : k + keys] for k in range(0, wide.shape[1], keys)], axis=0)


def early_body(bits, part, rows, *refs):
    groups = lax.axis_size("groups")
    a = lax.axis_index("adapter")
    token_refs, rest = refs[:groups], refs[groups:]
    blocks, rest = rest[: len(bits)], rest[len(bits) :]
    kept, got, folded, mask, named_by, ups, keep, give, base = rest
    base[...] = kept[...] + got[...]
    halves(base, 1, keep, give)
    columns = blocks[0].shape[1]
    for n, block in enumerate(blocks):
        ups[n] = stacked(block[part:, :], ups.shape[2])
    adapter = adapters(rows, columns)
    for n, tokens in enumerate(token_refs):
        owner, slot = id_columns(tokens, rows, rows)
        if n == 0:
            for bit in range(OWNERS):
                named = (owner == (a ^ bit).astype(jnp.float32)) & (adapter == slot)
                named_by[bit] = named.astype(jnp.float32).astype(jnp.bfloat16)
        right = adapter == slot
        picked = jnp.zeros((rows, columns), jnp.float32)
        for bit, block in zip(bits, blocks):
            wide = jnp.dot(tokens[:rows, :], block[:part, :], preferred_element_type=jnp.float32)
            number = jnp.where((bit != 3) | (a == 1) | (a == 2), a ^ bit, -1)
            picked = jnp.where(owner == number.astype(jnp.float32), wide, picked)
        folded[n] = fold(jnp.where(right, picked, 0.0))
        mask[n] = jnp.where(owner == (a ^ 2).astype(jnp.float32), right.astype(jnp.float32), 0.0)


def hop_mask_body(capacity, hop, _, out):
    _, slot = id_columns(hop, capacity, capacity)
    out[...] = (adapters(capacity, out.shape[1]) == slot).astype(jnp.float32)


def last_body(part, rows, capacity, *refs):
    groups = lax.axis_size("groups")
    a = lax.axis_index("adapter")
    token_refs, rest = refs[:groups], refs[groups:]
    hops, rest = rest[:groups], rest[groups:]
    hop_mask, rest = rest[0], rest[1:]
    folded, mask, inside, outside, low, hop_low, away, last_up = rest
    columns = inside.shape[1]

    def finish(block):
        for n, tokens in enumerate(token_refs):
            wide = jnp.dot(tokens[:rows, :], block[:part, :], preferred_element_type=jnp.float32)
            kept = fold(jnp.where(mask[n] > 0, wide, 0.0))
            if n:
                away[:, :rows] = low_rank(folded[n] + kept)
            else:
                low[...] = low_rank(folded[n] + kept)

    middle = (a == 1) | (a == 2)

    @pl.when(middle)
    def _():
        finish(inside)
        last_up[...] = stacked(inside[part:, :], last_up.shape[1])
        for n, hop in enumerate(hops):
            wide = jnp.dot(hop[:capacity, :], inside[:part, :], preferred_element_type=jnp.float32)
            if n:
                _, slot = id_columns(hop, capacity, capacity)
                wanted = adapters(capacity, columns) == slot
            else:
                wanted = hop_mask[...] > 0
            kept = fold(jnp.where(wanted, wide, 0.0))
            rest_rows = -capacity % LANES
            kept = jnp.concatenate([kept, jnp.zeros((rest_rows, LANES), jnp.float32)], axis=0)
            if n:
                away[:, rows:] = low_rank(kept)[:, :capacity]
            else:
                hop_low[...] = low_rank(kept)[:, :capacity]

    @pl.when(jnp.logical_not(middle))
    def _():
        finish(outside)
        last_up[...] = stacked(outside[part:, :], last_up.shape[1])
        hop_low[...] = jnp.zeros(hop_low.shape, jnp.float32)
        away[:, rows:] = jnp.zeros(hop_low.shape, jnp.float32)


def near_body(low, hop_low, near, low_out, hop_out, hop_wide):
    rows = low.shape[1]
    capacity = hop_low.shape[1]
    low_out[...] = low[...] + near[:, :rows]
    hop = hop_low[...] + near[:, rows:]
    hop_out[...] = hop
    hop_wide[...] = jnp.zeros(hop_wide.shape, jnp.float32)
    hop_wide[:, :capacity] = hop


def merge_body(low, far, places, hop_far, hop, out):
    capacity = places.shape[0]
    back = hop[...] + hop_far[:, :capacity]
    spread = jnp.zeros(low.shape, jnp.float32)
    for _ in range(3):
        piece = back.astype(jnp.bfloat16)
        back = back - piece.astype(jnp.float32)
        spread = spread + jnp.dot(piece, places[...], preferred_element_type=jnp.float32)
    out[...] = low[...] + far[...] + spread


def finish_body(near, far, keep, got, named_by, ups, last_up, distant, out):
    a = lax.axis_index("adapter")
    rows = out.shape[0]
    columns = last_up.shape[0]
    column = lax.broadcasted_iota(jnp.int32, (ADAPTER_RANK, columns), 1)
    row = lax.broadcasted_iota(jnp.int32, (ADAPTER_RANK, columns), 0)
    repeat = (lax.rem(column, ADAPTER_RANK) == row).astype(jnp.bfloat16)
    shrunk = (near[...] + far[...]).astype(jnp.bfloat16)
    spread = lax.dot_general(shrunk, repeat, TN, preferred_element_type=jnp.float32)
    spread = spread.astype(jnp.bfloat16)
    middle = (a == 1) | (a == 2)
    mirrored = jnp.where(middle, ups[1].astype(jnp.float32), distant[...].astype(jnp.float32))
    blocks = ((0, ups[0]), (1, ups[2]), (2, last_up[...]), (3, mirrored.astype(jnp.bfloat16)))
    updates = jnp.zeros(out.shape, jnp.float32)
    for bit, up in blocks:
        chosen = spread * named_by[bit]
        updates = updates + jnp.dot(chosen, up, preferred_element_type=jnp.float32)
    updates = updates.astype(jnp.bfloat16).astype(jnp.float32)
    base = keep[...] + got[...]
    out[...] = (base + ADAPTER_SCALE * updates).astype(jnp.bfloat16)


def gather(
    tokens,
    base_key_weight,
    stacked_down_weight,
    stacked_up_weight,
    request_adapter_owner,
    request_adapter_slot,
):
    rows, features = tokens.shape
    groups, owners, shares = (lax.axis_size(name) for name in AXES)
    columns = stacked_down_weight.shape[1]
    keys = stacked_up_weight.shape[1]
    part = features // groups
    half = columns // keys
    capacity = -(-row_limit(rows) // ID_ROWS) * ID_ROWS

    def narrow(*dims):
        return jax.ShapeDtypeStruct(dims, jnp.bfloat16)

    def wide(*dims):
        return jax.ShapeDtypeStruct(dims, jnp.float32)

    own = kernel(
        pack_body,
        narrow(part + columns // half, columns),
        (in_hbm(stacked_down_weight), in_hbm(stacked_up_weight)),
        0,
        (pl.ANY, pl.ANY),
        [pltpu.SemaphoreType.DMA((1 + half,))],
    )
    beside = exchange(own, 0, 0, BESIDE)
    mirror = exchange(own, 0, 0, MIDDLE)

    tok_own, tok_away = kernel(
        split_body,
        [narrow(rows + ID_ROWS, part)] * groups,
        (
            in_hbm(tokens),
            in_hbm(request_adapter_owner.reshape(1, rows)),
            in_hbm(request_adapter_slot),
            own,
        ),
        0,
        (pl.ANY, pl.ANY, pl.ANY, pl.ANY),
        [
            pltpu.VMEM((1, rows), jnp.int32),
            pltpu.VMEM((rows,), jnp.int32),
            pltpu.SemaphoreType.DMA((4,)),
        ],
    )
    token_parts = [tok_own, exchange(tok_away, 1, 0, SAME)]
    hop_own, hop_away, places = kernel(
        functools.partial(hop_body, rows, capacity),
        [narrow(capacity + ID_ROWS, part)] * groups
        + [narrow(capacity, rows)],
        (tok_own, tok_away),
        2 * rows * features * capacity,
    )

    keep, give = kernel(
        functools.partial(base_body, 2, rows),
        [wide(rows, shares * keys // 2)] * 2,
        (tok_own, tok_away, base_key_weight, places),
        2 * rows * features * shares * keys,
        (None, None, None, pl.ANY),
        [pltpu.VMEM((rows, shares * keys), jnp.float32)],
    )
    got = exchange(give, 0, 2, SAME)

    inside = exchange(after(beside, places), 0, 0, MIDDLE)
    outside = exchange(mirror, 0, 0, OUTWARD)
    hops = [
        exchange(after(hop_own, beside), 0, 0, INWARD),
        exchange(hop_away, 1, 0, INWARD),
    ]

    folded, mask, named_by, ups, keep, give = kernel(
        functools.partial(early_body, (0, 3, 1), part, rows),
        [
            wide(groups, rows, LANES),
            wide(groups, rows, columns),
            narrow(owners, rows, columns),
            narrow(3, columns, keys),
            wide(rows, keys),
            wide(rows, keys),
        ],
        (*token_parts, own, mirror, beside, keep, got),
        scratch=[pltpu.VMEM((rows, 2 * keys), jnp.float32)],
        light=True,
    )
    hop_masks, latest = [], folded
    for hop, urgency in zip(hops[:1], HOP_URGENCY):
        latest = kernel(
            functools.partial(hop_mask_body, capacity),
            wide(capacity, columns),
            (hop, latest),
            urgency,
            (None, pl.ANY),
        )
        hop_masks.append(latest)
    low, hop_low, away, last_up = kernel(
        functools.partial(last_body, part, rows, capacity),
        [
            wide(ADAPTER_RANK, rows),
            wide(ADAPTER_RANK, capacity),
            wide(ADAPTER_RANK, rows + capacity),
            narrow(columns, keys),
        ],
        (*token_parts, *hops, *hop_masks, folded, mask, inside, outside),
        2 * groups * (rows + capacity) * part * columns,
    )

    near = exchange(away, 1, 0, SAME)
    distant = exchange(last_up, 0, 0, BESIDE)
    low, hop_low, hop_wide = kernel(
        near_body,
        [
            wide(ADAPTER_RANK, rows),
            wide(ADAPTER_RANK, capacity),
            wide(ADAPTER_RANK, rows + LANES),
        ],
        (low, hop_low, near),
    )
    back = exchange(hop_low, 0, 0, BESIDE)
    back_far = exchange(hop_wide, 0, 2, BESIDE)
    low_far = exchange(low, 0, 2, SAME)
    low = kernel(
        merge_body,
        wide(ADAPTER_RANK, rows),
        (low, low_far, places, back_far, back),
    )
    got = exchange(give, 0, 1, SAME)
    low_far = exchange(low, 0, 1, SAME)
    return kernel(
        finish_body, narrow(rows, keys), (low, low_far, keep, got, named_by, ups, last_up, distant)
    )


def row_limit(rows):
    return max(2, 3 * rows // (2 * lax.axis_size("adapter")))


def local(*args):
    rows, columns = args[0].shape[0], args[2].shape[1]
    groups, owners, shares = (lax.axis_size(name) for name in AXES)
    fits = owners == OWNERS and groups == 2 and shares == 4
    travels = fits and columns <= groups * row_limit(rows)
    return (gather if travels else dispatch)(*args)


def solution(mesh):
    placed = (
        P(("groups", "adapter"), "mp"),
        P("mp", None),
        P("mp", "adapter"),
        P("adapter", "mp"),
        P(("groups", "adapter"), None),
        P(("groups", "adapter")),
    )
    return jax.shard_map(
        local, mesh=mesh, in_specs=placed, out_specs=P(("groups", "adapter"), "mp"), check_vma=False
    )
```

```python
import functools

import jax
import jax.numpy as jnp
from jax import lax
from jax.experimental import pallas as pl
from jax.experimental.pallas import tpu as pltpu
from jax.sharding import PartitionSpec as P

ADAPTER_RANK = 16


ADAPTER_SCALE = 2.0


def dispatch(
    tokens,
    base_key_weight,
    stacked_down_weight,
    stacked_up_weight,
    request_adapter_owner,
    request_adapter_slot,
):
    rows_here = tokens.shape[0]
    feature_share = tokens.shape[1]
    owner_count = lax.axis_size("adapter")
    capacity = max(2, 3 * rows_here // (2 * owner_count))
    local_adapters = stacked_down_weight.shape[1] // ADAPTER_RANK
    key_output_share = stacked_up_weight.shape[1]
    owners = request_adapter_owner.reshape(-1)
    onehot = (owners[:, None] == jnp.arange(owner_count, dtype=jnp.int32)[None, :]).astype(
        jnp.int32
    )
    before = jnp.sum((jnp.cumsum(onehot, axis=0) - onehot) * onehot, axis=1)
    places = owners * capacity + before
    send_rows = (
        jnp.zeros((owner_count * capacity, feature_share), jnp.bfloat16).at[places].set(tokens)
    )
    send_rows = send_rows.reshape(owner_count, capacity, feature_share)
    send_slots = (
        jnp.full((owner_count * capacity,), -1, jnp.int32).at[places].set(request_adapter_slot)
    )
    send_slots = send_slots.reshape(owner_count, capacity)
    input_rows = lax.all_to_all(send_rows, "adapter", split_axis=0, concat_axis=0, tiled=True)
    slots_in = lax.all_to_all(send_slots, "adapter", split_axis=0, concat_axis=0, tiled=True)
    key_projection_output = jnp.einsum(
        "rzq,qt->rzt", input_rows, stacked_down_weight, preferred_element_type=jnp.float32
    )
    key_projection_output = key_projection_output.reshape(
        input_rows.shape[0], input_rows.shape[1], local_adapters, ADAPTER_RANK
    )
    chosen = slots_in[:, :, None] == jnp.arange(local_adapters, dtype=jnp.int32)[None, None, :]
    partial_low = jnp.sum(jnp.where(chosen[:, :, :, None], key_projection_output, 0.0), axis=2)
    shrunk = lax.psum(partial_low, "mp")
    shrunk_bf = shrunk.astype(jnp.bfloat16)
    returned = lax.all_to_all(shrunk_bf, "adapter", split_axis=0, concat_axis=0, tiled=True)
    low_rows = returned.reshape(owner_count * capacity, ADAPTER_RANK)[places]
    gathered_up_weight = lax.all_gather(stacked_up_weight, "adapter", axis=0, tiled=True)
    adapter_ids = owners * local_adapters + request_adapter_slot
    up_taken = gathered_up_weight.reshape(-1, ADAPTER_RANK, key_output_share)[adapter_ids]
    adapter_updates = jnp.einsum(
        "tr,trk->tk", low_rows, up_taken, preferred_element_type=jnp.float32
    ).astype(jnp.bfloat16)
    base_output_share = lax.psum_scatter(
        lax.dot_general(
            base_key_weight, tokens, (((0,), (1,)), ((), ())), preferred_element_type=jnp.float32
        ),
        "mp",
        scatter_dimension=0,
        tiled=True,
    )
    return (base_output_share.T + ADAPTER_SCALE * adapter_updates.astype(jnp.float32)).astype(
        jnp.bfloat16
    )


AXES = ("groups", "adapter", "mp")
ID_ROWS = 16
HOP_URGENCY = (42 * 10**8, 0)
OWNERS = 4
LANES = 128
NT = (((1,), (1,)), ((), ()))
TN = (((0,), (0,)), ((), ()))


def exchange(x, group_bits, share_bits, owners):
    groups, count, shares = (lax.axis_size(name) for name in AXES)

    def number(g, a, m):
        return (g * count + a) * shares + m

    pairs = [
        (number(g, a, m), number(g ^ group_bits, b, m ^ share_bits))
        for g in range(groups)
        for a, b in owners
        for m in range(shares)
    ]
    return lax.ppermute(x, AXES, pairs)


SAME = tuple((a, a) for a in range(OWNERS))
BESIDE = ((0, 1), (1, 0), (2, 3), (3, 2))
MIDDLE = ((0, 0), (1, 2), (2, 1), (3, 3))
OUTWARD = ((1, 0), (2, 3))
INWARD = ((0, 1), (3, 2))


def after(x, *others):
    return lax.optimization_barrier((x, *others))[0]


def in_hbm(x):
    return pltpu.with_memory_space_constraint(x, pltpu.HBM)


def kernel(body, outs, operands, flops=0, spaces=None, scratch=(), light=False):
    inner = pl.BlockSpec(memory_space=pltpu.VMEM)
    specs = [inner if s is None else pl.BlockSpec(memory_space=s) for s in spaces or ()]
    touched = sum(x.size * x.dtype.itemsize for x in jax.tree.leaves((operands, outs)))
    return pl.pallas_call(
        body,
        out_shape=outs,
        in_specs=specs or [inner] * len(operands),
        out_specs=jax.tree.map(lambda _: inner, outs),
        scratch_shapes=scratch,
        compiler_params=pltpu.CompilerParams(vmem_limit_bytes=16 * 1024 * 1024),
        cost_estimate=pl.CostEstimate(
            flops=flops, bytes_accessed=0 if light else touched, transcendentals=0
        ),
    )(*operands)


def pack_body(down, up, out, sems):
    g = lax.axis_index("groups")
    columns, keys = down.shape[1], up.shape[1]
    count = columns // keys
    size = up.shape[0] // count
    part = out.shape[0] - size
    mine = down.at[pl.ds(pl.multiple_of(g * part, part), part), :]
    copies = [pltpu.make_async_copy(mine, out.at[pl.ds(0, part), :], sems.at[count])]
    for k in range(count):
        copies.append(
            pltpu.make_async_copy(
                up.at[pl.ds(k * size, size), :],
                out.at[pl.ds(part, size), pl.ds(k * keys, keys)],
                sems.at[k],
            )
        )
    for copy in copies:
        copy.start()
    for copy in copies:
        copy.wait()


def split_body(tokens, owner_in, slot_in, _, own, away, owner, slot, sems):
    g = lax.axis_index("groups")
    rows, part = tokens.shape[0], own.shape[1]
    copies = []
    for n, (out, half) in enumerate(((own, g), (away, 1 - g))):
        taken = tokens.at[:, pl.ds(pl.multiple_of(half * part, part), part)]
        copies.append(pltpu.make_async_copy(taken, out.at[pl.ds(0, rows), :], sems.at[n]))
    id_copies = [
        pltpu.make_async_copy(owner_in, owner, sems.at[2]),
        pltpu.make_async_copy(slot_in, slot, sems.at[3]),
    ]
    for copy in id_copies + copies:
        copy.start()
    for copy in id_copies:
        copy.wait()
    row = lax.broadcasted_iota(jnp.int32, (ID_ROWS, rows), 0)
    ids = jnp.where(row == 0, owner[...], jnp.where(row == 1, slot[...].reshape(1, rows), 0))
    ids = ids.astype(jnp.float32).astype(jnp.bfloat16)
    for out in (own, away):
        out[rows:, :rows] = ids
        out[rows:, rows:] = jnp.zeros((ID_ROWS, part - rows), jnp.bfloat16)
    for copy in copies:
        copy.wait()


def hop_body(rows, capacity, own, away, own_out, away_out, places):
    a = lax.axis_index("adapter")
    part = own.shape[1]
    ids = own[rows:, :rows]
    match = (ids.astype(jnp.float32) == (OWNERS - 1 - a).astype(jnp.float32)).astype(jnp.bfloat16)
    earlier = lax.broadcasted_iota(jnp.int32, (rows, rows), 0) < lax.broadcasted_iota(
        jnp.int32, (rows, rows), 1
    )
    rank = jnp.dot(match, earlier.astype(jnp.bfloat16), preferred_element_type=jnp.float32)
    place = lax.broadcasted_iota(jnp.int32, (capacity, rows), 0).astype(jnp.float32)
    taken = (place == rank[0:1]) & (match[0:1].astype(jnp.float32) > 0)
    chosen = taken.astype(jnp.bfloat16)
    places[...] = chosen
    kept = lax.dot_general(ids, chosen, NT, preferred_element_type=jnp.float32)
    for tokens, out in ((own, own_out), (away, away_out)):
        packed = jnp.dot(chosen, tokens[:rows, :], preferred_element_type=jnp.float32)
        out[:capacity, :] = packed.astype(jnp.bfloat16)
        out[capacity:, :] = jnp.zeros((ID_ROWS, part), jnp.bfloat16)
        out[capacity:, :capacity] = kept.astype(jnp.bfloat16)


def base_body(bit, rows, own, away, weights, _, keep, give, base):
    g = lax.axis_index("groups")
    part = own.shape[1]
    total = jnp.zeros(base.shape, jnp.float32)
    for tokens, half in ((own, g), (away, 1 - g)):
        part_weights = weights[pl.ds(pl.multiple_of(half * part, part), part), :]
        total = total + jnp.dot(tokens[:rows, :], part_weights, preferred_element_type=jnp.float32)
    base[...] = total
    halves(base, bit, keep, give)


def halves(base, bit, keep, give):
    m = lax.axis_index("mp")
    width = keep.shape[1]
    side = (m // bit) % 2
    keep[...] = base[:, pl.ds(pl.multiple_of(side * width, width), width)]
    give[...] = base[:, pl.ds(pl.multiple_of((1 - side) * width, width), width)]


def id_columns(rows_ref, start, count):
    eye = (
        lax.broadcasted_iota(jnp.int32, (ID_ROWS, ID_ROWS), 0)
        == lax.broadcasted_iota(jnp.int32, (ID_ROWS, ID_ROWS), 1)
    ).astype(jnp.bfloat16)
    ids = lax.dot_general(
        rows_ref[start : start + ID_ROWS, :count], eye, TN, preferred_element_type=jnp.float32
    )
    return ids[:, 0:1], ids[:, 1:2]


def adapters(rows, columns):
    column = lax.broadcasted_iota(jnp.int32, (rows, columns), 1)
    return (column // ADAPTER_RANK).astype(jnp.float32)


def fold(wide):
    folded = wide[:, :LANES]
    for k in range(1, wide.shape[1] // LANES):
        folded = folded + wide[:, k * LANES : (k + 1) * LANES]
    return folded


def low_rank(folded):
    turned = folded.T
    low = turned[:ADAPTER_RANK]
    for k in range(1, LANES // ADAPTER_RANK):
        low = low + turned[k * ADAPTER_RANK : (k + 1) * ADAPTER_RANK]
    return low


def stacked(wide, keys):
    return jnp.concatenate([wide[:, k : k + keys] for k in range(0, wide.shape[1], keys)], axis=0)


def early_body(bits, part, rows, *refs):
    groups = lax.axis_size("groups")
    a = lax.axis_index("adapter")
    token_refs, rest = refs[:groups], refs[groups:]
    blocks, rest = rest[: len(bits)], rest[len(bits) :]
    kept, got, folded, mask, named_by, ups, keep, give, base = rest
    base[...] = kept[...] + got[...]
    halves(base, 1, keep, give)
    columns = blocks[0].shape[1]
    for n, block in enumerate(blocks):
        ups[n] = stacked(block[part:, :], ups.shape[2])
    adapter = adapters(rows, columns)
    for n, tokens in enumerate(token_refs):
        owner, slot = id_columns(tokens, rows, rows)
        if n == 0:
            for bit in range(OWNERS):
                named = (owner == (a ^ bit).astype(jnp.float32)) & (adapter == slot)
                named_by[bit] = named.astype(jnp.float32).astype(jnp.bfloat16)
        right = adapter == slot
        picked = jnp.zeros((rows, columns), jnp.float32)
        for bit, block in zip(bits, blocks):
            wide = jnp.dot(tokens[:rows, :], block[:part, :], preferred_element_type=jnp.float32)
            number = jnp.where((bit != 3) | (a == 1) | (a == 2), a ^ bit, -1)
            picked = jnp.where(owner == number.astype(jnp.float32), wide, picked)
        folded[n] = fold(jnp.where(right, picked, 0.0))
        mask[n] = jnp.where(owner == (a ^ 2).astype(jnp.float32), right.astype(jnp.float32), 0.0)


def hop_mask_body(capacity, hop, _, out):
    _, slot = id_columns(hop, capacity, capacity)
    out[...] = (adapters(capacity, out.shape[1]) == slot).astype(jnp.float32)


def last_body(part, rows, capacity, *refs):
    groups = lax.axis_size("groups")
    a = lax.axis_index("adapter")
    token_refs, rest = refs[:groups], refs[groups:]
    hops, rest = rest[:groups], rest[groups:]
    hop_mask, rest = rest[0], rest[1:]
    folded, mask, inside, outside, low, hop_low, away, last_up = rest
    columns = inside.shape[1]

    def finish(block):
        for n, tokens in enumerate(token_refs):
            wide = jnp.dot(tokens[:rows, :], block[:part, :], preferred_element_type=jnp.float32)
            kept = fold(jnp.where(mask[n] > 0, wide, 0.0))
            if n:
                away[:, :rows] = low_rank(folded[n] + kept)
            else:
                low[...] = low_rank(folded[n] + kept)

    middle = (a == 1) | (a == 2)

    @pl.when(middle)
    def _():
        finish(inside)
        last_up[...] = stacked(inside[part:, :], last_up.shape[1])
        for n, hop in enumerate(hops):
            wide = jnp.dot(hop[:capacity, :], inside[:part, :], preferred_element_type=jnp.float32)
            if n:
                _, slot = id_columns(hop, capacity, capacity)
                wanted = adapters(capacity, columns) == slot
            else:
                wanted = hop_mask[...] > 0
            kept = fold(jnp.where(wanted, wide, 0.0))
            rest_rows = -capacity % LANES
            kept = jnp.concatenate([kept, jnp.zeros((rest_rows, LANES), jnp.float32)], axis=0)
            if n:
                away[:, rows:] = low_rank(kept)[:, :capacity]
            else:
                hop_low[...] = low_rank(kept)[:, :capacity]

    @pl.when(jnp.logical_not(middle))
    def _():
        finish(outside)
        last_up[...] = stacked(outside[part:, :], last_up.shape[1])
        hop_low[...] = jnp.zeros(hop_low.shape, jnp.float32)
        away[:, rows:] = jnp.zeros(hop_low.shape, jnp.float32)


def near_body(low, hop_low, near, low_out, hop_out, hop_wide):
    rows = low.shape[1]
    capacity = hop_low.shape[1]
    low_out[...] = low[...] + near[:, :rows]
    hop = hop_low[...] + near[:, rows:]
    hop_out[...] = hop
    hop_wide[...] = jnp.zeros(hop_wide.shape, jnp.float32)
    hop_wide[:, :capacity] = hop


def merge_body(low, far, places, hop_far, hop, out):
    capacity = places.shape[0]
    back = hop[...] + hop_far[:, :capacity]
    spread = jnp.zeros(low.shape, jnp.float32)
    for _ in range(3):
        piece = back.astype(jnp.bfloat16)
        back = back - piece.astype(jnp.float32)
        spread = spread + jnp.dot(piece, places[...], preferred_element_type=jnp.float32)
    out[...] = low[...] + far[...] + spread


def finish_body(near, far, keep, got, named_by, ups, last_up, distant, out):
    a = lax.axis_index("adapter")
    rows = out.shape[0]
    columns = last_up.shape[0]
    column = lax.broadcasted_iota(jnp.int32, (ADAPTER_RANK, columns), 1)
    row = lax.broadcasted_iota(jnp.int32, (ADAPTER_RANK, columns), 0)
    repeat = (lax.rem(column, ADAPTER_RANK) == row).astype(jnp.bfloat16)
    shrunk = (near[...] + far[...]).astype(jnp.bfloat16)
    spread = lax.dot_general(shrunk, repeat, TN, preferred_element_type=jnp.float32)
    spread = spread.astype(jnp.bfloat16)
    middle = (a == 1) | (a == 2)
    mirrored = jnp.where(middle, ups[1].astype(jnp.float32), distant[...].astype(jnp.float32))
    blocks = ((0, ups[0]), (1, ups[2]), (2, last_up[...]), (3, mirrored.astype(jnp.bfloat16)))
    updates = jnp.zeros(out.shape, jnp.float32)
    for bit, up in blocks:
        chosen = spread * named_by[bit]
        updates = updates + jnp.dot(chosen, up, preferred_element_type=jnp.float32)
    updates = updates.astype(jnp.bfloat16).astype(jnp.float32)
    base = keep[...] + got[...]
    out[...] = (base + ADAPTER_SCALE * updates).astype(jnp.bfloat16)


def gather(
    tokens,
    base_key_weight,
    stacked_down_weight,
    stacked_up_weight,
    request_adapter_owner,
    request_adapter_slot,
):
    rows, features = tokens.shape
    groups, owners, shares = (lax.axis_size(name) for name in AXES)
    columns = stacked_down_weight.shape[1]
    keys = stacked_up_weight.shape[1]
    part = features // groups
    half = columns // keys
    capacity = -(-row_limit(rows) // ID_ROWS) * ID_ROWS

    def narrow(*dims):
        return jax.ShapeDtypeStruct(dims, jnp.bfloat16)

    def wide(*dims):
        return jax.ShapeDtypeStruct(dims, jnp.float32)

    own = kernel(
        pack_body,
        narrow(part + columns // half, columns),
        (in_hbm(stacked_down_weight), in_hbm(stacked_up_weight)),
        0,
        (pl.ANY, pl.ANY),
        [pltpu.SemaphoreType.DMA((1 + half,))],
    )
    beside = exchange(own, 0, 0, BESIDE)
    mirror = exchange(own, 0, 0, MIDDLE)

    tok_own, tok_away = kernel(
        split_body,
        [narrow(rows + ID_ROWS, part)] * groups,
        (
            in_hbm(tokens),
            in_hbm(request_adapter_owner.reshape(1, rows)),
            in_hbm(request_adapter_slot),
            own,
        ),
        0,
        (pl.ANY, pl.ANY, pl.ANY, pl.ANY),
        [
            pltpu.VMEM((1, rows), jnp.int32),
            pltpu.VMEM((rows,), jnp.int32),
            pltpu.SemaphoreType.DMA((4,)),
        ],
    )
    token_parts = [tok_own, exchange(tok_away, 1, 0, SAME)]
    hop_own, hop_away, places = kernel(
        functools.partial(hop_body, rows, capacity),
        [narrow(capacity + ID_ROWS, part)] * groups
        + [narrow(capacity, rows)],
        (tok_own, tok_away),
        2 * rows * features * capacity,
    )

    keep, give = kernel(
        functools.partial(base_body, 2, rows),
        [wide(rows, shares * keys // 2)] * 2,
        (tok_own, tok_away, base_key_weight, places),
        2 * rows * features * shares * keys,
        (None, None, None, pl.ANY),
        [pltpu.VMEM((rows, shares * keys), jnp.float32)],
    )
    got = exchange(give, 0, 2, SAME)

    inside = exchange(after(beside, places), 0, 0, MIDDLE)
    outside = exchange(mirror, 0, 0, OUTWARD)
    hops = [
        exchange(after(hop_own, beside), 0, 0, INWARD),
        exchange(hop_away, 1, 0, INWARD),
    ]

    folded, mask, named_by, ups, keep, give = kernel(
        functools.partial(early_body, (0, 3, 1), part, rows),
        [
            wide(groups, rows, LANES),
            wide(groups, rows, columns),
            narrow(owners, rows, columns),
            narrow(3, columns, keys),
            wide(rows, keys),
            wide(rows, keys),
        ],
        (*token_parts, own, mirror, beside, keep, got),
        scratch=[pltpu.VMEM((rows, 2 * keys), jnp.float32)],
        light=True,
    )
    hop_masks, latest = [], folded
    for hop, urgency in zip(hops[:1], HOP_URGENCY):
        latest = kernel(
            functools.partial(hop_mask_body, capacity),
            wide(capacity, columns),
            (hop, latest),
            urgency,
            (None, pl.ANY),
        )
        hop_masks.append(latest)
    low, hop_low, away, last_up = kernel(
        functools.partial(last_body, part, rows, capacity),
        [
            wide(ADAPTER_RANK, rows),
            wide(ADAPTER_RANK, capacity),
            wide(ADAPTER_RANK, rows + capacity),
            narrow(columns, keys),
        ],
        (*token_parts, *hops, *hop_masks, folded, mask, inside, outside),
        2 * groups * (rows + capacity) * part * columns,
    )

    near = exchange(away, 1, 0, SAME)
    distant = exchange(last_up, 0, 0, BESIDE)
    low, hop_low, hop_wide = kernel(
        near_body,
        [
            wide(ADAPTER_RANK, rows),
            wide(ADAPTER_RANK, capacity),
            wide(ADAPTER_RANK, rows + LANES),
        ],
        (low, hop_low, near),
    )
    back = exchange(hop_low, 0, 0, BESIDE)
    back_far = exchange(hop_wide, 0, 2, BESIDE)
    low_far = exchange(low, 0, 2, SAME)
    low = kernel(
        merge_body,
        wide(ADAPTER_RANK, rows),
        (low, low_far, places, back_far, back),
    )
    got = exchange(give, 0, 1, SAME)
    low_far = exchange(low, 0, 1, SAME)
    return kernel(
        finish_body, narrow(rows, keys), (low, low_far, keep, got, named_by, ups, last_up, distant)
    )


def row_limit(rows):
    return max(2, 3 * rows // (2 * lax.axis_size("adapter")))


def local(*args):
    rows, columns = args[0].shape[0], args[2].shape[1]
    groups, owners, shares = (lax.axis_size(name) for name in AXES)
    fits = owners == OWNERS and groups == 2 and shares == 4
    travels = fits and columns <= groups * row_limit(rows)
    return (gather if travels else dispatch)(*args)


def solution(mesh):
    placed = (
        P(("groups", "adapter"), "mp"),
        P("mp", None),
        P("mp", "adapter"),
        P("adapter", "mp"),
        P(("groups", "adapter"), None),
        P(("groups", "adapter")),
    )
    return jax.shard_map(
        local, mesh=mesh, in_specs=placed, out_specs=P(("groups", "adapter"), "mp"), check_vma=False
    )
```
